32 devices in a mesh: dp: 4 (over y, x), mp: 8 (over z, core).
Axes of the slice: x: 2, y: 2, z: 4, core: 2. Of those that a mesh axis runs over, the one named last changes fastest.
Arguments:
- layer_input: bfloat16 [8192, 2048], P(('dp', 'mp')), may hold values from -6 to 6
- width_choice: int32 [8192, 2], P('dp'), may hold values from 0 to 3
- routed_flag: int32 [8192, 2], P('dp'), may hold values 0 or 1
- mixer_gain: float32 [2048], replicated, may hold values from 0.1 to 1.9
- mixer_router: float32 [2048, 4], replicated, may hold values from -0.09375 to 0.09375
- attention_weight: bfloat16 [2048, 3, 2048], P(None, None, 'mp'), may hold values from -0.125 to 0.125
- output_weight: bfloat16 [2048, 2048], P('mp'), may hold values from -0.75 to 0.75
- hidden_gain: float32 [2048], replicated, may hold values from 0.1 to 1.9
- hidden_router: float32 [2048, 4], replicated, may hold values from -0.09375 to 0.09375
- up_weight: bfloat16 [2048, 8192], P(None, 'mp'), may hold values from -0.125 to 0.125
- down_weight: bfloat16 [8192, 2048], P('mp'), may hold values from -0.0625 to 0.0625
- out_grad: bfloat16 [8192, 2048], P(('dp', 'mp')), may hold values from -6 to 6
Outputs:
- layer_output: bfloat16 [8192, 2048], P(('dp', 'mp'))
- input_grad: bfloat16 [8192, 2048], P(('dp', 'mp'))
- mixer_gain_grad: float32 [2048], replicated
- mixer_router_grad: float32 [2048, 4], replicated
- attention_weight_grad: float32 [2048, 3, 2048], P(None, None, 'mp')
- output_weight_grad: float32 [2048, 2048], P('mp')
- hidden_gain_grad: float32 [2048], replicated
- hidden_router_grad: float32 [2048, 4], replicated
- up_weight_grad: float32 [2048, 8192], P(None, 'mp')
- down_weight_grad: float32 [8192, 2048], P('mp')
The draws below stay inside these ranges and needn't reach their ends.
All inputs are finite; a program needn't handle non-finite values. No bound on the sum of `routed_flag` on one device may be relied on, other than what follows from the above.
Results may differ from the reference program's by a relative error of at most 0.02.
Values may be sent and summed in bfloat16 or wider, within the bound.
No kernel may reach another device: no remote copies, remote signals or barrier semaphores. Data moves between devices by JAX's collectives and lax.ppermute only.
A program may use at most 192 MiB of HBM per device.

```python
import math
import jax
import jax.numpy as jnp
from jax import lax

D = 2048
H = 16
HD = 128
FF = 8192
SEQ_LEN = 1024
TOK_DP = 2048
TOKENS = 8192
N_DP = 4


def with_ends(values, own_key, smallest, high):
    place = [jax.random.randint(jax.random.fold_in(own_key, axis), (), 0, length) for axis, length in enumerate(values.shape)]
    widest = values.shape.index(max(values.shape))
    neighbour = place[:widest] + [(place[widest] + 1) % values.shape[widest]] + place[widest + 1:]
    return values.at[tuple(place)].set(smallest).at[tuple(neighbour)].set(high)


def levels(rng, shape, shards, least, top_value):
    def one(axis_at, shards_of):
        steps = jax.random.uniform(jax.random.fold_in(jax.random.fold_in(rng, 6), axis_at), (shards_of,), jnp.float32, least / len(shards), top_value / len(shards))
        return jnp.repeat(jnp.exp(steps), shape[axis_at] // shards_of).reshape((-1,) + (1,) * (len(shape) - axis_at - 1))

    factor_of = one(*shards[0])
    for cut in shards[1:]:
        factor_of = factor_of * one(*cut)
    return factor_of


def normal_values(rng, shape, spread, bound, cuts=(), kind=jnp.bfloat16):
    factor_of = levels(rng, shape, cuts, -0.22, 0.18) if cuts else 1.0
    entries = jax.random.normal(rng, shape, jnp.float32) * spread * factor_of
    return jnp.minimum(jnp.maximum(entries, -bound), bound).astype(kind)


def setup_inputs(seed: int = 0) -> dict:
    streams_of = jax.random.split(jax.random.key(seed), 13)
    layer_input = normal_values(streams_of[0], (TOKENS, D), 1.0, 6.0, ((0, 32),))
    width_choice = with_ends(jax.random.randint(streams_of[1], (TOKENS, 2), 0, 4), jax.random.fold_in(streams_of[1], 1), 0, 3).astype(jnp.int32)
    routed_flag = with_ends((jax.random.randint(streams_of[2], (TOKENS, 2), 0, 2) < 1).astype(jnp.int32), jax.random.fold_in(streams_of[2], 1), 0, 1)
    mixer_gain = jnp.clip(1.0 + 0.18 * jax.random.normal(streams_of[3], (D,), jnp.float32), 0.1, 1.9)
    mixer_router = normal_values(streams_of[4], (D, 4), (2 * D) ** -0.5, 0.09375, (), jnp.float32)
    attention_weight = normal_values(streams_of[5], (D, 3, H * HD), D ** -0.5, 0.125, ((2, 8),))
    output_weight = normal_values(streams_of[6], (H * HD, D), (HD // 2) ** -0.5, 0.75, ((0, 8),))
    hidden_gain = jnp.clip(1.0 + 0.18 * jax.random.normal(streams_of[7], (D,), jnp.float32), 0.1, 1.9)
    hidden_router = normal_values(streams_of[8], (D, 4), (2 * D) ** -0.5, 0.09375, (), jnp.float32)
    up_weight = normal_values(streams_of[9], (D, FF), D ** -0.5, 0.125, ((1, 8),))
    down_weight = normal_values(streams_of[10], (FF, D), FF ** -0.5, 0.0625, ((0, 8),))
    out_grad = normal_values(streams_of[11], (TOKENS, D), 1.0, 6.0, ((0, 32),))
    return {"layer_input": layer_input, "width_choice": width_choice, "routed_flag": routed_flag, "mixer_gain": mixer_gain, "mixer_router": mixer_router, "attention_weight": attention_weight, "output_weight": output_weight, "hidden_gain": hidden_gain, "hidden_router": hidden_router, "up_weight": up_weight, "down_weight": down_weight, "out_grad": out_grad}


@jax.custom_vjp
def low(v):
    return lax.optimization_barrier(v.astype(jnp.bfloat16)).astype(jnp.float32)

@jax.custom_vjp
def low_back(v):
    return v

def low_keep(v):
    return (low(v), None)

def low_pass(kept, grad):
    return (grad,)

def back_keep(v):
    return (v, None)

def back_low(kept, grad):
    return (low(grad),)
low.defvjp(low_keep, low_pass)
low_back.defvjp(back_keep, back_low)
EPSILON = 1e-05
NEG_LARGE = -1e+30

def product(left, right):
    return jnp.dot(left, right, precision=lax.Precision.HIGHEST, preferred_element_type=jnp.float32)

def layer_norm(values, gain_vec):
    row_mean = lax.optimization_barrier(jnp.mean(values, axis=1, keepdims=True))
    centred = values - row_mean
    row_variance = lax.optimization_barrier(jnp.mean(centred * centred, axis=1, keepdims=True))
    return centred * lax.rsqrt(row_variance + EPSILON) * gain_vec[None, :]

def width_gate(normed, router, width_col, routed_col):
    soft_probs = jax.nn.softmax(product(normed, router), axis=1)
    one_hot = (width_col[:, None] == jnp.arange(4, dtype=jnp.int32)[None, :]).astype(jnp.float32)
    chosen = lax.optimization_barrier(jnp.sum(soft_probs * one_hot, axis=1))
    route_flags = routed_col.astype(jnp.float32)
    return route_flags * 4.0 * chosen + (1.0 - route_flags)

def rope_tables(token_count, head_width):
    positions = jnp.arange(token_count, dtype=jnp.float32)
    frequency = jnp.exp(jnp.arange(head_width // 2, dtype=jnp.float32) * (-2.0 * math.log(10000.0) / head_width))
    angles = positions[:, None] * frequency[None, :]
    return (jnp.cos(angles)[:, None, :], jnp.sin(angles)[:, None, :])

def rotate(halves, cosine_table, sine_table):
    half_size = halves.shape[-1] // 2
    first_half = halves[..., :half_size]
    second_half = halves[..., half_size:]
    return jnp.concatenate([first_half * cosine_table - second_half * sine_table, second_half * cosine_table + first_half * sine_table], axis=-1)

def attend(packed):
    queries, keys_all, values_all = packed
    token_count = queries.shape[0]
    scores = jnp.einsum('qhd,khd->hqk', queries, keys_all, precision=lax.Precision.HIGHEST) * (1.0 / math.sqrt(HD))
    scores = low_back(scores)
    positions = jnp.arange(token_count, dtype=jnp.int32)
    causal = positions[None, :] <= positions[:, None]
    scores = jnp.where(causal[None, :, :], scores, NEG_LARGE)
    soft_probs = jax.nn.softmax(scores, axis=2)
    return jnp.einsum('hqk,khd->qhd', low(soft_probs), values_all, precision=lax.Precision.HIGHEST)

def block_forward(block_input, block_width, block_routed, weights):
    mixer_gain, mixer_router, attention_weight, output_weight, hidden_gain, hidden_router, up_weight, down_weight = weights
    row_count = block_input.shape[0]
    normed_one = layer_norm(block_input, mixer_gain)
    gate_one = width_gate(normed_one, mixer_router, block_width[:, 0], block_routed[:, 0])
    mixer_in = low(normed_one)
    qkv_rows = low_back(product(mixer_in, attention_weight.reshape(D, 3 * H * HD)))
    shaped = qkv_rows.reshape(row_count // SEQ_LEN, SEQ_LEN, 3, H, HD)
    cosine_table, sine_table = rope_tables(SEQ_LEN, HD)
    queries = low(rotate(shaped[:, :, 0], cosine_table, sine_table))
    keys_all = low(rotate(shaped[:, :, 1], cosine_table, sine_table))
    values_all = low(shaped[:, :, 2])
    head_mix = lax.map(jax.checkpoint(attend), (queries, keys_all, values_all))
    head_mask = (jnp.arange(H, dtype=jnp.int32)[None, :] * 4 < (block_width[:, 0:1] + 1) * H).astype(jnp.float32)
    masked = head_mix.reshape(row_count, H, HD) * head_mask[:, :, None]
    heads_out = low(low_back(masked.reshape(row_count, H * HD)))
    mixer_branch = low_back(product(heads_out, output_weight))
    middle = block_input + gate_one[:, None] * mixer_branch
    normed_two = layer_norm(middle, hidden_gain)
    gate_two = width_gate(normed_two, hidden_router, block_width[:, 1], block_routed[:, 1])
    hidden_in = low(normed_two)
    pre_act = low_back(product(hidden_in, up_weight))
    col_mask = (jnp.arange(FF, dtype=jnp.int32)[None, :] * 4 < (block_width[:, 1:2] + 1) * FF).astype(jnp.float32)
    hidden = low(jnp.square(jax.nn.relu(pre_act)) * col_mask)
    hidden_branch = low_back(product(hidden, down_weight))
    return middle + gate_two[:, None] * hidden_branch

def reference(layer_input, width_choice, routed_flag, mixer_gain, mixer_router, attention_weight, output_weight, hidden_gain, hidden_router, up_weight, down_weight, out_grad):
    weights = (mixer_gain.astype(jnp.float32), mixer_router.astype(jnp.float32), attention_weight.astype(jnp.float32), output_weight.astype(jnp.float32), hidden_gain.astype(jnp.float32), hidden_router.astype(jnp.float32), up_weight.astype(jnp.float32), down_weight.astype(jnp.float32))
    block_widths = width_choice.reshape(N_DP, TOK_DP, 2)
    block_routed = routed_flag.reshape(N_DP, TOK_DP, 2)

    def forward(input_wide, weight_set):

        def one_block(packed):
            return block_forward(packed[0], packed[1], packed[2], weight_set)
        outputs = lax.map(one_block, (input_wide.reshape(N_DP, TOK_DP, D), block_widths, block_routed))
        return outputs.reshape(TOKENS, D)
    result, pullback = jax.vjp(forward, layer_input.astype(jnp.float32), weights)
    input_grad, grad_all = pullback(out_grad.astype(jnp.float32))
    return (result.astype(jnp.bfloat16), input_grad.astype(jnp.bfloat16), grad_all[0], grad_all[1], grad_all[2], grad_all[3], grad_all[4], grad_all[5], grad_all[6], grad_all[7])
```

```python
import math

import jax
import jax.numpy as jnp
from jax import lax
from jax.experimental import pallas as pl
from jax.experimental.pallas import tpu as pltpu
from jax.sharding import PartitionSpec as P

H = 16
HD = 128
FF = 8192
SEQ_LEN = 1024


EPSILON = 1e-05
NEG_LARGE = -1e30
HIGHEST = lax.Precision.HIGHEST


def norm_forward(values, gain_vec):
    row_mean = jnp.mean(values, axis=1, keepdims=True)
    centred = values - row_mean
    row_variance = jnp.mean(centred * centred, axis=1, keepdims=True)
    inverse_scale = lax.rsqrt(row_variance + EPSILON)
    scaled = centred * inverse_scale
    return (scaled * gain_vec[None, :], scaled, inverse_scale)


def norm_backward(normed_grad, scaled, inverse_scale, gain_vec):
    gain_grad = jnp.sum(normed_grad * scaled, axis=0)
    scaled_grad = normed_grad * gain_vec[None, :]
    first_mean = jnp.mean(scaled_grad, axis=1, keepdims=True)
    second_mean = jnp.mean(scaled_grad * scaled, axis=1, keepdims=True)
    return (inverse_scale * (scaled_grad - first_mean - scaled * second_mean), gain_grad)


def gate_forward(normed, router, width_col, routed_col):
    logits = jnp.dot(normed, router, precision=HIGHEST, preferred_element_type=jnp.float32)
    soft_probs = jax.nn.softmax(logits, axis=1)
    one_hot = (width_col[:, None] == jnp.arange(4, dtype=jnp.int32)[None, :]).astype(jnp.float32)
    chosen = jnp.sum(soft_probs * one_hot, axis=1)
    route_flags = routed_col.astype(jnp.float32)
    return (
        route_flags * 4.0 * chosen + (1.0 - route_flags),
        (soft_probs, one_hot, chosen, route_flags),
    )


def gate_backward(normed, router, gate_state, gate_grad):
    soft_probs, one_hot, chosen, route_flags = gate_state
    coefficient = route_flags * 4.0 * chosen * gate_grad
    logit_grad = coefficient[:, None] * (one_hot - soft_probs)
    router_grad = lax.dot_general(
        normed,
        logit_grad,
        (((0,), (0,)), ((), ())),
        precision=HIGHEST,
        preferred_element_type=jnp.float32,
    )
    normed_grad = lax.dot_general(
        logit_grad,
        router,
        (((1,), (1,)), ((), ())),
        precision=HIGHEST,
        preferred_element_type=jnp.float32,
    )
    return (normed_grad, router_grad)


Q_BLOCK = 256


def rope_tables(token_count, head_width):
    positions = jnp.arange(token_count, dtype=jnp.float32)
    frequency = jnp.exp(
        jnp.arange(head_width // 2, dtype=jnp.float32) * (-2.0 * math.log(10000.0) / head_width)
    )
    angles = positions[:, None] * frequency[None, :]
    cosine, sine = jnp.cos(angles), jnp.sin(angles)
    return jnp.concatenate([cosine, cosine], axis=1), jnp.concatenate([-sine, sine], axis=1)


def wide(x):
    return x.astype(jnp.float32)


def narrow(x):
    return x.astype(jnp.bfloat16)


def product(a, b, dims):
    return lax.dot_general(a, b, ((dims[:1], dims[1:]), ((), ())), preferred_element_type=jnp.float32)


def block_scores(queries, keys_all, start):
    scores = product(queries, keys_all, (1, 1)) * (1.0 / math.sqrt(HD))
    row = lax.broadcasted_iota(jnp.int32, scores.shape, 0) + start
    col = lax.broadcasted_iota(jnp.int32, scores.shape, 1)
    return jnp.where(col <= row, scores, NEG_LARGE)


def forward_kernel(x_ref, w_ref, cos_ref, sin_ref, mask_ref, qkv_ref, heads_ref, log_ref):
    tokens, heads = x_ref.shape[0], mask_ref.shape[1]
    block = min(Q_BLOCK, tokens)
    for start in range(0, tokens, block):
        here, end = slice(start, start + block), start + block
        x = x_ref[here, :]
        cos, sin = cos_ref[here, :], sin_ref[here, :]
        for part in range(3):
            rows = product(x, w_ref[part], (1, 0))
            for head in range(heads):
                lanes = slice(head * HD, (head + 1) * HD)
                value = rows[:, lanes]
                if part < 2:
                    value = value * cos + pltpu.roll(value, HD // 2, 1) * sin
                qkv_ref[part, here, lanes] = narrow(value)
        for head in range(heads):
            lanes = slice(head * HD, (head + 1) * HD)
            scores = block_scores(qkv_ref[0, here, lanes], qkv_ref[1, :end, lanes], start)
            row_max = jnp.max(scores, axis=1, keepdims=True)
            shifted = jnp.exp(scores - row_max)
            total = jnp.sum(shifted, axis=1, keepdims=True)
            mix = product(narrow(shifted / total), qkv_ref[2, :end, lanes], (1, 0))
            heads_ref[here, lanes] = narrow(mix * mask_ref[here, head : head + 1])
            log_ref[here, head : head + 1] = row_max + jnp.log(total)


def backward_kernel(g_ref, w_ref, qkv_ref, log_ref, cos_ref, sin_ref, mask_ref, out_ref, keys_acc, values_acc):
    tokens, heads = g_ref.shape[0], mask_ref.shape[1]
    block = min(Q_BLOCK, tokens)
    scale = 1.0 / math.sqrt(HD)
    for start in range(0, tokens, block):
        here, end = slice(start, start + block), start + block
        cos, sin = cos_ref[here, :], sin_ref[here, :]
        rows = narrow(product(g_ref[here, :], w_ref[0], (1, 0)))
        for head in range(heads):
            lanes = slice(head * HD, (head + 1) * HD)
            heads_grad = rows[:, lanes] * narrow(mask_ref[here, head : head + 1])
            queries, keys_all = qkv_ref[0, here, lanes], qkv_ref[1, :end, lanes]
            scores = block_scores(queries, keys_all, start)
            probs = jnp.exp(scores - log_ref[here, head : head + 1])
            values_part = product(narrow(probs), heads_grad, (0, 0))
            probs_grad = product(heads_grad, qkv_ref[2, :end, lanes], (1, 1))
            centre = jnp.sum(probs * probs_grad, axis=1, keepdims=True)
            score_grad = narrow(probs * (probs_grad - centre))
            queries_grad = product(score_grad, keys_all, (1, 0)) * scale
            keys_part = product(score_grad, queries, (0, 0)) * scale
            turned = queries_grad * cos - pltpu.roll(queries_grad, HD // 2, 1) * sin
            out_ref[0, here, lanes] = narrow(turned)
            if start:
                values_acc[:start, lanes] += values_part[:start]
                keys_acc[:start, lanes] += keys_part[:start]
            values_acc[here, lanes] = values_part[start:]
            keys_acc[here, lanes] = keys_part[start:]
    for start in range(0, tokens, block):
        here = slice(start, start + block)
        cos, sin = cos_ref[here, :], sin_ref[here, :]
        out_ref[2, here, :] = narrow(values_acc[here, :])
        for head in range(heads):
            lanes = slice(head * HD, (head + 1) * HD)
            value = keys_acc[here, lanes]
            out_ref[1, here, lanes] = narrow(value * cos - pltpu.roll(value, HD // 2, 1) * sin)


VMEM_LIMIT = 56 * 1024 * 1024


def whole_specs(count):
    return [pl.BlockSpec(memory_space=pltpu.VMEM)] * count


def attend_forward(x, w, cos, sin, mask):
    tokens, heads = mask.shape
    dim, width = w.shape[1:]
    flops = 2 * tokens * dim * width * 3 + 2 * tokens * tokens * width
    return pl.pallas_call(
        forward_kernel,
        out_shape=(
            jax.ShapeDtypeStruct((3, tokens, width), jnp.bfloat16),
            jax.ShapeDtypeStruct((tokens, width), jnp.bfloat16),
            jax.ShapeDtypeStruct((tokens, heads), jnp.float32),
        ),
        in_specs=whole_specs(5),
        out_specs=tuple(whole_specs(3)),
        compiler_params=pltpu.CompilerParams(vmem_limit_bytes=VMEM_LIMIT),
        cost_estimate=pl.CostEstimate(flops=flops, bytes_accessed=12 << 20, transcendentals=tokens * tokens * heads // 2),
        name="attend_forward",
    )(x, w, cos, sin, mask)


def attend_backward(g, w, qkv, log_total, cos, sin, mask):
    tokens, heads = mask.shape
    dim, width = w.shape[1:]
    flops = 2 * tokens * dim * width + 5 * tokens * tokens * width
    fixed = whole_specs(1)[0]
    return pl.pallas_call(
        backward_kernel,
        grid=(1,),
        out_shape=jax.ShapeDtypeStruct((3, tokens, width), jnp.bfloat16),
        in_specs=[fixed, pl.BlockSpec((1, dim, width), lambda i: (3, 0, 0))] + [fixed] * 5,
        out_specs=fixed,
        scratch_shapes=[pltpu.VMEM((tokens, width), jnp.float32)] * 2,
        compiler_params=pltpu.CompilerParams(vmem_limit_bytes=VMEM_LIMIT),
        cost_estimate=pl.CostEstimate(flops=flops, bytes_accessed=8 << 20, transcendentals=tokens * tokens * heads // 2),
        name="attend_backward",
    )(g, w, qkv, log_total, cos, sin, mask)


def swap_pairs(size, bit):
    return [(i, i ^ bit) for i in range(size)]


def shift_pairs(size, shift):
    return [(i, (i - shift) % size) for i in range(size)]


def bits_of(size):
    return [1 << i for i in range(size.bit_length() - 1)]


def pick(x, index, axis=0):
    return lax.dynamic_index_in_dim(x, index, axis, keepdims=False)


def after(x, *others):
    return lax.optimization_barrier((x,) + others)[0]


def xor_gather(x, axis, size, bits):
    held = {0: x}
    for bit in bits:
        for far in list(held):
            held[far ^ bit] = lax.ppermute(held[far], axis, swap_pairs(size, bit))
    return held


def by_index(held, index, axis=0):
    shape = held[0].shape
    out = jnp.zeros(shape[:axis] + (len(held),) + shape[axis:], held[0].dtype)
    for far, block in held.items():
        out = lax.dynamic_update_index_in_dim(out, block, index ^ far, axis)
    return out


def xor_scatter(blocks, axis_name, size, bits, steps, index, axis):
    count = blocks.shape[axis].bit_length() - 1
    blocks = blocks.reshape(blocks.shape[:axis] + (2,) * count + blocks.shape[axis + 1 :])
    left = [1 << (count - 1 - i) for i in range(count)]
    for bit, step in zip(bits, steps):
        at = axis + left.index(step)
        left.remove(step)
        side = (index // step) % 2
        got = lax.ppermute(narrow(pick(blocks, 1 - side, at)), axis_name, swap_pairs(size, bit))
        blocks = wide(pick(blocks, side, at)) + wide(got)
    return blocks


def column_gather(x, size, column):
    bits, half = bits_of(size), x.shape[1] // 2
    parts = [
        by_index(xor_gather(x[:, :half], "dp", size, bits), column, 1),
        by_index(xor_gather(x[:, half:], "dp", size, bits[::-1]), column, 1),
    ]
    return jnp.concatenate(parts, axis=2).reshape(x.shape[0], -1, x.shape[2])


def column_scatter(x, size, column):
    bits = bits_of(size)
    blocks = x.reshape(x.shape[0], size, -1, x.shape[2])
    half = blocks.shape[2] // 2
    return jnp.concatenate(
        [
            narrow(xor_scatter(blocks[:, :, :half], "dp", size, bits, bits, column, 1)),
            narrow(xor_scatter(blocks[:, :, half:], "dp", size, bits[::-1], bits[::-1], column, 1)),
        ],
        axis=1,
    )


def all_sum(x, sizes):
    for axis, size in sizes.items():
        for bit in bits_of(size):
            x = x + lax.ppermute(x, axis, swap_pairs(size, bit))
    return x


def make_local(columns, ranks):
    def local(
        layer_input, width_choice, routed_flag, mixer_gain, mixer_router, attention_weight,
        output_weight, hidden_gain, hidden_router, up_weight, down_weight, out_grad,
    ):
        column, rank = lax.axis_index("dp"), lax.axis_index("mp")
        rows, dim = layer_input.shape
        core = rank % 2
        group = SEQ_LEN // rows
        sequences = ranks // group
        place, sequence = rank % group, rank // group
        pair_bits = [b for b in bits_of(group) if b > 1]
        own_heads = output_weight.shape[0] // HD
        cols_local = up_weight.shape[1]
        width_own = lax.dynamic_slice_in_dim(width_choice, rank * rows, rows, 0)
        routed_own = lax.dynamic_slice_in_dim(routed_flag, rank * rows, rows, 0)
        cos, sin = rope_tables(SEQ_LEN, HD)

        def to_sequence(x):
            held = xor_gather(x, "mp", ranks, pair_bits + [1])
            return by_index(held, place).reshape(SEQ_LEN, -1), held

        def from_sequence(x):
            blocks = x.reshape(group // 2, 2, -1, x.shape[1])
            got = lax.ppermute(narrow(pick(blocks, 1 - core, 1)), "mp", swap_pairs(ranks, 1))
            blocks = wide(pick(blocks, core, 1)) + wide(got)
            bits = pair_bits[::-1]
            return xor_scatter(blocks, "mp", ranks, bits, [b // 2 for b in bits], place // 2, 0)

        planes = jnp.concatenate([attention_weight.transpose(1, 0, 2), output_weight.T[None]], axis=0)
        plane_rows = dim // columns
        chunk = lax.dynamic_slice_in_dim(planes, column * plane_rows, plane_rows, 1)
        weights, fetched = [planes], []
        for k in range(1, sequences):
            got = lax.ppermute(chunk, "mp", shift_pairs(ranks, k * group))
            fetched.append(got)
            weights.append(column_gather(got, columns, column))

        input_wide = wide(layer_input)
        normed_one, scaled_one, inverse_one = norm_forward(input_wide, mixer_gain)
        inputs_one, held_one = to_sequence(narrow(normed_one))
        gate_one, state_one = gate_forward(normed_one, mixer_router, width_own[:, 0], routed_own[:, 0])
        grads_all = lax.all_gather(after(out_grad, *fetched), "mp", axis=0, tiled=True)

        sequence_width = lax.dynamic_slice_in_dim(width_choice[:, 0], sequence * SEQ_LEN, SEQ_LEN, 0)
        kept = []
        branch = None
        for k in range(sequences):
            heads = ((rank + k * group) % ranks) * own_heads + jnp.arange(own_heads, dtype=jnp.int32)
            mask = (heads[None, :] * 4 < (sequence_width[:, None] + 1) * H).astype(jnp.float32)
            qkv, heads_out, log_total = attend_forward(inputs_one, weights[k], cos, sin, mask)
            kept.append((qkv, heads_out, log_total, mask))
            share = product(heads_out, weights[k][3], (1, 1))
            branch = share if branch is None else branch + share
        mixer_branch = from_sequence(branch)

        middle = input_wide + gate_one[:, None] * mixer_branch
        normed_two, scaled_two, inverse_two = norm_forward(middle, hidden_gain)
        gate_two, state_two = gate_forward(normed_two, hidden_router, width_own[:, 1], routed_own[:, 1])
        inputs_two = lax.all_gather(narrow(normed_two), "mp", axis=0, tiled=True)
        gates = by_index(xor_gather(gate_two.reshape(-1, 128), "mp", ranks, bits_of(ranks)), rank).reshape(-1)

        col_ids = rank * cols_local + jnp.arange(cols_local, dtype=jnp.int32)
        col_mask = (col_ids[None, :] * 4 < (width_choice[:, 1:2] + 1) * FF).astype(jnp.float32)
        top_down = product(grads_all, down_weight, (1, 1))
        pre = product(inputs_two, up_weight, (1, 0))
        relu_act = jax.nn.relu(pre)
        hidden = narrow(relu_act * relu_act * col_mask)
        pre_grad = narrow(top_down * gates[:, None] * col_mask * 2.0 * relu_act)
        normed_grad_two = wide(
            lax.psum_scatter(narrow(product(pre_grad, up_weight, (1, 1))), "mp", scatter_dimension=0, tiled=True)
        )
        dots = jnp.sum(wide(hidden) * top_down, axis=1).reshape(-1, 128)
        gate_grad_two = lax.dynamic_slice_in_dim(all_sum(dots, {"mp": ranks}).reshape(-1), rank * rows, rows, 0)
        router_part, router_two = gate_backward(normed_two, hidden_router, state_two, gate_grad_two)
        middle_part, gain_two = norm_backward(normed_grad_two + router_part, scaled_two, inverse_two, hidden_gain)
        middle_grad = wide(out_grad) + middle_part
        gated = narrow(gates[:, None] * wide(grads_all))
        down_grad = narrow(product(hidden, gated, (0, 0)))
        up_grad = narrow(product(inputs_two, pre_grad, (0, 0)))

        def column_total(x):
            return wide(column_gather(column_scatter(x[None], columns, column), columns, column)[0])

        down_sum = column_total(down_grad)
        up_sum = column_total(up_grad)

        grads_one, held_grads = to_sequence(narrow(gate_one[:, None] * middle_grad))
        share = narrow(product(hidden, down_weight, (1, 0)))
        share = after(share, *held_grads.values())
        hidden_branch = wide(lax.psum_scatter(share, "mp", scatter_dimension=0, tiled=True))
        layer_output = narrow(middle + gate_two[:, None] * hidden_branch)

        gate_grad_one = jnp.sum(middle_grad * mixer_branch, axis=1)
        share_one = None
        plane_grads = [None] * sequences
        for k in range(sequences)[::-1]:
            qkv, heads_out, log_total, mask = kept[k]
            qkv_grad = attend_backward(grads_one, weights[k], qkv, log_total, cos, sin, mask)
            in_grads = [product(inputs_one, qkv_grad[p], (0, 0)) for p in range(3)]
            plane_grads[k] = jnp.stack([narrow(x) for x in in_grads] + [narrow(product(grads_one, heads_out, (0, 0)))])
            for p in range(3):
                share = product(qkv_grad[p], weights[k][p], (1, 1))
                share_one = share if share_one is None else share_one + share
        normed_grad_one = from_sequence(share_one)

        piece = wide(column_scatter(plane_grads[0], columns, column))
        for k in range(1, sequences):
            there = column_scatter(plane_grads[k], columns, column)
            piece = piece + wide(lax.ppermute(there, "mp", shift_pairs(ranks, -k * group)))
        plane_sum = wide(column_gather(narrow(piece), columns, column))
        attention_sum = plane_sum[:3].transpose(1, 0, 2)
        output_sum = plane_sum[3].T

        router_part_one, router_one = gate_backward(normed_one, mixer_router, state_one, gate_grad_one)
        input_part, gain_one = norm_backward(normed_grad_one + router_part_one, scaled_one, inverse_one, mixer_gain)
        input_grad = narrow(middle_grad + input_part)

        sizes = {"mp": ranks, "dp": columns}

        def small_total(gain, router):
            packed = jnp.concatenate([gain.reshape(-1, 128), router.T.reshape(-1, 128)], axis=0)
            packed = all_sum(packed, sizes)
            cut = dim // 128
            return packed[:cut].reshape(dim), packed[cut:].reshape(-1, dim).T

        hidden_gain_sum, hidden_router_sum = small_total(gain_two, router_two)
        mixer_gain_sum, mixer_router_sum = small_total(gain_one, router_one)
        return (
            layer_output, input_grad, mixer_gain_sum, mixer_router_sum, attention_sum, output_sum,
            hidden_gain_sum, hidden_router_sum, up_sum, down_sum,
        )

    return local


def solution(mesh):
    return jax.shard_map(
        make_local(mesh.shape["dp"], mesh.shape["mp"]),
        mesh=mesh,
        in_specs=(
            P(("dp", "mp"), None),
            P("dp", None),
            P("dp", None),
            P(),
            P(),
            P(None, None, "mp"),
            P("mp", None),
            P(),
            P(),
            P(None, "mp"),
            P("mp", None),
            P(("dp", "mp"), None),
        ),
        out_specs=(
            P(("dp", "mp"), None),
            P(("dp", "mp"), None),
            P(),
            P(),
            P(None, None, "mp"),
            P("mp", None),
            P(),
            P(),
            P(None, "mp"),
            P("mp", None),
        ),
        check_vma=False,
    )
```

```python
import functools
import math

import jax
import jax.numpy as jnp
from jax import lax
from jax.experimental import pallas as pl
from jax.experimental.pallas import tpu as pltpu
from jax.sharding import PartitionSpec as P

H = 16
HD = 128
FF = 8192
SEQ_LEN = 1024


EPSILON = 1e-05
NEG_LARGE = -1e30
HIGHEST = lax.Precision.HIGHEST


def norm_forward(values, gain_vec):
    row_mean = jnp.mean(values, axis=1, keepdims=True)
    centred = values - row_mean
    row_variance = jnp.mean(centred * centred, axis=1, keepdims=True)
    inverse_scale = lax.rsqrt(row_variance + EPSILON)
    scaled = centred * inverse_scale
    return (scaled * gain_vec[None, :], scaled, inverse_scale)


def norm_backward(normed_grad, scaled, inverse_scale, gain_vec):
    gain_grad = jnp.sum(normed_grad * scaled, axis=0)
    scaled_grad = normed_grad * gain_vec[None, :]
    first_mean = jnp.mean(scaled_grad, axis=1, keepdims=True)
    second_mean = jnp.mean(scaled_grad * scaled, axis=1, keepdims=True)
    return (inverse_scale * (scaled_grad - first_mean - scaled * second_mean), gain_grad)


def gate_forward(normed, router, width_col, routed_col):
    logits = jnp.dot(normed, router, precision=HIGHEST, preferred_element_type=jnp.float32)
    soft_probs = jax.nn.softmax(logits, axis=1)
    one_hot = (width_col[:, None] == jnp.arange(4, dtype=jnp.int32)[None, :]).astype(jnp.float32)
    chosen = jnp.sum(soft_probs * one_hot, axis=1)
    route_flags = routed_col.astype(jnp.float32)
    return (
        route_flags * 4.0 * chosen + (1.0 - route_flags),
        (soft_probs, one_hot, chosen, route_flags),
    )


def gate_backward(normed, router, gate_state, gate_grad):
    soft_probs, one_hot, chosen, route_flags = gate_state
    coefficient = route_flags * 4.0 * chosen * gate_grad
    logit_grad = coefficient[:, None] * (one_hot - soft_probs)
    router_grad = lax.dot_general(
        normed,
        logit_grad,
        (((0,), (0,)), ((), ())),
        precision=HIGHEST,
        preferred_element_type=jnp.float32,
    )
    normed_grad = lax.dot_general(
        logit_grad,
        router,
        (((1,), (1,)), ((), ())),
        precision=HIGHEST,
        preferred_element_type=jnp.float32,
    )
    return (normed_grad, router_grad)


Q_BLOCK = 256


def rope_tables(token_count, head_width):
    positions = jnp.arange(token_count, dtype=jnp.float32)
    frequency = jnp.exp(
        jnp.arange(head_width // 2, dtype=jnp.float32) * (-2.0 * math.log(10000.0) / head_width)
    )
    angles = positions[:, None] * frequency[None, :]
    cosine, sine = jnp.cos(angles), jnp.sin(angles)
    return jnp.concatenate([cosine, cosine], axis=1), jnp.concatenate([-sine, sine], axis=1)


def wide(x):
    return x.astype(jnp.float32)


def narrow(x):
    return x.astype(jnp.bfloat16)


def product(a, b, dims):
    return lax.dot_general(a, b, ((dims[:1], dims[1:]), ((), ())), preferred_element_type=jnp.float32)


def block_scores(queries, keys_all, start):
    scores = product(queries, keys_all, (1, 1)) * (1.0 / math.sqrt(HD))
    row = lax.broadcasted_iota(jnp.int32, scores.shape, 0) + start
    col = lax.broadcasted_iota(jnp.int32, scores.shape, 1)
    return jnp.where(col <= row, scores, NEG_LARGE)


def forward_kernel(earlier, *refs):
    x_ref, w_ref, cos_ref, sin_ref, mask_ref = refs[:5]
    others = refs[5 : 5 + 2 * earlier]
    qkv_ref, heads_ref, log_ref, *share_ref = refs[5 + 2 * earlier :]
    tokens, heads = x_ref.shape[0], mask_ref.shape[1]
    width = heads * HD
    block = min(Q_BLOCK, tokens)
    for start in range(0, tokens, block):
        here, end = slice(start, start + block), start + block
        x = x_ref[here, :]
        cos, sin = cos_ref[here, :], sin_ref[here, :]
        for part in range(3):
            rows = product(x, w_ref[:, part * width : (part + 1) * width], (1, 0))
            for head in range(heads):
                value = rows[:, head * HD : (head + 1) * HD]
                if part < 2:
                    value = value * cos + pltpu.roll(value, HD // 2, 1) * sin
                at = part * width + head * HD
                qkv_ref[here, at : at + HD] = narrow(value)
        for head in range(heads):
            at = head * HD
            lanes, key_lanes, value_lanes = (slice(at + p * width, at + p * width + HD) for p in range(3))
            scores = block_scores(qkv_ref[here, lanes], qkv_ref[:end, key_lanes], start)
            row_max = jnp.max(scores, axis=1, keepdims=True)
            shifted = jnp.exp(scores - row_max)
            total = jnp.sum(shifted, axis=1, keepdims=True)
            mix = product(narrow(shifted / total), qkv_ref[:end, value_lanes], (1, 0))
            heads_ref[here, lanes] = narrow(mix * mask_ref[here, head : head + 1])
            log_ref[here, head : head + 1] = row_max + jnp.log(total)
        if share_ref:
            share = product(heads_ref[here, :], w_ref[:, 3 * width :], (1, 1))
            for k in range(earlier):
                share = share + product(others[2 * k][here, :], others[2 * k + 1][:, 3 * width :], (1, 1))
            share_ref[0][here, :] = narrow(share)


def backward_kernel(earlier, *refs):
    g_ref, w_ref, qkv_ref, log_ref, cos_ref, sin_ref, mask_ref = refs[:7]
    others = refs[7 : 7 + 2 * earlier]
    *outs, keys_acc, values_acc = refs[7 + 2 * earlier :]
    out_ref = outs[0]
    tokens, heads = g_ref.shape[0], mask_ref.shape[1]
    width = heads * HD
    block = min(Q_BLOCK, tokens)
    scale = 1.0 / math.sqrt(HD)
    for start in range(0, tokens, block):
        here, end = slice(start, start + block), start + block
        cos, sin = cos_ref[here, :], sin_ref[here, :]
        rows = narrow(product(g_ref[here, :], w_ref[:, 3 * width :], (1, 0)))
        for head in range(heads):
            at = head * HD
            lanes, key_lanes, value_lanes = (slice(at + p * width, at + p * width + HD) for p in range(3))
            heads_grad = rows[:, lanes] * narrow(mask_ref[here, head : head + 1])
            queries, keys_all = qkv_ref[here, lanes], qkv_ref[:end, key_lanes]
            scores = block_scores(queries, keys_all, start)
            probs = jnp.exp(scores - log_ref[here, head : head + 1])
            values_part = product(narrow(probs), heads_grad, (0, 0))
            probs_grad = product(heads_grad, qkv_ref[:end, value_lanes], (1, 1))
            centre = jnp.sum(probs * probs_grad, axis=1, keepdims=True)
            score_grad = narrow(probs * (probs_grad - centre))
            queries_grad = product(score_grad, keys_all, (1, 0)) * scale
            keys_part = product(score_grad, queries, (0, 0)) * scale
            turned = queries_grad * cos - pltpu.roll(queries_grad, HD // 2, 1) * sin
            out_ref[here, lanes] = narrow(turned)
            if start:
                values_acc[:start, lanes] += values_part[:start]
                keys_acc[:start, lanes] += keys_part[:start]
            values_acc[here, lanes] = values_part[start:]
            keys_acc[here, lanes] = keys_part[start:]
    for start in range(0, tokens, block):
        here = slice(start, start + block)
        cos, sin = cos_ref[here, :], sin_ref[here, :]
        out_ref[here, 2 * width :] = narrow(values_acc[here, :])
        for head in range(heads):
            at = head * HD
            value = keys_acc[here, at : at + HD]
            out_ref[here, width + at : width + at + HD] = narrow(value * cos - pltpu.roll(value, HD // 2, 1) * sin)
        if outs[1:]:
            share = product(out_ref[here, :], w_ref[:, : 3 * width], (1, 1))
            for k in range(earlier):
                share = share + product(others[2 * k][here, :], others[2 * k + 1][:, : 3 * width], (1, 1))
            outs[1][here, :] = narrow(share)


def weight_kernel(x_ref, q_ref, g_ref, h_ref, *outs):
    width = h_ref.shape[1]
    half = x_ref.shape[1] // 2
    for lane, out_ref in enumerate(outs):
        here = slice(lane * half, (lane + 1) * half)
        out_ref[0, :, : 3 * width] = narrow(product(x_ref[:, here], q_ref[...], (0, 0)))
        out_ref[0, :, 3 * width :] = narrow(product(g_ref[:, here], h_ref[...], (0, 0)))


def place_kernel(count, widths, turned, at_ref, *refs):
    blocks, outs = refs[: 2 * count], refs[2 * count :]
    half = blocks[0].shape[0]
    for far in range(count):

        @pl.when((pl.program_id(0) ^ at_ref[0]) == far)
        def _():
            for lane in range(2):
                here = slice(lane * half, (lane + 1) * half)
                block = blocks[lane * count + far]
                start = 0
                for out_ref, width, turn in zip(outs, widths, turned):
                    for part in range(out_ref.shape[0] if len(out_ref.shape) == 3 else 1):
                        value = block[:, start : start + width].astype(out_ref.dtype)
                        start += width
                        if turn:
                            out_ref[:, here] = value.T
                        elif len(out_ref.shape) == 3:
                            out_ref[part, here, :] = value
                        else:
                            out_ref[here, :] = value


VMEM_LIMIT = 56 * 1024 * 1024


def whole_specs(count):
    return [pl.BlockSpec(memory_space=pltpu.VMEM)] * count


def attend_forward(x, w, cos, sin, mask, earlier, last):
    tokens, heads = mask.shape
    dim, width = w.shape[0], heads * HD
    flops = 2 * tokens * dim * width * 3 + 2 * tokens * tokens * width
    out = [
        jax.ShapeDtypeStruct((tokens, 3 * width), jnp.bfloat16),
        jax.ShapeDtypeStruct((tokens, width), jnp.bfloat16),
        jax.ShapeDtypeStruct((tokens, heads), jnp.float32),
    ]
    given = [a for pair in earlier for a in pair] if last else []
    if last:
        out.append(jax.ShapeDtypeStruct((tokens, dim), jnp.bfloat16))
        flops += 2 * tokens * dim * width * (1 + len(earlier))
    return pl.pallas_call(
        functools.partial(forward_kernel, len(given) // 2),
        out_shape=out,
        in_specs=whole_specs(5 + len(given)),
        out_specs=whole_specs(len(out)),
        compiler_params=pltpu.CompilerParams(vmem_limit_bytes=VMEM_LIMIT),
        cost_estimate=pl.CostEstimate(flops=flops, bytes_accessed=12 << 20, transcendentals=tokens * tokens * heads // 2),
        name="attend_forward",
    )(x, w, cos, sin, mask, *given)


def attend_backward(g, w, qkv, log_total, cos, sin, mask, earlier, last):
    tokens, heads = mask.shape
    dim, width = w.shape[0], heads * HD
    flops = 2 * tokens * dim * width + 5 * tokens * tokens * width
    out = [jax.ShapeDtypeStruct((tokens, 3 * width), jnp.bfloat16)]
    given = [a for pair in earlier for a in pair] if last else []
    if last:
        out.append(jax.ShapeDtypeStruct((tokens, dim), jnp.bfloat16))
        flops += 6 * tokens * dim * width * (1 + len(earlier))
    return pl.pallas_call(
        functools.partial(backward_kernel, len(given) // 2),
        out_shape=out,
        in_specs=whole_specs(7 + len(given)),
        out_specs=whole_specs(len(out)),
        scratch_shapes=[pltpu.VMEM((tokens, width), jnp.float32)] * 2,
        compiler_params=pltpu.CompilerParams(vmem_limit_bytes=VMEM_LIMIT),
        cost_estimate=pl.CostEstimate(flops=flops, bytes_accessed=12 << 20, transcendentals=tokens * tokens * heads // 2),
        name="attend_backward",
    )(g, w, qkv, log_total, cos, sin, mask, *given)


def weight_grads(x, qkv_grad, g, heads_out, count):
    tokens, dim = x.shape
    width = heads_out.shape[1]
    block = dim // count
    out = jax.ShapeDtypeStruct((count, block // 2, 4 * width), jnp.bfloat16)
    return pl.pallas_call(
        weight_kernel,
        grid=(count,),
        out_shape=[out, out],
        in_specs=[
            pl.BlockSpec((tokens, block), lambda i: (0, i)),
            pl.BlockSpec((tokens, 3 * width), lambda i: (0, 0)),
            pl.BlockSpec((tokens, block), lambda i: (0, i)),
            pl.BlockSpec((tokens, width), lambda i: (0, 0)),
        ],
        out_specs=[pl.BlockSpec((1, block // 2, 4 * width), lambda i: (i, 0, 0))] * 2,
        compiler_params=pltpu.CompilerParams(vmem_limit_bytes=VMEM_LIMIT),
        cost_estimate=pl.CostEstimate(flops=8 * tokens * dim * width, bytes_accessed=14 << 20, transcendentals=0),
        name="weight_grads",
    )(x, qkv_grad, g, heads_out)


def place_blocks(lanes, index, outs):
    count = len(lanes[0])
    half, total = lanes[0][0].shape
    rows = 2 * half
    shapes, specs = [], []
    for planes, width, kind, turned in outs:
        if turned:
            shapes.append(jax.ShapeDtypeStruct((width, rows * count), kind))
            specs.append(pl.BlockSpec((width, rows), lambda i, at: (0, i)))
        elif planes > 1:
            shapes.append(jax.ShapeDtypeStruct((planes, rows * count, width), kind))
            specs.append(pl.BlockSpec((planes, rows, width), lambda i, at: (0, i, 0)))
        else:
            shapes.append(jax.ShapeDtypeStruct((rows * count, width), kind))
            specs.append(pl.BlockSpec((rows, width), lambda i, at: (i, 0)))
    given = [held[far] for held in lanes for far in range(count)]
    return pl.pallas_call(
        functools.partial(place_kernel, count, [o[1] for o in outs], [o[3] for o in outs]),
        grid_spec=pltpu.PrefetchScalarGridSpec(
            num_scalar_prefetch=1,
            grid=(count,),
            in_specs=[pl.BlockSpec((half, total), lambda i, at: (0, 0))] * len(given),
            out_specs=specs,
        ),
        out_shape=shapes,
        compiler_params=pltpu.CompilerParams(vmem_limit_bytes=VMEM_LIMIT),
        cost_estimate=pl.CostEstimate(flops=0, bytes_accessed=12 << 20, transcendentals=0),
        name="place_blocks",
    )(index.astype(jnp.int32).reshape(1), *given)


def swap_pairs(size, bit):
    return [(i, i ^ bit) for i in range(size)]


def shift_pairs(size, shift):
    return [(i, (i - shift) % size) for i in range(size)]


def bits_of(size):
    return [1 << i for i in range(size.bit_length() - 1)]


def pick(x, index, axis=0):
    return lax.dynamic_index_in_dim(x, index, axis, keepdims=False)


def after(x, *others):
    return lax.optimization_barrier((x,) + others)[0]


def xor_gather(x, axis, size, bits):
    held = dict(x) if isinstance(x, dict) else {0: x}
    for bit in bits:
        for far in list(held):
            held[far ^ bit] = lax.ppermute(held[far], axis, swap_pairs(size, bit))
    return held


def by_index(held, index, axis=0):
    shape = held[0].shape
    out = jnp.zeros(shape[:axis] + (len(held),) + shape[axis:], held[0].dtype)
    for far, block in held.items():
        out = lax.dynamic_update_index_in_dim(out, block, index ^ far, axis)
    return out


def xor_scatter(blocks, axis_name, size, bits, steps, index, axis):
    count = blocks.shape[axis].bit_length() - 1
    blocks = blocks.reshape(blocks.shape[:axis] + (2,) * count + blocks.shape[axis + 1 :])
    left = [1 << (count - 1 - i) for i in range(count)]
    for bit, step in zip(bits, steps):
        at = axis + left.index(step)
        left.remove(step)
        side = (index // step) % 2
        got = lax.ppermute(narrow(pick(blocks, 1 - side, at)), axis_name, swap_pairs(size, bit))
        blocks = wide(pick(blocks, side, at)) + wide(got)
    return blocks


def lane_bits(size):
    return bits_of(size), bits_of(size)[::-1]


def column_gather(lanes, size, cut=None, start=None):
    return [xor_gather(x, "dp", size, bits[start:cut]) for x, bits in zip(lanes, lane_bits(size))]


def gate_lanes(lanes, *gates):
    flat = [held[far] for held in lanes for far in held]
    flat = lax.optimization_barrier((*flat, *gates))
    flat = iter(flat)
    return [{far: next(flat) for far in held} for held in lanes]


def column_scatter(lanes, size, column):
    return [narrow(xor_scatter(x, "dp", size, bits, bits, column, 0)) for x, bits in zip(lanes, lane_bits(size))]


def two_lanes(x, size):
    blocks = x.reshape(size, 2, -1, x.shape[1])
    return [blocks[:, 0], blocks[:, 1]]


def all_sum(x, sizes):
    for axis, size in sizes.items():
        for bit in bits_of(size):
            x = x + lax.ppermute(x, axis, swap_pairs(size, bit))
    return x


def make_local(columns, ranks):
    def local(
        layer_input, width_choice, routed_flag, mixer_gain, mixer_router, attention_weight,
        output_weight, hidden_gain, hidden_router, up_weight, down_weight, out_grad,
    ):
        column, rank = lax.axis_index("dp"), lax.axis_index("mp")
        rows, dim = layer_input.shape
        core = rank % 2
        group = SEQ_LEN // rows
        sequences = ranks // group
        place, sequence = rank % group, rank // group
        pair_bits = [b for b in bits_of(group) if b > 1]
        own_heads = output_weight.shape[0] // HD
        cols_local = up_weight.shape[1]
        width_own = lax.dynamic_slice_in_dim(width_choice, rank * rows, rows, 0)
        routed_own = lax.dynamic_slice_in_dim(routed_flag, rank * rows, rows, 0)
        cos, sin = rope_tables(SEQ_LEN, HD)

        def to_sequence(x):
            held = xor_gather(x, "mp", ranks, pair_bits + [1])
            return by_index(held, place).reshape(SEQ_LEN, -1), held

        def from_sequence(x):
            blocks = x.reshape(group // 2, 2, -1, x.shape[1])
            got = lax.ppermute(narrow(pick(blocks, 1 - core, 1)), "mp", swap_pairs(ranks, 1))
            blocks = wide(pick(blocks, core, 1)) + wide(got)
            bits = pair_bits[::-1]
            return xor_scatter(blocks, "mp", ranks, bits, [b // 2 for b in bits], place // 2, 0)

        width = own_heads * HD
        packed = jnp.concatenate([attention_weight[:, p] for p in range(3)] + [output_weight.T], axis=1)
        chunk_rows = dim // columns
        chunks = [
            lax.dynamic_slice_in_dim(packed, column * chunk_rows + at, chunk_rows // 2, 0)
            for at in (0, chunk_rows // 2)
        ]
        input_wide = wide(layer_input)
        normed_one, scaled_one, inverse_one = norm_forward(input_wide, mixer_gain)
        inputs_one, held_one = to_sequence(narrow(normed_one))
        fetched = [
            lax.ppermute(lane, "mp", shift_pairs(ranks, k * group)) for k in range(1, sequences) for lane in chunks
        ]
        inputs_one, *fetched = lax.optimization_barrier((inputs_one, *fetched))
        weights = [packed]
        for k in range(1, sequences):
            held = column_gather(fetched[2 * k - 2 : 2 * k], columns)
            weights += place_blocks(held, column, [(1, packed.shape[1], jnp.bfloat16, False)])
        gate_one, state_one = gate_forward(normed_one, mixer_router, width_own[:, 0], routed_own[:, 0])
        grads_all = lax.all_gather(after(out_grad, *fetched), "mp", axis=0, tiled=True)

        sequence_width = lax.dynamic_slice_in_dim(width_choice[:, 0], sequence * SEQ_LEN, SEQ_LEN, 0)
        kept, earlier = [], []
        for k in range(sequences):
            heads = ((rank + k * group) % ranks) * own_heads + jnp.arange(own_heads, dtype=jnp.int32)
            mask = (heads[None, :] * 4 < (sequence_width[:, None] + 1) * H).astype(jnp.float32)
            last = k == sequences - 1
            qkv, heads_out, log_total, *share = attend_forward(inputs_one, weights[k], cos, sin, mask, earlier, last)
            kept.append((qkv, heads_out, log_total, mask))
            earlier.append((heads_out, weights[k]))
        mixer_branch = from_sequence(share[0])
        top_down = product(grads_all, down_weight, (1, 1))
        mixer_branch, top_down = lax.optimization_barrier((mixer_branch, top_down))

        middle = input_wide + gate_one[:, None] * mixer_branch
        normed_two, scaled_two, inverse_two = norm_forward(middle, hidden_gain)
        gate_two, state_two = gate_forward(normed_two, hidden_router, width_own[:, 1], routed_own[:, 1])
        inputs_two = lax.all_gather(narrow(normed_two), "mp", axis=0, tiled=True)
        gates = by_index(xor_gather(gate_two.reshape(-1, 128), "mp", ranks, bits_of(ranks)), rank).reshape(-1)

        col_ids = rank * cols_local + jnp.arange(cols_local, dtype=jnp.int32)
        col_mask = (col_ids[None, :] * 4 < (width_choice[:, 1:2] + 1) * FF).astype(jnp.float32)
        pre = product(inputs_two, up_weight, (1, 0))
        relu_act = jax.nn.relu(pre)
        hidden = narrow(relu_act * relu_act * col_mask)
        pre_grad = narrow(top_down * gates[:, None] * col_mask * 2.0 * relu_act)
        dots = jnp.sum(wide(hidden) * top_down, axis=1).reshape(-1, 128)
        share = narrow(product(pre_grad, up_weight, (1, 1)))
        share, hidden, pre_grad = lax.optimization_barrier((share, hidden, pre_grad))
        normed_grad_two = wide(lax.psum_scatter(share, "mp", scatter_dimension=0, tiled=True))
        gate_grad_two = lax.dynamic_slice_in_dim(all_sum(dots, {"mp": ranks}).reshape(-1), rank * rows, rows, 0)
        gated = narrow(gates[:, None] * wide(grads_all))
        down_piece = column_scatter(two_lanes(narrow(product(hidden, gated, (0, 0))), columns), columns, column)
        up_piece = column_scatter(two_lanes(narrow(product(inputs_two, pre_grad, (0, 0))), columns), columns, column)
        hidden_share = narrow(product(hidden, down_weight, (1, 0)))

        router_part, router_two = gate_backward(normed_two, hidden_router, state_two, gate_grad_two)
        middle_part, gain_two = norm_backward(normed_grad_two + router_part, scaled_two, inverse_two, hidden_gain)
        middle_grad = wide(out_grad) + middle_part
        grads_one, held_grads = to_sequence(narrow(gate_one[:, None] * middle_grad))
        grads_one, hidden_share = lax.optimization_barrier((grads_one, hidden_share))
        hidden_branch = wide(lax.psum_scatter(hidden_share, "mp", scatter_dimension=0, tiled=True))
        layer_output = narrow(middle + gate_two[:, None] * hidden_branch)

        gate_grad_one = jnp.sum(middle_grad * mixer_branch, axis=1)
        down_held = column_gather(down_piece, columns, cut=1)
        up_held = column_gather(up_piece, columns, cut=1)
        earlier, weight_parts = [], [None] * sequences
        grads_now = grads_one
        for k in range(sequences)[::-1]:
            qkv, heads_out, log_total, mask = kept[k]
            qkv_grad, *share = attend_backward(
                grads_now, weights[k], qkv, log_total, cos, sin, mask, earlier, k == 0
            )
            earlier.append((qkv_grad, weights[k]))
            weight_parts[k] = weight_grads(inputs_one, qkv_grad, grads_one, heads_out, columns)
            if k:
                grads_now, *weight_parts[k] = lax.optimization_barrier((grads_now, *weight_parts[k]))
        down_held = gate_lanes(down_held, earlier[0][0])
        up_held = gate_lanes(up_held, earlier[0][0])
        normed_grad_one = from_sequence(share[0])

        down_held = column_gather(down_held, columns, start=1)
        up_held = column_gather(up_held, columns, start=1)
        down_sum, = place_blocks(down_held, column, [(1, dim, jnp.float32, False)])
        up_sum, = place_blocks(up_held, column, [(1, cols_local, jnp.float32, False)])

        pieces = column_scatter(weight_parts[0], columns, column)
        for k in range(1, sequences):
            there = column_scatter(weight_parts[k], columns, column)
            back = shift_pairs(ranks, -k * group)
            pieces = [narrow(wide(p) + wide(lax.ppermute(t, "mp", back))) for p, t in zip(pieces, there)]
        attention_sum, output_sum = place_blocks(
            column_gather(pieces, columns),
            column,
            [(3, width, jnp.float32, False), (1, width, jnp.float32, True)],
        )
        attention_sum = attention_sum.transpose(1, 0, 2)

        router_part_one, router_one = gate_backward(normed_one, mixer_router, state_one, gate_grad_one)
        input_part, gain_one = norm_backward(normed_grad_one + router_part_one, scaled_one, inverse_one, mixer_gain)
        input_grad = narrow(middle_grad + input_part)

        sizes = {"mp": ranks, "dp": columns}

        smalls = [gain_two, gain_one, router_two.T, router_one.T]
        small_sum = all_sum(jnp.concatenate([x.reshape(-1, 128) for x in smalls], axis=0), sizes)
        cuts = [dim // 128, 2 * dim // 128, (2 * dim + router_two.size) // 128]
        hidden_gain_sum, mixer_gain_sum, hidden_router_sum, mixer_router_sum = (
            x.reshape(-1, dim) for x in jnp.split(small_sum, cuts)
        )
        hidden_gain_sum, mixer_gain_sum = hidden_gain_sum[0], mixer_gain_sum[0]
        hidden_router_sum, mixer_router_sum = hidden_router_sum.T, mixer_router_sum.T
        return (
            layer_output, input_grad, mixer_gain_sum, mixer_router_sum, attention_sum, output_sum,
            hidden_gain_sum, hidden_router_sum, up_sum, down_sum,
        )

    return local


def solution(mesh):
    return jax.shard_map(
        make_local(mesh.shape["dp"], mesh.shape["mp"]),
        mesh=mesh,
        in_specs=(
            P(("dp", "mp"), None),
            P("dp", None),
            P("dp", None),
            P(),
            P(),
            P(None, None, "mp"),
            P("mp", None),
            P(),
            P(),
            P(None, "mp"),
            P("mp", None),
            P(("dp", "mp"), None),
        ),
        out_specs=(
            P(("dp", "mp"), None),
            P(("dp", "mp"), None),
            P(),
            P(),
            P(None, None, "mp"),
            P("mp", None),
            P(),
            P(),
            P(None, "mp"),
            P("mp", None),
        ),
        check_vma=False,
    )
```

```python
import functools
import math

import jax
import jax.numpy as jnp
from jax import lax
from jax.experimental import pallas as pl
from jax.experimental.pallas import tpu as pltpu
from jax.sharding import PartitionSpec as P

H = 16
HD = 128
FF = 8192
SEQ_LEN = 1024


EPSILON = 1e-05
NEG_LARGE = -1e30
HIGHEST = lax.Precision.HIGHEST


def norm_forward(values, gain_vec):
    row_mean = jnp.mean(values, axis=1, keepdims=True)
    centred = values - row_mean
    row_variance = jnp.mean(centred * centred, axis=1, keepdims=True)
    inverse_scale = lax.rsqrt(row_variance + EPSILON)
    scaled = centred * inverse_scale
    return (scaled * gain_vec[None, :], scaled, inverse_scale)


def norm_backward(normed_grad, scaled, inverse_scale, gain_vec):
    gain_grad = jnp.sum(normed_grad * scaled, axis=0)
    scaled_grad = normed_grad * gain_vec[None, :]
    first_mean = jnp.mean(scaled_grad, axis=1, keepdims=True)
    second_mean = jnp.mean(scaled_grad * scaled, axis=1, keepdims=True)
    return (inverse_scale * (scaled_grad - first_mean - scaled * second_mean), gain_grad)


def gate_forward(normed, router, width_col, routed_col):
    logits = jnp.dot(normed, router, precision=HIGHEST, preferred_element_type=jnp.float32)
    soft_probs = jax.nn.softmax(logits, axis=1)
    one_hot = (width_col[:, None] == jnp.arange(4, dtype=jnp.int32)[None, :]).astype(jnp.float32)
    chosen = jnp.sum(soft_probs * one_hot, axis=1)
    route_flags = routed_col.astype(jnp.float32)
    return (
        route_flags * 4.0 * chosen + (1.0 - route_flags),
        (soft_probs, one_hot, chosen, route_flags),
    )


def gate_backward(normed, router, gate_state, gate_grad):
    soft_probs, one_hot, chosen, route_flags = gate_state
    coefficient = route_flags * 4.0 * chosen * gate_grad
    logit_grad = coefficient[:, None] * (one_hot - soft_probs)
    router_grad = lax.dot_general(
        normed,
        logit_grad,
        (((0,), (0,)), ((), ())),
        precision=HIGHEST,
        preferred_element_type=jnp.float32,
    )
    normed_grad = lax.dot_general(
        logit_grad,
        router,
        (((1,), (1,)), ((), ())),
        precision=HIGHEST,
        preferred_element_type=jnp.float32,
    )
    return (normed_grad, router_grad)


Q_BLOCK = 256


def rope_tables(token_count, head_width):
    positions = jnp.arange(token_count, dtype=jnp.float32)
    frequency = jnp.exp(
        jnp.arange(head_width // 2, dtype=jnp.float32) * (-2.0 * math.log(10000.0) / head_width)
    )
    angles = positions[:, None] * frequency[None, :]
    cosine, sine = jnp.cos(angles), jnp.sin(angles)
    return jnp.concatenate([cosine, cosine], axis=1), jnp.concatenate([-sine, sine], axis=1)


def wide(x):
    return x.astype(jnp.float32)


def narrow(x):
    return x.astype(jnp.bfloat16)


def product(a, b, dims):
    return lax.dot_general(a, b, ((dims[:1], dims[1:]), ((), ())), preferred_element_type=jnp.float32)


def block_scores(queries, keys_all, start):
    scores = product(queries, keys_all, (1, 1)) * (1.0 / math.sqrt(HD))
    row = lax.broadcasted_iota(jnp.int32, scores.shape, 0) + start
    col = lax.broadcasted_iota(jnp.int32, scores.shape, 1)
    return jnp.where(col <= row, scores, NEG_LARGE)


def forward_kernel(earlier, *refs):
    x_ref, w_ref, cos_ref, sin_ref, mask_ref = refs[:5]
    others = refs[5 : 5 + 2 * earlier]
    qkv_ref, heads_ref, log_ref, *share_ref = refs[5 + 2 * earlier :]
    tokens, heads = x_ref.shape[0], mask_ref.shape[1]
    width = heads * HD
    block = min(Q_BLOCK, tokens)
    for start in range(0, tokens, block):
        here, end = slice(start, start + block), start + block
        x = x_ref[here, :]
        cos, sin = cos_ref[here, :], sin_ref[here, :]
        for part in range(3):
            rows = product(x, w_ref[:, part * width : (part + 1) * width], (1, 0))
            for head in range(heads):
                value = rows[:, head * HD : (head + 1) * HD]
                if part < 2:
                    value = value * cos + pltpu.roll(value, HD // 2, 1) * sin
                at = part * width + head * HD
                qkv_ref[here, at : at + HD] = narrow(value)
        for head in range(heads):
            at = head * HD
            lanes, key_lanes, value_lanes = (slice(at + p * width, at + p * width + HD) for p in range(3))
            scores = block_scores(qkv_ref[here, lanes], qkv_ref[:end, key_lanes], start)
            row_max = jnp.max(scores, axis=1, keepdims=True)
            shifted = jnp.exp(scores - row_max)
            total = jnp.sum(shifted, axis=1, keepdims=True)
            mix = product(narrow(shifted / total), qkv_ref[:end, value_lanes], (1, 0))
            heads_ref[here, lanes] = narrow(mix * mask_ref[here, head : head + 1])
            log_ref[here, head : head + 1] = row_max + jnp.log(total)
        if share_ref:
            share = product(heads_ref[here, :], w_ref[:, 3 * width :], (1, 1))
            for k in range(earlier):
                share = share + product(others[2 * k][here, :], others[2 * k + 1][:, 3 * width :], (1, 1))
            share_ref[0][here, :] = narrow(share)


def backward_kernel(earlier, *refs):
    g_ref, w_ref, qkv_ref, log_ref, cos_ref, sin_ref, mask_ref = refs[:7]
    others = refs[7 : 7 + 2 * earlier]
    *outs, keys_acc, values_acc = refs[7 + 2 * earlier :]
    out_ref = outs[0]
    tokens, heads = g_ref.shape[0], mask_ref.shape[1]
    width = heads * HD
    block = min(Q_BLOCK, tokens)
    scale = 1.0 / math.sqrt(HD)
    for start in range(0, tokens, block):
        here, end = slice(start, start + block), start + block
        cos, sin = cos_ref[here, :], sin_ref[here, :]
        rows = narrow(product(g_ref[here, :], w_ref[:, 3 * width :], (1, 0)))
        for head in range(heads):
            at = head * HD
            lanes, key_lanes, value_lanes = (slice(at + p * width, at + p * width + HD) for p in range(3))
            heads_grad = rows[:, lanes] * narrow(mask_ref[here, head : head + 1])
            queries, keys_all = qkv_ref[here, lanes], qkv_ref[:end, key_lanes]
            scores = block_scores(queries, keys_all, start)
            probs = jnp.exp(scores - log_ref[here, head : head + 1])
            values_part = product(narrow(probs), heads_grad, (0, 0))
            probs_grad = product(heads_grad, qkv_ref[:end, value_lanes], (1, 1))
            centre = jnp.sum(probs * probs_grad, axis=1, keepdims=True)
            score_grad = narrow(probs * (probs_grad - centre))
            queries_grad = product(score_grad, keys_all, (1, 0)) * scale
            keys_part = product(score_grad, queries, (0, 0)) * scale
            turned = queries_grad * cos - pltpu.roll(queries_grad, HD // 2, 1) * sin
            out_ref[here, lanes] = narrow(turned)
            if start:
                values_acc[:start, lanes] += values_part[:start]
                keys_acc[:start, lanes] += keys_part[:start]
            values_acc[here, lanes] = values_part[start:]
            keys_acc[here, lanes] = keys_part[start:]
    for start in range(0, tokens, block):
        here = slice(start, start + block)
        cos, sin = cos_ref[here, :], sin_ref[here, :]
        out_ref[here, 2 * width :] = narrow(values_acc[here, :])
        for head in range(heads):
            at = head * HD
            value = keys_acc[here, at : at + HD]
            out_ref[here, width + at : width + at + HD] = narrow(value * cos - pltpu.roll(value, HD // 2, 1) * sin)
        if outs[1:]:
            share = product(out_ref[here, :], w_ref[:, : 3 * width], (1, 1))
            for k in range(earlier):
                share = share + product(others[2 * k][here, :], others[2 * k + 1][:, : 3 * width], (1, 1))
            outs[1][here, :] = narrow(share)


def weight_kernel(x_ref, q_ref, g_ref, h_ref, *outs):
    width = h_ref.shape[1]
    half = x_ref.shape[1] // 2
    for lane, out_ref in enumerate(outs):
        here = slice(lane * half, (lane + 1) * half)
        out_ref[0, :, : 3 * width] = narrow(product(x_ref[:, here], q_ref[...], (0, 0)))
        out_ref[0, :, 3 * width :] = narrow(product(g_ref[:, here], h_ref[...], (0, 0)))


def place_kernel(count, widths, turned, at_ref, *refs):
    lanes = (len(refs) - len(widths)) // count
    blocks, outs = refs[: lanes * count], refs[lanes * count :]
    half = blocks[0].shape[0]
    for far in range(count):

        @pl.when((pl.program_id(0) ^ at_ref[0]) == far)
        def _():
            for lane in range(lanes):
                here = slice(lane * half, (lane + 1) * half)
                block = blocks[lane * count + far]
                start = 0
                for out_ref, width, turn in zip(outs, widths, turned):
                    for part in range(out_ref.shape[0] if len(out_ref.shape) == 3 else 1):
                        value = block[:, start : start + width].astype(out_ref.dtype)
                        start += width
                        if turn:
                            out_ref[:, here] = value.T
                        elif len(out_ref.shape) == 3:
                            out_ref[part, here, :] = value
                        else:
                            out_ref[here, :] = value


VMEM_LIMIT = 56 * 1024 * 1024


def whole_specs(count):
    return [pl.BlockSpec(memory_space=pltpu.VMEM)] * count


def attend_forward(x, w, cos, sin, mask, earlier, last):
    tokens, heads = mask.shape
    dim, width = w.shape[0], heads * HD
    flops = 2 * tokens * dim * width * 3 + 2 * tokens * tokens * width
    out = [
        jax.ShapeDtypeStruct((tokens, 3 * width), jnp.bfloat16),
        jax.ShapeDtypeStruct((tokens, width), jnp.bfloat16),
        jax.ShapeDtypeStruct((tokens, heads), jnp.float32),
    ]
    given = [a for pair in earlier for a in pair] if last else []
    if last:
        out.append(jax.ShapeDtypeStruct((tokens, dim), jnp.bfloat16))
        flops += 2 * tokens * dim * width * (1 + len(earlier))
    return pl.pallas_call(
        functools.partial(forward_kernel, len(given) // 2),
        out_shape=out,
        in_specs=whole_specs(5 + len(given)),
        out_specs=whole_specs(len(out)),
        compiler_params=pltpu.CompilerParams(vmem_limit_bytes=VMEM_LIMIT),
        cost_estimate=pl.CostEstimate(flops=flops, bytes_accessed=12 << 20, transcendentals=tokens * tokens * heads // 2),
        name="attend_forward",
    )(x, w, cos, sin, mask, *given)


def attend_backward(g, w, qkv, log_total, cos, sin, mask, earlier, last):
    tokens, heads = mask.shape
    dim, width = w.shape[0], heads * HD
    flops = 2 * tokens * dim * width + 5 * tokens * tokens * width
    out = [jax.ShapeDtypeStruct((tokens, 3 * width), jnp.bfloat16)]
    given = [a for pair in earlier for a in pair] if last else []
    if last:
        out.append(jax.ShapeDtypeStruct((tokens, dim), jnp.bfloat16))
        flops += 6 * tokens * dim * width * (1 + len(earlier))
    return pl.pallas_call(
        functools.partial(backward_kernel, len(given) // 2),
        out_shape=out,
        in_specs=whole_specs(7 + len(given)),
        out_specs=whole_specs(len(out)),
        scratch_shapes=[pltpu.VMEM((tokens, width), jnp.float32)] * 2,
        compiler_params=pltpu.CompilerParams(vmem_limit_bytes=VMEM_LIMIT),
        cost_estimate=pl.CostEstimate(flops=flops, bytes_accessed=12 << 20, transcendentals=tokens * tokens * heads // 2),
        name="attend_backward",
    )(g, w, qkv, log_total, cos, sin, mask, *given)


def weight_grads(x, qkv_grad, g, heads_out, count):
    tokens, dim = x.shape
    width = heads_out.shape[1]
    block = dim // count
    out = jax.ShapeDtypeStruct((count, block // 2, 4 * width), jnp.bfloat16)
    return pl.pallas_call(
        weight_kernel,
        grid=(count,),
        out_shape=[out, out],
        in_specs=[
            pl.BlockSpec((tokens, block), lambda i: (0, i)),
            pl.BlockSpec((tokens, 3 * width), lambda i: (0, 0)),
            pl.BlockSpec((tokens, block), lambda i: (0, i)),
            pl.BlockSpec((tokens, width), lambda i: (0, 0)),
        ],
        out_specs=[pl.BlockSpec((1, block // 2, 4 * width), lambda i: (i, 0, 0))] * 2,
        compiler_params=pltpu.CompilerParams(vmem_limit_bytes=VMEM_LIMIT),
        cost_estimate=pl.CostEstimate(flops=8 * tokens * dim * width, bytes_accessed=14 << 20, transcendentals=0),
        name="weight_grads",
    )(x, qkv_grad, g, heads_out)


def place_blocks(lanes, index, outs):
    count = len(lanes[0])
    half, total = lanes[0][0].shape
    rows = len(lanes) * half
    shapes, specs = [], []
    for planes, width, kind, turned in outs:
        if turned:
            shapes.append(jax.ShapeDtypeStruct((width, rows * count), kind))
            specs.append(pl.BlockSpec((width, rows), lambda i, at: (0, i)))
        elif planes > 1:
            shapes.append(jax.ShapeDtypeStruct((planes, rows * count, width), kind))
            specs.append(pl.BlockSpec((planes, rows, width), lambda i, at: (0, i, 0)))
        else:
            shapes.append(jax.ShapeDtypeStruct((rows * count, width), kind))
            specs.append(pl.BlockSpec((rows, width), lambda i, at: (i, 0)))
    given = [held[far] for held in lanes for far in range(count)]
    return pl.pallas_call(
        functools.partial(place_kernel, count, [o[1] for o in outs], [o[3] for o in outs]),
        grid_spec=pltpu.PrefetchScalarGridSpec(
            num_scalar_prefetch=1,
            grid=(count,),
            in_specs=[pl.BlockSpec((half, total), lambda i, at: (0, 0))] * len(given),
            out_specs=specs,
        ),
        out_shape=shapes,
        compiler_params=pltpu.CompilerParams(vmem_limit_bytes=VMEM_LIMIT),
        cost_estimate=pl.CostEstimate(flops=0, bytes_accessed=12 << 20, transcendentals=0),
        name="place_blocks",
    )(index.astype(jnp.int32).reshape(1), *given)


def swap_pairs(size, bit):
    return [(i, i ^ bit) for i in range(size)]


def shift_pairs(size, shift):
    return [(i, (i - shift) % size) for i in range(size)]


def bits_of(size):
    return [1 << i for i in range(size.bit_length() - 1)]


def pick(x, index, axis=0):
    return lax.dynamic_index_in_dim(x, index, axis, keepdims=False)


def after(x, *others):
    return lax.optimization_barrier((x,) + others)[0]


def xor_gather(x, axis, size, bits):
    held = dict(x) if isinstance(x, dict) else {0: x}
    for bit in bits:
        for far in list(held):
            held[far ^ bit] = lax.ppermute(held[far], axis, swap_pairs(size, bit))
    return held


def by_index(held, index, axis=0):
    shape = held[0].shape
    out = jnp.zeros(shape[:axis] + (len(held),) + shape[axis:], held[0].dtype)
    for far, block in held.items():
        out = lax.dynamic_update_index_in_dim(out, block, index ^ far, axis)
    return out


def xor_scatter(blocks, axis_name, size, bits, steps, index, axis, all_steps=None):
    all_steps = list(all_steps or steps)
    left = sorted(all_steps[all_steps.index(steps[0]) :], reverse=True)
    blocks = blocks.reshape(blocks.shape[:axis] + (2,) * len(left) + blocks.shape[axis + 1 :])
    for bit, step in zip(bits, steps):
        at = axis + left.index(step)
        left.remove(step)
        side = (index // step) % 2
        got = lax.ppermute(narrow(pick(blocks, 1 - side, at)), axis_name, swap_pairs(size, bit))
        blocks = wide(pick(blocks, side, at)) + wide(got)
    tail = blocks.shape[axis + len(left) :]
    return blocks.reshape(blocks.shape[:axis] + ((2 ** len(left),) if left else ()) + tail)


def lane_bits(size):
    return bits_of(size), bits_of(size)[::-1]


def column_gather(lanes, size, cut=None, start=None):
    return [xor_gather(x, "dp", size, bits[start:cut]) for x, bits in zip(lanes, lane_bits(size))]


def gate_lanes(lanes, *gates):
    flat = [held[far] for held in lanes for far in held]
    flat = lax.optimization_barrier((*flat, *gates))
    flat = iter(flat)
    return [{far: next(flat) for far in held} for held in lanes]


def column_scatter(lanes, size, column, cut=None, start=None):
    return [
        xor_scatter(x, "dp", size, bits[start:cut], bits[start:cut], column, 0, bits)
        for x, bits in zip(lanes, lane_bits(size))
    ]


def all_sum(x, sizes):
    for axis, size in sizes.items():
        for bit in bits_of(size):
            x = x + lax.ppermute(x, axis, swap_pairs(size, bit))
    return x


def make_local(columns, ranks):
    def local(
        layer_input, width_choice, routed_flag, mixer_gain, mixer_router, attention_weight,
        output_weight, hidden_gain, hidden_router, up_weight, down_weight, out_grad,
    ):
        column, rank = lax.axis_index("dp"), lax.axis_index("mp")
        rows, dim = layer_input.shape
        core = rank % 2
        group = SEQ_LEN // rows
        sequences = ranks // group
        place, sequence = rank % group, rank // group
        pair_bits = [b for b in bits_of(group) if b > 1]
        own_heads = output_weight.shape[0] // HD
        cols_local = up_weight.shape[1]
        width_own = lax.dynamic_slice_in_dim(width_choice, rank * rows, rows, 0)
        routed_own = lax.dynamic_slice_in_dim(routed_flag, rank * rows, rows, 0)
        cos, sin = rope_tables(SEQ_LEN, HD)

        def to_sequence(x):
            held = xor_gather(x, "mp", ranks, pair_bits + [1])
            return by_index(held, place).reshape(SEQ_LEN, -1), held

        def from_sequence(x):
            blocks = x.reshape(group // 2, 2, -1, x.shape[1])
            got = lax.ppermute(narrow(pick(blocks, 1 - core, 1)), "mp", swap_pairs(ranks, 1))
            blocks = wide(pick(blocks, core, 1)) + wide(got)
            bits = pair_bits[::-1]
            return xor_scatter(blocks, "mp", ranks, bits, [b // 2 for b in bits], place // 2, 0)

        width = own_heads * HD
        packed = jnp.concatenate([attention_weight[:, p] for p in range(3)] + [output_weight.T], axis=1)
        chunk_rows = dim // columns
        chunks = [
            lax.dynamic_slice_in_dim(packed, column * chunk_rows + at, chunk_rows // 2, 0)
            for at in (0, chunk_rows // 2)
        ]
        input_wide = wide(layer_input)
        normed_one, scaled_one, inverse_one = norm_forward(input_wide, mixer_gain)
        inputs_one, held_one = to_sequence(narrow(normed_one))
        fetched = [
            lax.ppermute(lane, "mp", shift_pairs(ranks, k * group)) for k in range(1, sequences) for lane in chunks
        ]
        inputs_one, *fetched = lax.optimization_barrier((inputs_one, *fetched))
        helds = [column_gather(fetched[2 * k - 2 : 2 * k], columns, cut=1) for k in range(1, sequences)]
        gate_one, state_one = gate_forward(normed_one, mixer_router, width_own[:, 0], routed_own[:, 0])
        grads_all = lax.all_gather(after(out_grad, *fetched), "mp", axis=0, tiled=True)

        sequence_width = lax.dynamic_slice_in_dim(width_choice[:, 0], sequence * SEQ_LEN, SEQ_LEN, 0)
        weights, kept, earlier = [packed], [], []
        for k in range(sequences):
            heads = ((rank + k * group) % ranks) * own_heads + jnp.arange(own_heads, dtype=jnp.int32)
            mask = (heads[None, :] * 4 < (sequence_width[:, None] + 1) * H).astype(jnp.float32)
            last = k == sequences - 1
            if k:
                held = column_gather(gate_lanes(helds[k - 1], kept[0][0]), columns, start=1)
                weights += place_blocks(held, column, [(1, packed.shape[1], jnp.bfloat16, False)])
            qkv, heads_out, log_total, *share = attend_forward(inputs_one, weights[k], cos, sin, mask, earlier, last)
            kept.append((qkv, heads_out, log_total, mask))
            earlier.append((heads_out, weights[k]))
        mixer_branch = from_sequence(share[0])
        mixer_branch, grads_all = lax.optimization_barrier((mixer_branch, grads_all))
        top_down = product(grads_all, down_weight, (1, 1))

        middle = input_wide + gate_one[:, None] * mixer_branch
        normed_two, scaled_two, inverse_two = norm_forward(middle, hidden_gain)
        gate_two, state_two = gate_forward(normed_two, hidden_router, width_own[:, 1], routed_own[:, 1])
        inputs_two = lax.all_gather(narrow(normed_two), "mp", axis=0, tiled=True)
        gates = by_index(xor_gather(gate_two.reshape(-1, 128), "mp", ranks, bits_of(ranks)), rank).reshape(-1)

        col_ids = rank * cols_local + jnp.arange(cols_local, dtype=jnp.int32)
        col_mask = (col_ids[None, :] * 4 < (width_choice[:, 1:2] + 1) * FF).astype(jnp.float32)
        inputs_two, top_down = lax.optimization_barrier((inputs_two, top_down))
        pre = product(inputs_two, up_weight, (1, 0))
        relu_act = jax.nn.relu(pre)
        hidden = narrow(relu_act * relu_act * col_mask)
        pre_grad = narrow(top_down * gates[:, None] * col_mask * 2.0 * relu_act)
        dots = jnp.sum(wide(hidden) * top_down, axis=1).reshape(-1, 128)
        share = narrow(product(pre_grad, up_weight, (1, 1)))
        share, hidden, pre_grad = lax.optimization_barrier((share, hidden, pre_grad))
        normed_grad_two = wide(lax.psum_scatter(share, "mp", scatter_dimension=0, tiled=True))
        gate_grad_two = lax.dynamic_slice_in_dim(all_sum(dots, {"mp": ranks}).reshape(-1), rank * rows, rows, 0)
        gated = narrow(gates[:, None] * wide(grads_all))
        lanes = [narrow(product(hidden, gated, (0, 0))), narrow(product(inputs_two, pre_grad, (0, 0)))]
        lanes = [x.reshape(columns, -1, x.shape[1]) for x in lanes]
        lanes = column_scatter(lanes, columns, column, cut=1)
        hidden_share = narrow(product(hidden, down_weight, (1, 0)))
        normed_grad_two, hidden_share, *lanes = lax.optimization_barrier((normed_grad_two, hidden_share, *lanes))
        lanes = [narrow(x) for x in column_scatter(lanes, columns, column, start=1)]

        router_part, router_two = gate_backward(normed_two, hidden_router, state_two, gate_grad_two)
        middle_part, gain_two = norm_backward(normed_grad_two + router_part, scaled_two, inverse_two, hidden_gain)
        middle_grad = wide(out_grad) + middle_part
        grads_one, held_grads = to_sequence(narrow(gate_one[:, None] * middle_grad))
        grads_one, hidden_share, *lanes = lax.optimization_barrier((grads_one, hidden_share, *lanes))
        hidden_branch = wide(lax.psum_scatter(hidden_share, "mp", scatter_dimension=0, tiled=True))
        layer_output = narrow(middle + gate_two[:, None] * hidden_branch)

        gate_grad_one = jnp.sum(middle_grad * mixer_branch, axis=1)
        helds = column_gather(lanes, columns, cut=1)
        earlier, weight_parts = [], [None] * sequences
        grads_now = grads_one
        for k in range(sequences)[::-1]:
            qkv, heads_out, log_total, mask = kept[k]
            qkv_grad, *share = attend_backward(
                grads_now, weights[k], qkv, log_total, cos, sin, mask, earlier, k == 0
            )
            earlier.append((qkv_grad, weights[k]))
            if k == 0:
                helds = column_gather(helds, columns, start=1)
                flat = [held[far] for held in helds for far in held]
                qkv_grad, *flat = lax.optimization_barrier((qkv_grad, *flat))
                helds = [dict(zip(held, flat[i * columns :])) for i, held in enumerate(helds)]
            weight_parts[k] = weight_grads(inputs_one, qkv_grad, grads_one, heads_out, columns)
            if k == sequences - 1:
                flat = [held[far] for held in helds for far in held]
                grads_now, *rest = lax.optimization_barrier((grads_now, *weight_parts[k], *flat))
                weight_parts[k], flat = rest[:2], rest[2:]
                helds = [dict(zip(held, flat[i * 2 :])) for i, held in enumerate(helds)]
        normed_grad_one = from_sequence(share[0])

        down_sum, = place_blocks(helds[:1], column, [(1, dim, jnp.float32, False)])
        up_sum, = place_blocks(helds[1:], column, [(1, cols_local, jnp.float32, False)])

        pieces = column_scatter(weight_parts[0], columns, column)
        for k in range(1, sequences):
            there = [narrow(x) for x in column_scatter(weight_parts[k], columns, column)]
            back = shift_pairs(ranks, -k * group)
            pieces = [narrow(p + wide(lax.ppermute(t, "mp", back))) for p, t in zip(pieces, there)]
        attention_sum, output_sum = place_blocks(
            column_gather(pieces, columns),
            column,
            [(3, width, jnp.float32, False), (1, width, jnp.float32, True)],
        )
        attention_sum = attention_sum.transpose(1, 0, 2)

        router_part_one, router_one = gate_backward(normed_one, mixer_router, state_one, gate_grad_one)
        input_part, gain_one = norm_backward(normed_grad_one + router_part_one, scaled_one, inverse_one, mixer_gain)
        input_grad = narrow(middle_grad + input_part)

        sizes = {"mp": ranks, "dp": columns}

        smalls = [gain_two, gain_one, router_two.T, router_one.T]
        small_sum = all_sum(jnp.concatenate([x.reshape(-1, 128) for x in smalls], axis=0), sizes)
        cuts = [dim // 128, 2 * dim // 128, (2 * dim + router_two.size) // 128]
        hidden_gain_sum, mixer_gain_sum, hidden_router_sum, mixer_router_sum = (
            x.reshape(-1, dim) for x in jnp.split(small_sum, cuts)
        )
        hidden_gain_sum, mixer_gain_sum = hidden_gain_sum[0], mixer_gain_sum[0]
        hidden_router_sum, mixer_router_sum = hidden_router_sum.T, mixer_router_sum.T
        return (
            layer_output, input_grad, mixer_gain_sum, mixer_router_sum, attention_sum, output_sum,
            hidden_gain_sum, hidden_router_sum, up_sum, down_sum,
        )

    return local


def solution(mesh):
    return jax.shard_map(
        make_local(mesh.shape["dp"], mesh.shape["mp"]),
        mesh=mesh,
        in_specs=(
            P(("dp", "mp"), None),
            P("dp", None),
            P("dp", None),
            P(),
            P(),
            P(None, None, "mp"),
            P("mp", None),
            P(),
            P(),
            P(None, "mp"),
            P("mp", None),
            P(("dp", "mp"), None),
        ),
        out_specs=(
            P(("dp", "mp"), None),
            P(("dp", "mp"), None),
            P(),
            P(),
            P(None, None, "mp"),
            P("mp", None),
            P(),
            P(),
            P(None, "mp"),
            P("mp", None),
        ),
        check_vma=False,
    )
```

```python
import functools
import math

import jax
import jax.numpy as jnp
from jax import lax
from jax.experimental import pallas as pl
from jax.experimental.pallas import tpu as pltpu
from jax.sharding import PartitionSpec as P

H = 16
HD = 128
FF = 8192
SEQ_LEN = 1024


EPSILON = 1e-05
NEG_LARGE = -1e30
HIGHEST = lax.Precision.HIGHEST


def norm_forward(values, gain_vec):
    row_mean = jnp.mean(values, axis=1, keepdims=True)
    centred = values - row_mean
    row_variance = jnp.mean(centred * centred, axis=1, keepdims=True)
    inverse_scale = lax.rsqrt(row_variance + EPSILON)
    scaled = centred * inverse_scale
    return (scaled * gain_vec[None, :], scaled, inverse_scale)


def norm_backward(normed_grad, scaled, inverse_scale, gain_vec):
    gain_grad = jnp.sum(normed_grad * scaled, axis=0)
    scaled_grad = normed_grad * gain_vec[None, :]
    first_mean = jnp.mean(scaled_grad, axis=1, keepdims=True)
    second_mean = jnp.mean(scaled_grad * scaled, axis=1, keepdims=True)
    return (inverse_scale * (scaled_grad - first_mean - scaled * second_mean), gain_grad)


def gate_forward(normed, router, width_col, routed_col):
    logits = jnp.dot(normed, router, precision=HIGHEST, preferred_element_type=jnp.float32)
    soft_probs = jax.nn.softmax(logits, axis=1)
    one_hot = (width_col[:, None] == jnp.arange(4, dtype=jnp.int32)[None, :]).astype(jnp.float32)
    chosen = jnp.sum(soft_probs * one_hot, axis=1)
    route_flags = routed_col.astype(jnp.float32)
    return (
        route_flags * 4.0 * chosen + (1.0 - route_flags),
        (soft_probs, one_hot, chosen, route_flags),
    )


def gate_backward(normed, router, gate_state, gate_grad):
    soft_probs, one_hot, chosen, route_flags = gate_state
    coefficient = route_flags * 4.0 * chosen * gate_grad
    logit_grad = coefficient[:, None] * (one_hot - soft_probs)
    router_grad = lax.dot_general(
        normed,
        logit_grad,
        (((0,), (0,)), ((), ())),
        precision=HIGHEST,
        preferred_element_type=jnp.float32,
    )
    normed_grad = lax.dot_general(
        logit_grad,
        router,
        (((1,), (1,)), ((), ())),
        precision=HIGHEST,
        preferred_element_type=jnp.float32,
    )
    return (normed_grad, router_grad)


Q_BLOCK = 256


def rope_tables(token_count, head_width):
    positions = jnp.arange(token_count, dtype=jnp.float32)
    frequency = jnp.exp(
        jnp.arange(head_width // 2, dtype=jnp.float32) * (-2.0 * math.log(10000.0) / head_width)
    )
    angles = positions[:, None] * frequency[None, :]
    cosine, sine = jnp.cos(angles), jnp.sin(angles)
    return jnp.concatenate([cosine, cosine], axis=1), jnp.concatenate([-sine, sine], axis=1)


def wide(x):
    return x.astype(jnp.float32)


def narrow(x):
    return x.astype(jnp.bfloat16)


def product(a, b, dims):
    return lax.dot_general(a, b, ((dims[:1], dims[1:]), ((), ())), preferred_element_type=jnp.float32)


def block_scores(queries, keys_all, start):
    scores = product(queries, keys_all, (1, 1)) * (1.0 / math.sqrt(HD))
    row = lax.broadcasted_iota(jnp.int32, scores.shape, 0) + start
    col = lax.broadcasted_iota(jnp.int32, scores.shape, 1)
    return jnp.where(col <= row, scores, NEG_LARGE)


def store_share(refs, start, value):
    rows, parts = refs[0].shape[2], len(refs)
    for at in range(0, value.shape[0], rows):
        device, part = divmod((start + at) // rows, parts)
        refs[part][device % 2, device // 2] = value[at : at + rows]


def forward_kernel(earlier, *refs):
    x_ref, w_ref, cos_ref, sin_ref, mask_ref = refs[:5]
    others = refs[5 : 5 + 2 * earlier]
    qkv_ref, heads_ref, log_ref, *share_ref = refs[5 + 2 * earlier :]
    tokens, heads = x_ref.shape[0], mask_ref.shape[1]
    width = heads * HD
    block = min(Q_BLOCK, tokens)
    for start in range(0, tokens, block):
        here, end = slice(start, start + block), start + block
        x = x_ref[here, :]
        cos, sin = cos_ref[here, :], sin_ref[here, :]
        for part in range(3):
            rows = product(x, w_ref[:, part * width : (part + 1) * width], (1, 0))
            for head in range(heads):
                value = rows[:, head * HD : (head + 1) * HD]
                if part < 2:
                    value = value * cos + pltpu.roll(value, HD // 2, 1) * sin
                at = part * width + head * HD
                qkv_ref[here, at : at + HD] = narrow(value)
        for head in range(heads):
            at = head * HD
            lanes, key_lanes, value_lanes = (slice(at + p * width, at + p * width + HD) for p in range(3))
            scores = block_scores(qkv_ref[here, lanes], qkv_ref[:end, key_lanes], start)
            row_max = jnp.max(scores, axis=1, keepdims=True)
            shifted = jnp.exp(scores - row_max)
            total = jnp.sum(shifted, axis=1, keepdims=True)
            mix = product(narrow(shifted / total), qkv_ref[:end, value_lanes], (1, 0))
            heads_ref[here, lanes] = narrow(mix * mask_ref[here, head : head + 1])
            log_ref[here, head : head + 1] = row_max + jnp.log(total)
        if share_ref:
            share = product(heads_ref[here, :], w_ref[:, 3 * width :], (1, 1))
            for k in range(earlier):
                share = share + product(others[2 * k][here, :], others[2 * k + 1][:, 3 * width :], (1, 1))
            store_share(share_ref, start, narrow(share))


def backward_kernel(earlier, *refs):
    g_ref, w_ref, qkv_ref, log_ref, cos_ref, sin_ref, mask_ref = refs[:7]
    others = refs[7 : 7 + 2 * earlier]
    *outs, keys_acc, values_acc = refs[7 + 2 * earlier :]
    out_ref = outs[0]
    tokens, heads = g_ref.shape[0], mask_ref.shape[1]
    width = heads * HD
    block = min(Q_BLOCK, tokens)
    scale = 1.0 / math.sqrt(HD)
    for start in range(0, tokens, block):
        here, end = slice(start, start + block), start + block
        cos, sin = cos_ref[here, :], sin_ref[here, :]
        rows = narrow(product(g_ref[here, :], w_ref[:, 3 * width :], (1, 0)))
        for head in range(heads):
            at = head * HD
            lanes, key_lanes, value_lanes = (slice(at + p * width, at + p * width + HD) for p in range(3))
            heads_grad = rows[:, lanes] * narrow(mask_ref[here, head : head + 1])
            queries, keys_all = qkv_ref[here, lanes], qkv_ref[:end, key_lanes]
            scores = block_scores(queries, keys_all, start)
            probs = jnp.exp(scores - log_ref[here, head : head + 1])
            values_part = product(narrow(probs), heads_grad, (0, 0))
            probs_grad = product(heads_grad, qkv_ref[:end, value_lanes], (1, 1))
            centre = jnp.sum(probs * probs_grad, axis=1, keepdims=True)
            score_grad = narrow(probs * (probs_grad - centre))
            queries_grad = product(score_grad, keys_all, (1, 0)) * scale
            keys_part = product(score_grad, queries, (0, 0)) * scale
            turned = queries_grad * cos - pltpu.roll(queries_grad, HD // 2, 1) * sin
            out_ref[here, lanes] = narrow(turned)
            if start:
                values_acc[:start, lanes] += values_part[:start]
                keys_acc[:start, lanes] += keys_part[:start]
            values_acc[here, lanes] = values_part[start:]
            keys_acc[here, lanes] = keys_part[start:]
    for start in range(0, tokens, block):
        here = slice(start, start + block)
        cos, sin = cos_ref[here, :], sin_ref[here, :]
        out_ref[here, 2 * width :] = narrow(values_acc[here, :])
        for head in range(heads):
            at = head * HD
            value = keys_acc[here, at : at + HD]
            out_ref[here, width + at : width + at + HD] = narrow(value * cos - pltpu.roll(value, HD // 2, 1) * sin)
        if outs[1:]:
            share = product(out_ref[here, :], w_ref[:, : 3 * width], (1, 1))
            for k in range(earlier):
                share = share + product(others[2 * k][here, :], others[2 * k + 1][:, : 3 * width], (1, 1))
            store_share(outs[1:], start, narrow(share))


def weight_kernel(x_ref, q_ref, g_ref, h_ref, *outs):
    width = h_ref.shape[1]
    half = x_ref.shape[1] // 2
    for lane, out_ref in enumerate(outs):
        here = slice(lane * half, (lane + 1) * half)
        out_ref[0, :, : 3 * width] = narrow(product(x_ref[:, here], q_ref[...], (0, 0)))
        out_ref[0, :, 3 * width :] = narrow(product(g_ref[:, here], h_ref[...], (0, 0)))


def place_kernel(count, widths, turned, at_ref, *refs):
    lanes = (len(refs) - len(widths)) // count
    blocks, outs = refs[: lanes * count], refs[lanes * count :]
    half = blocks[0].shape[0]
    for far in range(count):

        @pl.when((pl.program_id(0) ^ at_ref[0]) == far)
        def _():
            for lane in range(lanes):
                here = slice(lane * half, (lane + 1) * half)
                block = blocks[lane * count + far]
                start = 0
                for out_ref, width, turn in zip(outs, widths, turned):
                    for part in range(out_ref.shape[0] if len(out_ref.shape) == 3 else 1):
                        value = block[:, start : start + width].astype(out_ref.dtype)
                        start += width
                        if turn:
                            out_ref[:, here] = value.T
                        elif len(out_ref.shape) == 3:
                            out_ref[part, here, :] = value
                        else:
                            out_ref[here, :] = value


VMEM_LIMIT = 56 * 1024 * 1024


def whole_specs(count):
    return [pl.BlockSpec(memory_space=pltpu.VMEM)] * count


def attend_forward(x, w, cos, sin, mask, earlier, share):
    tokens, heads = mask.shape
    dim, width = w.shape[0], heads * HD
    flops = 2 * tokens * dim * width * 3 + 2 * tokens * tokens * width
    out = [
        jax.ShapeDtypeStruct((tokens, 3 * width), jnp.bfloat16),
        jax.ShapeDtypeStruct((tokens, width), jnp.bfloat16),
        jax.ShapeDtypeStruct((tokens, heads), jnp.float32),
    ]
    given = [a for pair in earlier for a in pair] if share else []
    if share:
        out += [jax.ShapeDtypeStruct(share[1:], jnp.bfloat16)] * share[0]
        flops += 2 * tokens * dim * width * (1 + len(earlier))
    return pl.pallas_call(
        functools.partial(forward_kernel, len(given) // 2),
        out_shape=out,
        in_specs=whole_specs(5 + len(given)),
        out_specs=whole_specs(len(out)),
        compiler_params=pltpu.CompilerParams(vmem_limit_bytes=VMEM_LIMIT),
        cost_estimate=pl.CostEstimate(flops=flops, bytes_accessed=12 << 20, transcendentals=tokens * tokens * heads // 2),
        name="attend_forward",
    )(x, w, cos, sin, mask, *given)


def attend_backward(g, w, qkv, log_total, cos, sin, mask, earlier, share):
    tokens, heads = mask.shape
    dim, width = w.shape[0], heads * HD
    flops = 2 * tokens * dim * width + 5 * tokens * tokens * width
    out = [jax.ShapeDtypeStruct((tokens, 3 * width), jnp.bfloat16)]
    given = [a for pair in earlier for a in pair] if share else []
    if share:
        out += [jax.ShapeDtypeStruct(share[1:], jnp.bfloat16)] * share[0]
        flops += 6 * tokens * dim * width * (1 + len(earlier))
    return pl.pallas_call(
        functools.partial(backward_kernel, len(given) // 2),
        out_shape=out,
        in_specs=whole_specs(7 + len(given)),
        out_specs=whole_specs(len(out)),
        scratch_shapes=[pltpu.VMEM((tokens, width), jnp.float32)] * 2,
        compiler_params=pltpu.CompilerParams(vmem_limit_bytes=VMEM_LIMIT),
        cost_estimate=pl.CostEstimate(flops=flops, bytes_accessed=12 << 20, transcendentals=tokens * tokens * heads // 2),
        name="attend_backward",
    )(g, w, qkv, log_total, cos, sin, mask, *given)


def weight_grads(x, qkv_grad, g, heads_out, count):
    tokens, dim = x.shape
    width = heads_out.shape[1]
    block = dim // count
    out = jax.ShapeDtypeStruct((count, block // 2, 4 * width), jnp.bfloat16)
    return pl.pallas_call(
        weight_kernel,
        grid=(count,),
        out_shape=[out, out],
        in_specs=[
            pl.BlockSpec((tokens, block), lambda i: (0, i)),
            pl.BlockSpec((tokens, 3 * width), lambda i: (0, 0)),
            pl.BlockSpec((tokens, block), lambda i: (0, i)),
            pl.BlockSpec((tokens, width), lambda i: (0, 0)),
        ],
        out_specs=[pl.BlockSpec((1, block // 2, 4 * width), lambda i: (i, 0, 0))] * 2,
        compiler_params=pltpu.CompilerParams(vmem_limit_bytes=VMEM_LIMIT),
        cost_estimate=pl.CostEstimate(flops=8 * tokens * dim * width, bytes_accessed=14 << 20, transcendentals=0),
        name="weight_grads",
    )(x, qkv_grad, g, heads_out)


def place_blocks(lanes, index, outs):
    count = len(lanes[0])
    half, total = lanes[0][0].shape
    rows = len(lanes) * half
    shapes, specs = [], []
    for planes, width, kind, turned in outs:
        if turned:
            shapes.append(jax.ShapeDtypeStruct((width, rows * count), kind))
            specs.append(pl.BlockSpec((width, rows), lambda i, at: (0, i)))
        elif planes > 1:
            shapes.append(jax.ShapeDtypeStruct((planes, rows * count, width), kind))
            specs.append(pl.BlockSpec((planes, rows, width), lambda i, at: (0, i, 0)))
        else:
            shapes.append(jax.ShapeDtypeStruct((rows * count, width), kind))
            specs.append(pl.BlockSpec((rows, width), lambda i, at: (i, 0)))
    given = [held[far] for held in lanes for far in range(count)]
    return pl.pallas_call(
        functools.partial(place_kernel, count, [o[1] for o in outs], [o[3] for o in outs]),
        grid_spec=pltpu.PrefetchScalarGridSpec(
            num_scalar_prefetch=1,
            grid=(count,),
            in_specs=[pl.BlockSpec((half, total), lambda i, at: (0, 0))] * len(given),
            out_specs=specs,
        ),
        out_shape=shapes,
        compiler_params=pltpu.CompilerParams(vmem_limit_bytes=VMEM_LIMIT),
        cost_estimate=pl.CostEstimate(flops=0, bytes_accessed=12 << 20, transcendentals=0),
        name="place_blocks",
    )(index.astype(jnp.int32).reshape(1), *given)


def swap_pairs(size, bit):
    return [(i, i ^ bit) for i in range(size)]


def shift_pairs(size, shift):
    return [(i, (i - shift) % size) for i in range(size)]


def bits_of(size):
    return [1 << i for i in range(size.bit_length() - 1)]


def pick(x, index, axis=0):
    return lax.dynamic_index_in_dim(x, index, axis, keepdims=False)


def after(x, *others):
    return lax.optimization_barrier((x,) + others)[0]


def xor_gather(x, axis, size, bits):
    held = dict(x) if isinstance(x, dict) else {0: x}
    for bit in bits:
        for far in list(held):
            held[far ^ bit] = lax.ppermute(held[far], axis, swap_pairs(size, bit))
    return held


def by_index(held, index, axis=0):
    shape = held[0].shape
    out = jnp.zeros(shape[:axis] + (len(held),) + shape[axis:], held[0].dtype)
    for far, block in held.items():
        out = lax.dynamic_update_index_in_dim(out, block, index ^ far, axis)
    return out


def xor_scatter(blocks, axis_name, size, bits, steps, index, axis, all_steps=None):
    all_steps = list(all_steps or steps)
    left = sorted(all_steps[all_steps.index(steps[0]) :], reverse=True)
    blocks = blocks.reshape(blocks.shape[:axis] + (2,) * len(left) + blocks.shape[axis + 1 :])
    for bit, step in zip(bits, steps):
        at = axis + left.index(step)
        left.remove(step)
        side = (index // step) % 2
        got = lax.ppermute(narrow(pick(blocks, 1 - side, at)), axis_name, swap_pairs(size, bit))
        blocks = wide(pick(blocks, side, at)) + wide(got)
    tail = blocks.shape[axis + len(left) :]
    return blocks.reshape(blocks.shape[:axis] + ((2 ** len(left),) if left else ()) + tail)


def chain_step(up, down, step, chips):
    up_pairs = [(z * 2 + c, z * 2 + 2 + c) for z in range(step - 1, chips - 1) for c in (0, 1)]
    down_pairs = [(z * 2 + c, z * 2 - 2 + c) for z in range(1, chips - step + 1) for c in (0, 1)]
    return lax.ppermute(up, "mp", up_pairs), lax.ppermute(down, "mp", down_pairs)


def lane_bits(size):
    return bits_of(size), bits_of(size)[::-1]


def column_gather(lanes, size, cut=None, start=None):
    return [xor_gather(x, "dp", size, bits[start:cut]) for x, bits in zip(lanes, lane_bits(size))]


def gate_lanes(lanes, *gates):
    flat = [held[far] for held in lanes for far in held]
    flat = lax.optimization_barrier((*flat, *gates))
    flat = iter(flat)
    return [{far: next(flat) for far in held} for held in lanes]


def column_scatter(lanes, size, column, cut=None, start=None):
    return [
        xor_scatter(x, "dp", size, bits[start:cut], bits[start:cut], column, 0, bits)
        for x, bits in zip(lanes, lane_bits(size))
    ]


def all_sum(x, sizes):
    for axis, size in sizes.items():
        for bit in bits_of(size):
            x = x + lax.ppermute(x, axis, swap_pairs(size, bit))
    return x


def make_local(columns, ranks):
    def local(
        layer_input, width_choice, routed_flag, mixer_gain, mixer_router, attention_weight,
        output_weight, hidden_gain, hidden_router, up_weight, down_weight, out_grad,
    ):
        column, rank = lax.axis_index("dp"), lax.axis_index("mp")
        rows, dim = layer_input.shape
        core = rank % 2
        group = SEQ_LEN // rows
        sequences = ranks // group
        place, sequence = rank % group, rank // group
        pair_bits = [b for b in bits_of(group) if b > 1]
        own_heads = output_weight.shape[0] // HD
        cols_local = up_weight.shape[1]
        width_own = lax.dynamic_slice_in_dim(width_choice, rank * rows, rows, 0)
        routed_own = lax.dynamic_slice_in_dim(routed_flag, rank * rows, rows, 0)
        cos, sin = rope_tables(SEQ_LEN, HD)

        parts = 2
        part_rows = rows // parts
        chips, chip = ranks // 2, rank // 2

        def from_sequence(blocks):
            got = lax.ppermute(pick(blocks, 1 - core), "mp", swap_pairs(ranks, 1))
            blocks = wide(pick(blocks, core)) + wide(got)
            bits = pair_bits[::-1]
            return xor_scatter(blocks, "mp", ranks, bits, [b // 2 for b in bits], place // 2, 0)

        width = own_heads * HD
        packed = jnp.concatenate([attention_weight[:, p] for p in range(3)] + [output_weight.T], axis=1)
        chunk_rows = dim // columns
        chunks = [
            lax.dynamic_slice_in_dim(packed, column * chunk_rows + at, chunk_rows // 2, 0)
            for at in (0, chunk_rows // 2)
        ]
        input_wide = wide(layer_input)
        normed_one, scaled_one, inverse_one = norm_forward(input_wide, mixer_gain)
        held = xor_gather(narrow(normed_one), "mp", ranks, pair_bits)
        fetched = [
            lax.ppermute(lane, "mp", shift_pairs(ranks, k * group)) for k in range(1, sequences) for lane in chunks
        ]
        held, fetched = lax.optimization_barrier((held, fetched))
        inputs_one = by_index(xor_gather(held, "mp", ranks, [1]), place).reshape(SEQ_LEN, -1)
        inputs_one, fetched = lax.optimization_barrier((inputs_one, fetched))
        helds = [column_gather(fetched[2 * k - 2 : 2 * k], columns, cut=1) for k in range(1, sequences)]
        gate_one, state_one = gate_forward(normed_one, mixer_router, width_own[:, 0], routed_own[:, 0])
        grads_all = lax.all_gather(after(out_grad, *fetched), "mp", axis=0, tiled=True)

        sequence_width = lax.dynamic_slice_in_dim(width_choice[:, 0], sequence * SEQ_LEN, SEQ_LEN, 0)
        weights, kept, earlier = [packed], [], []
        for k in range(sequences):
            heads = ((rank + k * group) % ranks) * own_heads + jnp.arange(own_heads, dtype=jnp.int32)
            mask = (heads[None, :] * 4 < (sequence_width[:, None] + 1) * H).astype(jnp.float32)
            share_shape = (parts, 2, group // 2, part_rows, dim) if k == sequences - 1 else None
            if k:
                held = column_gather(gate_lanes(helds[k - 1], kept[0][0]), columns, start=1)
                weights += place_blocks(held, column, [(1, packed.shape[1], jnp.bfloat16, False)])
            qkv, heads_out, log_total, *share = attend_forward(inputs_one, weights[k], cos, sin, mask, earlier, share_shape)
            kept.append((qkv, heads_out, log_total, mask))
            earlier.append((heads_out, weights[k]))
        mixer_branches = [from_sequence(share[j]) for j in range(parts)]
        col_ids = rank * cols_local + jnp.arange(cols_local, dtype=jnp.int32)
        widths = width_choice[:, 1].reshape(ranks, parts, part_rows)
        fronts = []
        for j in range(parts):
            here = slice(j * part_rows, (j + 1) * part_rows)
            if j == 0:
                mixer_branches[j], grads_all = lax.optimization_barrier((mixer_branches[j], grads_all))
            middle = input_wide[here] + gate_one[here, None] * mixer_branches[j]
            normed_two, scaled_two, inverse_two = norm_forward(middle, hidden_gain)
            gate_two, state_two = gate_forward(normed_two, hidden_router, width_own[here, 1], routed_own[here, 1])
            high = lax.optimization_barrier(narrow(gate_two))
            low = narrow(gate_two - wide(high))
            tail = jnp.pad(jnp.stack([high, low]), ((0, 14), (0, dim - part_rows)))
            block = jnp.concatenate([narrow(normed_two), tail], axis=0)
            first = chain_step(block, block, 1, chips)
            other = lax.ppermute(block, "mp", swap_pairs(ranks, 1))
            if j < parts - 1:
                mixer_branches[j + 1], other = lax.optimization_barrier((mixer_branches[j + 1], other))
            fronts.append((middle, normed_two, scaled_two, inverse_two, gate_two, state_two, block, first, other))

        starts = [f[-1] for f in fronts]
        inputs_parts, gates_parts = [], []
        for j in range(parts):
            block, (up, down), other = fronts[j][-3:]
            if j < parts - 1:
                up, down, starts[j + 1] = lax.optimization_barrier((up, down, starts[j + 1]))
            ups, downs = [up], [down]
            for step in range(2, chips):
                up, down = chain_step(up, down, step, chips)
                ups.append(up)
                downs.append(down)
            inputs_two = jnp.zeros((chips, 2, part_rows, dim), jnp.bfloat16)
            gates = jnp.zeros((chips, 2, 2, part_rows), jnp.bfloat16)
            for k in range(chips):
                if k:
                    block = jnp.where(chip + k < chips, downs[k - 1], ups[chips - k - 1])
                    other = lax.ppermute(block, "mp", swap_pairs(ranks, 1))
                else:
                    other = starts[j]
                for value, side in ((block, core), (other, 1 - core)):
                    at = ((chip + k) % chips, side, 0, 0)
                    inputs_two = lax.dynamic_update_slice(inputs_two, value[None, None, :part_rows], at)
                    gates = lax.dynamic_update_slice(
                        gates, value[None, None, part_rows : part_rows + 2, :part_rows], at
                    )
            inputs_parts.append(inputs_two.reshape(-1, dim))
            gates_parts.append(jnp.sum(wide(gates), axis=2).reshape(-1))

        tops = [grads_all.reshape(ranks, parts, part_rows, dim)[:, j].reshape(-1, dim) for j in range(parts)]
        top_downs = [product(top, down_weight, (1, 1)) for top in tops]
        hiddens, pre_grads, sums, dots = [], [], [], []
        for j in range(parts):
            inputs_two, gates = inputs_parts[j], gates_parts[j]
            if j:
                inputs_two, shared = lax.optimization_barrier((inputs_two, shared))
            else:
                inputs_two, top_downs = lax.optimization_barrier((inputs_two, top_downs))
            inputs_parts[j] = inputs_two
            col_mask = (col_ids[None, :] * 4 < (widths[:, j].reshape(-1)[:, None] + 1) * FF).astype(jnp.float32)
            pre = product(inputs_two, up_weight, (1, 0))
            relu_act = jax.nn.relu(pre)
            hidden = narrow(relu_act * relu_act * col_mask)
            pre_grad = narrow(top_downs[j] * gates[:, None] * col_mask * 2.0 * relu_act)
            dots.append(jnp.sum(wide(hidden) * top_downs[j], axis=1))
            shared = narrow(product(pre_grad, up_weight, (1, 1)))
            shared, hidden, pre_grad = lax.optimization_barrier((shared, hidden, pre_grad))
            hiddens.append(hidden)
            pre_grads.append(pre_grad)
            sums.append(shared)
        last_sum, hiddens, pre_grads = lax.optimization_barrier((sums[-1], hiddens, pre_grads))
        sums = sums[:-1] + [last_sum]
        normed_grads = []
        for x in sums:
            x = after(x, *normed_grads)
            normed_grads.append(lax.psum_scatter(x, "mp", scatter_dimension=0, tiled=True))
        dots = all_sum(jnp.concatenate(dots).reshape(-1, 128), {"mp": ranks}).reshape(parts, ranks, part_rows)
        gate_grad_two = pick(dots, rank, 1)

        lanes = [
            narrow(sum(product(a, narrow(f[:, None] * wide(t)), (0, 0)) for a, f, t in zip(hiddens, gates_parts, tops))),
            narrow(sum(product(a, b, (0, 0)) for a, b in zip(inputs_parts, pre_grads))),
        ]
        lanes = [x.reshape(columns, -1, x.shape[1]) for x in lanes]
        lanes = column_scatter(lanes, columns, column, cut=1)
        hidden_share = [narrow(product(x, down_weight, (1, 0))) for x in hiddens]
        normed_grads[-1], hidden_share, lanes = lax.optimization_barrier((normed_grads[-1], hidden_share, lanes))
        lanes = [narrow(x) for x in column_scatter(lanes, columns, column, start=1)]

        middle_grads, gain_two, router_two = [], 0.0, 0.0
        grads_one = jnp.zeros((group, parts, part_rows, dim), jnp.bfloat16)
        for j in range(parts):
            here = slice(j * part_rows, (j + 1) * part_rows)
            _, normed_two, scaled_two, inverse_two, _, state_two = fronts[j][:6]
            router_part, router_grad = gate_backward(normed_two, hidden_router, state_two, gate_grad_two[j])
            middle_part, gain_grad = norm_backward(
                wide(normed_grads[j]) + router_part, scaled_two, inverse_two, hidden_gain
            )
            middle_grads.append(wide(out_grad[here]) + middle_part)
            gain_two, router_two = gain_two + gain_grad, router_two + router_grad
            held = xor_gather(narrow(gate_one[here, None] * middle_grads[j]), "mp", ranks, pair_bits + [1])
            for far, block in held.items():
                grads_one = lax.dynamic_update_slice(grads_one, block[None, None], (place ^ far, j, 0, 0))
        grads_one = grads_one.reshape(SEQ_LEN, dim)
        middle_grad = jnp.concatenate(middle_grads)
        middle = jnp.concatenate([f[0] for f in fronts])
        gate_two = jnp.concatenate([f[4] for f in fronts])
        mixer_branch = jnp.concatenate(mixer_branches)
        grads_one, hidden_share, lanes = lax.optimization_barrier((grads_one, hidden_share, lanes))
        hidden_branch = [lax.psum_scatter(x, "mp", scatter_dimension=0, tiled=True) for x in hidden_share]
        hidden_branch = wide(jnp.concatenate(hidden_branch))
        layer_output = narrow(middle + gate_two[:, None] * hidden_branch)

        gate_grad_one = jnp.sum(middle_grad * mixer_branch, axis=1)
        helds = column_gather(lanes, columns, cut=1)
        earlier, weight_parts = [], [None] * sequences
        grads_now = grads_one
        for k in range(sequences)[::-1]:
            qkv, heads_out, log_total, mask = kept[k]
            qkv_grad, *share = attend_backward(
                grads_now, weights[k], qkv, log_total, cos, sin, mask, earlier,
                None if k else (1, 2, group // 2, rows, dim),
            )
            earlier.append((qkv_grad, weights[k]))
            if k == 0:
                helds = column_gather(helds, columns, start=1)
                flat = [held[far] for held in helds for far in held]
                qkv_grad, *flat = lax.optimization_barrier((qkv_grad, *flat))
                helds = [dict(zip(held, flat[i * columns :])) for i, held in enumerate(helds)]
            weight_parts[k] = weight_grads(inputs_one, qkv_grad, grads_one, heads_out, columns)
            if k == sequences - 1:
                flat = [held[far] for held in helds for far in held]
                grads_now, *rest = lax.optimization_barrier((grads_now, *weight_parts[k], *flat))
                weight_parts[k], flat = rest[:2], rest[2:]
                helds = [dict(zip(held, flat[i * 2 :])) for i, held in enumerate(helds)]
        normed_grad_one = from_sequence(share[0])

        down_sum, = place_blocks(helds[:1], column, [(1, dim, jnp.float32, False)])
        up_sum, = place_blocks(helds[1:], column, [(1, cols_local, jnp.float32, False)])

        pieces = column_scatter(weight_parts[0], columns, column, cut=1)
        pieces, normed_grad_one, down_sum, up_sum = lax.optimization_barrier(
            (pieces, normed_grad_one, down_sum, up_sum)
        )
        pieces = column_scatter(pieces, columns, column, start=1)
        for k in range(1, sequences):
            there = [narrow(x) for x in column_scatter(weight_parts[k], columns, column)]
            back = shift_pairs(ranks, -k * group)
            pieces = [narrow(p + wide(lax.ppermute(t, "mp", back))) for p, t in zip(pieces, there)]
        attention_sum, output_sum = place_blocks(
            column_gather(pieces, columns),
            column,
            [(3, width, jnp.float32, False), (1, width, jnp.float32, True)],
        )
        attention_sum = attention_sum.transpose(1, 0, 2)

        router_part_one, router_one = gate_backward(normed_one, mixer_router, state_one, gate_grad_one)
        input_part, gain_one = norm_backward(normed_grad_one + router_part_one, scaled_one, inverse_one, mixer_gain)
        input_grad = narrow(middle_grad + input_part)

        sizes = {"mp": ranks, "dp": columns}

        smalls = [gain_two, gain_one, router_two.T, router_one.T]
        small_sum = all_sum(jnp.concatenate([x.reshape(-1, 128) for x in smalls], axis=0), sizes)
        cuts = [dim // 128, 2 * dim // 128, (2 * dim + router_two.size) // 128]
        hidden_gain_sum, mixer_gain_sum, hidden_router_sum, mixer_router_sum = (
            x.reshape(-1, dim) for x in jnp.split(small_sum, cuts)
        )
        hidden_gain_sum, mixer_gain_sum = hidden_gain_sum[0], mixer_gain_sum[0]
        hidden_router_sum, mixer_router_sum = hidden_router_sum.T, mixer_router_sum.T
        return (
            layer_output, input_grad, mixer_gain_sum, mixer_router_sum, attention_sum, output_sum,
            hidden_gain_sum, hidden_router_sum, up_sum, down_sum,
        )

    return local


def solution(mesh):
    return jax.shard_map(
        make_local(mesh.shape["dp"], mesh.shape["mp"]),
        mesh=mesh,
        in_specs=(
            P(("dp", "mp"), None),
            P("dp", None),
            P("dp", None),
            P(),
            P(),
            P(None, None, "mp"),
            P("mp", None),
            P(),
            P(),
            P(None, "mp"),
            P("mp", None),
            P(("dp", "mp"), None),
        ),
        out_specs=(
            P(("dp", "mp"), None),
            P(("dp", "mp"), None),
            P(),
            P(),
            P(None, None, "mp"),
            P("mp", None),
            P(),
            P(),
            P(None, "mp"),
            P("mp", None),
        ),
        check_vma=False,
    )
```

```python
import functools
import math

import jax
import jax.numpy as jnp
from jax import lax
from jax.experimental import pallas as pl
from jax.experimental.pallas import tpu as pltpu
from jax.sharding import PartitionSpec as P

H = 16
HD = 128
FF = 8192
SEQ_LEN = 1024


EPSILON = 1e-05
NEG_LARGE = -1e30
HIGHEST = lax.Precision.HIGHEST


def norm_forward(values, gain_vec):
    row_mean = jnp.mean(values, axis=1, keepdims=True)
    centred = values - row_mean
    row_variance = jnp.mean(centred * centred, axis=1, keepdims=True)
    inverse_scale = lax.rsqrt(row_variance + EPSILON)
    scaled = centred * inverse_scale
    return (scaled * gain_vec[None, :], scaled, inverse_scale)


def norm_backward(normed_grad, scaled, inverse_scale, gain_vec):
    gain_grad = jnp.sum(normed_grad * scaled, axis=0)
    scaled_grad = normed_grad * gain_vec[None, :]
    first_mean = jnp.mean(scaled_grad, axis=1, keepdims=True)
    second_mean = jnp.mean(scaled_grad * scaled, axis=1, keepdims=True)
    return (inverse_scale * (scaled_grad - first_mean - scaled * second_mean), gain_grad)


def gate_forward(normed, router, width_col, routed_col):
    logits = jnp.dot(normed, router, precision=HIGHEST, preferred_element_type=jnp.float32)
    soft_probs = jax.nn.softmax(logits, axis=1)
    one_hot = (width_col[:, None] == jnp.arange(4, dtype=jnp.int32)[None, :]).astype(jnp.float32)
    chosen = jnp.sum(soft_probs * one_hot, axis=1)
    route_flags = routed_col.astype(jnp.float32)
    return (
        route_flags * 4.0 * chosen + (1.0 - route_flags),
        (soft_probs, one_hot, chosen, route_flags),
    )


def gate_backward(normed, router, gate_state, gate_grad):
    soft_probs, one_hot, chosen, route_flags = gate_state
    coefficient = route_flags * 4.0 * chosen * gate_grad
    logit_grad = coefficient[:, None] * (one_hot - soft_probs)
    router_grad = lax.dot_general(
        normed,
        logit_grad,
        (((0,), (0,)), ((), ())),
        precision=HIGHEST,
        preferred_element_type=jnp.float32,
    )
    normed_grad = lax.dot_general(
        logit_grad,
        router,
        (((1,), (1,)), ((), ())),
        precision=HIGHEST,
        preferred_element_type=jnp.float32,
    )
    return (normed_grad, router_grad)


Q_BLOCK = 256


def rope_tables(token_count, head_width):
    positions = jnp.arange(token_count, dtype=jnp.float32)
    frequency = jnp.exp(
        jnp.arange(head_width // 2, dtype=jnp.float32) * (-2.0 * math.log(10000.0) / head_width)
    )
    angles = positions[:, None] * frequency[None, :]
    cosine, sine = jnp.cos(angles), jnp.sin(angles)
    return jnp.concatenate([cosine, cosine], axis=1), jnp.concatenate([-sine, sine], axis=1)


def wide(x):
    return x.astype(jnp.float32)


def narrow(x):
    return x.astype(jnp.bfloat16)


def product(a, b, dims):
    return lax.dot_general(a, b, ((dims[:1], dims[1:]), ((), ())), preferred_element_type=jnp.float32)


def block_scores(queries, keys_all, start):
    scores = product(queries, keys_all, (1, 1)) * (1.0 / math.sqrt(HD))
    row = lax.broadcasted_iota(jnp.int32, scores.shape, 0) + start
    col = lax.broadcasted_iota(jnp.int32, scores.shape, 1)
    return jnp.where(col <= row, scores, NEG_LARGE)


def forward_kernel(x_ref, w_ref, cos_ref, sin_ref, mask_ref, qkv_ref, heads_ref, log_ref):
    tokens, heads = x_ref.shape[0], mask_ref.shape[1]
    width = heads * HD
    block = min(Q_BLOCK, tokens)
    for start in range(0, tokens, block):
        here, end = slice(start, start + block), start + block
        x = x_ref[here, :]
        cos, sin = cos_ref[here, :], sin_ref[here, :]
        for part in range(3):
            rows = product(x, w_ref[:, part * width : (part + 1) * width], (1, 0))
            for head in range(heads):
                value = rows[:, head * HD : (head + 1) * HD]
                if part < 2:
                    value = value * cos + pltpu.roll(value, HD // 2, 1) * sin
                at = part * width + head * HD
                qkv_ref[here, at : at + HD] = narrow(value)
        for head in range(heads):
            at = head * HD
            lanes, key_lanes, value_lanes = (slice(at + p * width, at + p * width + HD) for p in range(3))
            scores = block_scores(qkv_ref[here, lanes], qkv_ref[:end, key_lanes], start)
            row_max = jnp.max(scores, axis=1, keepdims=True)
            shifted = jnp.exp(scores - row_max)
            total = jnp.sum(shifted, axis=1, keepdims=True)
            mix = product(narrow(shifted / total), qkv_ref[:end, value_lanes], (1, 0))
            heads_ref[here, lanes] = narrow(mix * mask_ref[here, head : head + 1])
            log_ref[here, head : head + 1] = row_max + jnp.log(total)


def backward_kernel(g_ref, w_ref, qkv_ref, log_ref, cos_ref, sin_ref, mask_ref, out_ref, keys_acc, values_acc):
    tokens, heads = g_ref.shape[0], mask_ref.shape[1]
    width = heads * HD
    block = min(Q_BLOCK, tokens)
    scale = 1.0 / math.sqrt(HD)
    for start in range(0, tokens, block):
        here, end = slice(start, start + block), start + block
        cos, sin = cos_ref[here, :], sin_ref[here, :]
        rows = narrow(product(g_ref[here, :], w_ref[...], (1, 0)))
        for head in range(heads):
            at = head * HD
            lanes, key_lanes, value_lanes = (slice(at + p * width, at + p * width + HD) for p in range(3))
            heads_grad = rows[:, lanes] * narrow(mask_ref[here, head : head + 1])
            queries, keys_all = qkv_ref[here, lanes], qkv_ref[:end, key_lanes]
            scores = block_scores(queries, keys_all, start)
            probs = jnp.exp(scores - log_ref[here, head : head + 1])
            values_part = product(narrow(probs), heads_grad, (0, 0))
            probs_grad = product(heads_grad, qkv_ref[:end, value_lanes], (1, 1))
            centre = jnp.sum(probs * probs_grad, axis=1, keepdims=True)
            score_grad = narrow(probs * (probs_grad - centre))
            queries_grad = product(score_grad, keys_all, (1, 0)) * scale
            keys_part = product(score_grad, queries, (0, 0)) * scale
            turned = queries_grad * cos - pltpu.roll(queries_grad, HD // 2, 1) * sin
            out_ref[here, lanes] = narrow(turned)
            if start:
                values_acc[:start, lanes] += values_part[:start]
                keys_acc[:start, lanes] += keys_part[:start]
            values_acc[here, lanes] = values_part[start:]
            keys_acc[here, lanes] = keys_part[start:]
    for start in range(0, tokens, block):
        here = slice(start, start + block)
        cos, sin = cos_ref[here, :], sin_ref[here, :]
        out_ref[here, 2 * width :] = narrow(values_acc[here, :])
        for head in range(heads):
            at = head * HD
            value = keys_acc[here, at : at + HD]
            out_ref[here, width + at : width + at + HD] = narrow(value * cos - pltpu.roll(value, HD // 2, 1) * sin)


def share_kernel(*refs):
    *given, out_ref = refs
    total = product(given[0][...], given[1][...], (1, 1))
    for a_ref, w_ref in zip(given[2::2], given[3::2]):
        total = total + product(a_ref[...], w_ref[...], (1, 1))
    out_ref[0, 0] = narrow(total)


def weight_kernel(x_ref, q_ref, g_ref, h_ref, *outs):
    width = h_ref.shape[1]
    half = x_ref.shape[1] // 2
    for lane, out_ref in enumerate(outs):
        here = slice(lane * half, (lane + 1) * half)
        out_ref[0, :, : 3 * width] = narrow(product(x_ref[:, here], q_ref[...], (0, 0)))
        out_ref[0, :, 3 * width :] = narrow(product(g_ref[:, here], h_ref[...], (0, 0)))


def place_kernel(count, widths, turned, at_ref, *refs):
    lanes = (len(refs) - len(widths)) // count
    blocks, outs = refs[: lanes * count], refs[lanes * count :]
    half = blocks[0].shape[0]
    for far in range(count):

        @pl.when((pl.program_id(0) ^ at_ref[0]) == far)
        def _():
            for lane in range(lanes):
                here = slice(lane * half, (lane + 1) * half)
                block = blocks[lane * count + far]
                start = 0
                for out_ref, width, turn in zip(outs, widths, turned):
                    for part in range(out_ref.shape[0] if len(out_ref.shape) == 3 else 1):
                        value = block[:, start : start + width].astype(out_ref.dtype)
                        start += width
                        if turn:
                            out_ref[:, here] = value.T
                        elif len(out_ref.shape) == 3:
                            out_ref[part, here, :] = value
                        else:
                            out_ref[here, :] = value


VMEM_LIMIT = 56 * 1024 * 1024


def whole_specs(count):
    return [pl.BlockSpec(memory_space=pltpu.VMEM)] * count


def attend_forward(x, w, cos, sin, mask):
    tokens, heads = mask.shape
    dim, width = w.shape[0], heads * HD
    return pl.pallas_call(
        forward_kernel,
        out_shape=[
            jax.ShapeDtypeStruct((tokens, 3 * width), jnp.bfloat16),
            jax.ShapeDtypeStruct((tokens, width), jnp.bfloat16),
            jax.ShapeDtypeStruct((tokens, heads), jnp.float32),
        ],
        in_specs=whole_specs(5),
        out_specs=whole_specs(3),
        compiler_params=pltpu.CompilerParams(vmem_limit_bytes=VMEM_LIMIT),
        cost_estimate=pl.CostEstimate(
            flops=6 * tokens * dim * width + 2 * tokens * tokens * width,
            bytes_accessed=12 << 20,
            transcendentals=tokens * tokens * heads // 2,
        ),
        name="attend_forward",
    )(x, w, cos, sin, mask)


def attend_backward(g, w, qkv, log_total, cos, sin, mask):
    tokens, heads = mask.shape
    dim, width = w.shape[0], heads * HD
    return pl.pallas_call(
        backward_kernel,
        out_shape=jax.ShapeDtypeStruct((tokens, 3 * width), jnp.bfloat16),
        in_specs=whole_specs(7),
        out_specs=whole_specs(1)[0],
        scratch_shapes=[pltpu.VMEM((tokens, width), jnp.float32)] * 2,
        compiler_params=pltpu.CompilerParams(vmem_limit_bytes=VMEM_LIMIT),
        cost_estimate=pl.CostEstimate(
            flops=2 * tokens * dim * width + 5 * tokens * tokens * width,
            bytes_accessed=12 << 20,
            transcendentals=tokens * tokens * heads // 2,
        ),
        name="attend_backward",
    )(g, w, qkv, log_total, cos, sin, mask)


def share_of(pairs, rows):
    tokens, depth = pairs[0][0].shape
    dim = pairs[0][1].shape[0]
    specs = [
        pl.BlockSpec((rows, depth), lambda i: (i, 0)),
        pl.BlockSpec((dim, depth), lambda i: (0, 0)),
    ] * len(pairs)
    return pl.pallas_call(
        share_kernel,
        grid=(tokens // rows,),
        out_shape=jax.ShapeDtypeStruct((2, tokens // rows // 2, rows, dim), jnp.bfloat16),
        in_specs=specs,
        out_specs=pl.BlockSpec((1, 1, rows, dim), lambda i: (i % 2, i // 2, 0, 0)),
        compiler_params=pltpu.CompilerParams(vmem_limit_bytes=VMEM_LIMIT),
        cost_estimate=pl.CostEstimate(
            flops=2 * tokens * dim * depth * len(pairs), bytes_accessed=12 << 20, transcendentals=0
        ),
        name="share_of",
    )(*[x for pair in pairs for x in pair])


def weight_grads(x, qkv_grad, g, heads_out, count):
    tokens, dim = x.shape
    width = heads_out.shape[1]
    block = dim // count
    out = jax.ShapeDtypeStruct((count, block // 2, 4 * width), jnp.bfloat16)
    return pl.pallas_call(
        weight_kernel,
        grid=(count,),
        out_shape=[out, out],
        in_specs=[
            pl.BlockSpec((tokens, block), lambda i: (0, i)),
            pl.BlockSpec((tokens, 3 * width), lambda i: (0, 0)),
            pl.BlockSpec((tokens, block), lambda i: (0, i)),
            pl.BlockSpec((tokens, width), lambda i: (0, 0)),
        ],
        out_specs=[pl.BlockSpec((1, block // 2, 4 * width), lambda i: (i, 0, 0))] * 2,
        compiler_params=pltpu.CompilerParams(vmem_limit_bytes=VMEM_LIMIT),
        cost_estimate=pl.CostEstimate(flops=8 * tokens * dim * width, bytes_accessed=14 << 20, transcendentals=0),
        name="weight_grads",
    )(x, qkv_grad, g, heads_out)


def place_blocks(lanes, index, outs):
    count = len(lanes[0])
    half, total = lanes[0][0].shape
    rows = len(lanes) * half
    shapes, specs = [], []
    for planes, width, kind, turned in outs:
        if turned:
            shapes.append(jax.ShapeDtypeStruct((width, rows * count), kind))
            specs.append(pl.BlockSpec((width, rows), lambda i, at: (0, i)))
        elif planes > 1:
            shapes.append(jax.ShapeDtypeStruct((planes, rows * count, width), kind))
            specs.append(pl.BlockSpec((planes, rows, width), lambda i, at: (0, i, 0)))
        else:
            shapes.append(jax.ShapeDtypeStruct((rows * count, width), kind))
            specs.append(pl.BlockSpec((rows, width), lambda i, at: (i, 0)))
    given = [held[far] for held in lanes for far in range(count)]
    return pl.pallas_call(
        functools.partial(place_kernel, count, [o[1] for o in outs], [o[3] for o in outs]),
        grid_spec=pltpu.PrefetchScalarGridSpec(
            num_scalar_prefetch=1,
            grid=(count,),
            in_specs=[pl.BlockSpec((half, total), lambda i, at: (0, 0))] * len(given),
            out_specs=specs,
        ),
        out_shape=shapes,
        compiler_params=pltpu.CompilerParams(vmem_limit_bytes=VMEM_LIMIT),
        cost_estimate=pl.CostEstimate(flops=0, bytes_accessed=12 << 20, transcendentals=0),
        name="place_blocks",
    )(index.astype(jnp.int32).reshape(1), *given)


def swap_pairs(size, bit):
    return [(i, i ^ bit) for i in range(size)]


def shift_pairs(size, shift):
    return [(i, (i - shift) % size) for i in range(size)]


def bits_of(size):
    return [1 << i for i in range(size.bit_length() - 1)]


def pick(x, index, axis=0):
    return lax.dynamic_index_in_dim(x, index, axis, keepdims=False)


def after(x, *others):
    return lax.optimization_barrier((x,) + others)[0]


def xor_gather(x, axis, size, bits):
    held = dict(x) if isinstance(x, dict) else {0: x}
    for bit in bits:
        for far in list(held):
            held[far ^ bit] = lax.ppermute(held[far], axis, swap_pairs(size, bit))
    return held


def by_index(held, index, axis=0):
    shape = held[0].shape
    out = jnp.zeros(shape[:axis] + (len(held),) + shape[axis:], held[0].dtype)
    for far, block in held.items():
        out = lax.dynamic_update_index_in_dim(out, block, index ^ far, axis)
    return out


def xor_scatter(blocks, axis_name, size, bits, steps, index, axis, all_steps=None):
    all_steps = list(all_steps or steps)
    left = sorted(all_steps[all_steps.index(steps[0]) :], reverse=True)
    blocks = blocks.reshape(blocks.shape[:axis] + (2,) * len(left) + blocks.shape[axis + 1 :])
    for bit, step in zip(bits, steps):
        at = axis + left.index(step)
        left.remove(step)
        side = (index // step) % 2
        got = lax.ppermute(narrow(pick(blocks, 1 - side, at)), axis_name, swap_pairs(size, bit))
        blocks = wide(pick(blocks, side, at)) + wide(got)
    tail = blocks.shape[axis + len(left) :]
    return blocks.reshape(blocks.shape[:axis] + ((2 ** len(left),) if left else ()) + tail)


def lane_bits(size):
    return bits_of(size), bits_of(size)[::-1]


def column_gather(lanes, size, cut=None, start=None):
    return [xor_gather(x, "dp", size, bits[start:cut]) for x, bits in zip(lanes, lane_bits(size))]


def gate_lanes(lanes, *gates):
    flat = [held[far] for held in lanes for far in held]
    flat = lax.optimization_barrier((*flat, *gates))
    flat = iter(flat)
    return [{far: next(flat) for far in held} for held in lanes]


def column_scatter(lanes, size, column, cut=None, start=None):
    return [
        xor_scatter(x, "dp", size, bits[start:cut], bits[start:cut], column, 0, bits)
        for x, bits in zip(lanes, lane_bits(size))
    ]


def all_sum(x, sizes):
    for axis, size in sizes.items():
        for bit in bits_of(size):
            x = x + lax.ppermute(x, axis, swap_pairs(size, bit))
    return x


def make_local(columns, ranks):
    def local(
        layer_input, width_choice, routed_flag, mixer_gain, mixer_router, attention_weight,
        output_weight, hidden_gain, hidden_router, up_weight, down_weight, out_grad,
    ):
        column, rank = lax.axis_index("dp"), lax.axis_index("mp")
        rows, dim = layer_input.shape
        core = rank % 2
        group = SEQ_LEN // rows
        sequences = ranks // group
        place, sequence = rank % group, rank // group
        pair_bits = [b for b in bits_of(group) if b > 1]
        own_heads = output_weight.shape[0] // HD
        cols_local = up_weight.shape[1]
        width_own = lax.dynamic_slice_in_dim(width_choice, rank * rows, rows, 0)
        routed_own = lax.dynamic_slice_in_dim(routed_flag, rank * rows, rows, 0)
        cos, sin = rope_tables(SEQ_LEN, HD)

        def place_sequence(held):
            return by_index(held, place).reshape(SEQ_LEN, -1)

        def from_sequence(blocks):
            got = lax.ppermute(pick(blocks, 1 - core), "mp", swap_pairs(ranks, 1))
            blocks = wide(pick(blocks, core)) + wide(got)
            bits = pair_bits[::-1]
            return xor_scatter(blocks, "mp", ranks, bits, [b // 2 for b in bits], place // 2, 0)

        width = own_heads * HD
        chunk_rows = dim // columns
        half_rows = chunk_rows // 2

        def in_slice(w):
            return jnp.concatenate([w[:, p] for p in range(3)], axis=1)

        lanes_in = [
            in_slice(lax.dynamic_slice_in_dim(attention_weight, column * chunk_rows + at, half_rows, 0))
            for at in (0, half_rows)
        ]
        lanes_out = [
            lax.dynamic_slice_in_dim(output_weight, column * chunk_rows + at, half_rows, 1).T
            for at in (0, half_rows)
        ]
        input_wide = wide(layer_input)
        normed_one, scaled_one, inverse_one = norm_forward(input_wide, mixer_gain)
        low_one = narrow(normed_one)
        low_one, lanes_in, lanes_out = lax.optimization_barrier((low_one, lanes_in, lanes_out))
        held = xor_gather(low_one, "mp", ranks, pair_bits)
        fetched_in, fetched_out = [
            [[lax.ppermute(x, "mp", shift_pairs(ranks, k * group)) for x in lanes] for k in range(1, sequences)]
            for lanes in (lanes_in, lanes_out)
        ]
        sequence_width = lax.dynamic_slice_in_dim(width_choice[:, 0], sequence * SEQ_LEN, SEQ_LEN, 0)
        masks = []
        for k in range(sequences):
            heads = ((rank + k * group) % ranks) * own_heads + jnp.arange(own_heads, dtype=jnp.int32)
            masks.append((heads[None, :] * 4 < (sequence_width[:, None] + 1) * H).astype(jnp.float32))
        weights_in, weights_out = [in_slice(attention_weight)], [output_weight.T]
        held, fetched_in, masks, weights_in, weights_out, cos, sin = lax.optimization_barrier(
            (held, fetched_in, masks, weights_in, weights_out, cos, sin)
        )
        inputs_one = place_sequence(xor_gather(held, "mp", ranks, [1]))
        grads_all = lax.all_gather(after(out_grad, *[x for lanes in fetched_in for x in lanes]), "mp", axis=0, tiled=True)
        steps_in = [column_gather(x, columns, cut=1) for x in fetched_in]
        inputs_one, fetched_out = lax.optimization_barrier((inputs_one, fetched_out))
        gate_one, state_one = gate_forward(normed_one, mixer_router, width_own[:, 0], routed_own[:, 0])

        kept = []
        for k in range(sequences):
            mask = masks[k]
            if k:
                steps, fetched, _ = lax.optimization_barrier((steps_in[k - 1], fetched_out[k - 1], kept[0][0]))
                held = column_gather(steps, columns, start=1)
                held_out = column_gather(fetched, columns)
                weights_in += place_blocks(held, column, [(1, 3 * width, jnp.bfloat16, False)])
                weights_out += place_blocks(held_out, column, [(1, width, jnp.bfloat16, False)])
            kept.append((*attend_forward(inputs_one, weights_in[k], cos, sin, mask), mask))
        mixer_branch = from_sequence(share_of([(x[1], w) for x, w in zip(kept, weights_out)], rows))
        mixer_branch, grads_all = lax.optimization_barrier((mixer_branch, grads_all))
        top_down = product(grads_all, down_weight, (1, 1))

        middle = input_wide + gate_one[:, None] * mixer_branch
        normed_two, scaled_two, inverse_two = norm_forward(middle, hidden_gain)
        gate_two, state_two = gate_forward(normed_two, hidden_router, width_own[:, 1], routed_own[:, 1])
        inputs_two = lax.all_gather(narrow(normed_two), "mp", axis=0, tiled=True)
        gates = by_index(xor_gather(gate_two.reshape(-1, 128), "mp", ranks, bits_of(ranks)), rank).reshape(-1)

        col_ids = rank * cols_local + jnp.arange(cols_local, dtype=jnp.int32)
        col_mask = (col_ids[None, :] * 4 < (width_choice[:, 1:2] + 1) * FF).astype(jnp.float32)
        inputs_two, top_down = lax.optimization_barrier((inputs_two, top_down))
        pre = product(inputs_two, up_weight, (1, 0))
        relu_act = jax.nn.relu(pre)
        hidden = narrow(relu_act * relu_act * col_mask)
        pre_grad = narrow(top_down * gates[:, None] * col_mask * 2.0 * relu_act)
        dots = jnp.sum(wide(hidden) * top_down, axis=1).reshape(-1, 128)
        share = narrow(product(pre_grad, up_weight, (1, 1)))
        share, hidden, pre_grad = lax.optimization_barrier((share, hidden, pre_grad))
        normed_grad_two = wide(lax.psum_scatter(share, "mp", scatter_dimension=0, tiled=True))
        gate_grad_two = lax.dynamic_slice_in_dim(all_sum(dots, {"mp": ranks}).reshape(-1), rank * rows, rows, 0)
        gated = narrow(gates[:, None] * wide(grads_all))
        lanes = [narrow(product(hidden, gated, (0, 0))), narrow(product(inputs_two, pre_grad, (0, 0)))]
        lanes = [x.reshape(columns, -1, x.shape[1]) for x in lanes]
        lanes = column_scatter(lanes, columns, column, cut=1)
        hidden_share = narrow(product(hidden, down_weight, (1, 0)))
        normed_grad_two, hidden_share, *lanes = lax.optimization_barrier((normed_grad_two, hidden_share, *lanes))
        lanes = [narrow(x) for x in column_scatter(lanes, columns, column, start=1)]

        router_part, router_two = gate_backward(normed_two, hidden_router, state_two, gate_grad_two)
        middle_part, gain_two = norm_backward(normed_grad_two + router_part, scaled_two, inverse_two, hidden_gain)
        middle_grad = wide(out_grad) + middle_part
        grads_one = place_sequence(
            xor_gather(narrow(gate_one[:, None] * middle_grad), "mp", ranks, pair_bits + [1])
        )
        helds = column_gather(lanes, columns, cut=1)
        grads_one, hidden_share, lanes = lax.optimization_barrier((grads_one, hidden_share, lanes))
        hidden_branch = wide(lax.psum_scatter(hidden_share, "mp", scatter_dimension=0, tiled=True))
        layer_output = narrow(middle + gate_two[:, None] * hidden_branch)

        gate_grad_one = jnp.sum(middle_grad * mixer_branch, axis=1)
        weight_parts, pairs = [None] * sequences, []
        grads_now = grads_one
        for k in range(sequences)[::-1]:
            qkv, heads_out, log_total, mask = kept[k]
            qkv_grad = attend_backward(grads_now, weights_out[k], qkv, log_total, cos, sin, mask)
            pairs.append((qkv_grad, weights_in[k]))
            weight_parts[k] = weight_grads(inputs_one, qkv_grad, grads_one, heads_out, columns)
            if k == sequences - 1:
                grads_now, weight_parts[k], helds = lax.optimization_barrier((grads_now, weight_parts[k], helds))
        helds = column_gather(helds, columns, start=1)
        pieces = column_scatter(weight_parts[0], columns, column, cut=1)
        pairs, helds, _ = lax.optimization_barrier((pairs, helds, weight_parts[0]))
        normed_grad_one = from_sequence(share_of(pairs, rows))
        down_sum, = place_blocks(helds[:1], column, [(1, dim, jnp.float32, False)])
        up_sum, = place_blocks(helds[1:], column, [(1, cols_local, jnp.float32, False)])

        pieces, normed_grad_one, down_sum, up_sum = lax.optimization_barrier(
            (pieces, normed_grad_one, down_sum, up_sum)
        )
        pieces = column_scatter(pieces, columns, column, start=1)
        for k in range(1, sequences):
            there = [narrow(x) for x in column_scatter(weight_parts[k], columns, column)]
            back = shift_pairs(ranks, -k * group)
            pieces = [narrow(p + wide(lax.ppermute(t, "mp", back))) for p, t in zip(pieces, there)]
        attention_sum, output_sum = place_blocks(
            column_gather(pieces, columns),
            column,
            [(3, width, jnp.float32, False), (1, width, jnp.float32, True)],
        )
        attention_sum = attention_sum.transpose(1, 0, 2)

        router_part_one, router_one = gate_backward(normed_one, mixer_router, state_one, gate_grad_one)
        input_part, gain_one = norm_backward(normed_grad_one + router_part_one, scaled_one, inverse_one, mixer_gain)
        input_grad = narrow(middle_grad + input_part)

        sizes = {"mp": ranks, "dp": columns}

        smalls = [gain_two, gain_one, router_two.T, router_one.T]
        small_sum = all_sum(jnp.concatenate([x.reshape(-1, 128) for x in smalls], axis=0), sizes)
        cuts = [dim // 128, 2 * dim // 128, (2 * dim + router_two.size) // 128]
        hidden_gain_sum, mixer_gain_sum, hidden_router_sum, mixer_router_sum = (
            x.reshape(-1, dim) for x in jnp.split(small_sum, cuts)
        )
        hidden_gain_sum, mixer_gain_sum = hidden_gain_sum[0], mixer_gain_sum[0]
        hidden_router_sum, mixer_router_sum = hidden_router_sum.T, mixer_router_sum.T
        return (
            layer_output, input_grad, mixer_gain_sum, mixer_router_sum, attention_sum, output_sum,
            hidden_gain_sum, hidden_router_sum, up_sum, down_sum,
        )

    return local


def solution(mesh):
    return jax.shard_map(
        make_local(mesh.shape["dp"], mesh.shape["mp"]),
        mesh=mesh,
        in_specs=(
            P(("dp", "mp"), None),
            P("dp", None),
            P("dp", None),
            P(),
            P(),
            P(None, None, "mp"),
            P("mp", None),
            P(),
            P(),
            P(None, "mp"),
            P("mp", None),
            P(("dp", "mp"), None),
        ),
        out_specs=(
            P(("dp", "mp"), None),
            P(("dp", "mp"), None),
            P(),
            P(),
            P(None, None, "mp"),
            P("mp", None),
            P(),
            P(),
            P(None, "mp"),
            P("mp", None),
        ),
        check_vma=False,
    )
```

```python
import functools
import math

import jax
import jax.numpy as jnp
from jax import lax
from jax.experimental import pallas as pl
from jax.experimental.pallas import tpu as pltpu
from jax.sharding import PartitionSpec as P

H = 16
HD = 128
FF = 8192
SEQ_LEN = 1024


EPSILON = 1e-05
NEG_LARGE = -1e30
HIGHEST = lax.Precision.HIGHEST


def norm_forward(values, gain_vec):
    row_mean = jnp.mean(values, axis=1, keepdims=True)
    centred = values - row_mean
    row_variance = jnp.mean(centred * centred, axis=1, keepdims=True)
    inverse_scale = lax.rsqrt(row_variance + EPSILON)
    scaled = centred * inverse_scale
    return (scaled * gain_vec[None, :], scaled, inverse_scale)


def norm_backward(normed_grad, scaled, inverse_scale, gain_vec):
    gain_grad = jnp.sum(normed_grad * scaled, axis=0)
    scaled_grad = normed_grad * gain_vec[None, :]
    first_mean = jnp.mean(scaled_grad, axis=1, keepdims=True)
    second_mean = jnp.mean(scaled_grad * scaled, axis=1, keepdims=True)
    return (inverse_scale * (scaled_grad - first_mean - scaled * second_mean), gain_grad)


def gate_forward(normed, router, width_col, routed_col):
    logits = jnp.dot(normed, router, precision=HIGHEST, preferred_element_type=jnp.float32)
    soft_probs = jax.nn.softmax(logits, axis=1)
    one_hot = (width_col[:, None] == jnp.arange(4, dtype=jnp.int32)[None, :]).astype(jnp.float32)
    chosen = jnp.sum(soft_probs * one_hot, axis=1)
    route_flags = routed_col.astype(jnp.float32)
    return (
        route_flags * 4.0 * chosen + (1.0 - route_flags),
        (soft_probs, one_hot, chosen, route_flags),
    )


def gate_backward(normed, router, gate_state, gate_grad):
    soft_probs, one_hot, chosen, route_flags = gate_state
    coefficient = route_flags * 4.0 * chosen * gate_grad
    logit_grad = coefficient[:, None] * (one_hot - soft_probs)
    router_grad = lax.dot_general(
        normed,
        logit_grad,
        (((0,), (0,)), ((), ())),
        precision=HIGHEST,
        preferred_element_type=jnp.float32,
    )
    normed_grad = lax.dot_general(
        logit_grad,
        router,
        (((1,), (1,)), ((), ())),
        precision=HIGHEST,
        preferred_element_type=jnp.float32,
    )
    return (normed_grad, router_grad)


Q_BLOCK = 256


def rope_tables(token_count, head_width):
    positions = jnp.arange(token_count, dtype=jnp.float32)
    frequency = jnp.exp(
        jnp.arange(head_width // 2, dtype=jnp.float32) * (-2.0 * math.log(10000.0) / head_width)
    )
    angles = positions[:, None] * frequency[None, :]
    cosine, sine = jnp.cos(angles), jnp.sin(angles)
    return jnp.concatenate([cosine, cosine], axis=1), jnp.concatenate([-sine, sine], axis=1)


def wide(x):
    return x.astype(jnp.float32)


def narrow(x):
    return x.astype(jnp.bfloat16)


def product(a, b, dims):
    return lax.dot_general(a, b, ((dims[:1], dims[1:]), ((), ())), preferred_element_type=jnp.float32)


def block_scores(queries, keys_all, start):
    scores = product(queries, keys_all, (1, 1)) * (1.0 / math.sqrt(HD))
    row = lax.broadcasted_iota(jnp.int32, scores.shape, 0) + start
    col = lax.broadcasted_iota(jnp.int32, scores.shape, 1)
    return jnp.where(col <= row, scores, NEG_LARGE)


def forward_kernel(x_ref, w_ref, cos_ref, sin_ref, mask_ref, qkv_ref, heads_ref, log_ref):
    tokens, heads = x_ref.shape[0], mask_ref.shape[1]
    width = heads * HD
    block = min(Q_BLOCK, tokens)
    for start in range(0, tokens, block):
        here, end = slice(start, start + block), start + block
        x = x_ref[here, :]
        cos, sin = cos_ref[here, :], sin_ref[here, :]
        for part in range(3):
            rows = product(x, w_ref[:, part * width : (part + 1) * width], (1, 0))
            for head in range(heads):
                value = rows[:, head * HD : (head + 1) * HD]
                if part < 2:
                    value = value * cos + pltpu.roll(value, HD // 2, 1) * sin
                at = part * width + head * HD
                qkv_ref[here, at : at + HD] = narrow(value)
        for head in range(heads):
            at = head * HD
            lanes, key_lanes, value_lanes = (slice(at + p * width, at + p * width + HD) for p in range(3))
            scores = block_scores(qkv_ref[here, lanes], qkv_ref[:end, key_lanes], start)
            row_max = jnp.max(scores, axis=1, keepdims=True)
            shifted = jnp.exp(scores - row_max)
            total = jnp.sum(shifted, axis=1, keepdims=True)
            mix = product(narrow(shifted / total), qkv_ref[:end, value_lanes], (1, 0))
            heads_ref[here, lanes] = narrow(mix * mask_ref[here, head : head + 1])
            log_ref[here, head : head + 1] = row_max + jnp.log(total)


def backward_kernel(g_ref, w_ref, qkv_ref, log_ref, cos_ref, sin_ref, mask_ref, out_ref, keys_acc, values_acc):
    tokens, heads = g_ref.shape[0], mask_ref.shape[1]
    width = heads * HD
    block = min(Q_BLOCK, tokens)
    scale = 1.0 / math.sqrt(HD)
    for start in range(0, tokens, block):
        here, end = slice(start, start + block), start + block
        cos, sin = cos_ref[here, :], sin_ref[here, :]
        rows = narrow(product(g_ref[here, :], w_ref[...], (1, 0)))
        for head in range(heads):
            at = head * HD
            lanes, key_lanes, value_lanes = (slice(at + p * width, at + p * width + HD) for p in range(3))
            heads_grad = rows[:, lanes] * narrow(mask_ref[here, head : head + 1])
            queries, keys_all = qkv_ref[here, lanes], qkv_ref[:end, key_lanes]
            scores = block_scores(queries, keys_all, start)
            probs = jnp.exp(scores - log_ref[here, head : head + 1])
            values_part = product(narrow(probs), heads_grad, (0, 0))
            probs_grad = product(heads_grad, qkv_ref[:end, value_lanes], (1, 1))
            centre = jnp.sum(probs * probs_grad, axis=1, keepdims=True)
            score_grad = narrow(probs * (probs_grad - centre))
            queries_grad = product(score_grad, keys_all, (1, 0)) * scale
            keys_part = product(score_grad, queries, (0, 0)) * scale
            turned = queries_grad * cos - pltpu.roll(queries_grad, HD // 2, 1) * sin
            out_ref[here, lanes] = narrow(turned)
            if start:
                values_acc[:start, lanes] += values_part[:start]
                keys_acc[:start, lanes] += keys_part[:start]
            values_acc[here, lanes] = values_part[start:]
            keys_acc[here, lanes] = keys_part[start:]
    for start in range(0, tokens, block):
        here = slice(start, start + block)
        cos, sin = cos_ref[here, :], sin_ref[here, :]
        out_ref[here, 2 * width :] = narrow(values_acc[here, :])
        for head in range(heads):
            at = head * HD
            value = keys_acc[here, at : at + HD]
            out_ref[here, width + at : width + at + HD] = narrow(value * cos - pltpu.roll(value, HD // 2, 1) * sin)


def share_kernel(*refs):
    *given, out_ref = refs
    total = product(given[0][...], given[1][...], (1, 1))
    for a_ref, w_ref in zip(given[2::2], given[3::2]):
        total = total + product(a_ref[...], w_ref[...], (1, 1))
    out_ref[0, 0] = narrow(total)


def weight_kernel(x_ref, q_ref, g_ref, h_ref, *outs):
    width = h_ref.shape[1]
    half = x_ref.shape[1] // 2
    for lane, out_ref in enumerate(outs):
        here = slice(lane * half, (lane + 1) * half)
        out_ref[0, :, : 3 * width] = narrow(product(x_ref[:, here], q_ref[...], (0, 0)))
        out_ref[0, :, 3 * width :] = narrow(product(g_ref[:, here], h_ref[...], (0, 0)))


def place_kernel(count, widths, turned, at_ref, *refs):
    lanes = (len(refs) - len(widths)) // count
    blocks, outs = refs[: lanes * count], refs[lanes * count :]
    half = blocks[0].shape[0]
    for far in range(count):

        @pl.when((pl.program_id(0) ^ at_ref[0]) == far)
        def _():
            for lane in range(lanes):
                here = slice(lane * half, (lane + 1) * half)
                block = blocks[lane * count + far]
                start = 0
                for out_ref, width, turn in zip(outs, widths, turned):
                    for part in range(out_ref.shape[0] if len(out_ref.shape) == 3 else 1):
                        value = block[:, start : start + width].astype(out_ref.dtype)
                        start += width
                        if turn:
                            out_ref[:, here] = value.T
                        elif len(out_ref.shape) == 3:
                            out_ref[part, here, :] = value
                        else:
                            out_ref[here, :] = value


VMEM_LIMIT = 56 * 1024 * 1024


def whole_specs(count):
    return [pl.BlockSpec(memory_space=pltpu.VMEM)] * count


def attend_forward(x, w, cos, sin, mask):
    tokens, heads = mask.shape
    dim, width = w.shape[0], heads * HD
    return pl.pallas_call(
        forward_kernel,
        out_shape=[
            jax.ShapeDtypeStruct((tokens, 3 * width), jnp.bfloat16),
            jax.ShapeDtypeStruct((tokens, width), jnp.bfloat16),
            jax.ShapeDtypeStruct((tokens, heads), jnp.float32),
        ],
        in_specs=whole_specs(5),
        out_specs=whole_specs(3),
        compiler_params=pltpu.CompilerParams(vmem_limit_bytes=VMEM_LIMIT),
        cost_estimate=pl.CostEstimate(
            flops=6 * tokens * dim * width + 2 * tokens * tokens * width,
            bytes_accessed=12 << 20,
            transcendentals=tokens * tokens * heads // 2,
        ),
        name="attend_forward",
    )(x, w, cos, sin, mask)


def attend_backward(g, w, qkv, log_total, cos, sin, mask):
    tokens, heads = mask.shape
    dim, width = w.shape[0], heads * HD
    return pl.pallas_call(
        backward_kernel,
        out_shape=jax.ShapeDtypeStruct((tokens, 3 * width), jnp.bfloat16),
        in_specs=whole_specs(7),
        out_specs=whole_specs(1)[0],
        scratch_shapes=[pltpu.VMEM((tokens, width), jnp.float32)] * 2,
        compiler_params=pltpu.CompilerParams(vmem_limit_bytes=VMEM_LIMIT),
        cost_estimate=pl.CostEstimate(
            flops=2 * tokens * dim * width + 5 * tokens * tokens * width,
            bytes_accessed=12 << 20,
            transcendentals=tokens * tokens * heads // 2,
        ),
        name="attend_backward",
    )(g, w, qkv, log_total, cos, sin, mask)


def share_of(pairs, rows):
    tokens, depth = pairs[0][0].shape
    dim = pairs[0][1].shape[0]
    specs = [
        pl.BlockSpec((rows, depth), lambda i: (i, 0)),
        pl.BlockSpec((dim, depth), lambda i: (0, 0)),
    ] * len(pairs)
    return pl.pallas_call(
        share_kernel,
        grid=(tokens // rows,),
        out_shape=jax.ShapeDtypeStruct((2, tokens // rows // 2, rows, dim), jnp.bfloat16),
        in_specs=specs,
        out_specs=pl.BlockSpec((1, 1, rows, dim), lambda i: (i % 2, i // 2, 0, 0)),
        compiler_params=pltpu.CompilerParams(vmem_limit_bytes=VMEM_LIMIT),
        cost_estimate=pl.CostEstimate(
            flops=2 * tokens * dim * depth * len(pairs), bytes_accessed=12 << 20, transcendentals=0
        ),
        name="share_of",
    )(*[x for pair in pairs for x in pair])


def weight_grads(x, qkv_grad, g, heads_out, count):
    tokens, dim = x.shape
    width = heads_out.shape[1]
    block = dim // count
    out = jax.ShapeDtypeStruct((count, block // 2, 4 * width), jnp.bfloat16)
    return pl.pallas_call(
        weight_kernel,
        grid=(count,),
        out_shape=[out, out],
        in_specs=[
            pl.BlockSpec((tokens, block), lambda i: (0, i)),
            pl.BlockSpec((tokens, 3 * width), lambda i: (0, 0)),
            pl.BlockSpec((tokens, block), lambda i: (0, i)),
            pl.BlockSpec((tokens, width), lambda i: (0, 0)),
        ],
        out_specs=[pl.BlockSpec((1, block // 2, 4 * width), lambda i: (i, 0, 0))] * 2,
        compiler_params=pltpu.CompilerParams(vmem_limit_bytes=VMEM_LIMIT),
        cost_estimate=pl.CostEstimate(flops=8 * tokens * dim * width, bytes_accessed=14 << 20, transcendentals=0),
        name="weight_grads",
    )(x, qkv_grad, g, heads_out)


def place_blocks(lanes, index, outs):
    count = len(lanes[0])
    half, total = lanes[0][0].shape
    rows = len(lanes) * half
    shapes, specs = [], []
    for planes, width, kind, turned in outs:
        if turned:
            shapes.append(jax.ShapeDtypeStruct((width, rows * count), kind))
            specs.append(pl.BlockSpec((width, rows), lambda i, at: (0, i)))
        elif planes > 1:
            shapes.append(jax.ShapeDtypeStruct((planes, rows * count, width), kind))
            specs.append(pl.BlockSpec((planes, rows, width), lambda i, at: (0, i, 0)))
        else:
            shapes.append(jax.ShapeDtypeStruct((rows * count, width), kind))
            specs.append(pl.BlockSpec((rows, width), lambda i, at: (i, 0)))
    given = [held[far] for held in lanes for far in range(count)]
    return pl.pallas_call(
        functools.partial(place_kernel, count, [o[1] for o in outs], [o[3] for o in outs]),
        grid_spec=pltpu.PrefetchScalarGridSpec(
            num_scalar_prefetch=1,
            grid=(count,),
            in_specs=[pl.BlockSpec((half, total), lambda i, at: (0, 0))] * len(given),
            out_specs=specs,
        ),
        out_shape=shapes,
        compiler_params=pltpu.CompilerParams(vmem_limit_bytes=VMEM_LIMIT),
        cost_estimate=pl.CostEstimate(flops=0, bytes_accessed=12 << 20, transcendentals=0),
        name="place_blocks",
    )(index.astype(jnp.int32).reshape(1), *given)


def swap_pairs(size, bit):
    return [(i, i ^ bit) for i in range(size)]


def shift_pairs(size, shift):
    return [(i, (i - shift) % size) for i in range(size)]


def bits_of(size):
    return [1 << i for i in range(size.bit_length() - 1)]


def pick(x, index, axis=0):
    return lax.dynamic_index_in_dim(x, index, axis, keepdims=False)


def after(x, *others):
    return lax.optimization_barrier((x,) + others)[0]


def xor_gather(x, axis, size, bits):
    held = dict(x) if isinstance(x, dict) else {0: x}
    for bit in bits:
        for far in list(held):
            held[far ^ bit] = lax.ppermute(held[far], axis, swap_pairs(size, bit))
    return held


def by_index(held, index, axis=0):
    shape = held[0].shape
    out = jnp.zeros(shape[:axis] + (len(held),) + shape[axis:], held[0].dtype)
    for far, block in held.items():
        out = lax.dynamic_update_index_in_dim(out, block, index ^ far, axis)
    return out


def xor_scatter(blocks, axis_name, size, bits, steps, index, axis, all_steps=None):
    all_steps = list(all_steps or steps)
    left = sorted(all_steps[all_steps.index(steps[0]) :], reverse=True)
    blocks = blocks.reshape(blocks.shape[:axis] + (2,) * len(left) + blocks.shape[axis + 1 :])
    for bit, step in zip(bits, steps):
        at = axis + left.index(step)
        left.remove(step)
        side = (index // step) % 2
        got = lax.ppermute(narrow(pick(blocks, 1 - side, at)), axis_name, swap_pairs(size, bit))
        blocks = wide(pick(blocks, side, at)) + wide(got)
    tail = blocks.shape[axis + len(left) :]
    return blocks.reshape(blocks.shape[:axis] + ((2 ** len(left),) if left else ()) + tail)


def lane_bits(size):
    return bits_of(size), bits_of(size)[::-1]


def column_gather(lanes, size, cut=None, start=None):
    return [xor_gather(x, "dp", size, bits[start:cut]) for x, bits in zip(lanes, lane_bits(size))]


def gate_lanes(lanes, *gates):
    flat = [held[far] for held in lanes for far in held]
    flat = lax.optimization_barrier((*flat, *gates))
    flat = iter(flat)
    return [{far: next(flat) for far in held} for held in lanes]


def column_scatter(lanes, size, column, cut=None, start=None):
    return [
        xor_scatter(x, "dp", size, bits[start:cut], bits[start:cut], column, 0, bits)
        for x, bits in zip(lanes, lane_bits(size))
    ]


def all_sum(x, sizes):
    for axis, size in sizes.items():
        for bit in bits_of(size):
            x = x + lax.ppermute(x, axis, swap_pairs(size, bit))
    return x


def make_local(columns, ranks):
    def local(
        layer_input, width_choice, routed_flag, mixer_gain, mixer_router, attention_weight,
        output_weight, hidden_gain, hidden_router, up_weight, down_weight, out_grad,
    ):
        column, rank = lax.axis_index("dp"), lax.axis_index("mp")
        rows, dim = layer_input.shape
        core = rank % 2
        group = SEQ_LEN // rows
        sequences = ranks // group
        place, sequence = rank % group, rank // group
        pair_bits = [b for b in bits_of(group) if b > 1]
        own_heads = output_weight.shape[0] // HD
        cols_local = up_weight.shape[1]
        width_own = lax.dynamic_slice_in_dim(width_choice, rank * rows, rows, 0)
        routed_own = lax.dynamic_slice_in_dim(routed_flag, rank * rows, rows, 0)
        cos, sin = rope_tables(SEQ_LEN, HD)

        def place_sequence(held):
            return by_index(held, place).reshape(SEQ_LEN, -1)

        def core_sum(blocks):
            got = lax.ppermute(pick(blocks, 1 - core), "mp", swap_pairs(ranks, 1))
            return wide(pick(blocks, core)) + wide(got)

        def chip_sum(blocks):
            bits = pair_bits[::-1]
            return xor_scatter(blocks, "mp", ranks, bits, [b // 2 for b in bits], place // 2, 0)

        width = own_heads * HD
        chunk_rows = dim // columns
        half_rows = chunk_rows // 2

        def in_slice(w):
            return jnp.concatenate([w[:, p] for p in range(3)], axis=1)

        lanes_in = [
            in_slice(lax.dynamic_slice_in_dim(attention_weight, column * chunk_rows + at, half_rows, 0))
            for at in (0, half_rows)
        ]
        lanes_out = [
            lax.dynamic_slice_in_dim(output_weight, column * chunk_rows + at, half_rows, 1).T
            for at in (0, half_rows)
        ]
        input_wide = wide(layer_input)
        normed_one, scaled_one, inverse_one = norm_forward(input_wide, mixer_gain)
        low_one = narrow(normed_one)
        low_one, lanes_in, lanes_out = lax.optimization_barrier((low_one, lanes_in, lanes_out))
        held = xor_gather(low_one, "mp", ranks, pair_bits)
        fetched_in, fetched_out = [
            [[lax.ppermute(x, "mp", shift_pairs(ranks, k * group)) for x in lanes] for k in range(1, sequences)]
            for lanes in (lanes_in, lanes_out)
        ]
        sequence_width = lax.dynamic_slice_in_dim(width_choice[:, 0], sequence * SEQ_LEN, SEQ_LEN, 0)
        masks = []
        for k in range(sequences):
            heads = ((rank + k * group) % ranks) * own_heads + jnp.arange(own_heads, dtype=jnp.int32)
            masks.append((heads[None, :] * 4 < (sequence_width[:, None] + 1) * H).astype(jnp.float32))
        weights_in, weights_out = [in_slice(attention_weight)], [output_weight.T]
        held, fetched_in, masks, weights_in, weights_out, cos, sin = lax.optimization_barrier(
            (held, fetched_in, masks, weights_in, weights_out, cos, sin)
        )
        inputs_one = place_sequence(xor_gather(held, "mp", ranks, [1]))
        grads_all = lax.all_gather(after(out_grad, *[x for lanes in fetched_in for x in lanes]), "mp", axis=0, tiled=True)
        steps_in = [column_gather(x, columns, cut=1) for x in fetched_in]
        gate_one, state_one = gate_forward(normed_one, mixer_router, width_own[:, 0], routed_own[:, 0])

        kept = []
        for k in range(sequences):
            mask = masks[k]
            if k:
                steps, fetched, _ = lax.optimization_barrier((steps_in[k - 1], fetched_out[k - 1], kept[0][0]))
                held = column_gather(steps, columns, start=1)
                held_out = column_gather(fetched, columns, cut=1)
                held, held_out = lax.optimization_barrier((held, held_out))
                held_out = column_gather(held_out, columns, start=1)
                weights_in += place_blocks(held, column, [(1, 3 * width, jnp.bfloat16, False)])
                weights_out += place_blocks(held_out, column, [(1, width, jnp.bfloat16, False)])
            kept.append((*attend_forward(inputs_one, weights_in[k], cos, sin, mask), mask))
        mixer_branch = chip_sum(core_sum(share_of([(x[1], w) for x, w in zip(kept, weights_out)], rows)))
        mixer_branch, grads_all = lax.optimization_barrier((mixer_branch, grads_all))
        top_down = product(grads_all, down_weight, (1, 1))

        middle = input_wide + gate_one[:, None] * mixer_branch
        normed_two, scaled_two, inverse_two = norm_forward(middle, hidden_gain)
        gate_two, state_two = gate_forward(normed_two, hidden_router, width_own[:, 1], routed_own[:, 1])
        inputs_two = lax.all_gather(narrow(normed_two), "mp", axis=0, tiled=True)
        gates = by_index(xor_gather(gate_two.reshape(-1, 128), "mp", ranks, bits_of(ranks)), rank).reshape(-1)

        col_ids = rank * cols_local + jnp.arange(cols_local, dtype=jnp.int32)
        col_mask = (col_ids[None, :] * 4 < (width_choice[:, 1:2] + 1) * FF).astype(jnp.float32)
        inputs_two, top_down = lax.optimization_barrier((inputs_two, top_down))
        pre = product(inputs_two, up_weight, (1, 0))
        relu_act = jax.nn.relu(pre)
        hidden = narrow(relu_act * relu_act * col_mask)
        pre_grad = narrow(top_down * gates[:, None] * col_mask * 2.0 * relu_act)
        dots = jnp.sum(wide(hidden) * top_down, axis=1).reshape(-1, 128)
        share = narrow(product(pre_grad, up_weight, (1, 1)))
        share, hidden, pre_grad = lax.optimization_barrier((share, hidden, pre_grad))
        normed_grad_two = wide(lax.psum_scatter(share, "mp", scatter_dimension=0, tiled=True))
        gate_grad_two = lax.dynamic_slice_in_dim(all_sum(dots, {"mp": ranks}).reshape(-1), rank * rows, rows, 0)
        gated = narrow(gates[:, None] * wide(grads_all))
        lanes = [narrow(product(hidden, gated, (0, 0))), narrow(product(inputs_two, pre_grad, (0, 0)))]
        lanes = [x.reshape(columns, -1, x.shape[1]) for x in lanes]
        lanes = column_scatter(lanes, columns, column, cut=1)
        hidden_share = narrow(product(hidden, down_weight, (1, 0)))
        normed_grad_two, hidden_share, *lanes = lax.optimization_barrier((normed_grad_two, hidden_share, *lanes))
        lanes = [narrow(x) for x in column_scatter(lanes, columns, column, start=1)]

        router_part, router_two = gate_backward(normed_two, hidden_router, state_two, gate_grad_two)
        middle_part, gain_two = norm_backward(normed_grad_two + router_part, scaled_two, inverse_two, hidden_gain)
        middle_grad = wide(out_grad) + middle_part
        grads_one = place_sequence(
            xor_gather(narrow(gate_one[:, None] * middle_grad), "mp", ranks, pair_bits + [1])
        )
        helds = column_gather(lanes, columns, cut=1)
        grads_one, hidden_share, lanes = lax.optimization_barrier((grads_one, hidden_share, lanes))
        hidden_branch = wide(lax.psum_scatter(hidden_share, "mp", scatter_dimension=0, tiled=True))
        layer_output = narrow(middle + gate_two[:, None] * hidden_branch)

        gate_grad_one = jnp.sum(middle_grad * mixer_branch, axis=1)
        pairs, sent = [], []
        grads_now = grads_one
        for k in range(sequences)[::-1]:
            qkv, heads_out, log_total, mask = kept[k]
            qkv_grad = attend_backward(grads_now, weights_out[k], qkv, log_total, cos, sin, mask)
            if sent:
                qkv_grad, sent[-1] = lax.optimization_barrier((qkv_grad, sent[-1]))
            pairs.append((qkv_grad, weights_in[k]))
            part = weight_grads(inputs_one, qkv_grad, grads_one, heads_out, columns)
            if k:
                grads_now, part, helds = lax.optimization_barrier((grads_now, part, helds))
                sent.append(column_scatter(part, columns, column, cut=1))
        sent = [[narrow(x) for x in column_scatter(lanes, columns, column, start=1)] for lanes in sent]
        pairs, sent, part = lax.optimization_barrier((pairs, sent, part))
        there = [
            [lax.ppermute(x, "mp", shift_pairs(ranks, -k * group)) for x in lanes]
            for k, lanes in zip(range(1, sequences)[::-1], sent)
        ]
        helds, sent = lax.optimization_barrier((helds, sent))
        helds = column_gather(helds, columns, start=1)
        pieces = column_scatter(part, columns, column, cut=1)
        blocks = core_sum(share_of(pairs, rows))
        blocks, pieces = lax.optimization_barrier((blocks, pieces))
        normed_grad_one = chip_sum(blocks)
        pieces = column_scatter(pieces, columns, column, start=1)
        for lanes in there:
            pieces = [p + wide(t) for p, t in zip(pieces, lanes)]
        spread = column_gather([narrow(p) for p in pieces], columns, cut=1)
        spread, helds = lax.optimization_barrier((spread, helds))
        spread = column_gather(spread, columns, start=1)
        down_sum, = place_blocks(helds[:1], column, [(1, dim, jnp.float32, False)])
        up_sum, = place_blocks(helds[1:], column, [(1, cols_local, jnp.float32, False)])
        attention_sum, output_sum = place_blocks(
            spread,
            column,
            [(3, width, jnp.float32, False), (1, width, jnp.float32, True)],
        )
        attention_sum = attention_sum.transpose(1, 0, 2)

        router_part_one, router_one = gate_backward(normed_one, mixer_router, state_one, gate_grad_one)
        input_part, gain_one = norm_backward(normed_grad_one + router_part_one, scaled_one, inverse_one, mixer_gain)
        input_grad = narrow(middle_grad + input_part)

        sizes = {"mp": ranks, "dp": columns}

        smalls = [gain_two, gain_one, router_two.T, router_one.T]
        small_sum = all_sum(jnp.concatenate([x.reshape(-1, 128) for x in smalls], axis=0), sizes)
        cuts = [dim // 128, 2 * dim // 128, (2 * dim + router_two.size) // 128]
        hidden_gain_sum, mixer_gain_sum, hidden_router_sum, mixer_router_sum = (
            x.reshape(-1, dim) for x in jnp.split(small_sum, cuts)
        )
        hidden_gain_sum, mixer_gain_sum = hidden_gain_sum[0], mixer_gain_sum[0]
        hidden_router_sum, mixer_router_sum = hidden_router_sum.T, mixer_router_sum.T
        return (
            layer_output, input_grad, mixer_gain_sum, mixer_router_sum, attention_sum, output_sum,
            hidden_gain_sum, hidden_router_sum, up_sum, down_sum,
        )

    return local


def solution(mesh):
    return jax.shard_map(
        make_local(mesh.shape["dp"], mesh.shape["mp"]),
        mesh=mesh,
        in_specs=(
            P(("dp", "mp"), None),
            P("dp", None),
            P("dp", None),
            P(),
            P(),
            P(None, None, "mp"),
            P("mp", None),
            P(),
            P(),
            P(None, "mp"),
            P("mp", None),
            P(("dp", "mp"), None),
        ),
        out_specs=(
            P(("dp", "mp"), None),
            P(("dp", "mp"), None),
            P(),
            P(),
            P(None, None, "mp"),
            P("mp", None),
            P(),
            P(),
            P(None, "mp"),
            P("mp", None),
        ),
        check_vma=False,
    )
```

```python
import functools
import math

import jax
import jax.numpy as jnp
from jax import lax
from jax.experimental import pallas as pl
from jax.experimental.pallas import tpu as pltpu
from jax.sharding import PartitionSpec as P

H = 16
HD = 128
FF = 8192
SEQ_LEN = 1024


EPSILON = 1e-05
NEG_LARGE = -1e30
HIGHEST = lax.Precision.HIGHEST


def norm_forward(values, gain_vec):
    row_mean = jnp.mean(values, axis=1, keepdims=True)
    centred = values - row_mean
    row_variance = jnp.mean(centred * centred, axis=1, keepdims=True)
    inverse_scale = lax.rsqrt(row_variance + EPSILON)
    scaled = centred * inverse_scale
    return (scaled * gain_vec[None, :], scaled, inverse_scale)


def norm_backward(normed_grad, scaled, inverse_scale, gain_vec):
    gain_grad = jnp.sum(normed_grad * scaled, axis=0)
    scaled_grad = normed_grad * gain_vec[None, :]
    first_mean = jnp.mean(scaled_grad, axis=1, keepdims=True)
    second_mean = jnp.mean(scaled_grad * scaled, axis=1, keepdims=True)
    return (inverse_scale * (scaled_grad - first_mean - scaled * second_mean), gain_grad)


def gate_forward(normed, router, width_col, routed_col):
    logits = jnp.dot(normed, router, precision=HIGHEST, preferred_element_type=jnp.float32)
    soft_probs = jax.nn.softmax(logits, axis=1)
    one_hot = (width_col[:, None] == jnp.arange(4, dtype=jnp.int32)[None, :]).astype(jnp.float32)
    chosen = jnp.sum(soft_probs * one_hot, axis=1)
    route_flags = routed_col.astype(jnp.float32)
    return (
        route_flags * 4.0 * chosen + (1.0 - route_flags),
        (soft_probs, one_hot, chosen, route_flags),
    )


def gate_backward(normed, router, gate_state, gate_grad):
    soft_probs, one_hot, chosen, route_flags = gate_state
    coefficient = route_flags * 4.0 * chosen * gate_grad
    logit_grad = coefficient[:, None] * (one_hot - soft_probs)
    router_grad = lax.dot_general(
        normed,
        logit_grad,
        (((0,), (0,)), ((), ())),
        precision=HIGHEST,
        preferred_element_type=jnp.float32,
    )
    normed_grad = lax.dot_general(
        logit_grad,
        router,
        (((1,), (1,)), ((), ())),
        precision=HIGHEST,
        preferred_element_type=jnp.float32,
    )
    return (normed_grad, router_grad)


Q_BLOCK = 256


def rope_tables(token_count, head_width):
    positions = jnp.arange(token_count, dtype=jnp.float32)
    frequency = jnp.exp(
        jnp.arange(head_width // 2, dtype=jnp.float32) * (-2.0 * math.log(10000.0) / head_width)
    )
    angles = positions[:, None] * frequency[None, :]
    cosine, sine = jnp.cos(angles), jnp.sin(angles)
    return jnp.concatenate([cosine, cosine], axis=1), jnp.concatenate([-sine, sine], axis=1)


def wide(x):
    return x.astype(jnp.float32)


def narrow(x):
    return x.astype(jnp.bfloat16)


def product(a, b, dims):
    return lax.dot_general(a, b, ((dims[:1], dims[1:]), ((), ())), preferred_element_type=jnp.float32)


def block_scores(queries, keys_all, start):
    scores = product(queries, keys_all, (1, 1)) * (1.0 / math.sqrt(HD))
    row = lax.broadcasted_iota(jnp.int32, scores.shape, 0) + start
    col = lax.broadcasted_iota(jnp.int32, scores.shape, 1)
    return jnp.where(col <= row, scores, NEG_LARGE)


def forward_kernel(x_ref, w_ref, cos_ref, sin_ref, mask_ref, qkv_ref, heads_ref, log_ref):
    tokens, heads = x_ref.shape[0], mask_ref.shape[1]
    width = heads * HD
    block = min(Q_BLOCK, tokens)
    for start in range(0, tokens, block):
        here, end = slice(start, start + block), start + block
        x = x_ref[here, :]
        cos, sin = cos_ref[here, :], sin_ref[here, :]
        for part in range(3):
            rows = product(x, w_ref[:, part * width : (part + 1) * width], (1, 0))
            for head in range(heads):
                value = rows[:, head * HD : (head + 1) * HD]
                if part < 2:
                    value = value * cos + pltpu.roll(value, HD // 2, 1) * sin
                at = part * width + head * HD
                qkv_ref[here, at : at + HD] = narrow(value)
        for head in range(heads):
            at = head * HD
            lanes, key_lanes, value_lanes = (slice(at + p * width, at + p * width + HD) for p in range(3))
            scores = block_scores(qkv_ref[here, lanes], qkv_ref[:end, key_lanes], start)
            row_max = jnp.max(scores, axis=1, keepdims=True)
            shifted = jnp.exp(scores - row_max)
            total = jnp.sum(shifted, axis=1, keepdims=True)
            mix = product(narrow(shifted * (1.0 / total)), qkv_ref[:end, value_lanes], (1, 0))
            heads_ref[here, lanes] = narrow(mix * mask_ref[here, head : head + 1])
            log_ref[here, head : head + 1] = row_max + jnp.log(total)


def backward_kernel(g_ref, w_ref, qkv_ref, log_ref, cos_ref, sin_ref, mask_ref, out_ref, keys_acc, values_acc):
    tokens, heads = g_ref.shape[0], mask_ref.shape[1]
    width = heads * HD
    block = min(Q_BLOCK, tokens)
    scale = 1.0 / math.sqrt(HD)
    for start in range(0, tokens, block):
        here, end = slice(start, start + block), start + block
        cos, sin = cos_ref[here, :], sin_ref[here, :]
        rows = narrow(product(g_ref[here, :], w_ref[...], (1, 0)))
        for head in range(heads):
            at = head * HD
            lanes, key_lanes, value_lanes = (slice(at + p * width, at + p * width + HD) for p in range(3))
            heads_grad = rows[:, lanes] * narrow(mask_ref[here, head : head + 1])
            queries, keys_all = qkv_ref[here, lanes], qkv_ref[:end, key_lanes]
            scores = block_scores(queries, keys_all, start)
            probs = jnp.exp(scores - log_ref[here, head : head + 1])
            values_part = product(narrow(probs), heads_grad, (0, 0))
            probs_grad = product(heads_grad, qkv_ref[:end, value_lanes], (1, 1))
            centre = jnp.sum(probs * probs_grad, axis=1, keepdims=True)
            score_grad = narrow(probs * (probs_grad - centre))
            queries_grad = product(score_grad, keys_all, (1, 0)) * scale
            keys_part = product(score_grad, queries, (0, 0)) * scale
            turned = queries_grad * cos - pltpu.roll(queries_grad, HD // 2, 1) * sin
            out_ref[here, lanes] = narrow(turned)
            if start:
                values_acc[:start, lanes] += values_part[:start]
                keys_acc[:start, lanes] += keys_part[:start]
            values_acc[here, lanes] = values_part[start:]
            keys_acc[here, lanes] = keys_part[start:]
    for start in range(0, tokens, block):
        here = slice(start, start + block)
        cos, sin = cos_ref[here, :], sin_ref[here, :]
        out_ref[here, 2 * width :] = narrow(values_acc[here, :])
        for head in range(heads):
            at = head * HD
            value = keys_acc[here, at : at + HD]
            out_ref[here, width + at : width + at + HD] = narrow(value * cos - pltpu.roll(value, HD // 2, 1) * sin)


def share_kernel(side_ref, *refs):
    *given, out_ref = refs
    total = product(given[0][...], given[1][...], (1, 1))
    for a_ref, w_ref in zip(given[2::2], given[3::2]):
        total = total + product(a_ref[...], w_ref[...], (1, 1))
    out_ref[0] = narrow(total)


def weight_kernel(x_ref, q_ref, g_ref, h_ref, *outs):
    width = h_ref.shape[1]
    half = x_ref.shape[1] // 2
    for lane, out_ref in enumerate(outs):
        here = slice(lane * half, (lane + 1) * half)
        out_ref[0, :, : 3 * width] = narrow(product(x_ref[:, here], q_ref[...], (0, 0)))
        out_ref[0, :, 3 * width :] = narrow(product(g_ref[:, here], h_ref[...], (0, 0)))


def place_kernel(count, widths, turned, at_ref, *refs):
    lanes = (len(refs) - len(widths)) // count
    blocks, outs = refs[: lanes * count], refs[lanes * count :]
    half = blocks[0].shape[0]
    for far in range(count):

        @pl.when((pl.program_id(0) ^ at_ref[0]) == far)
        def _():
            for lane in range(lanes):
                here = slice(lane * half, (lane + 1) * half)
                block = blocks[lane * count + far]
                start = 0
                for out_ref, width, turn in zip(outs, widths, turned):
                    for part in range(out_ref.shape[0] if len(out_ref.shape) == 3 else 1):
                        value = block[:, start : start + width].astype(out_ref.dtype)
                        start += width
                        if turn:
                            out_ref[:, here] = value.T
                        elif len(out_ref.shape) == 3:
                            out_ref[part, here, :] = value
                        else:
                            out_ref[here, :] = value


VMEM_LIMIT = 56 * 1024 * 1024


def whole_specs(count):
    return [pl.BlockSpec(memory_space=pltpu.VMEM)] * count


def attend_forward(x, w, cos, sin, mask):
    tokens, heads = mask.shape
    dim, width = w.shape[0], heads * HD
    return pl.pallas_call(
        forward_kernel,
        out_shape=[
            jax.ShapeDtypeStruct((tokens, 3 * width), jnp.bfloat16),
            jax.ShapeDtypeStruct((tokens, width), jnp.bfloat16),
            jax.ShapeDtypeStruct((tokens, heads), jnp.float32),
        ],
        in_specs=whole_specs(5),
        out_specs=whole_specs(3),
        compiler_params=pltpu.CompilerParams(vmem_limit_bytes=VMEM_LIMIT),
        cost_estimate=pl.CostEstimate(
            flops=6 * tokens * dim * width + 2 * tokens * tokens * width,
            bytes_accessed=12 << 20,
            transcendentals=tokens * tokens * heads // 2,
        ),
        name="attend_forward",
    )(x, w, cos, sin, mask)


def attend_backward(g, w, qkv, log_total, cos, sin, mask):
    tokens, heads = mask.shape
    dim, width = w.shape[0], heads * HD
    return pl.pallas_call(
        backward_kernel,
        out_shape=jax.ShapeDtypeStruct((tokens, 3 * width), jnp.bfloat16),
        in_specs=whole_specs(7),
        out_specs=whole_specs(1)[0],
        scratch_shapes=[pltpu.VMEM((tokens, width), jnp.float32)] * 2,
        compiler_params=pltpu.CompilerParams(vmem_limit_bytes=VMEM_LIMIT),
        cost_estimate=pl.CostEstimate(
            flops=2 * tokens * dim * width + 5 * tokens * tokens * width,
            bytes_accessed=12 << 20,
            transcendentals=tokens * tokens * heads // 2,
        ),
        name="attend_backward",
    )(g, w, qkv, log_total, cos, sin, mask)


def share_of(pairs, rows, side):
    tokens, depth = pairs[0][0].shape
    dim = pairs[0][1].shape[0]
    chips = tokens // rows // 2
    specs = [
        pl.BlockSpec((rows, depth), lambda i, side: (2 * i + side[0], 0)),
        pl.BlockSpec((dim, depth), lambda i, side: (0, 0)),
    ] * len(pairs)
    return pl.pallas_call(
        share_kernel,
        grid_spec=pltpu.PrefetchScalarGridSpec(
            num_scalar_prefetch=1,
            grid=(chips,),
            in_specs=specs,
            out_specs=pl.BlockSpec((1, rows, dim), lambda i, side: (i, 0, 0)),
        ),
        out_shape=jax.ShapeDtypeStruct((chips, rows, dim), jnp.bfloat16),
        compiler_params=pltpu.CompilerParams(vmem_limit_bytes=VMEM_LIMIT),
        cost_estimate=pl.CostEstimate(
            flops=tokens * dim * depth * len(pairs), bytes_accessed=12 << 20, transcendentals=0
        ),
        name="share_of",
    )(side.astype(jnp.int32).reshape(1), *[x for pair in pairs for x in pair])


def weight_grads(x, qkv_grad, g, heads_out, count):
    tokens, dim = x.shape
    width = heads_out.shape[1]
    block = dim // count
    out = jax.ShapeDtypeStruct((count, block // 2, 4 * width), jnp.bfloat16)
    return pl.pallas_call(
        weight_kernel,
        grid=(count,),
        out_shape=[out, out],
        in_specs=[
            pl.BlockSpec((tokens, block), lambda i: (0, i)),
            pl.BlockSpec((tokens, 3 * width), lambda i: (0, 0)),
            pl.BlockSpec((tokens, block), lambda i: (0, i)),
            pl.BlockSpec((tokens, width), lambda i: (0, 0)),
        ],
        out_specs=[pl.BlockSpec((1, block // 2, 4 * width), lambda i: (i, 0, 0))] * 2,
        compiler_params=pltpu.CompilerParams(vmem_limit_bytes=VMEM_LIMIT),
        cost_estimate=pl.CostEstimate(flops=8 * tokens * dim * width, bytes_accessed=14 << 20, transcendentals=0),
        name="weight_grads",
    )(x, qkv_grad, g, heads_out)


def place_blocks(lanes, index, outs):
    count = len(lanes[0])
    half, total = lanes[0][0].shape
    rows = len(lanes) * half
    shapes, specs = [], []
    for planes, width, kind, turned in outs:
        if turned:
            shapes.append(jax.ShapeDtypeStruct((width, rows * count), kind))
            specs.append(pl.BlockSpec((width, rows), lambda i, at: (0, i)))
        elif planes > 1:
            shapes.append(jax.ShapeDtypeStruct((planes, rows * count, width), kind))
            specs.append(pl.BlockSpec((planes, rows, width), lambda i, at: (0, i, 0)))
        else:
            shapes.append(jax.ShapeDtypeStruct((rows * count, width), kind))
            specs.append(pl.BlockSpec((rows, width), lambda i, at: (i, 0)))
    given = [held[far] for held in lanes for far in range(count)]
    return pl.pallas_call(
        functools.partial(place_kernel, count, [o[1] for o in outs], [o[3] for o in outs]),
        grid_spec=pltpu.PrefetchScalarGridSpec(
            num_scalar_prefetch=1,
            grid=(count,),
            in_specs=[pl.BlockSpec((half, total), lambda i, at: (0, 0))] * len(given),
            out_specs=specs,
        ),
        out_shape=shapes,
        compiler_params=pltpu.CompilerParams(vmem_limit_bytes=VMEM_LIMIT),
        cost_estimate=pl.CostEstimate(flops=0, bytes_accessed=12 << 20, transcendentals=0),
        name="place_blocks",
    )(index.astype(jnp.int32).reshape(1), *given)


def swap_pairs(size, bit):
    return [(i, i ^ bit) for i in range(size)]


def shift_pairs(size, shift):
    return [(i, (i - shift) % size) for i in range(size)]


def bits_of(size):
    return [1 << i for i in range(size.bit_length() - 1)]


def pick(x, index, axis=0):
    return lax.dynamic_index_in_dim(x, index, axis, keepdims=False)


def after(x, *others):
    return lax.optimization_barrier((x,) + others)[0]


def xor_gather(x, axis, size, bits):
    held = dict(x) if isinstance(x, dict) else {0: x}
    for bit in bits:
        for far in list(held):
            held[far ^ bit] = lax.ppermute(held[far], axis, swap_pairs(size, bit))
    return held


def by_index(held, index, axis=0):
    shape = held[0].shape
    out = jnp.zeros(shape[:axis] + (len(held),) + shape[axis:], held[0].dtype)
    for far, block in held.items():
        out = lax.dynamic_update_index_in_dim(out, block, index ^ far, axis)
    return out


def xor_scatter(blocks, axis_name, size, bits, steps, index, axis, all_steps=None):
    all_steps = list(all_steps or steps)
    left = sorted(all_steps[all_steps.index(steps[0]) :], reverse=True)
    blocks = blocks.reshape(blocks.shape[:axis] + (2,) * len(left) + blocks.shape[axis + 1 :])
    for bit, step in zip(bits, steps):
        at = axis + left.index(step)
        left.remove(step)
        side = (index // step) % 2
        got = lax.ppermute(narrow(pick(blocks, 1 - side, at)), axis_name, swap_pairs(size, bit))
        blocks = wide(pick(blocks, side, at)) + wide(got)
    tail = blocks.shape[axis + len(left) :]
    return blocks.reshape(blocks.shape[:axis] + ((2 ** len(left),) if left else ()) + tail)


def lane_bits(size):
    return bits_of(size), bits_of(size)[::-1]


def column_gather(lanes, size, cut=None, start=None):
    return [xor_gather(x, "dp", size, bits[start:cut]) for x, bits in zip(lanes, lane_bits(size))]


def gate_lanes(lanes, *gates):
    flat = [held[far] for held in lanes for far in held]
    flat = lax.optimization_barrier((*flat, *gates))
    flat = iter(flat)
    return [{far: next(flat) for far in held} for held in lanes]


def column_scatter(lanes, size, column, cut=None, start=None):
    return [
        xor_scatter(x, "dp", size, bits[start:cut], bits[start:cut], column, 0, bits)
        for x, bits in zip(lanes, lane_bits(size))
    ]


def all_sum(x, sizes):
    for axis, size in sizes.items():
        for bit in bits_of(size):
            x = x + lax.ppermute(x, axis, swap_pairs(size, bit))
    return x


def make_local(columns, ranks):
    def local(
        layer_input, width_choice, routed_flag, mixer_gain, mixer_router, attention_weight,
        output_weight, hidden_gain, hidden_router, up_weight, down_weight, out_grad,
    ):
        column, rank = lax.axis_index("dp"), lax.axis_index("mp")
        rows, dim = layer_input.shape
        core = rank % 2
        group = SEQ_LEN // rows
        sequences = ranks // group
        place, sequence = rank % group, rank // group
        pair_bits = [b for b in bits_of(group) if b > 1]
        own_heads = output_weight.shape[0] // HD
        cols_local = up_weight.shape[1]
        width_own = lax.dynamic_slice_in_dim(width_choice, rank * rows, rows, 0)
        routed_own = lax.dynamic_slice_in_dim(routed_flag, rank * rows, rows, 0)
        cos, sin = rope_tables(SEQ_LEN, HD)

        def place_sequence(held):
            return by_index(held, place).reshape(SEQ_LEN, -1)

        def core_sum(pairs):
            theirs = share_of(pairs, rows, 1 - core)
            got = lax.ppermute(theirs, "mp", swap_pairs(ranks, 1))
            pairs, theirs = lax.optimization_barrier((pairs, theirs))
            return wide(share_of(pairs, rows, core)) + wide(got)

        def chip_sum(blocks):
            bits = pair_bits[::-1]
            return xor_scatter(blocks, "mp", ranks, bits, [b // 2 for b in bits], place // 2, 0)

        width = own_heads * HD
        chunk_rows = dim // columns
        half_rows = chunk_rows // 2

        def in_slice(w):
            return jnp.concatenate([w[:, p] for p in range(3)], axis=1)

        lanes_in = [
            in_slice(lax.dynamic_slice_in_dim(attention_weight, column * chunk_rows + at, half_rows, 0))
            for at in (0, half_rows)
        ]
        lanes_out = [
            lax.dynamic_slice_in_dim(output_weight, column * chunk_rows + at, half_rows, 1).T
            for at in (0, half_rows)
        ]
        input_wide = wide(layer_input)
        normed_one, scaled_one, inverse_one = norm_forward(input_wide, mixer_gain)
        low_one = narrow(normed_one)
        low_one, lanes_in, lanes_out = lax.optimization_barrier((low_one, lanes_in, lanes_out))
        held = xor_gather(low_one, "mp", ranks, pair_bits)
        fetched_in, fetched_out = [
            [[lax.ppermute(x, "mp", shift_pairs(ranks, k * group)) for x in lanes] for k in range(1, sequences)]
            for lanes in (lanes_in, lanes_out)
        ]
        sequence_width = lax.dynamic_slice_in_dim(width_choice[:, 0], sequence * SEQ_LEN, SEQ_LEN, 0)
        masks = []
        for k in range(sequences):
            heads = ((rank + k * group) % ranks) * own_heads + jnp.arange(own_heads, dtype=jnp.int32)
            masks.append((heads[None, :] * 4 < (sequence_width[:, None] + 1) * H).astype(jnp.float32))
        weights_in, weights_out = [in_slice(attention_weight)], [output_weight.T]
        held, fetched_in, masks, weights_in, weights_out, cos, sin = lax.optimization_barrier(
            (held, fetched_in, masks, weights_in, weights_out, cos, sin)
        )
        inputs_one = place_sequence(xor_gather(held, "mp", ranks, [1]))
        grads_all = lax.all_gather(after(out_grad, *[x for lanes in fetched_in for x in lanes]), "mp", axis=0, tiled=True)
        steps_in = [column_gather(x, columns, cut=1) for x in fetched_in]
        gate_one, state_one = gate_forward(normed_one, mixer_router, width_own[:, 0], routed_own[:, 0])

        kept = []
        for k in range(sequences):
            mask = masks[k]
            if k:
                steps, fetched, _ = lax.optimization_barrier((steps_in[k - 1], fetched_out[k - 1], kept[0][0]))
                held = column_gather(steps, columns, start=1)
                held_out = column_gather(fetched, columns, cut=1)
                held, held_out = lax.optimization_barrier((held, held_out))
                held_out = column_gather(held_out, columns, start=1)
                weights_in += place_blocks(held, column, [(1, 3 * width, jnp.bfloat16, False)])
                weights_out += place_blocks(held_out, column, [(1, width, jnp.bfloat16, False)])
            kept.append((*attend_forward(inputs_one, weights_in[k], cos, sin, mask), mask))
        mixer_branch = chip_sum(core_sum([(x[1], w) for x, w in zip(kept, weights_out)]))
        mixer_branch, grads_all = lax.optimization_barrier((mixer_branch, grads_all))
        top_down = product(grads_all, down_weight, (1, 1))

        middle = input_wide + gate_one[:, None] * mixer_branch
        normed_two, scaled_two, inverse_two = norm_forward(middle, hidden_gain)
        gate_two, state_two = gate_forward(normed_two, hidden_router, width_own[:, 1], routed_own[:, 1])
        inputs_two = lax.all_gather(narrow(normed_two), "mp", axis=0, tiled=True)
        gates = by_index(xor_gather(gate_two.reshape(-1, 128), "mp", ranks, bits_of(ranks)), rank).reshape(-1)

        col_ids = rank * cols_local + jnp.arange(cols_local, dtype=jnp.int32)
        col_mask = (col_ids[None, :] * 4 < (width_choice[:, 1:2] + 1) * FF).astype(jnp.float32)
        inputs_two, top_down = lax.optimization_barrier((inputs_two, top_down))
        pre = product(inputs_two, up_weight, (1, 0))
        relu_act = jax.nn.relu(pre)
        hidden = narrow(relu_act * relu_act * col_mask)
        pre_grad = narrow(top_down * gates[:, None] * col_mask * 2.0 * relu_act)
        dots = jnp.sum(wide(hidden) * top_down, axis=1).reshape(-1, 128)
        share = narrow(product(pre_grad, up_weight, (1, 1)))
        share, hidden, pre_grad = lax.optimization_barrier((share, hidden, pre_grad))
        normed_grad_two = wide(lax.psum_scatter(share, "mp", scatter_dimension=0, tiled=True))
        gate_grad_two = lax.dynamic_slice_in_dim(all_sum(dots, {"mp": ranks}).reshape(-1), rank * rows, rows, 0)
        gated = narrow(gates[:, None] * wide(grads_all))
        lanes = [narrow(product(hidden, gated, (0, 0))), narrow(product(inputs_two, pre_grad, (0, 0)))]
        lanes = [x.reshape(columns, -1, x.shape[1]) for x in lanes]
        lanes = column_scatter(lanes, columns, column, cut=1)
        hidden_share = narrow(product(hidden, down_weight, (1, 0)))
        normed_grad_two, hidden_share, *lanes = lax.optimization_barrier((normed_grad_two, hidden_share, *lanes))
        lanes = [narrow(x) for x in column_scatter(lanes, columns, column, start=1)]

        router_part, router_two = gate_backward(normed_two, hidden_router, state_two, gate_grad_two)
        middle_part, gain_two = norm_backward(normed_grad_two + router_part, scaled_two, inverse_two, hidden_gain)
        middle_grad = wide(out_grad) + middle_part
        grads_one = place_sequence(
            xor_gather(narrow(gate_one[:, None] * middle_grad), "mp", ranks, pair_bits + [1])
        )
        helds = column_gather(lanes, columns, cut=1)
        grads_one, hidden_share, lanes = lax.optimization_barrier((grads_one, hidden_share, lanes))
        hidden_branch = wide(lax.psum_scatter(hidden_share, "mp", scatter_dimension=0, tiled=True))
        layer_output = narrow(middle + gate_two[:, None] * hidden_branch)

        gate_grad_one = jnp.sum(middle_grad * mixer_branch, axis=1)
        pairs, sent = [], []
        grads_now = grads_one
        for k in range(sequences)[::-1]:
            qkv, heads_out, log_total, mask = kept[k]
            qkv_grad = attend_backward(grads_now, weights_out[k], qkv, log_total, cos, sin, mask)
            if sent:
                qkv_grad, sent[-1] = lax.optimization_barrier((qkv_grad, sent[-1]))
            pairs.append((qkv_grad, weights_in[k]))
            part = weight_grads(inputs_one, qkv_grad, grads_one, heads_out, columns)
            if k:
                grads_now, part, helds = lax.optimization_barrier((grads_now, part, helds))
                sent.append(column_scatter(part, columns, column, cut=1))
        helds, sent = lax.optimization_barrier((helds, sent))
        sent = [[narrow(x) for x in column_scatter(lanes, columns, column, start=1)] for lanes in sent]
        helds = column_gather(helds, columns, start=1)
        pairs, sent, helds, _ = lax.optimization_barrier((pairs, sent, helds, part))
        there = [
            [lax.ppermute(x, "mp", shift_pairs(ranks, -k * group)) for x in lanes]
            for k, lanes in zip(range(1, sequences)[::-1], sent)
        ]
        pieces = column_scatter(part, columns, column, cut=1)
        blocks = core_sum(pairs)
        blocks, pieces, there = lax.optimization_barrier((blocks, pieces, there))
        normed_grad_one = chip_sum(blocks)
        pieces = column_scatter(pieces, columns, column, start=1)
        down_sum, = place_blocks(helds[:1], column, [(1, dim, jnp.float32, False)])
        up_sum, = place_blocks(helds[1:], column, [(1, cols_local, jnp.float32, False)])
        pieces, down_sum, up_sum = lax.optimization_barrier((pieces, down_sum, up_sum))
        for lanes in there:
            pieces = [p + wide(t) for p, t in zip(pieces, lanes)]
        spread = column_gather([narrow(p) for p in pieces], columns)
        attention_sum, output_sum = place_blocks(
            spread,
            column,
            [(3, width, jnp.float32, False), (1, width, jnp.float32, True)],
        )
        attention_sum = attention_sum.transpose(1, 0, 2)

        router_part_one, router_one = gate_backward(normed_one, mixer_router, state_one, gate_grad_one)
        input_part, gain_one = norm_backward(normed_grad_one + router_part_one, scaled_one, inverse_one, mixer_gain)
        input_grad = narrow(middle_grad + input_part)

        sizes = {"mp": ranks, "dp": columns}

        smalls = [gain_two, gain_one, router_two.T, router_one.T]
        small_sum = all_sum(jnp.concatenate([x.reshape(-1, 128) for x in smalls], axis=0), sizes)
        cuts = [dim // 128, 2 * dim // 128, (2 * dim + router_two.size) // 128]
        hidden_gain_sum, mixer_gain_sum, hidden_router_sum, mixer_router_sum = (
            x.reshape(-1, dim) for x in jnp.split(small_sum, cuts)
        )
        hidden_gain_sum, mixer_gain_sum = hidden_gain_sum[0], mixer_gain_sum[0]
        hidden_router_sum, mixer_router_sum = hidden_router_sum.T, mixer_router_sum.T
        return (
            layer_output, input_grad, mixer_gain_sum, mixer_router_sum, attention_sum, output_sum,
            hidden_gain_sum, hidden_router_sum, up_sum, down_sum,
        )

    return local


def solution(mesh):
    return jax.shard_map(
        make_local(mesh.shape["dp"], mesh.shape["mp"]),
        mesh=mesh,
        in_specs=(
            P(("dp", "mp"), None),
            P("dp", None),
            P("dp", None),
            P(),
            P(),
            P(None, None, "mp"),
            P("mp", None),
            P(),
            P(),
            P(None, "mp"),
            P("mp", None),
            P(("dp", "mp"), None),
        ),
        out_specs=(
            P(("dp", "mp"), None),
            P(("dp", "mp"), None),
            P(),
            P(),
            P(None, None, "mp"),
            P("mp", None),
            P(),
            P(),
            P(None, "mp"),
            P("mp", None),
        ),
        check_vma=False,
    )
```

```python
import functools
import math

import jax
import jax.numpy as jnp
from jax import lax
from jax.experimental import pallas as pl
from jax.experimental.pallas import tpu as pltpu
from jax.sharding import PartitionSpec as P

H = 16
HD = 128
FF = 8192
SEQ_LEN = 1024


EPSILON = 1e-05
NEG_LARGE = -1e30
HIGHEST = lax.Precision.HIGHEST


def norm_forward(values, gain_vec):
    row_mean = jnp.mean(values, axis=1, keepdims=True)
    centred = values - row_mean
    row_variance = jnp.mean(centred * centred, axis=1, keepdims=True)
    inverse_scale = lax.rsqrt(row_variance + EPSILON)
    scaled = centred * inverse_scale
    return (scaled * gain_vec[None, :], scaled, inverse_scale)


def norm_backward(normed_grad, scaled, inverse_scale, gain_vec):
    gain_grad = jnp.sum(normed_grad * scaled, axis=0)
    scaled_grad = normed_grad * gain_vec[None, :]
    first_mean = jnp.mean(scaled_grad, axis=1, keepdims=True)
    second_mean = jnp.mean(scaled_grad * scaled, axis=1, keepdims=True)
    return (inverse_scale * (scaled_grad - first_mean - scaled * second_mean), gain_grad)


def gate_forward(normed, router, width_col, routed_col):
    logits = jnp.dot(normed, router, precision=HIGHEST, preferred_element_type=jnp.float32)
    soft_probs = jax.nn.softmax(logits, axis=1)
    one_hot = (width_col[:, None] == jnp.arange(4, dtype=jnp.int32)[None, :]).astype(jnp.float32)
    chosen = jnp.sum(soft_probs * one_hot, axis=1)
    route_flags = routed_col.astype(jnp.float32)
    return (
        route_flags * 4.0 * chosen + (1.0 - route_flags),
        (soft_probs, one_hot, chosen, route_flags),
    )


def gate_backward(normed, router, gate_state, gate_grad):
    soft_probs, one_hot, chosen, route_flags = gate_state
    coefficient = route_flags * 4.0 * chosen * gate_grad
    logit_grad = coefficient[:, None] * (one_hot - soft_probs)
    router_grad = lax.dot_general(
        normed,
        logit_grad,
        (((0,), (0,)), ((), ())),
        precision=HIGHEST,
        preferred_element_type=jnp.float32,
    )
    normed_grad = lax.dot_general(
        logit_grad,
        router,
        (((1,), (1,)), ((), ())),
        precision=HIGHEST,
        preferred_element_type=jnp.float32,
    )
    return (normed_grad, router_grad)


Q_BLOCK = 256


def rope_tables(token_count, head_width):
    positions = jnp.arange(token_count, dtype=jnp.float32)
    frequency = jnp.exp(
        jnp.arange(head_width // 2, dtype=jnp.float32) * (-2.0 * math.log(10000.0) / head_width)
    )
    angles = positions[:, None] * frequency[None, :]
    cosine, sine = jnp.cos(angles), jnp.sin(angles)
    return jnp.concatenate([cosine, cosine], axis=1), jnp.concatenate([-sine, sine], axis=1)


def wide(x):
    return x.astype(jnp.float32)


def narrow(x):
    return x.astype(jnp.bfloat16)


def product(a, b, dims):
    return lax.dot_general(a, b, ((dims[:1], dims[1:]), ((), ())), preferred_element_type=jnp.float32)


def block_scores(queries, keys_all, start):
    scores = product(queries, keys_all, (1, 1)) * (1.0 / math.sqrt(HD))
    row = lax.broadcasted_iota(jnp.int32, scores.shape, 0) + start
    col = lax.broadcasted_iota(jnp.int32, scores.shape, 1)
    return jnp.where(col <= row, scores, NEG_LARGE)


def forward_kernel(x_ref, w_ref, cos_ref, sin_ref, mask_ref, qkv_ref, heads_ref, log_ref):
    tokens, heads = x_ref.shape[0], mask_ref.shape[1]
    width = heads * HD
    block = min(Q_BLOCK, tokens)
    for start in range(0, tokens, block):
        here, end = slice(start, start + block), start + block
        x = x_ref[here, :]
        cos, sin = cos_ref[here, :], sin_ref[here, :]
        for part in range(3):
            rows = product(x, w_ref[:, part * width : (part + 1) * width], (1, 0))
            for head in range(heads):
                value = rows[:, head * HD : (head + 1) * HD]
                if part < 2:
                    value = value * cos + pltpu.roll(value, HD // 2, 1) * sin
                at = part * width + head * HD
                qkv_ref[here, at : at + HD] = narrow(value)
        for head in range(heads):
            at = head * HD
            lanes, key_lanes, value_lanes = (slice(at + p * width, at + p * width + HD) for p in range(3))
            scores = block_scores(qkv_ref[here, lanes], qkv_ref[:end, key_lanes], start)
            row_max = jnp.max(scores, axis=1, keepdims=True)
            shifted = jnp.exp(scores - row_max)
            total = jnp.sum(shifted, axis=1, keepdims=True)
            mix = product(narrow(shifted * (1.0 / total)), qkv_ref[:end, value_lanes], (1, 0))
            heads_ref[here, lanes] = narrow(mix * mask_ref[here, head : head + 1])
            log_ref[here, head : head + 1] = row_max + jnp.log(total)


def backward_kernel(g_ref, w_ref, qkv_ref, log_ref, cos_ref, sin_ref, mask_ref, out_ref, keys_acc, values_acc):
    tokens, heads = g_ref.shape[0], mask_ref.shape[1]
    width = heads * HD
    block = min(Q_BLOCK, tokens)
    scale = 1.0 / math.sqrt(HD)
    for start in range(0, tokens, block):
        here, end = slice(start, start + block), start + block
        cos, sin = cos_ref[here, :], sin_ref[here, :]
        rows = narrow(product(g_ref[here, :], w_ref[...], (1, 0)))
        for head in range(heads):
            at = head * HD
            lanes, key_lanes, value_lanes = (slice(at + p * width, at + p * width + HD) for p in range(3))
            heads_grad = rows[:, lanes] * narrow(mask_ref[here, head : head + 1])
            queries, keys_all = qkv_ref[here, lanes], qkv_ref[:end, key_lanes]
            scores = block_scores(queries, keys_all, start)
            probs = jnp.exp(scores - log_ref[here, head : head + 1])
            values_part = product(narrow(probs), heads_grad, (0, 0))
            probs_grad = product(heads_grad, qkv_ref[:end, value_lanes], (1, 1))
            centre = jnp.sum(probs * probs_grad, axis=1, keepdims=True)
            score_grad = narrow(probs * (probs_grad - centre))
            queries_grad = product(score_grad, keys_all, (1, 0)) * scale
            keys_part = product(score_grad, queries, (0, 0)) * scale
            turned = queries_grad * cos - pltpu.roll(queries_grad, HD // 2, 1) * sin
            out_ref[here, lanes] = narrow(turned)
            if start:
                values_acc[:start, lanes] += values_part[:start]
                keys_acc[:start, lanes] += keys_part[:start]
            values_acc[here, lanes] = values_part[start:]
            keys_acc[here, lanes] = keys_part[start:]
    for start in range(0, tokens, block):
        here = slice(start, start + block)
        cos, sin = cos_ref[here, :], sin_ref[here, :]
        out_ref[here, 2 * width :] = narrow(values_acc[here, :])
        for head in range(heads):
            at = head * HD
            value = keys_acc[here, at : at + HD]
            out_ref[here, width + at : width + at + HD] = narrow(value * cos - pltpu.roll(value, HD // 2, 1) * sin)


def share_kernel(side_ref, *refs):
    *given, out_ref = refs
    total = product(given[0][...], given[1][...], (1, 1))
    for a_ref, w_ref in zip(given[2::2], given[3::2]):
        total = total + product(a_ref[...], w_ref[...], (1, 1))
    out_ref[0] = narrow(total)


def weight_kernel(x_ref, q_ref, g_ref, h_ref, *outs):
    width = h_ref.shape[1]
    half = x_ref.shape[1] // 2
    for lane, out_ref in enumerate(outs):
        here = slice(lane * half, (lane + 1) * half)
        out_ref[0, :, : 3 * width] = narrow(product(x_ref[:, here], q_ref[...], (0, 0)))
        out_ref[0, :, 3 * width :] = narrow(product(g_ref[:, here], h_ref[...], (0, 0)))


def place_kernel(count, widths, turned, at_ref, *refs):
    lanes = (len(refs) - len(widths)) // count
    blocks, outs = refs[: lanes * count], refs[lanes * count :]
    half = blocks[0].shape[0]
    for far in range(count):

        @pl.when((pl.program_id(0) ^ at_ref[0]) == far)
        def _():
            for lane in range(lanes):
                here = slice(lane * half, (lane + 1) * half)
                block = blocks[lane * count + far]
                start = 0
                for out_ref, width, turn in zip(outs, widths, turned):
                    for part in range(out_ref.shape[0] if len(out_ref.shape) == 3 else 1):
                        value = block[:, start : start + width].astype(out_ref.dtype)
                        start += width
                        if turn:
                            out_ref[:, here] = value.T
                        elif len(out_ref.shape) == 3:
                            out_ref[part, here, :] = value
                        else:
                            out_ref[here, :] = value


def widen_kernel(both_ref, down_ref, up_ref):
    rows, width = down_ref.shape[0], up_ref.shape[1]
    down_ref[...] = both_ref[0, :rows].astype(down_ref.dtype)
    low = both_ref.shape[1] - rows
    for group in range(up_ref.shape[0] // low):
        value = both_ref[0, rows:, group * width : (group + 1) * width]
        up_ref[group * low : (group + 1) * low] = value.astype(up_ref.dtype)


VMEM_LIMIT = 56 * 1024 * 1024


def whole_specs(count):
    return [pl.BlockSpec(memory_space=pltpu.VMEM)] * count


def attend_forward(x, w, cos, sin, mask):
    tokens, heads = mask.shape
    dim, width = w.shape[0], heads * HD
    return pl.pallas_call(
        forward_kernel,
        out_shape=[
            jax.ShapeDtypeStruct((tokens, 3 * width), jnp.bfloat16),
            jax.ShapeDtypeStruct((tokens, width), jnp.bfloat16),
            jax.ShapeDtypeStruct((tokens, heads), jnp.float32),
        ],
        in_specs=whole_specs(5),
        out_specs=whole_specs(3),
        compiler_params=pltpu.CompilerParams(vmem_limit_bytes=VMEM_LIMIT),
        cost_estimate=pl.CostEstimate(
            flops=6 * tokens * dim * width + 2 * tokens * tokens * width,
            bytes_accessed=12 << 20,
            transcendentals=tokens * tokens * heads // 2,
        ),
        name="attend_forward",
    )(x, w, cos, sin, mask)


def attend_backward(g, w, qkv, log_total, cos, sin, mask):
    tokens, heads = mask.shape
    dim, width = w.shape[0], heads * HD
    return pl.pallas_call(
        backward_kernel,
        out_shape=jax.ShapeDtypeStruct((tokens, 3 * width), jnp.bfloat16),
        in_specs=whole_specs(7),
        out_specs=whole_specs(1)[0],
        scratch_shapes=[pltpu.VMEM((tokens, width), jnp.float32)] * 2,
        compiler_params=pltpu.CompilerParams(vmem_limit_bytes=VMEM_LIMIT),
        cost_estimate=pl.CostEstimate(
            flops=2 * tokens * dim * width + 5 * tokens * tokens * width,
            bytes_accessed=12 << 20,
            transcendentals=tokens * tokens * heads // 2,
        ),
        name="attend_backward",
    )(g, w, qkv, log_total, cos, sin, mask)


def share_of(pairs, rows, side):
    tokens, depth = pairs[0][0].shape
    dim = pairs[0][1].shape[0]
    chips = tokens // rows // 2
    specs = [
        pl.BlockSpec((rows, depth), lambda i, side: (2 * i + side[0], 0)),
        pl.BlockSpec((dim, depth), lambda i, side: (0, 0)),
    ] * len(pairs)
    return pl.pallas_call(
        share_kernel,
        grid_spec=pltpu.PrefetchScalarGridSpec(
            num_scalar_prefetch=1,
            grid=(chips,),
            in_specs=specs,
            out_specs=pl.BlockSpec((1, rows, dim), lambda i, side: (i, 0, 0)),
        ),
        out_shape=jax.ShapeDtypeStruct((chips, rows, dim), jnp.bfloat16),
        compiler_params=pltpu.CompilerParams(vmem_limit_bytes=VMEM_LIMIT),
        cost_estimate=pl.CostEstimate(
            flops=tokens * dim * depth * len(pairs), bytes_accessed=12 << 20, transcendentals=0
        ),
        name="share_of",
    )(side.astype(jnp.int32).reshape(1), *[x for pair in pairs for x in pair])


def widen(both, down_rows, up_width):
    count, rows, dim = both.shape
    up_rows = (rows - down_rows) * dim // up_width
    return pl.pallas_call(
        widen_kernel,
        grid=(count,),
        out_shape=[
            jax.ShapeDtypeStruct((count * down_rows, dim), jnp.float32),
            jax.ShapeDtypeStruct((count * up_rows, up_width), jnp.float32),
        ],
        in_specs=[pl.BlockSpec((1, rows, dim), lambda i: (i, 0, 0))],
        out_specs=[
            pl.BlockSpec((down_rows, dim), lambda i: (i, 0)),
            pl.BlockSpec((up_rows, up_width), lambda i: (i, 0)),
        ],
        compiler_params=pltpu.CompilerParams(vmem_limit_bytes=VMEM_LIMIT),
        cost_estimate=pl.CostEstimate(flops=0, bytes_accessed=24 << 20, transcendentals=0),
        name="widen",
    )(both)


def weight_grads(x, qkv_grad, g, heads_out, count):
    tokens, dim = x.shape
    width = heads_out.shape[1]
    block = dim // count
    out = jax.ShapeDtypeStruct((count, block // 2, 4 * width), jnp.bfloat16)
    return pl.pallas_call(
        weight_kernel,
        grid=(count,),
        out_shape=[out, out],
        in_specs=[
            pl.BlockSpec((tokens, block), lambda i: (0, i)),
            pl.BlockSpec((tokens, 3 * width), lambda i: (0, 0)),
            pl.BlockSpec((tokens, block), lambda i: (0, i)),
            pl.BlockSpec((tokens, width), lambda i: (0, 0)),
        ],
        out_specs=[pl.BlockSpec((1, block // 2, 4 * width), lambda i: (i, 0, 0))] * 2,
        compiler_params=pltpu.CompilerParams(vmem_limit_bytes=VMEM_LIMIT),
        cost_estimate=pl.CostEstimate(flops=8 * tokens * dim * width, bytes_accessed=14 << 20, transcendentals=0),
        name="weight_grads",
    )(x, qkv_grad, g, heads_out)


def place_blocks(lanes, index, outs):
    count = len(lanes[0])
    half, total = lanes[0][0].shape
    rows = len(lanes) * half
    shapes, specs = [], []
    for planes, width, kind, turned in outs:
        if turned:
            shapes.append(jax.ShapeDtypeStruct((width, rows * count), kind))
            specs.append(pl.BlockSpec((width, rows), lambda i, at: (0, i)))
        elif planes > 1:
            shapes.append(jax.ShapeDtypeStruct((planes, rows * count, width), kind))
            specs.append(pl.BlockSpec((planes, rows, width), lambda i, at: (0, i, 0)))
        else:
            shapes.append(jax.ShapeDtypeStruct((rows * count, width), kind))
            specs.append(pl.BlockSpec((rows, width), lambda i, at: (i, 0)))
    given = [held[far] for held in lanes for far in range(count)]
    return pl.pallas_call(
        functools.partial(place_kernel, count, [o[1] for o in outs], [o[3] for o in outs]),
        grid_spec=pltpu.PrefetchScalarGridSpec(
            num_scalar_prefetch=1,
            grid=(count,),
            in_specs=[pl.BlockSpec((half, total), lambda i, at: (0, 0))] * len(given),
            out_specs=specs,
        ),
        out_shape=shapes,
        compiler_params=pltpu.CompilerParams(vmem_limit_bytes=VMEM_LIMIT),
        cost_estimate=pl.CostEstimate(flops=0, bytes_accessed=12 << 20, transcendentals=0),
        name="place_blocks",
    )(index.astype(jnp.int32).reshape(1), *given)


def swap_pairs(size, bit):
    return [(i, i ^ bit) for i in range(size)]


def shift_pairs(size, shift):
    return [(i, (i - shift) % size) for i in range(size)]


def bits_of(size):
    return [1 << i for i in range(size.bit_length() - 1)]


def pick(x, index, axis=0):
    return lax.dynamic_index_in_dim(x, index, axis, keepdims=False)


def after(x, *others):
    return lax.optimization_barrier((x,) + others)[0]


def xor_gather(x, axis, size, bits):
    held = dict(x) if isinstance(x, dict) else {0: x}
    for bit in bits:
        for far in list(held):
            held[far ^ bit] = lax.ppermute(held[far], axis, swap_pairs(size, bit))
    return held


def by_index(held, index, axis=0):
    shape = held[0].shape
    out = jnp.zeros(shape[:axis] + (len(held),) + shape[axis:], held[0].dtype)
    for far, block in held.items():
        out = lax.dynamic_update_index_in_dim(out, block, index ^ far, axis)
    return out


def xor_scatter(blocks, axis_name, size, bits, steps, index, axis, all_steps=None):
    all_steps = list(all_steps or steps)
    left = sorted(all_steps[all_steps.index(steps[0]) :], reverse=True)
    blocks = blocks.reshape(blocks.shape[:axis] + (2,) * len(left) + blocks.shape[axis + 1 :])
    for bit, step in zip(bits, steps):
        at = axis + left.index(step)
        left.remove(step)
        side = (index // step) % 2
        got = lax.ppermute(narrow(pick(blocks, 1 - side, at)), axis_name, swap_pairs(size, bit))
        blocks = wide(pick(blocks, side, at)) + wide(got)
    tail = blocks.shape[axis + len(left) :]
    return blocks.reshape(blocks.shape[:axis] + ((2 ** len(left),) if left else ()) + tail)


def lane_bits(size):
    return bits_of(size), bits_of(size)[::-1]


def column_gather(lanes, size, cut=None, start=None):
    return [xor_gather(x, "dp", size, bits[start:cut]) for x, bits in zip(lanes, lane_bits(size))]


def gate_lanes(lanes, *gates):
    flat = [held[far] for held in lanes for far in held]
    flat = lax.optimization_barrier((*flat, *gates))
    flat = iter(flat)
    return [{far: next(flat) for far in held} for held in lanes]


def column_scatter(lanes, size, column, cut=None, start=None):
    return [
        xor_scatter(x, "dp", size, bits[start:cut], bits[start:cut], column, 0, bits)
        for x, bits in zip(lanes, lane_bits(size))
    ]


def all_sum(x, sizes):
    for axis, size in sizes.items():
        for bit in bits_of(size):
            x = x + lax.ppermute(x, axis, swap_pairs(size, bit))
    return x


def make_local(columns, ranks):
    def local(
        layer_input, width_choice, routed_flag, mixer_gain, mixer_router, attention_weight,
        output_weight, hidden_gain, hidden_router, up_weight, down_weight, out_grad,
    ):
        column, rank = lax.axis_index("dp"), lax.axis_index("mp")
        rows, dim = layer_input.shape
        core = rank % 2
        group = SEQ_LEN // rows
        sequences = ranks // group
        place, sequence = rank % group, rank // group
        pair_bits = [b for b in bits_of(group) if b > 1]
        own_heads = output_weight.shape[0] // HD
        cols_local = up_weight.shape[1]
        width_own = lax.dynamic_slice_in_dim(width_choice, rank * rows, rows, 0)
        routed_own = lax.dynamic_slice_in_dim(routed_flag, rank * rows, rows, 0)
        cos, sin = rope_tables(SEQ_LEN, HD)

        def place_sequence(held):
            return by_index(held, place).reshape(SEQ_LEN, -1)

        def core_sum(pairs):
            theirs = share_of(pairs, rows, 1 - core)
            got = lax.ppermute(theirs, "mp", swap_pairs(ranks, 1))
            pairs, theirs = lax.optimization_barrier((pairs, theirs))
            return wide(share_of(pairs, rows, core)) + wide(got)

        def chip_sum(blocks):
            bits = pair_bits[::-1]
            return xor_scatter(blocks, "mp", ranks, bits, [b // 2 for b in bits], place // 2, 0)

        width = own_heads * HD
        chunk_rows = dim // columns
        half_rows = chunk_rows // 2

        def in_slice(w):
            return jnp.concatenate([w[:, p] for p in range(3)], axis=1)

        lanes_in = [
            in_slice(lax.dynamic_slice_in_dim(attention_weight, column * chunk_rows + at, half_rows, 0))
            for at in (0, half_rows)
        ]
        lanes_out = [
            lax.dynamic_slice_in_dim(output_weight, column * chunk_rows + at, half_rows, 1).T
            for at in (0, half_rows)
        ]
        input_wide = wide(layer_input)
        normed_one, scaled_one, inverse_one = norm_forward(input_wide, mixer_gain)
        low_one = narrow(normed_one)
        low_one, lanes_in, lanes_out = lax.optimization_barrier((low_one, lanes_in, lanes_out))
        held = xor_gather(low_one, "mp", ranks, pair_bits)
        fetched_in, fetched_out = [
            [[lax.ppermute(x, "mp", shift_pairs(ranks, k * group)) for x in lanes] for k in range(1, sequences)]
            for lanes in (lanes_in, lanes_out)
        ]
        sequence_width = lax.dynamic_slice_in_dim(width_choice[:, 0], sequence * SEQ_LEN, SEQ_LEN, 0)
        masks = []
        for k in range(sequences):
            heads = ((rank + k * group) % ranks) * own_heads + jnp.arange(own_heads, dtype=jnp.int32)
            masks.append((heads[None, :] * 4 < (sequence_width[:, None] + 1) * H).astype(jnp.float32))
        weights_in, weights_out = [in_slice(attention_weight)], [output_weight.T]
        held, fetched_in, masks, weights_in, weights_out, cos, sin = lax.optimization_barrier(
            (held, fetched_in, masks, weights_in, weights_out, cos, sin)
        )
        inputs_one = place_sequence(xor_gather(held, "mp", ranks, [1]))
        grads_all = lax.all_gather(after(out_grad, *[x for lanes in fetched_in for x in lanes]), "mp", axis=0, tiled=True)
        steps_in = [column_gather(x, columns, cut=1) for x in fetched_in]
        gate_one, state_one = gate_forward(normed_one, mixer_router, width_own[:, 0], routed_own[:, 0])

        kept = []
        for k in range(sequences):
            mask = masks[k]
            if k:
                steps, fetched, _ = lax.optimization_barrier((steps_in[k - 1], fetched_out[k - 1], kept[0][0]))
                held = column_gather(steps, columns, start=1)
                held_out = column_gather(fetched, columns, cut=1)
                held, held_out = lax.optimization_barrier((held, held_out))
                held_out = column_gather(held_out, columns, start=1)
                weights_in += place_blocks(held, column, [(1, 3 * width, jnp.bfloat16, False)])
                weights_out += place_blocks(held_out, column, [(1, width, jnp.bfloat16, False)])
            kept.append((*attend_forward(inputs_one, weights_in[k], cos, sin, mask), mask))
        mixer_branch = chip_sum(core_sum([(x[1], w) for x, w in zip(kept, weights_out)]))
        mixer_branch, grads_all = lax.optimization_barrier((mixer_branch, grads_all))
        top_down = product(grads_all, down_weight, (1, 1))

        middle = input_wide + gate_one[:, None] * mixer_branch
        normed_two, scaled_two, inverse_two = norm_forward(middle, hidden_gain)
        gate_two, state_two = gate_forward(normed_two, hidden_router, width_own[:, 1], routed_own[:, 1])
        inputs_two = lax.all_gather(narrow(normed_two), "mp", axis=0, tiled=True)
        gates = by_index(xor_gather(gate_two.reshape(-1, 128), "mp", ranks, bits_of(ranks)), rank).reshape(-1)

        col_ids = rank * cols_local + jnp.arange(cols_local, dtype=jnp.int32)
        col_mask = (col_ids[None, :] * 4 < (width_choice[:, 1:2] + 1) * FF).astype(jnp.float32)
        inputs_two, top_down = lax.optimization_barrier((inputs_two, top_down))
        pre = product(inputs_two, up_weight, (1, 0))
        relu_act = jax.nn.relu(pre)
        hidden = narrow(relu_act * relu_act * col_mask)
        pre_grad = narrow(top_down * gates[:, None] * col_mask * 2.0 * relu_act)
        dots = jnp.sum(wide(hidden) * top_down, axis=1).reshape(-1, 128)
        share = narrow(product(pre_grad, up_weight, (1, 1)))
        share, hidden, pre_grad = lax.optimization_barrier((share, hidden, pre_grad))
        normed_grad_two = wide(lax.psum_scatter(share, "mp", scatter_dimension=0, tiled=True))
        gate_grad_two = lax.dynamic_slice_in_dim(all_sum(dots, {"mp": ranks}).reshape(-1), rank * rows, rows, 0)
        gated = narrow(gates[:, None] * wide(grads_all))
        lanes = [narrow(product(hidden, gated, (0, 0))), narrow(product(inputs_two, pre_grad, (0, 0)))]
        lanes = [x.reshape(columns, -1, x.shape[1]) for x in lanes]
        lanes = column_scatter(lanes, columns, column, cut=1)
        hidden_share = narrow(product(hidden, down_weight, (1, 0)))
        normed_grad_two, hidden_share, *lanes = lax.optimization_barrier((normed_grad_two, hidden_share, *lanes))
        lanes = [narrow(x) for x in column_scatter(lanes, columns, column, start=1)]

        router_part, router_two = gate_backward(normed_two, hidden_router, state_two, gate_grad_two)
        middle_part, gain_two = norm_backward(normed_grad_two + router_part, scaled_two, inverse_two, hidden_gain)
        middle_grad = wide(out_grad) + middle_part
        grads_one = place_sequence(
            xor_gather(narrow(gate_one[:, None] * middle_grad), "mp", ranks, pair_bits + [1])
        )
        grads_one, hidden_share, lanes = lax.optimization_barrier((grads_one, hidden_share, lanes))
        down_piece, up_piece = lanes
        groups = dim // cols_local
        up_wide = jnp.concatenate(jnp.split(up_piece, groups, axis=0), axis=1)
        both = lax.all_gather(jnp.concatenate([down_piece, up_wide], axis=0), "dp", axis=0)
        down_sum, up_sum = widen(both, down_piece.shape[0], cols_local)

        gate_grad_one = jnp.sum(middle_grad * mixer_branch, axis=1)
        pairs, sent = [], []
        grads_now = grads_one
        for k in range(sequences)[::-1]:
            qkv, heads_out, log_total, mask = kept[k]
            qkv_grad = attend_backward(grads_now, weights_out[k], qkv, log_total, cos, sin, mask)
            if sent:
                qkv_grad, sent[-1] = lax.optimization_barrier((qkv_grad, sent[-1]))
            pairs.append((qkv_grad, weights_in[k]))
            part = weight_grads(inputs_one, qkv_grad, grads_one, heads_out, columns)
            if k:
                grads_now, part = lax.optimization_barrier((grads_now, part))
                hidden_share = after(hidden_share, *part)
                sent.append(column_scatter(part, columns, column, cut=1))
        sent = [[narrow(x) for x in column_scatter(lanes, columns, column, start=1)] for lanes in sent]
        pairs, sent, part = lax.optimization_barrier((pairs, sent, part))
        there = [
            [lax.ppermute(x, "mp", shift_pairs(ranks, -k * group)) for x in lanes]
            for k, lanes in zip(range(1, sequences)[::-1], sent)
        ]
        normed_grad_one = chip_sum(core_sum(pairs))
        pieces = column_scatter(part, columns, column)
        for lanes in there:
            pieces = [p + wide(t) for p, t in zip(pieces, lanes)]
        spread = column_gather([narrow(p) for p in pieces], columns, cut=1)
        spread, down_sum, up_sum = lax.optimization_barrier((spread, down_sum, up_sum))
        spread = column_gather(spread, columns, start=1)
        hidden_branch = wide(lax.psum_scatter(hidden_share, "mp", scatter_dimension=0, tiled=True))
        layer_output = narrow(middle + gate_two[:, None] * hidden_branch)
        attention_sum, output_sum = place_blocks(
            spread,
            column,
            [(3, width, jnp.float32, False), (1, width, jnp.float32, True)],
        )
        attention_sum = attention_sum.transpose(1, 0, 2)

        router_part_one, router_one = gate_backward(normed_one, mixer_router, state_one, gate_grad_one)
        input_part, gain_one = norm_backward(normed_grad_one + router_part_one, scaled_one, inverse_one, mixer_gain)
        input_grad = narrow(middle_grad + input_part)

        sizes = {"mp": ranks, "dp": columns}

        smalls = [gain_two, gain_one, router_two.T, router_one.T]
        small_sum = all_sum(jnp.concatenate([x.reshape(-1, 128) for x in smalls], axis=0), sizes)
        cuts = [dim // 128, 2 * dim // 128, (2 * dim + router_two.size) // 128]
        hidden_gain_sum, mixer_gain_sum, hidden_router_sum, mixer_router_sum = (
            x.reshape(-1, dim) for x in jnp.split(small_sum, cuts)
        )
        hidden_gain_sum, mixer_gain_sum = hidden_gain_sum[0], mixer_gain_sum[0]
        hidden_router_sum, mixer_router_sum = hidden_router_sum.T, mixer_router_sum.T
        return (
            layer_output, input_grad, mixer_gain_sum, mixer_router_sum, attention_sum, output_sum,
            hidden_gain_sum, hidden_router_sum, up_sum, down_sum,
        )

    return local


def solution(mesh):
    return jax.shard_map(
        make_local(mesh.shape["dp"], mesh.shape["mp"]),
        mesh=mesh,
        in_specs=(
            P(("dp", "mp"), None),
            P("dp", None),
            P("dp", None),
            P(),
            P(),
            P(None, None, "mp"),
            P("mp", None),
            P(),
            P(),
            P(None, "mp"),
            P("mp", None),
            P(("dp", "mp"), None),
        ),
        out_specs=(
            P(("dp", "mp"), None),
            P(("dp", "mp"), None),
            P(),
            P(),
            P(None, None, "mp"),
            P("mp", None),
            P(),
            P(),
            P(None, "mp"),
            P("mp", None),
        ),
        check_vma=False,
    )
```

```python
import functools
import math

import jax
import jax.numpy as jnp
from jax import lax
from jax.experimental import pallas as pl
from jax.experimental.pallas import tpu as pltpu
from jax.sharding import PartitionSpec as P

H = 16
HD = 128
FF = 8192
SEQ_LEN = 1024


EPSILON = 1e-05
NEG_LARGE = -1e30
HIGHEST = lax.Precision.HIGHEST


def norm_forward(values, gain_vec):
    row_mean = jnp.mean(values, axis=1, keepdims=True)
    centred = values - row_mean
    row_variance = jnp.mean(centred * centred, axis=1, keepdims=True)
    inverse_scale = lax.rsqrt(row_variance + EPSILON)
    scaled = centred * inverse_scale
    return (scaled * gain_vec[None, :], scaled, inverse_scale)


def norm_backward(normed_grad, scaled, inverse_scale, gain_vec):
    gain_grad = jnp.sum(normed_grad * scaled, axis=0)
    scaled_grad = normed_grad * gain_vec[None, :]
    first_mean = jnp.mean(scaled_grad, axis=1, keepdims=True)
    second_mean = jnp.mean(scaled_grad * scaled, axis=1, keepdims=True)
    return (inverse_scale * (scaled_grad - first_mean - scaled * second_mean), gain_grad)


def gate_forward(normed, router, width_col, routed_col):
    logits = jnp.dot(normed, router, precision=HIGHEST, preferred_element_type=jnp.float32)
    soft_probs = jax.nn.softmax(logits, axis=1)
    one_hot = (width_col[:, None] == jnp.arange(4, dtype=jnp.int32)[None, :]).astype(jnp.float32)
    chosen = jnp.sum(soft_probs * one_hot, axis=1)
    route_flags = routed_col.astype(jnp.float32)
    return (
        route_flags * 4.0 * chosen + (1.0 - route_flags),
        (soft_probs, one_hot, chosen, route_flags),
    )


def gate_backward(normed, router, gate_state, gate_grad):
    soft_probs, one_hot, chosen, route_flags = gate_state
    coefficient = route_flags * 4.0 * chosen * gate_grad
    logit_grad = coefficient[:, None] * (one_hot - soft_probs)
    router_grad = lax.dot_general(
        normed,
        logit_grad,
        (((0,), (0,)), ((), ())),
        precision=HIGHEST,
        preferred_element_type=jnp.float32,
    )
    normed_grad = lax.dot_general(
        logit_grad,
        router,
        (((1,), (1,)), ((), ())),
        precision=HIGHEST,
        preferred_element_type=jnp.float32,
    )
    return (normed_grad, router_grad)


Q_BLOCK = 256


def rope_tables(token_count, head_width):
    positions = jnp.arange(token_count, dtype=jnp.float32)
    frequency = jnp.exp(
        jnp.arange(head_width // 2, dtype=jnp.float32) * (-2.0 * math.log(10000.0) / head_width)
    )
    angles = positions[:, None] * frequency[None, :]
    cosine, sine = jnp.cos(angles), jnp.sin(angles)
    return jnp.concatenate([cosine, cosine], axis=1), jnp.concatenate([-sine, sine], axis=1)


def wide(x):
    return x.astype(jnp.float32)


def narrow(x):
    return x.astype(jnp.bfloat16)


def product(a, b, dims):
    return lax.dot_general(a, b, ((dims[:1], dims[1:]), ((), ())), preferred_element_type=jnp.float32)


def block_scores(queries, keys_all, start):
    scores = product(queries, keys_all, (1, 1)) * (1.0 / math.sqrt(HD))
    row = lax.broadcasted_iota(jnp.int32, scores.shape, 0) + start
    col = lax.broadcasted_iota(jnp.int32, scores.shape, 1)
    return jnp.where(col <= row, scores, NEG_LARGE)


def forward_kernel(x_ref, w_ref, cos_ref, sin_ref, mask_ref, qkv_ref, heads_ref, log_ref):
    tokens, heads = x_ref.shape[0], mask_ref.shape[1]
    width = heads * HD
    block = min(Q_BLOCK, tokens)
    for start in range(0, tokens, block):
        here, end = slice(start, start + block), start + block
        x = x_ref[here, :]
        cos, sin = cos_ref[here, :], sin_ref[here, :]
        for part in range(3):
            rows = product(x, w_ref[:, part * width : (part + 1) * width], (1, 0))
            for head in range(heads):
                value = rows[:, head * HD : (head + 1) * HD]
                if part < 2:
                    value = value * cos + pltpu.roll(value, HD // 2, 1) * sin
                at = part * width + head * HD
                qkv_ref[here, at : at + HD] = narrow(value)
        for head in range(heads):
            at = head * HD
            lanes, key_lanes, value_lanes = (slice(at + p * width, at + p * width + HD) for p in range(3))
            scores = block_scores(qkv_ref[here, lanes], qkv_ref[:end, key_lanes], start)
            row_max = jnp.max(scores, axis=1, keepdims=True)
            shifted = jnp.exp(scores - row_max)
            total = jnp.sum(shifted, axis=1, keepdims=True)
            mix = product(narrow(shifted * (1.0 / total)), qkv_ref[:end, value_lanes], (1, 0))
            heads_ref[here, lanes] = narrow(mix * mask_ref[here, head : head + 1])
            log_ref[here, head : head + 1] = row_max + jnp.log(total)


def backward_kernel(g_ref, w_ref, qkv_ref, log_ref, cos_ref, sin_ref, mask_ref, out_ref, keys_acc, values_acc):
    tokens, heads = g_ref.shape[0], mask_ref.shape[1]
    width = heads * HD
    block = min(Q_BLOCK, tokens)
    scale = 1.0 / math.sqrt(HD)
    for start in range(0, tokens, block):
        here, end = slice(start, start + block), start + block
        cos, sin = cos_ref[here, :], sin_ref[here, :]
        rows = narrow(product(g_ref[here, :], w_ref[...], (1, 0)))
        for head in range(heads):
            at = head * HD
            lanes, key_lanes, value_lanes = (slice(at + p * width, at + p * width + HD) for p in range(3))
            heads_grad = rows[:, lanes] * narrow(mask_ref[here, head : head + 1])
            queries, keys_all = qkv_ref[here, lanes], qkv_ref[:end, key_lanes]
            scores = block_scores(queries, keys_all, start)
            probs = jnp.exp(scores - log_ref[here, head : head + 1])
            values_part = product(narrow(probs), heads_grad, (0, 0))
            probs_grad = product(heads_grad, qkv_ref[:end, value_lanes], (1, 1))
            centre = jnp.sum(probs * probs_grad, axis=1, keepdims=True)
            score_grad = narrow(probs * (probs_grad - centre))
            queries_grad = product(score_grad, keys_all, (1, 0)) * scale
            keys_part = product(score_grad, queries, (0, 0)) * scale
            turned = queries_grad * cos - pltpu.roll(queries_grad, HD // 2, 1) * sin
            out_ref[here, lanes] = narrow(turned)
            if start:
                values_acc[:start, lanes] += values_part[:start]
                keys_acc[:start, lanes] += keys_part[:start]
            values_acc[here, lanes] = values_part[start:]
            keys_acc[here, lanes] = keys_part[start:]
    for start in range(0, tokens, block):
        here = slice(start, start + block)
        cos, sin = cos_ref[here, :], sin_ref[here, :]
        out_ref[here, 2 * width :] = narrow(values_acc[here, :])
        for head in range(heads):
            at = head * HD
            value = keys_acc[here, at : at + HD]
            out_ref[here, width + at : width + at + HD] = narrow(value * cos - pltpu.roll(value, HD // 2, 1) * sin)


def share_kernel(side_ref, *refs):
    *given, out_ref = refs
    total = product(given[0][...], given[1][...], (1, 1))
    for a_ref, w_ref in zip(given[2::2], given[3::2]):
        total = total + product(a_ref[...], w_ref[...], (1, 1))
    out_ref[0] = narrow(total)


def weight_kernel(x_ref, q_ref, g_ref, h_ref, *outs):
    width = h_ref.shape[1]
    half = x_ref.shape[1] // 2
    for lane, out_ref in enumerate(outs):
        here = slice(lane * half, (lane + 1) * half)
        out_ref[0, :, : 3 * width] = narrow(product(x_ref[:, here], q_ref[...], (0, 0)))
        out_ref[0, :, 3 * width :] = narrow(product(g_ref[:, here], h_ref[...], (0, 0)))


def place_kernel(count, widths, turned, at_ref, *refs):
    lanes = (len(refs) - len(widths)) // count
    blocks, outs = refs[: lanes * count], refs[lanes * count :]
    half = blocks[0].shape[0]
    for far in range(count):

        @pl.when((pl.program_id(0) ^ at_ref[0]) == far)
        def _():
            for lane in range(lanes):
                here = slice(lane * half, (lane + 1) * half)
                block = blocks[lane * count + far]
                start = 0
                for out_ref, width, turn in zip(outs, widths, turned):
                    for part in range(out_ref.shape[0] if len(out_ref.shape) == 3 else 1):
                        value = block[:, start : start + width].astype(out_ref.dtype)
                        start += width
                        if turn:
                            out_ref[:, here] = value.T
                        elif len(out_ref.shape) == 3:
                            out_ref[part, here, :] = value
                        else:
                            out_ref[here, :] = value


VMEM_LIMIT = 56 * 1024 * 1024


def whole_specs(count):
    return [pl.BlockSpec(memory_space=pltpu.VMEM)] * count


def attend_forward(x, w, cos, sin, mask):
    tokens, heads = mask.shape
    dim, width = w.shape[0], heads * HD
    return pl.pallas_call(
        forward_kernel,
        out_shape=[
            jax.ShapeDtypeStruct((tokens, 3 * width), jnp.bfloat16),
            jax.ShapeDtypeStruct((tokens, width), jnp.bfloat16),
            jax.ShapeDtypeStruct((tokens, heads), jnp.float32),
        ],
        in_specs=whole_specs(5),
        out_specs=whole_specs(3),
        compiler_params=pltpu.CompilerParams(vmem_limit_bytes=VMEM_LIMIT),
        cost_estimate=pl.CostEstimate(
            flops=6 * tokens * dim * width + 2 * tokens * tokens * width,
            bytes_accessed=12 << 20,
            transcendentals=tokens * tokens * heads // 2,
        ),
        name="attend_forward",
    )(x, w, cos, sin, mask)


def attend_backward(g, w, qkv, log_total, cos, sin, mask):
    tokens, heads = mask.shape
    dim, width = w.shape[0], heads * HD
    return pl.pallas_call(
        backward_kernel,
        out_shape=jax.ShapeDtypeStruct((tokens, 3 * width), jnp.bfloat16),
        in_specs=whole_specs(7),
        out_specs=whole_specs(1)[0],
        scratch_shapes=[pltpu.VMEM((tokens, width), jnp.float32)] * 2,
        compiler_params=pltpu.CompilerParams(vmem_limit_bytes=VMEM_LIMIT),
        cost_estimate=pl.CostEstimate(
            flops=2 * tokens * dim * width + 5 * tokens * tokens * width,
            bytes_accessed=12 << 20,
            transcendentals=tokens * tokens * heads // 2,
        ),
        name="attend_backward",
    )(g, w, qkv, log_total, cos, sin, mask)


def share_of(pairs, rows, side):
    tokens, depth = pairs[0][0].shape
    dim = pairs[0][1].shape[0]
    chips = tokens // rows // 2
    specs = [
        pl.BlockSpec((rows, depth), lambda i, side: (2 * i + side[0], 0)),
        pl.BlockSpec((dim, depth), lambda i, side: (0, 0)),
    ] * len(pairs)
    return pl.pallas_call(
        share_kernel,
        grid_spec=pltpu.PrefetchScalarGridSpec(
            num_scalar_prefetch=1,
            grid=(chips,),
            in_specs=specs,
            out_specs=pl.BlockSpec((1, rows, dim), lambda i, side: (i, 0, 0)),
        ),
        out_shape=jax.ShapeDtypeStruct((chips, rows, dim), jnp.bfloat16),
        compiler_params=pltpu.CompilerParams(vmem_limit_bytes=VMEM_LIMIT),
        cost_estimate=pl.CostEstimate(
            flops=tokens * dim * depth * len(pairs), bytes_accessed=12 << 20, transcendentals=0
        ),
        name="share_of",
    )(side.astype(jnp.int32).reshape(1), *[x for pair in pairs for x in pair])


def weight_grads(x, qkv_grad, g, heads_out, count):
    tokens, dim = x.shape
    width = heads_out.shape[1]
    block = dim // count
    out = jax.ShapeDtypeStruct((count, block // 2, 4 * width), jnp.bfloat16)
    return pl.pallas_call(
        weight_kernel,
        grid=(count,),
        out_shape=[out, out],
        in_specs=[
            pl.BlockSpec((tokens, block), lambda i: (0, i)),
            pl.BlockSpec((tokens, 3 * width), lambda i: (0, 0)),
            pl.BlockSpec((tokens, block), lambda i: (0, i)),
            pl.BlockSpec((tokens, width), lambda i: (0, 0)),
        ],
        out_specs=[pl.BlockSpec((1, block // 2, 4 * width), lambda i: (i, 0, 0))] * 2,
        compiler_params=pltpu.CompilerParams(vmem_limit_bytes=VMEM_LIMIT),
        cost_estimate=pl.CostEstimate(flops=8 * tokens * dim * width, bytes_accessed=14 << 20, transcendentals=0),
        name="weight_grads",
    )(x, qkv_grad, g, heads_out)


def place_blocks(lanes, index, outs):
    count = len(lanes[0])
    half, total = lanes[0][0].shape
    rows = len(lanes) * half
    shapes, specs = [], []
    for planes, width, kind, turned in outs:
        if turned:
            shapes.append(jax.ShapeDtypeStruct((width, rows * count), kind))
            specs.append(pl.BlockSpec((width, rows), lambda i, at: (0, i)))
        elif planes > 1:
            shapes.append(jax.ShapeDtypeStruct((planes, rows * count, width), kind))
            specs.append(pl.BlockSpec((planes, rows, width), lambda i, at: (0, i, 0)))
        else:
            shapes.append(jax.ShapeDtypeStruct((rows * count, width), kind))
            specs.append(pl.BlockSpec((rows, width), lambda i, at: (i, 0)))
    given = [held[far] for held in lanes for far in range(count)]
    return pl.pallas_call(
        functools.partial(place_kernel, count, [o[1] for o in outs], [o[3] for o in outs]),
        grid_spec=pltpu.PrefetchScalarGridSpec(
            num_scalar_prefetch=1,
            grid=(count,),
            in_specs=[pl.BlockSpec((half, total), lambda i, at: (0, 0))] * len(given),
            out_specs=specs,
        ),
        out_shape=shapes,
        compiler_params=pltpu.CompilerParams(vmem_limit_bytes=VMEM_LIMIT),
        cost_estimate=pl.CostEstimate(flops=0, bytes_accessed=12 << 20, transcendentals=0),
        name="place_blocks",
    )(index.astype(jnp.int32).reshape(1), *given)


def swap_pairs(size, bit):
    return [(i, i ^ bit) for i in range(size)]


def shift_pairs(size, shift):
    return [(i, (i - shift) % size) for i in range(size)]


def bits_of(size):
    return [1 << i for i in range(size.bit_length() - 1)]


def pick(x, index, axis=0):
    return lax.dynamic_index_in_dim(x, index, axis, keepdims=False)


def after(x, *others):
    return lax.optimization_barrier((x,) + others)[0]


def xor_gather(x, axis, size, bits):
    held = dict(x) if isinstance(x, dict) else {0: x}
    for bit in bits:
        for far in list(held):
            held[far ^ bit] = lax.ppermute(held[far], axis, swap_pairs(size, bit))
    return held


def by_index(held, index, axis=0):
    shape = held[0].shape
    out = jnp.zeros(shape[:axis] + (len(held),) + shape[axis:], held[0].dtype)
    for far, block in held.items():
        out = lax.dynamic_update_index_in_dim(out, block, index ^ far, axis)
    return out


def xor_scatter(blocks, axis_name, size, bits, steps, index, axis, all_steps=None):
    all_steps = list(all_steps or steps)
    left = sorted(all_steps[all_steps.index(steps[0]) :], reverse=True)
    blocks = blocks.reshape(blocks.shape[:axis] + (2,) * len(left) + blocks.shape[axis + 1 :])
    for bit, step in zip(bits, steps):
        at = axis + left.index(step)
        left.remove(step)
        side = (index // step) % 2
        got = lax.ppermute(narrow(pick(blocks, 1 - side, at)), axis_name, swap_pairs(size, bit))
        blocks = wide(pick(blocks, side, at)) + wide(got)
    tail = blocks.shape[axis + len(left) :]
    return blocks.reshape(blocks.shape[:axis] + ((2 ** len(left),) if left else ()) + tail)


def lane_bits(size):
    return bits_of(size), bits_of(size)[::-1]


def column_gather(lanes, size, cut=None, start=None):
    return [xor_gather(x, "dp", size, bits[start:cut]) for x, bits in zip(lanes, lane_bits(size))]


def gate_lanes(lanes, *gates):
    flat = [held[far] for held in lanes for far in held]
    flat = lax.optimization_barrier((*flat, *gates))
    flat = iter(flat)
    return [{far: next(flat) for far in held} for held in lanes]


def column_scatter(lanes, size, column, cut=None, start=None):
    return [
        xor_scatter(x, "dp", size, bits[start:cut], bits[start:cut], column, 0, bits)
        for x, bits in zip(lanes, lane_bits(size))
    ]


def first_scatter(x, size, column):
    count = len(bits_of(size))
    view = x.reshape((2,) * count + x.shape[1:])
    out = []
    for lane, bits in enumerate(lane_bits(size)):
        at = count - 1 - bits_of(size).index(bits[0])
        sizes = tuple(1 if d in (at, count) else n for d, n in enumerate(view.shape))
        side = (column // bits[0]) % 2

        def half(which):
            starts = [0] * view.ndim
            starts[at], starts[count] = which, lane
            return lax.dynamic_slice(view, starts, sizes).reshape((-1,) + x.shape[2:])

        got = lax.ppermute(half(1 - side), "dp", swap_pairs(size, bits[0]))
        out.append(wide(half(side)) + wide(got))
    return out


def all_sum(x, sizes):
    for axis, size in sizes.items():
        for bit in bits_of(size):
            x = x + lax.ppermute(x, axis, swap_pairs(size, bit))
    return x


def make_local(columns, ranks):
    def local(
        layer_input, width_choice, routed_flag, mixer_gain, mixer_router, attention_weight,
        output_weight, hidden_gain, hidden_router, up_weight, down_weight, out_grad,
    ):
        column, rank = lax.axis_index("dp"), lax.axis_index("mp")
        rows, dim = layer_input.shape
        core = rank % 2
        group = SEQ_LEN // rows
        sequences = ranks // group
        place, sequence = rank % group, rank // group
        pair_bits = [b for b in bits_of(group) if b > 1]
        own_heads = output_weight.shape[0] // HD
        cols_local = up_weight.shape[1]
        width_own = lax.dynamic_slice_in_dim(width_choice, rank * rows, rows, 0)
        routed_own = lax.dynamic_slice_in_dim(routed_flag, rank * rows, rows, 0)
        cos, sin = rope_tables(SEQ_LEN, HD)

        def place_sequence(held):
            return by_index(held, place).reshape(SEQ_LEN, -1)

        def core_sum(pairs):
            theirs = share_of(pairs, rows, 1 - core)
            got = lax.ppermute(theirs, "mp", swap_pairs(ranks, 1))
            pairs, theirs = lax.optimization_barrier((pairs, theirs))
            return wide(share_of(pairs, rows, core)) + wide(got)

        def chip_sum(blocks):
            bits = pair_bits[::-1]
            return xor_scatter(blocks, "mp", ranks, bits, [b // 2 for b in bits], place // 2, 0)

        width = own_heads * HD
        chunk_rows = dim // columns
        half_rows = chunk_rows // 2

        def in_slice(w):
            return jnp.concatenate([w[:, p] for p in range(3)], axis=1)

        lanes_in = [
            in_slice(lax.dynamic_slice_in_dim(attention_weight, column * chunk_rows + at, half_rows, 0))
            for at in (0, half_rows)
        ]
        lanes_out = [
            lax.dynamic_slice_in_dim(output_weight, column * chunk_rows + at, half_rows, 1).T
            for at in (0, half_rows)
        ]
        input_wide = wide(layer_input)
        normed_one, scaled_one, inverse_one = norm_forward(input_wide, mixer_gain)
        low_one = narrow(normed_one)
        low_one, lanes_in, lanes_out = lax.optimization_barrier((low_one, lanes_in, lanes_out))
        held = xor_gather(low_one, "mp", ranks, pair_bits)
        fetched_in, fetched_out = [
            [[lax.ppermute(x, "mp", shift_pairs(ranks, k * group)) for x in lanes] for k in range(1, sequences)]
            for lanes in (lanes_in, lanes_out)
        ]
        sequence_width = lax.dynamic_slice_in_dim(width_choice[:, 0], sequence * SEQ_LEN, SEQ_LEN, 0)
        masks = []
        for k in range(sequences):
            heads = ((rank + k * group) % ranks) * own_heads + jnp.arange(own_heads, dtype=jnp.int32)
            masks.append((heads[None, :] * 4 < (sequence_width[:, None] + 1) * H).astype(jnp.float32))
        weights_in, weights_out = [in_slice(attention_weight)], [output_weight.T]
        held, fetched_in, masks, weights_in, weights_out, cos, sin = lax.optimization_barrier(
            (held, fetched_in, masks, weights_in, weights_out, cos, sin)
        )
        inputs_one = place_sequence(xor_gather(held, "mp", ranks, [1]))
        grads_all = lax.all_gather(after(out_grad, *[x for lanes in fetched_in for x in lanes]), "mp", axis=0, tiled=True)
        steps_in = [column_gather(x, columns, cut=1) for x in fetched_in]
        gate_one, state_one = gate_forward(normed_one, mixer_router, width_own[:, 0], routed_own[:, 0])

        kept = []
        for k in range(sequences):
            mask = masks[k]
            if k:
                steps, fetched, _ = lax.optimization_barrier((steps_in[k - 1], fetched_out[k - 1], kept[0][0]))
                held = column_gather(steps, columns, start=1)
                held_out = column_gather(fetched, columns, cut=1)
                held, held_out = lax.optimization_barrier((held, held_out))
                held_out = column_gather(held_out, columns, start=1)
                weights_in += place_blocks(held, column, [(1, 3 * width, jnp.bfloat16, False)])
                weights_out += place_blocks(held_out, column, [(1, width, jnp.bfloat16, False)])
            kept.append((*attend_forward(inputs_one, weights_in[k], cos, sin, mask), mask))
        mixer_branch = chip_sum(core_sum([(x[1], w) for x, w in zip(kept, weights_out)]))
        mixer_branch, grads_all = lax.optimization_barrier((mixer_branch, grads_all))
        top_down = product(grads_all, down_weight, (1, 1))

        middle = input_wide + gate_one[:, None] * mixer_branch
        normed_two, scaled_two, inverse_two = norm_forward(middle, hidden_gain)
        gate_two, state_two = gate_forward(normed_two, hidden_router, width_own[:, 1], routed_own[:, 1])
        inputs_two = lax.all_gather(narrow(normed_two), "mp", axis=0, tiled=True)
        gates = by_index(xor_gather(gate_two.reshape(-1, 128), "mp", ranks, bits_of(ranks)), rank).reshape(-1)

        col_ids = rank * cols_local + jnp.arange(cols_local, dtype=jnp.int32)
        col_mask = (col_ids[None, :] * 4 < (width_choice[:, 1:2] + 1) * FF).astype(jnp.float32)
        inputs_two, top_down = lax.optimization_barrier((inputs_two, top_down))
        pre = product(inputs_two, up_weight, (1, 0))
        relu_act = jax.nn.relu(pre)
        hidden = narrow(relu_act * relu_act * col_mask)
        pre_grad = narrow(top_down * gates[:, None] * col_mask * 2.0 * relu_act)
        dots = jnp.sum(wide(hidden) * top_down, axis=1).reshape(-1, 128)
        share = narrow(product(pre_grad, up_weight, (1, 1)))
        share, hidden, pre_grad = lax.optimization_barrier((share, hidden, pre_grad))
        normed_grad_two = wide(lax.psum_scatter(share, "mp", scatter_dimension=0, tiled=True))
        gate_grad_two = lax.dynamic_slice_in_dim(all_sum(dots, {"mp": ranks}).reshape(-1), rank * rows, rows, 0)
        gated = narrow(gates[:, None] * wide(grads_all))
        up_lanes, down_lanes = [
            first_scatter(narrow(product(a, b, (0, 0))).reshape(columns, 2, -1, b.shape[1]), columns, column)
            for a, b in ((inputs_two, pre_grad), (hidden, gated))
        ]
        hidden_share = narrow(product(hidden, down_weight, (1, 0)))
        up_lanes, hidden_share = lax.optimization_barrier((up_lanes, hidden_share))
        up_lanes = [narrow(x) for x in column_scatter(up_lanes, columns, column, start=1)]
        normed_grad_two, hidden_share, up_lanes, down_lanes = lax.optimization_barrier(
            (normed_grad_two, hidden_share, up_lanes, down_lanes)
        )
        down_lanes = [narrow(x) for x in column_scatter(down_lanes, columns, column, start=1)]
        up_held = column_gather(up_lanes, columns, cut=1)

        router_part, router_two = gate_backward(normed_two, hidden_router, state_two, gate_grad_two)
        middle_part, gain_two = norm_backward(normed_grad_two + router_part, scaled_two, inverse_two, hidden_gain)
        middle_grad = wide(out_grad) + middle_part
        held = xor_gather(narrow(gate_one[:, None] * middle_grad), "mp", ranks, pair_bits)
        held, down_lanes, up_held = lax.optimization_barrier((held, down_lanes, up_held))
        down_held = column_gather(down_lanes, columns, cut=1)
        up_held = column_gather(up_held, columns, start=1)
        grads_one = place_sequence(xor_gather(held, "mp", ranks, [1]))
        grads_one, hidden_share = lax.optimization_barrier((grads_one, hidden_share))
        hidden_branch = wide(lax.psum_scatter(hidden_share, "mp", scatter_dimension=0, tiled=True))
        layer_output = narrow(middle + gate_two[:, None] * hidden_branch)

        gate_grad_one = jnp.sum(middle_grad * mixer_branch, axis=1)
        pairs, sent = [], []
        grads_now = grads_one
        for k in range(sequences)[::-1]:
            qkv, heads_out, log_total, mask = kept[k]
            qkv_grad = attend_backward(grads_now, weights_out[k], qkv, log_total, cos, sin, mask)
            pairs.append((qkv_grad, weights_in[k]))
            if k == 0:
                down_held = column_gather(down_held, columns, start=1)
                sent, qkv_grad = lax.optimization_barrier((sent, qkv_grad))
            part = weight_grads(inputs_one, qkv_grad, grads_one, heads_out, columns)
            if k:
                grads_now, part, up_held, down_held = lax.optimization_barrier((grads_now, part, up_held, down_held))
                sent.append(column_scatter(part, columns, column, cut=1))
        pairs, part = lax.optimization_barrier((pairs, part))
        blocks, down_held = lax.optimization_barrier((core_sum(pairs), down_held))
        normed_grad_one = chip_sum(blocks)
        pieces = column_scatter(part, columns, column)
        sent = [[narrow(x) for x in column_scatter(lanes, columns, column, start=1)] for lanes in sent]
        for k, lanes in zip(range(1, sequences)[::-1], sent):
            back = shift_pairs(ranks, -k * group)
            pieces = [p + wide(lax.ppermute(x, "mp", back)) for p, x in zip(pieces, lanes)]
        spread = column_gather([narrow(p) for p in pieces], columns)
        attention_sum, output_sum = place_blocks(
            spread,
            column,
            [(3, width, jnp.float32, False), (1, width, jnp.float32, True)],
        )
        attention_sum = attention_sum.transpose(1, 0, 2)

        router_part_one, router_one = gate_backward(normed_one, mixer_router, state_one, gate_grad_one)
        input_part, gain_one = norm_backward(normed_grad_one + router_part_one, scaled_one, inverse_one, mixer_gain)
        input_grad = narrow(middle_grad + input_part)

        sizes = {"mp": ranks, "dp": columns}

        smalls = [gain_two, gain_one, router_two.T, router_one.T]
        small = jnp.concatenate([x.reshape(-1, 128) for x in smalls], axis=0)
        *steps, last = [(axis, size, bit) for axis, size in sizes.items() for bit in bits_of(size)]
        for axis, size, bit in steps:
            small = small + lax.ppermute(small, axis, swap_pairs(size, bit))
        small, down_held, up_held = lax.optimization_barrier((small, down_held, up_held))
        small_sum = small + lax.ppermute(small, last[0], swap_pairs(*last[1:]))
        down_sum, = place_blocks(down_held, column, [(1, dim, jnp.float32, False)])
        up_sum, = place_blocks(up_held, column, [(1, cols_local, jnp.float32, False)])
        cuts = [dim // 128, 2 * dim // 128, (2 * dim + router_two.size) // 128]
        hidden_gain_sum, mixer_gain_sum, hidden_router_sum, mixer_router_sum = (
            x.reshape(-1, dim) for x in jnp.split(small_sum, cuts)
        )
        hidden_gain_sum, mixer_gain_sum = hidden_gain_sum[0], mixer_gain_sum[0]
        hidden_router_sum, mixer_router_sum = hidden_router_sum.T, mixer_router_sum.T
        return (
            layer_output, input_grad, mixer_gain_sum, mixer_router_sum, attention_sum, output_sum,
            hidden_gain_sum, hidden_router_sum, up_sum, down_sum,
        )

    return local


def solution(mesh):
    return jax.shard_map(
        make_local(mesh.shape["dp"], mesh.shape["mp"]),
        mesh=mesh,
        in_specs=(
            P(("dp", "mp"), None),
            P("dp", None),
            P("dp", None),
            P(),
            P(),
            P(None, None, "mp"),
            P("mp", None),
            P(),
            P(),
            P(None, "mp"),
            P("mp", None),
            P(("dp", "mp"), None),
        ),
        out_specs=(
            P(("dp", "mp"), None),
            P(("dp", "mp"), None),
            P(),
            P(),
            P(None, None, "mp"),
            P("mp", None),
            P(),
            P(),
            P(None, "mp"),
            P("mp", None),
        ),
        check_vma=False,
    )
```

```python
import functools
import math

import jax
import jax.numpy as jnp
from jax import lax
from jax.experimental import pallas as pl
from jax.experimental.pallas import tpu as pltpu
from jax.sharding import PartitionSpec as P

H = 16
HD = 128
FF = 8192
SEQ_LEN = 1024


EPSILON = 1e-05
NEG_LARGE = -1e30
HIGHEST = lax.Precision.HIGHEST


def norm_forward(values, gain_vec):
    row_mean = jnp.mean(values, axis=1, keepdims=True)
    centred = values - row_mean
    row_variance = jnp.mean(centred * centred, axis=1, keepdims=True)
    inverse_scale = lax.rsqrt(row_variance + EPSILON)
    scaled = centred * inverse_scale
    return (scaled * gain_vec[None, :], scaled, inverse_scale)


def norm_backward(normed_grad, scaled, inverse_scale, gain_vec):
    gain_grad = jnp.sum(normed_grad * scaled, axis=0)
    scaled_grad = normed_grad * gain_vec[None, :]
    first_mean = jnp.mean(scaled_grad, axis=1, keepdims=True)
    second_mean = jnp.mean(scaled_grad * scaled, axis=1, keepdims=True)
    return (inverse_scale * (scaled_grad - first_mean - scaled * second_mean), gain_grad)


def gate_forward(normed, router, width_col, routed_col):
    logits = jnp.dot(normed, router, precision=HIGHEST, preferred_element_type=jnp.float32)
    soft_probs = jax.nn.softmax(logits, axis=1)
    one_hot = (width_col[:, None] == jnp.arange(4, dtype=jnp.int32)[None, :]).astype(jnp.float32)
    chosen = jnp.sum(soft_probs * one_hot, axis=1)
    route_flags = routed_col.astype(jnp.float32)
    return (
        route_flags * 4.0 * chosen + (1.0 - route_flags),
        (soft_probs, one_hot, chosen, route_flags),
    )


def gate_backward(normed, router, gate_state, gate_grad):
    soft_probs, one_hot, chosen, route_flags = gate_state
    coefficient = route_flags * 4.0 * chosen * gate_grad
    logit_grad = coefficient[:, None] * (one_hot - soft_probs)
    router_grad = lax.dot_general(
        normed,
        logit_grad,
        (((0,), (0,)), ((), ())),
        precision=HIGHEST,
        preferred_element_type=jnp.float32,
    )
    normed_grad = lax.dot_general(
        logit_grad,
        router,
        (((1,), (1,)), ((), ())),
        precision=HIGHEST,
        preferred_element_type=jnp.float32,
    )
    return (normed_grad, router_grad)


Q_BLOCK = 256


def rope_tables(token_count, head_width):
    positions = jnp.arange(token_count, dtype=jnp.float32)
    frequency = jnp.exp(
        jnp.arange(head_width // 2, dtype=jnp.float32) * (-2.0 * math.log(10000.0) / head_width)
    )
    angles = positions[:, None] * frequency[None, :]
    cosine, sine = jnp.cos(angles), jnp.sin(angles)
    return jnp.concatenate([cosine, cosine], axis=1), jnp.concatenate([-sine, sine], axis=1)


def wide(x):
    return x.astype(jnp.float32)


def narrow(x):
    return x.astype(jnp.bfloat16)


def product(a, b, dims):
    return lax.dot_general(a, b, ((dims[:1], dims[1:]), ((), ())), preferred_element_type=jnp.float32)


def block_scores(queries, keys_all, start):
    scores = product(queries, keys_all, (1, 1)) * (1.0 / math.sqrt(HD))
    row = lax.broadcasted_iota(jnp.int32, scores.shape, 0) + start
    col = lax.broadcasted_iota(jnp.int32, scores.shape, 1)
    return jnp.where(col <= row, scores, NEG_LARGE)


def forward_kernel(x_ref, w_ref, cos_ref, sin_ref, mask_ref, qkv_ref, heads_ref, log_ref):
    tokens, heads = x_ref.shape[0], mask_ref.shape[1]
    width = heads * HD
    block = min(Q_BLOCK, tokens)
    for start in range(0, tokens, block):
        here, end = slice(start, start + block), start + block
        x = x_ref[here, :]
        cos, sin = cos_ref[here, :], sin_ref[here, :]
        for part in range(3):
            rows = product(x, w_ref[:, part * width : (part + 1) * width], (1, 0))
            for head in range(heads):
                value = rows[:, head * HD : (head + 1) * HD]
                if part < 2:
                    value = value * cos + pltpu.roll(value, HD // 2, 1) * sin
                at = part * width + head * HD
                qkv_ref[here, at : at + HD] = narrow(value)
        for head in range(heads):
            at = head * HD
            lanes, key_lanes, value_lanes = (slice(at + p * width, at + p * width + HD) for p in range(3))
            scores = block_scores(qkv_ref[here, lanes], qkv_ref[:end, key_lanes], start)
            row_max = jnp.max(scores, axis=1, keepdims=True)
            shifted = jnp.exp(scores - row_max)
            total = jnp.sum(shifted, axis=1, keepdims=True)
            mix = product(narrow(shifted * (1.0 / total)), qkv_ref[:end, value_lanes], (1, 0))
            heads_ref[here, lanes] = narrow(mix * mask_ref[here, head : head + 1])
            log_ref[here, head : head + 1] = row_max + jnp.log(total)


def backward_kernel(g_ref, w_ref, qkv_ref, log_ref, cos_ref, sin_ref, mask_ref, out_ref, keys_acc, values_acc):
    tokens, heads = g_ref.shape[0], mask_ref.shape[1]
    width = heads * HD
    block = min(Q_BLOCK, tokens)
    scale = 1.0 / math.sqrt(HD)
    for start in range(0, tokens, block):
        here, end = slice(start, start + block), start + block
        cos, sin = cos_ref[here, :], sin_ref[here, :]
        rows = narrow(product(g_ref[here, :], w_ref[...], (1, 0)))
        for head in range(heads):
            at = head * HD
            lanes, key_lanes, value_lanes = (slice(at + p * width, at + p * width + HD) for p in range(3))
            heads_grad = rows[:, lanes] * narrow(mask_ref[here, head : head + 1])
            queries, keys_all = qkv_ref[here, lanes], qkv_ref[:end, key_lanes]
            scores = block_scores(queries, keys_all, start)
            probs = jnp.exp(scores - log_ref[here, head : head + 1])
            values_part = product(narrow(probs), heads_grad, (0, 0))
            probs_grad = product(heads_grad, qkv_ref[:end, value_lanes], (1, 1))
            centre = jnp.sum(probs * probs_grad, axis=1, keepdims=True)
            score_grad = narrow(probs * (probs_grad - centre))
            queries_grad = product(score_grad, keys_all, (1, 0)) * scale
            keys_part = product(score_grad, queries, (0, 0)) * scale
            turned = queries_grad * cos - pltpu.roll(queries_grad, HD // 2, 1) * sin
            out_ref[here, lanes] = narrow(turned)
            if start:
                values_acc[:start, lanes] += values_part[:start]
                keys_acc[:start, lanes] += keys_part[:start]
            values_acc[here, lanes] = values_part[start:]
            keys_acc[here, lanes] = keys_part[start:]
    for start in range(0, tokens, block):
        here = slice(start, start + block)
        cos, sin = cos_ref[here, :], sin_ref[here, :]
        out_ref[here, 2 * width :] = narrow(values_acc[here, :])
        for head in range(heads):
            at = head * HD
            value = keys_acc[here, at : at + HD]
            out_ref[here, width + at : width + at + HD] = narrow(value * cos - pltpu.roll(value, HD // 2, 1) * sin)


def share_kernel(side_ref, *refs):
    *given, out_ref = refs
    total = product(given[0][...], given[1][...], (1, 1))
    for a_ref, w_ref in zip(given[2::2], given[3::2]):
        total = total + product(a_ref[...], w_ref[...], (1, 1))
    out_ref[0] = narrow(total)


def weight_kernel(x_ref, q_ref, g_ref, h_ref, *outs):
    width = h_ref.shape[1]
    half = x_ref.shape[1] // 2
    for lane, out_ref in enumerate(outs):
        here = slice(lane * half, (lane + 1) * half)
        out_ref[0, :, : 3 * width] = narrow(product(x_ref[:, here], q_ref[...], (0, 0)))
        out_ref[0, :, 3 * width :] = narrow(product(g_ref[:, here], h_ref[...], (0, 0)))


def place_kernel(count, widths, turned, at_ref, *refs):
    lanes = (len(refs) - len(widths)) // count
    blocks, outs = refs[: lanes * count], refs[lanes * count :]
    half = blocks[0].shape[0]
    for far in range(count):

        @pl.when((pl.program_id(0) ^ at_ref[0]) == far)
        def _():
            for lane in range(lanes):
                here = slice(lane * half, (lane + 1) * half)
                block = blocks[lane * count + far]
                start = 0
                for out_ref, width, turn in zip(outs, widths, turned):
                    for part in range(out_ref.shape[0] if len(out_ref.shape) == 3 else 1):
                        value = block[:, start : start + width].astype(out_ref.dtype)
                        start += width
                        if turn:
                            out_ref[:, here] = value.T
                        elif len(out_ref.shape) == 3:
                            out_ref[part, here, :] = value
                        else:
                            out_ref[here, :] = value


VMEM_LIMIT = 56 * 1024 * 1024


def whole_specs(count):
    return [pl.BlockSpec(memory_space=pltpu.VMEM)] * count


def attend_forward(x, w, cos, sin, mask):
    tokens, heads = mask.shape
    dim, width = w.shape[0], heads * HD
    return pl.pallas_call(
        forward_kernel,
        out_shape=[
            jax.ShapeDtypeStruct((tokens, 3 * width), jnp.bfloat16),
            jax.ShapeDtypeStruct((tokens, width), jnp.bfloat16),
            jax.ShapeDtypeStruct((tokens, heads), jnp.float32),
        ],
        in_specs=whole_specs(5),
        out_specs=whole_specs(3),
        compiler_params=pltpu.CompilerParams(vmem_limit_bytes=VMEM_LIMIT),
        cost_estimate=pl.CostEstimate(
            flops=6 * tokens * dim * width + 2 * tokens * tokens * width,
            bytes_accessed=12 << 20,
            transcendentals=tokens * tokens * heads // 2,
        ),
        name="attend_forward",
    )(x, w, cos, sin, mask)


def attend_backward(g, w, qkv, log_total, cos, sin, mask):
    tokens, heads = mask.shape
    dim, width = w.shape[0], heads * HD
    return pl.pallas_call(
        backward_kernel,
        out_shape=jax.ShapeDtypeStruct((tokens, 3 * width), jnp.bfloat16),
        in_specs=whole_specs(7),
        out_specs=whole_specs(1)[0],
        scratch_shapes=[pltpu.VMEM((tokens, width), jnp.float32)] * 2,
        compiler_params=pltpu.CompilerParams(vmem_limit_bytes=VMEM_LIMIT),
        cost_estimate=pl.CostEstimate(
            flops=2 * tokens * dim * width + 5 * tokens * tokens * width,
            bytes_accessed=12 << 20,
            transcendentals=tokens * tokens * heads // 2,
        ),
        name="attend_backward",
    )(g, w, qkv, log_total, cos, sin, mask)


def share_of(pairs, rows, side):
    tokens, depth = pairs[0][0].shape
    dim = pairs[0][1].shape[0]
    chips = tokens // rows // 2
    specs = [
        pl.BlockSpec((rows, depth), lambda i, side: (2 * i + side[0], 0)),
        pl.BlockSpec((dim, depth), lambda i, side: (0, 0)),
    ] * len(pairs)
    return pl.pallas_call(
        share_kernel,
        grid_spec=pltpu.PrefetchScalarGridSpec(
            num_scalar_prefetch=1,
            grid=(chips,),
            in_specs=specs,
            out_specs=pl.BlockSpec((1, rows, dim), lambda i, side: (i, 0, 0)),
        ),
        out_shape=jax.ShapeDtypeStruct((chips, rows, dim), jnp.bfloat16),
        compiler_params=pltpu.CompilerParams(vmem_limit_bytes=VMEM_LIMIT),
        cost_estimate=pl.CostEstimate(
            flops=tokens * dim * depth * len(pairs), bytes_accessed=12 << 20, transcendentals=0
        ),
        name="share_of",
    )(side.astype(jnp.int32).reshape(1), *[x for pair in pairs for x in pair])


def weight_grads(x, qkv_grad, g, heads_out, count):
    tokens, dim = x.shape
    width = heads_out.shape[1]
    block = dim // count
    out = jax.ShapeDtypeStruct((count, block // 2, 4 * width), jnp.bfloat16)
    return pl.pallas_call(
        weight_kernel,
        grid=(count,),
        out_shape=[out, out],
        in_specs=[
            pl.BlockSpec((tokens, block), lambda i: (0, i)),
            pl.BlockSpec((tokens, 3 * width), lambda i: (0, 0)),
            pl.BlockSpec((tokens, block), lambda i: (0, i)),
            pl.BlockSpec((tokens, width), lambda i: (0, 0)),
        ],
        out_specs=[pl.BlockSpec((1, block // 2, 4 * width), lambda i: (i, 0, 0))] * 2,
        compiler_params=pltpu.CompilerParams(vmem_limit_bytes=VMEM_LIMIT),
        cost_estimate=pl.CostEstimate(flops=8 * tokens * dim * width, bytes_accessed=14 << 20, transcendentals=0),
        name="weight_grads",
    )(x, qkv_grad, g, heads_out)


def place_blocks(lanes, index, outs):
    count = len(lanes[0])
    half, total = lanes[0][0].shape
    rows = len(lanes) * half
    shapes, specs = [], []
    for planes, width, kind, turned in outs:
        if turned:
            shapes.append(jax.ShapeDtypeStruct((width, rows * count), kind))
            specs.append(pl.BlockSpec((width, rows), lambda i, at: (0, i)))
        elif planes > 1:
            shapes.append(jax.ShapeDtypeStruct((planes, rows * count, width), kind))
            specs.append(pl.BlockSpec((planes, rows, width), lambda i, at: (0, i, 0)))
        else:
            shapes.append(jax.ShapeDtypeStruct((rows * count, width), kind))
            specs.append(pl.BlockSpec((rows, width), lambda i, at: (i, 0)))
    given = [held[far] for held in lanes for far in range(count)]
    return pl.pallas_call(
        functools.partial(place_kernel, count, [o[1] for o in outs], [o[3] for o in outs]),
        grid_spec=pltpu.PrefetchScalarGridSpec(
            num_scalar_prefetch=1,
            grid=(count,),
            in_specs=[pl.BlockSpec((half, total), lambda i, at: (0, 0))] * len(given),
            out_specs=specs,
        ),
        out_shape=shapes,
        compiler_params=pltpu.CompilerParams(vmem_limit_bytes=VMEM_LIMIT),
        cost_estimate=pl.CostEstimate(flops=0, bytes_accessed=12 << 20, transcendentals=0),
        name="place_blocks",
    )(index.astype(jnp.int32).reshape(1), *given)


def swap_pairs(size, bit):
    return [(i, i ^ bit) for i in range(size)]


def shift_pairs(size, shift):
    return [(i, (i - shift) % size) for i in range(size)]


def bits_of(size):
    return [1 << i for i in range(size.bit_length() - 1)]


def pick(x, index, axis=0):
    return lax.dynamic_index_in_dim(x, index, axis, keepdims=False)


def after(x, *others):
    return lax.optimization_barrier((x,) + others)[0]


def xor_gather(x, axis, size, bits):
    held = dict(x) if isinstance(x, dict) else {0: x}
    for bit in bits:
        for far in list(held):
            held[far ^ bit] = lax.ppermute(held[far], axis, swap_pairs(size, bit))
    return held


def by_index(held, index, axis=0):
    shape = held[0].shape
    out = jnp.zeros(shape[:axis] + (len(held),) + shape[axis:], held[0].dtype)
    for far, block in held.items():
        out = lax.dynamic_update_index_in_dim(out, block, index ^ far, axis)
    return out


def xor_scatter(blocks, axis_name, size, bits, steps, index, axis, all_steps=None):
    all_steps = list(all_steps or steps)
    left = sorted(all_steps[all_steps.index(steps[0]) :], reverse=True)
    blocks = blocks.reshape(blocks.shape[:axis] + (2,) * len(left) + blocks.shape[axis + 1 :])
    for bit, step in zip(bits, steps):
        at = axis + left.index(step)
        left.remove(step)
        side = (index // step) % 2
        got = lax.ppermute(narrow(pick(blocks, 1 - side, at)), axis_name, swap_pairs(size, bit))
        blocks = wide(pick(blocks, side, at)) + wide(got)
    tail = blocks.shape[axis + len(left) :]
    return blocks.reshape(blocks.shape[:axis] + ((2 ** len(left),) if left else ()) + tail)


def lane_bits(size):
    return bits_of(size), bits_of(size)[::-1]


def column_gather(lanes, size, cut=None, start=None):
    return [xor_gather(x, "dp", size, bits[start:cut]) for x, bits in zip(lanes, lane_bits(size))]


def gate_lanes(lanes, *gates):
    flat = [held[far] for held in lanes for far in held]
    flat = lax.optimization_barrier((*flat, *gates))
    flat = iter(flat)
    return [{far: next(flat) for far in held} for held in lanes]


def column_scatter(lanes, size, column, cut=None, start=None):
    return [
        xor_scatter(x, "dp", size, bits[start:cut], bits[start:cut], column, 0, bits)
        for x, bits in zip(lanes, lane_bits(size))
    ]


def all_sum(x, sizes):
    for axis, size in sizes.items():
        for bit in bits_of(size):
            x = x + lax.ppermute(x, axis, swap_pairs(size, bit))
    return x


def make_local(columns, ranks):
    def local(
        layer_input, width_choice, routed_flag, mixer_gain, mixer_router, attention_weight,
        output_weight, hidden_gain, hidden_router, up_weight, down_weight, out_grad,
    ):
        column, rank = lax.axis_index("dp"), lax.axis_index("mp")
        rows, dim = layer_input.shape
        core = rank % 2
        group = SEQ_LEN // rows
        sequences = ranks // group
        place, sequence = rank % group, rank // group
        pair_bits = [b for b in bits_of(group) if b > 1]
        own_heads = output_weight.shape[0] // HD
        cols_local = up_weight.shape[1]
        width_own = lax.dynamic_slice_in_dim(width_choice, rank * rows, rows, 0)
        routed_own = lax.dynamic_slice_in_dim(routed_flag, rank * rows, rows, 0)
        cos, sin = rope_tables(SEQ_LEN, HD)

        def place_sequence(held):
            return by_index(held, place).reshape(SEQ_LEN, -1)

        def core_sum(pairs):
            theirs = share_of(pairs, rows, 1 - core)
            got = lax.ppermute(theirs, "mp", swap_pairs(ranks, 1))
            pairs, theirs = lax.optimization_barrier((pairs, theirs))
            return wide(share_of(pairs, rows, core)) + wide(got)

        def chip_sum(blocks):
            bits = pair_bits[::-1]
            return xor_scatter(blocks, "mp", ranks, bits, [b // 2 for b in bits], place // 2, 0)

        width = own_heads * HD
        chunk_rows = dim // columns
        half_rows = chunk_rows // 2

        def in_slice(w):
            return jnp.concatenate([w[:, p] for p in range(3)], axis=1)

        lanes_in = [
            in_slice(lax.dynamic_slice_in_dim(attention_weight, column * chunk_rows + at, half_rows, 0))
            for at in (0, half_rows)
        ]
        lanes_out = [
            lax.dynamic_slice_in_dim(output_weight, column * chunk_rows + at, half_rows, 1).T
            for at in (0, half_rows)
        ]
        input_wide = wide(layer_input)
        normed_one, scaled_one, inverse_one = norm_forward(input_wide, mixer_gain)
        low_one = narrow(normed_one)
        low_one, lanes_in, lanes_out = lax.optimization_barrier((low_one, lanes_in, lanes_out))
        held = xor_gather(low_one, "mp", ranks, pair_bits)
        fetched_in, fetched_out = [
            [[lax.ppermute(x, "mp", shift_pairs(ranks, k * group)) for x in lanes] for k in range(1, sequences)]
            for lanes in (lanes_in, lanes_out)
        ]
        sequence_width = lax.dynamic_slice_in_dim(width_choice[:, 0], sequence * SEQ_LEN, SEQ_LEN, 0)
        masks = []
        for k in range(sequences):
            heads = ((rank + k * group) % ranks) * own_heads + jnp.arange(own_heads, dtype=jnp.int32)
            masks.append((heads[None, :] * 4 < (sequence_width[:, None] + 1) * H).astype(jnp.float32))
        weights_in, weights_out = [in_slice(attention_weight)], [output_weight.T]
        held, fetched_in, masks, weights_in, weights_out, cos, sin = lax.optimization_barrier(
            (held, fetched_in, masks, weights_in, weights_out, cos, sin)
        )
        inputs_one = place_sequence(xor_gather(held, "mp", ranks, [1]))
        grads_all = lax.all_gather(after(out_grad, *[x for lanes in fetched_in for x in lanes]), "mp", axis=0, tiled=True)
        steps_in = [column_gather(x, columns, cut=1) for x in fetched_in]
        gate_one, state_one = gate_forward(normed_one, mixer_router, width_own[:, 0], routed_own[:, 0])

        kept = []
        for k in range(sequences):
            mask = masks[k]
            if k:
                steps, fetched, _ = lax.optimization_barrier((steps_in[k - 1], fetched_out[k - 1], kept[0][0]))
                held = column_gather(steps, columns, start=1)
                held_out = column_gather(fetched, columns, cut=1)
                held, held_out = lax.optimization_barrier((held, held_out))
                held_out = column_gather(held_out, columns, start=1)
                weights_in += place_blocks(held, column, [(1, 3 * width, jnp.bfloat16, False)])
                weights_out += place_blocks(held_out, column, [(1, width, jnp.bfloat16, False)])
            kept.append((*attend_forward(inputs_one, weights_in[k], cos, sin, mask), mask))
        mixer_branch = chip_sum(core_sum([(x[1], w) for x, w in zip(kept, weights_out)]))
        mixer_branch, grads_all = lax.optimization_barrier((mixer_branch, grads_all))
        top_down = product(grads_all, down_weight, (1, 1))

        middle = input_wide + gate_one[:, None] * mixer_branch
        normed_two, scaled_two, inverse_two = norm_forward(middle, hidden_gain)
        gate_two, state_two = gate_forward(normed_two, hidden_router, width_own[:, 1], routed_own[:, 1])
        inputs_two = lax.all_gather(narrow(normed_two), "mp", axis=0, tiled=True)
        gates = by_index(xor_gather(gate_two.reshape(-1, 128), "mp", ranks, bits_of(ranks)), rank).reshape(-1)

        col_ids = rank * cols_local + jnp.arange(cols_local, dtype=jnp.int32)
        col_mask = (col_ids[None, :] * 4 < (width_choice[:, 1:2] + 1) * FF).astype(jnp.float32)
        inputs_two, top_down = lax.optimization_barrier((inputs_two, top_down))
        pre = product(inputs_two, up_weight, (1, 0))
        relu_act = jax.nn.relu(pre)
        hidden = narrow(relu_act * relu_act * col_mask)
        pre_grad = narrow(top_down * gates[:, None] * col_mask * 2.0 * relu_act)
        dots = jnp.sum(wide(hidden) * top_down, axis=1).reshape(-1, 128)
        share = narrow(product(pre_grad, up_weight, (1, 1)))
        share, hidden, pre_grad = lax.optimization_barrier((share, hidden, pre_grad))
        normed_grad_two = wide(lax.psum_scatter(share, "mp", scatter_dimension=0, tiled=True))
        gate_grad_two = lax.dynamic_slice_in_dim(all_sum(dots, {"mp": ranks}).reshape(-1), rank * rows, rows, 0)
        gated = narrow(gates[:, None] * wide(grads_all))
        lanes = [narrow(product(hidden, gated, (0, 0))), narrow(product(inputs_two, pre_grad, (0, 0)))]
        lanes = [x.reshape(columns, -1, x.shape[1]) for x in lanes]
        lanes = column_scatter(lanes, columns, column, cut=1)
        hidden_share = narrow(product(hidden, down_weight, (1, 0)))
        normed_grad_two, hidden_share, *lanes = lax.optimization_barrier((normed_grad_two, hidden_share, *lanes))
        lanes = [narrow(x) for x in column_scatter(lanes, columns, column, start=1)]

        router_part, router_two = gate_backward(normed_two, hidden_router, state_two, gate_grad_two)
        middle_part, gain_two = norm_backward(normed_grad_two + router_part, scaled_two, inverse_two, hidden_gain)
        middle_grad = wide(out_grad) + middle_part
        grads_one = place_sequence(
            xor_gather(narrow(gate_one[:, None] * middle_grad), "mp", ranks, pair_bits + [1])
        )
        helds = column_gather(lanes, columns, cut=1)
        grads_one, hidden_share, lanes = lax.optimization_barrier((grads_one, hidden_share, lanes))
        hidden_branch = wide(lax.psum_scatter(hidden_share, "mp", scatter_dimension=0, tiled=True))
        layer_output = narrow(middle + gate_two[:, None] * hidden_branch)

        gate_grad_one = jnp.sum(middle_grad * mixer_branch, axis=1)
        pairs, sent = [], []
        grads_now = grads_one
        for k in range(sequences)[::-1]:
            qkv, heads_out, log_total, mask = kept[k]
            qkv_grad = attend_backward(grads_now, weights_out[k], qkv, log_total, cos, sin, mask)
            pairs.append((qkv_grad, weights_in[k]))
            if k == 0:
                helds = column_gather(helds, columns, start=1)
                qkv_grad, helds = lax.optimization_barrier((qkv_grad, helds))
            part = weight_grads(inputs_one, qkv_grad, grads_one, heads_out, columns)
            if k:
                grads_now, part, helds = lax.optimization_barrier((grads_now, part, helds))
                sent.append((k, part))
        normed_grad_one = chip_sum(core_sum(pairs))
        pieces = column_scatter(part, columns, column)
        for k, lanes in sent:
            lanes = [narrow(x) for x in column_scatter(lanes, columns, column)]
            back = shift_pairs(ranks, -k * group)
            pieces = [p + wide(lax.ppermute(x, "mp", back)) for p, x in zip(pieces, lanes)]
        spread = column_gather([narrow(p) for p in pieces], columns, cut=1)
        spread, helds = lax.optimization_barrier((spread, helds))
        spread = column_gather(spread, columns, start=1)
        down_sum, = place_blocks(helds[:1], column, [(1, dim, jnp.float32, False)])
        up_sum, = place_blocks(helds[1:], column, [(1, cols_local, jnp.float32, False)])
        attention_sum, output_sum = place_blocks(
            spread,
            column,
            [(3, width, jnp.float32, False), (1, width, jnp.float32, True)],
        )
        attention_sum = attention_sum.transpose(1, 0, 2)

        router_part_one, router_one = gate_backward(normed_one, mixer_router, state_one, gate_grad_one)
        input_part, gain_one = norm_backward(normed_grad_one + router_part_one, scaled_one, inverse_one, mixer_gain)
        input_grad = narrow(middle_grad + input_part)

        sizes = {"mp": ranks, "dp": columns}

        smalls = [gain_two, gain_one, router_two.T, router_one.T]
        small_sum = all_sum(jnp.concatenate([x.reshape(-1, 128) for x in smalls], axis=0), sizes)
        cuts = [dim // 128, 2 * dim // 128, (2 * dim + router_two.size) // 128]
        hidden_gain_sum, mixer_gain_sum, hidden_router_sum, mixer_router_sum = (
            x.reshape(-1, dim) for x in jnp.split(small_sum, cuts)
        )
        hidden_gain_sum, mixer_gain_sum = hidden_gain_sum[0], mixer_gain_sum[0]
        hidden_router_sum, mixer_router_sum = hidden_router_sum.T, mixer_router_sum.T
        return (
            layer_output, input_grad, mixer_gain_sum, mixer_router_sum, attention_sum, output_sum,
            hidden_gain_sum, hidden_router_sum, up_sum, down_sum,
        )

    return local


def solution(mesh):
    return jax.shard_map(
        make_local(mesh.shape["dp"], mesh.shape["mp"]),
        mesh=mesh,
        in_specs=(
            P(("dp", "mp"), None),
            P("dp", None),
            P("dp", None),
            P(),
            P(),
            P(None, None, "mp"),
            P("mp", None),
            P(),
            P(),
            P(None, "mp"),
            P("mp", None),
            P(("dp", "mp"), None),
        ),
        out_specs=(
            P(("dp", "mp"), None),
            P(("dp", "mp"), None),
            P(),
            P(),
            P(None, None, "mp"),
            P("mp", None),
            P(),
            P(),
            P(None, "mp"),
            P("mp", None),
        ),
        check_vma=False,
    )
```

```python
import functools
import math

import jax
import jax.numpy as jnp
from jax import lax
from jax.experimental import pallas as pl
from jax.experimental.pallas import tpu as pltpu
from jax.sharding import PartitionSpec as P

H = 16
HD = 128
FF = 8192
SEQ_LEN = 1024


EPSILON = 1e-05
NEG_LARGE = -1e30
HIGHEST = lax.Precision.HIGHEST


def norm_forward(values, gain_vec):
    row_mean = jnp.mean(values, axis=1, keepdims=True)
    centred = values - row_mean
    row_variance = jnp.mean(centred * centred, axis=1, keepdims=True)
    inverse_scale = lax.rsqrt(row_variance + EPSILON)
    scaled = centred * inverse_scale
    return (scaled * gain_vec[None, :], scaled, inverse_scale)


def norm_backward(normed_grad, scaled, inverse_scale, gain_vec):
    gain_grad = jnp.sum(normed_grad * scaled, axis=0)
    scaled_grad = normed_grad * gain_vec[None, :]
    first_mean = jnp.mean(scaled_grad, axis=1, keepdims=True)
    second_mean = jnp.mean(scaled_grad * scaled, axis=1, keepdims=True)
    return (inverse_scale * (scaled_grad - first_mean - scaled * second_mean), gain_grad)


def gate_forward(normed, router, width_col, routed_col):
    logits = jnp.dot(normed, router, precision=HIGHEST, preferred_element_type=jnp.float32)
    soft_probs = jax.nn.softmax(logits, axis=1)
    one_hot = (width_col[:, None] == jnp.arange(4, dtype=jnp.int32)[None, :]).astype(jnp.float32)
    chosen = jnp.sum(soft_probs * one_hot, axis=1)
    route_flags = routed_col.astype(jnp.float32)
    return (
        route_flags * 4.0 * chosen + (1.0 - route_flags),
        (soft_probs, one_hot, chosen, route_flags),
    )


def gate_backward(normed, router, gate_state, gate_grad):
    soft_probs, one_hot, chosen, route_flags = gate_state
    coefficient = route_flags * 4.0 * chosen * gate_grad
    logit_grad = coefficient[:, None] * (one_hot - soft_probs)
    router_grad = lax.dot_general(
        normed,
        logit_grad,
        (((0,), (0,)), ((), ())),
        precision=HIGHEST,
        preferred_element_type=jnp.float32,
    )
    normed_grad = lax.dot_general(
        logit_grad,
        router,
        (((1,), (1,)), ((), ())),
        precision=HIGHEST,
        preferred_element_type=jnp.float32,
    )
    return (normed_grad, router_grad)


Q_BLOCK = 256


def rope_tables(token_count, head_width):
    positions = jnp.arange(token_count, dtype=jnp.float32)
    frequency = jnp.exp(
        jnp.arange(head_width // 2, dtype=jnp.float32) * (-2.0 * math.log(10000.0) / head_width)
    )
    angles = positions[:, None] * frequency[None, :]
    cosine, sine = jnp.cos(angles), jnp.sin(angles)
    return jnp.concatenate([cosine, cosine], axis=1), jnp.concatenate([-sine, sine], axis=1)


def wide(x):
    return x.astype(jnp.float32)


def narrow(x):
    return x.astype(jnp.bfloat16)


def product(a, b, dims):
    return lax.dot_general(a, b, ((dims[:1], dims[1:]), ((), ())), preferred_element_type=jnp.float32)


def block_scores(queries, keys_all, start):
    scores = product(queries, keys_all, (1, 1)) * (1.0 / math.sqrt(HD))
    row = lax.broadcasted_iota(jnp.int32, scores.shape, 0) + start
    col = lax.broadcasted_iota(jnp.int32, scores.shape, 1)
    return jnp.where(col <= row, scores, NEG_LARGE)


def forward_kernel(x_ref, w_ref, cos_ref, sin_ref, mask_ref, qkv_ref, heads_ref, log_ref):
    tokens, heads = x_ref.shape[0], mask_ref.shape[1]
    width = heads * HD
    block = min(Q_BLOCK, tokens)
    for start in range(0, tokens, block):
        here, end = slice(start, start + block), start + block
        x = x_ref[here, :]
        cos, sin = cos_ref[here, :], sin_ref[here, :]
        for part in range(3):
            rows = product(x, w_ref[:, part * width : (part + 1) * width], (1, 0))
            for head in range(heads):
                value = rows[:, head * HD : (head + 1) * HD]
                if part < 2:
                    value = value * cos + pltpu.roll(value, HD // 2, 1) * sin
                at = part * width + head * HD
                qkv_ref[here, at : at + HD] = narrow(value)
        for head in range(heads):
            at = head * HD
            lanes, key_lanes, value_lanes = (slice(at + p * width, at + p * width + HD) for p in range(3))
            scores = block_scores(qkv_ref[here, lanes], qkv_ref[:end, key_lanes], start)
            row_max = jnp.max(scores, axis=1, keepdims=True)
            shifted = jnp.exp(scores - row_max)
            total = jnp.sum(shifted, axis=1, keepdims=True)
            mix = product(narrow(shifted * (1.0 / total)), qkv_ref[:end, value_lanes], (1, 0))
            heads_ref[here, lanes] = narrow(mix * mask_ref[here, head : head + 1])
            log_ref[here, head : head + 1] = row_max + jnp.log(total)


def backward_kernel(g_ref, w_ref, qkv_ref, log_ref, cos_ref, sin_ref, mask_ref, out_ref, keys_acc, values_acc):
    tokens, heads = g_ref.shape[0], mask_ref.shape[1]
    width = heads * HD
    block = min(Q_BLOCK, tokens)
    scale = 1.0 / math.sqrt(HD)
    for start in range(0, tokens, block):
        here, end = slice(start, start + block), start + block
        cos, sin = cos_ref[here, :], sin_ref[here, :]
        rows = narrow(product(g_ref[here, :], w_ref[...], (1, 0)))
        for head in range(heads):
            at = head * HD
            lanes, key_lanes, value_lanes = (slice(at + p * width, at + p * width + HD) for p in range(3))
            heads_grad = rows[:, lanes] * narrow(mask_ref[here, head : head + 1])
            queries, keys_all = qkv_ref[here, lanes], qkv_ref[:end, key_lanes]
            scores = block_scores(queries, keys_all, start)
            probs = jnp.exp(scores - log_ref[here, head : head + 1])
            values_part = product(narrow(probs), heads_grad, (0, 0))
            probs_grad = product(heads_grad, qkv_ref[:end, value_lanes], (1, 1))
            centre = jnp.sum(probs * probs_grad, axis=1, keepdims=True)
            score_grad = narrow(probs * (probs_grad - centre))
            queries_grad = product(score_grad, keys_all, (1, 0)) * scale
            keys_part = product(score_grad, queries, (0, 0)) * scale
            turned = queries_grad * cos - pltpu.roll(queries_grad, HD // 2, 1) * sin
            out_ref[here, lanes] = narrow(turned)
            if start:
                values_acc[:start, lanes] += values_part[:start]
                keys_acc[:start, lanes] += keys_part[:start]
            values_acc[here, lanes] = values_part[start:]
            keys_acc[here, lanes] = keys_part[start:]
    for start in range(0, tokens, block):
        here = slice(start, start + block)
        cos, sin = cos_ref[here, :], sin_ref[here, :]
        out_ref[here, 2 * width :] = narrow(values_acc[here, :])
        for head in range(heads):
            at = head * HD
            value = keys_acc[here, at : at + HD]
            out_ref[here, width + at : width + at + HD] = narrow(value * cos - pltpu.roll(value, HD // 2, 1) * sin)


def share_kernel(side_ref, *refs):
    *given, out_ref = refs
    total = product(given[0][...], given[1][...], (1, 1))
    for a_ref, w_ref in zip(given[2::2], given[3::2]):
        total = total + product(a_ref[...], w_ref[...], (1, 1))
    out_ref[0] = narrow(total)


def weight_kernel(x_ref, q_ref, g_ref, h_ref, *outs):
    width = h_ref.shape[1]
    half = x_ref.shape[1] // 2
    for lane, out_ref in enumerate(outs):
        here = slice(lane * half, (lane + 1) * half)
        out_ref[0, :, : 3 * width] = narrow(product(x_ref[:, here], q_ref[...], (0, 0)))
        out_ref[0, :, 3 * width :] = narrow(product(g_ref[:, here], h_ref[...], (0, 0)))


def place_kernel(count, widths, turned, at_ref, *refs):
    lanes = (len(refs) - len(widths)) // count
    blocks, outs = refs[: lanes * count], refs[lanes * count :]
    half = blocks[0].shape[0]
    for far in range(count):

        @pl.when((pl.program_id(0) ^ at_ref[0]) == far)
        def _():
            for lane in range(lanes):
                here = slice(lane * half, (lane + 1) * half)
                block = blocks[lane * count + far]
                start = 0
                for out_ref, width, turn in zip(outs, widths, turned):
                    for part in range(out_ref.shape[0] if len(out_ref.shape) == 3 else 1):
                        value = block[:, start : start + width].astype(out_ref.dtype)
                        start += width
                        if turn:
                            out_ref[:, here] = value.T
                        elif len(out_ref.shape) == 3:
                            out_ref[part, here, :] = value
                        else:
                            out_ref[here, :] = value


VMEM_LIMIT = 56 * 1024 * 1024


def whole_specs(count):
    return [pl.BlockSpec(memory_space=pltpu.VMEM)] * count


def attend_forward(x, w, cos, sin, mask):
    tokens, heads = mask.shape
    dim, width = w.shape[0], heads * HD
    return pl.pallas_call(
        forward_kernel,
        out_shape=[
            jax.ShapeDtypeStruct((tokens, 3 * width), jnp.bfloat16),
            jax.ShapeDtypeStruct((tokens, width), jnp.bfloat16),
            jax.ShapeDtypeStruct((tokens, heads), jnp.float32),
        ],
        in_specs=whole_specs(5),
        out_specs=whole_specs(3),
        compiler_params=pltpu.CompilerParams(vmem_limit_bytes=VMEM_LIMIT),
        cost_estimate=pl.CostEstimate(
            flops=6 * tokens * dim * width + 2 * tokens * tokens * width,
            bytes_accessed=12 << 20,
            transcendentals=tokens * tokens * heads // 2,
        ),
        name="attend_forward",
    )(x, w, cos, sin, mask)


def attend_backward(g, w, qkv, log_total, cos, sin, mask):
    tokens, heads = mask.shape
    dim, width = w.shape[0], heads * HD
    return pl.pallas_call(
        backward_kernel,
        out_shape=jax.ShapeDtypeStruct((tokens, 3 * width), jnp.bfloat16),
        in_specs=whole_specs(7),
        out_specs=whole_specs(1)[0],
        scratch_shapes=[pltpu.VMEM((tokens, width), jnp.float32)] * 2,
        compiler_params=pltpu.CompilerParams(vmem_limit_bytes=VMEM_LIMIT),
        cost_estimate=pl.CostEstimate(
            flops=2 * tokens * dim * width + 5 * tokens * tokens * width,
            bytes_accessed=12 << 20,
            transcendentals=tokens * tokens * heads // 2,
        ),
        name="attend_backward",
    )(g, w, qkv, log_total, cos, sin, mask)


def share_of(pairs, rows, side):
    tokens, depth = pairs[0][0].shape
    dim = pairs[0][1].shape[0]
    chips = tokens // rows // 2
    specs = [
        pl.BlockSpec((rows, depth), lambda i, side: (2 * i + side[0], 0)),
        pl.BlockSpec((dim, depth), lambda i, side: (0, 0)),
    ] * len(pairs)
    return pl.pallas_call(
        share_kernel,
        grid_spec=pltpu.PrefetchScalarGridSpec(
            num_scalar_prefetch=1,
            grid=(chips,),
            in_specs=specs,
            out_specs=pl.BlockSpec((1, rows, dim), lambda i, side: (i, 0, 0)),
        ),
        out_shape=jax.ShapeDtypeStruct((chips, rows, dim), jnp.bfloat16),
        compiler_params=pltpu.CompilerParams(vmem_limit_bytes=VMEM_LIMIT),
        cost_estimate=pl.CostEstimate(
            flops=tokens * dim * depth * len(pairs), bytes_accessed=12 << 20, transcendentals=0
        ),
        name="share_of",
    )(side.astype(jnp.int32).reshape(1), *[x for pair in pairs for x in pair])


def weight_grads(x, qkv_grad, g, heads_out, count):
    tokens, dim = x.shape
    width = heads_out.shape[1]
    block = dim // count
    out = jax.ShapeDtypeStruct((count, block // 2, 4 * width), jnp.bfloat16)
    return pl.pallas_call(
        weight_kernel,
        grid=(count,),
        out_shape=[out, out],
        in_specs=[
            pl.BlockSpec((tokens, block), lambda i: (0, i)),
            pl.BlockSpec((tokens, 3 * width), lambda i: (0, 0)),
            pl.BlockSpec((tokens, block), lambda i: (0, i)),
            pl.BlockSpec((tokens, width), lambda i: (0, 0)),
        ],
        out_specs=[pl.BlockSpec((1, block // 2, 4 * width), lambda i: (i, 0, 0))] * 2,
        compiler_params=pltpu.CompilerParams(vmem_limit_bytes=VMEM_LIMIT),
        cost_estimate=pl.CostEstimate(flops=8 * tokens * dim * width, bytes_accessed=14 << 20, transcendentals=0),
        name="weight_grads",
    )(x, qkv_grad, g, heads_out)


def place_blocks(lanes, index, outs):
    count = len(lanes[0])
    half, total = lanes[0][0].shape
    rows = len(lanes) * half
    shapes, specs = [], []
    for planes, width, kind, turned in outs:
        if turned:
            shapes.append(jax.ShapeDtypeStruct((width, rows * count), kind))
            specs.append(pl.BlockSpec((width, rows), lambda i, at: (0, i)))
        elif planes > 1:
            shapes.append(jax.ShapeDtypeStruct((planes, rows * count, width), kind))
            specs.append(pl.BlockSpec((planes, rows, width), lambda i, at: (0, i, 0)))
        else:
            shapes.append(jax.ShapeDtypeStruct((rows * count, width), kind))
            specs.append(pl.BlockSpec((rows, width), lambda i, at: (i, 0)))
    given = [held[far] for held in lanes for far in range(count)]
    return pl.pallas_call(
        functools.partial(place_kernel, count, [o[1] for o in outs], [o[3] for o in outs]),
        grid_spec=pltpu.PrefetchScalarGridSpec(
            num_scalar_prefetch=1,
            grid=(count,),
            in_specs=[pl.BlockSpec((half, total), lambda i, at: (0, 0))] * len(given),
            out_specs=specs,
        ),
        out_shape=shapes,
        compiler_params=pltpu.CompilerParams(vmem_limit_bytes=VMEM_LIMIT),
        cost_estimate=pl.CostEstimate(flops=0, bytes_accessed=12 << 20, transcendentals=0),
        name="place_blocks",
    )(index.astype(jnp.int32).reshape(1), *given)


def swap_pairs(size, bit):
    return [(i, i ^ bit) for i in range(size)]


def shift_pairs(size, shift):
    return [(i, (i - shift) % size) for i in range(size)]


def bits_of(size):
    return [1 << i for i in range(size.bit_length() - 1)]


def pick(x, index, axis=0):
    return lax.dynamic_index_in_dim(x, index, axis, keepdims=False)


def after(x, *others):
    return lax.optimization_barrier((x,) + others)[0]


def xor_gather(x, axis, size, bits):
    held = dict(x) if isinstance(x, dict) else {0: x}
    for bit in bits:
        for far in list(held):
            held[far ^ bit] = lax.ppermute(held[far], axis, swap_pairs(size, bit))
    return held


def by_index(held, index, axis=0):
    shape = held[0].shape
    out = jnp.zeros(shape[:axis] + (len(held),) + shape[axis:], held[0].dtype)
    for far, block in held.items():
        out = lax.dynamic_update_index_in_dim(out, block, index ^ far, axis)
    return out


def xor_scatter(blocks, axis_name, size, bits, steps, index, axis, all_steps=None):
    all_steps = list(all_steps or steps)
    left = sorted(all_steps[all_steps.index(steps[0]) :], reverse=True)
    blocks = blocks.reshape(blocks.shape[:axis] + (2,) * len(left) + blocks.shape[axis + 1 :])
    for bit, step in zip(bits, steps):
        at = axis + left.index(step)
        left.remove(step)
        side = (index // step) % 2
        got = lax.ppermute(narrow(pick(blocks, 1 - side, at)), axis_name, swap_pairs(size, bit))
        blocks = wide(pick(blocks, side, at)) + wide(got)
    tail = blocks.shape[axis + len(left) :]
    return blocks.reshape(blocks.shape[:axis] + ((2 ** len(left),) if left else ()) + tail)


def lane_bits(size):
    return bits_of(size), bits_of(size)[::-1]


def column_gather(lanes, size, cut=None, start=None):
    return [xor_gather(x, "dp", size, bits[start:cut]) for x, bits in zip(lanes, lane_bits(size))]


def gate_lanes(lanes, *gates):
    flat = [held[far] for held in lanes for far in held]
    flat = lax.optimization_barrier((*flat, *gates))
    flat = iter(flat)
    return [{far: next(flat) for far in held} for held in lanes]


def column_scatter(lanes, size, column, cut=None, start=None):
    return [
        xor_scatter(x, "dp", size, bits[start:cut], bits[start:cut], column, 0, bits)
        for x, bits in zip(lanes, lane_bits(size))
    ]


def all_sum(x, sizes):
    for axis, size in sizes.items():
        for bit in bits_of(size):
            x = x + lax.ppermute(x, axis, swap_pairs(size, bit))
    return x


def make_local(columns, ranks):
    def local(
        layer_input, width_choice, routed_flag, mixer_gain, mixer_router, attention_weight,
        output_weight, hidden_gain, hidden_router, up_weight, down_weight, out_grad,
    ):
        column, rank = lax.axis_index("dp"), lax.axis_index("mp")
        rows, dim = layer_input.shape
        core = rank % 2
        group = SEQ_LEN // rows
        sequences = ranks // group
        place, sequence = rank % group, rank // group
        pair_bits = [b for b in bits_of(group) if b > 1]
        own_heads = output_weight.shape[0] // HD
        cols_local = up_weight.shape[1]
        width_own = lax.dynamic_slice_in_dim(width_choice, rank * rows, rows, 0)
        routed_own = lax.dynamic_slice_in_dim(routed_flag, rank * rows, rows, 0)
        cos, sin = rope_tables(SEQ_LEN, HD)

        def place_sequence(held):
            return by_index(held, place).reshape(SEQ_LEN, -1)

        def core_sum(pairs):
            theirs = share_of(pairs, rows, 1 - core)
            got = lax.ppermute(theirs, "mp", swap_pairs(ranks, 1))
            pairs, theirs = lax.optimization_barrier((pairs, theirs))
            return wide(share_of(pairs, rows, core)) + wide(got)

        def chip_sum(blocks):
            bits = pair_bits[::-1]
            return xor_scatter(blocks, "mp", ranks, bits, [b // 2 for b in bits], place // 2, 0)

        width = own_heads * HD
        chunk_rows = dim // columns
        half_rows = chunk_rows // 2

        def in_slice(w):
            return jnp.concatenate([w[:, p] for p in range(3)], axis=1)

        lanes_in = [
            in_slice(lax.dynamic_slice_in_dim(attention_weight, column * chunk_rows + at, half_rows, 0))
            for at in (0, half_rows)
        ]
        lanes_out = [
            lax.dynamic_slice_in_dim(output_weight, column * chunk_rows + at, half_rows, 1).T
            for at in (0, half_rows)
        ]
        input_wide = wide(layer_input)
        normed_one, scaled_one, inverse_one = norm_forward(input_wide, mixer_gain)
        low_one = narrow(normed_one)
        low_one, lanes_in, lanes_out = lax.optimization_barrier((low_one, lanes_in, lanes_out))
        held = xor_gather(low_one, "mp", ranks, pair_bits)
        fetched_in, fetched_out = [
            [[lax.ppermute(x, "mp", shift_pairs(ranks, k * group)) for x in lanes] for k in range(1, sequences)]
            for lanes in (lanes_in, lanes_out)
        ]
        sequence_width = lax.dynamic_slice_in_dim(width_choice[:, 0], sequence * SEQ_LEN, SEQ_LEN, 0)
        masks = []
        for k in range(sequences):
            heads = ((rank + k * group) % ranks) * own_heads + jnp.arange(own_heads, dtype=jnp.int32)
            masks.append((heads[None, :] * 4 < (sequence_width[:, None] + 1) * H).astype(jnp.float32))
        weights_in, weights_out = [in_slice(attention_weight)], [output_weight.T]
        held, fetched_in, masks, weights_in, weights_out, cos, sin = lax.optimization_barrier(
            (held, fetched_in, masks, weights_in, weights_out, cos, sin)
        )
        inputs_one = place_sequence(xor_gather(held, "mp", ranks, [1]))
        grads_all = lax.all_gather(after(out_grad, *[x for lanes in fetched_in for x in lanes]), "mp", axis=0, tiled=True)
        steps_in = [column_gather(x, columns, cut=1) for x in fetched_in]
        gate_one, state_one = gate_forward(normed_one, mixer_router, width_own[:, 0], routed_own[:, 0])

        kept = []
        for k in range(sequences):
            mask = masks[k]
            if k:
                steps, fetched, _ = lax.optimization_barrier((steps_in[k - 1], fetched_out[k - 1], kept[0][0]))
                held = column_gather(steps, columns, start=1)
                held_out = column_gather(fetched, columns, cut=1)
                held, held_out = lax.optimization_barrier((held, held_out))
                held_out = column_gather(held_out, columns, start=1)
                weights_in += place_blocks(held, column, [(1, 3 * width, jnp.bfloat16, False)])
                weights_out += place_blocks(held_out, column, [(1, width, jnp.bfloat16, False)])
            kept.append((*attend_forward(inputs_one, weights_in[k], cos, sin, mask), mask))
        mixer_branch = chip_sum(core_sum([(x[1], w) for x, w in zip(kept, weights_out)]))
        mixer_branch, grads_all = lax.optimization_barrier((mixer_branch, grads_all))
        top_down = product(grads_all, down_weight, (1, 1))

        middle = input_wide + gate_one[:, None] * mixer_branch
        normed_two, scaled_two, inverse_two = norm_forward(middle, hidden_gain)
        gate_two, state_two = gate_forward(normed_two, hidden_router, width_own[:, 1], routed_own[:, 1])
        inputs_two = lax.all_gather(narrow(normed_two), "mp", axis=0, tiled=True)
        gates = by_index(xor_gather(gate_two.reshape(-1, 128), "mp", ranks, bits_of(ranks)), rank).reshape(-1)

        col_ids = rank * cols_local + jnp.arange(cols_local, dtype=jnp.int32)
        col_mask = (col_ids[None, :] * 4 < (width_choice[:, 1:2] + 1) * FF).astype(jnp.float32)
        inputs_two, top_down = lax.optimization_barrier((inputs_two, top_down))
        pre = product(inputs_two, up_weight, (1, 0))
        relu_act = jax.nn.relu(pre)
        hidden = narrow(relu_act * relu_act * col_mask)
        pre_grad = narrow(top_down * gates[:, None] * col_mask * 2.0 * relu_act)
        dots = jnp.sum(wide(hidden) * top_down, axis=1).reshape(-1, 128)
        share = narrow(product(pre_grad, up_weight, (1, 1)))
        share, hidden, pre_grad = lax.optimization_barrier((share, hidden, pre_grad))
        normed_grad_two = wide(lax.psum_scatter(share, "mp", scatter_dimension=0, tiled=True))
        gate_grad_two = lax.dynamic_slice_in_dim(all_sum(dots, {"mp": ranks}).reshape(-1), rank * rows, rows, 0)
        gated = narrow(gates[:, None] * wide(grads_all))
        lanes = [narrow(product(hidden, gated, (0, 0))), narrow(product(inputs_two, pre_grad, (0, 0)))]
        lanes = [x.reshape(columns, -1, x.shape[1]) for x in lanes]
        lanes = column_scatter(lanes, columns, column, cut=1)
        hidden_share = narrow(product(hidden, down_weight, (1, 0)))
        normed_grad_two, hidden_share, *lanes = lax.optimization_barrier((normed_grad_two, hidden_share, *lanes))
        lanes = [narrow(x) for x in column_scatter(lanes, columns, column, start=1)]

        router_part, router_two = gate_backward(normed_two, hidden_router, state_two, gate_grad_two)
        middle_part, gain_two = norm_backward(normed_grad_two + router_part, scaled_two, inverse_two, hidden_gain)
        middle_grad = wide(out_grad) + middle_part
        grads_one = place_sequence(
            xor_gather(narrow(gate_one[:, None] * middle_grad), "mp", ranks, pair_bits + [1])
        )
        helds = column_gather(lanes, columns, cut=1)
        grads_one, hidden_share, lanes = lax.optimization_barrier((grads_one, hidden_share, lanes))
        hidden_branch = wide(lax.psum_scatter(hidden_share, "mp", scatter_dimension=0, tiled=True))
        layer_output = narrow(middle + gate_two[:, None] * hidden_branch)

        gate_grad_one = jnp.sum(middle_grad * mixer_branch, axis=1)
        pairs, sent = [], []
        grads_now = grads_one
        for k in range(sequences)[::-1]:
            qkv, heads_out, log_total, mask = kept[k]
            qkv_grad = attend_backward(grads_now, weights_out[k], qkv, log_total, cos, sin, mask)
            pairs.append((qkv_grad, weights_in[k]))
            if k == 0:
                helds = column_gather(helds, columns, start=1)
                qkv_grad, helds = lax.optimization_barrier((qkv_grad, helds))
            part = weight_grads(inputs_one, qkv_grad, grads_one, heads_out, columns)
            if k:
                grads_now, part, helds = lax.optimization_barrier((grads_now, part, helds))
                sent.append((k, part))
        blocks = core_sum(pairs)
        sent = [(k, column_scatter(lanes, columns, column, cut=1)) for k, lanes in sent]
        blocks, gated = lax.optimization_barrier((blocks, [lanes for _, lanes in sent]))
        sent = [(k, lanes) for (k, _), lanes in zip(sent, gated)]
        normed_grad_one = chip_sum(blocks)
        pieces = column_scatter(part, columns, column)
        for k, lanes in sent:
            lanes = [narrow(x) for x in column_scatter(lanes, columns, column, start=1)]
            back = shift_pairs(ranks, -k * group)
            pieces = [p + wide(lax.ppermute(x, "mp", back)) for p, x in zip(pieces, lanes)]
        spread = column_gather([narrow(p) for p in pieces], columns, cut=1)
        spread, helds = lax.optimization_barrier((spread, helds))
        spread = column_gather(spread, columns, start=1)
        down_sum, = place_blocks(helds[:1], column, [(1, dim, jnp.float32, False)])
        up_sum, = place_blocks(helds[1:], column, [(1, cols_local, jnp.float32, False)])
        attention_sum, output_sum = place_blocks(
            spread,
            column,
            [(3, width, jnp.float32, False), (1, width, jnp.float32, True)],
        )
        attention_sum = attention_sum.transpose(1, 0, 2)

        router_part_one, router_one = gate_backward(normed_one, mixer_router, state_one, gate_grad_one)
        input_part, gain_one = norm_backward(normed_grad_one + router_part_one, scaled_one, inverse_one, mixer_gain)
        input_grad = narrow(middle_grad + input_part)

        sizes = {"mp": ranks, "dp": columns}

        smalls = [gain_two, gain_one, router_two.T, router_one.T]
        small_sum = all_sum(jnp.concatenate([x.reshape(-1, 128) for x in smalls], axis=0), sizes)
        cuts = [dim // 128, 2 * dim // 128, (2 * dim + router_two.size) // 128]
        hidden_gain_sum, mixer_gain_sum, hidden_router_sum, mixer_router_sum = (
            x.reshape(-1, dim) for x in jnp.split(small_sum, cuts)
        )
        hidden_gain_sum, mixer_gain_sum = hidden_gain_sum[0], mixer_gain_sum[0]
        hidden_router_sum, mixer_router_sum = hidden_router_sum.T, mixer_router_sum.T
        return (
            layer_output, input_grad, mixer_gain_sum, mixer_router_sum, attention_sum, output_sum,
            hidden_gain_sum, hidden_router_sum, up_sum, down_sum,
        )

    return local


def solution(mesh):
    return jax.shard_map(
        make_local(mesh.shape["dp"], mesh.shape["mp"]),
        mesh=mesh,
        in_specs=(
            P(("dp", "mp"), None),
            P("dp", None),
            P("dp", None),
            P(),
            P(),
            P(None, None, "mp"),
            P("mp", None),
            P(),
            P(),
            P(None, "mp"),
            P("mp", None),
            P(("dp", "mp"), None),
        ),
        out_specs=(
            P(("dp", "mp"), None),
            P(("dp", "mp"), None),
            P(),
            P(),
            P(None, None, "mp"),
            P("mp", None),
            P(),
            P(),
            P(None, "mp"),
            P("mp", None),
        ),
        check_vma=False,
    )
```

```python
import functools
import math

import jax
import jax.numpy as jnp
from jax import lax
from jax.experimental import pallas as pl
from jax.experimental.pallas import tpu as pltpu
from jax.sharding import PartitionSpec as P

H = 16
HD = 128
FF = 8192
SEQ_LEN = 1024


EPSILON = 1e-05
NEG_LARGE = -1e30
HIGHEST = lax.Precision.HIGHEST


def norm_forward(values, gain_vec):
    row_mean = jnp.mean(values, axis=1, keepdims=True)
    centred = values - row_mean
    row_variance = jnp.mean(centred * centred, axis=1, keepdims=True)
    inverse_scale = lax.rsqrt(row_variance + EPSILON)
    scaled = centred * inverse_scale
    return (scaled * gain_vec[None, :], scaled, inverse_scale)


def norm_backward(normed_grad, scaled, inverse_scale, gain_vec):
    gain_grad = jnp.sum(normed_grad * scaled, axis=0)
    scaled_grad = normed_grad * gain_vec[None, :]
    first_mean = jnp.mean(scaled_grad, axis=1, keepdims=True)
    second_mean = jnp.mean(scaled_grad * scaled, axis=1, keepdims=True)
    return (inverse_scale * (scaled_grad - first_mean - scaled * second_mean), gain_grad)


def gate_forward(normed, router, width_col, routed_col):
    logits = jnp.dot(normed, router, precision=HIGHEST, preferred_element_type=jnp.float32)
    soft_probs = jax.nn.softmax(logits, axis=1)
    one_hot = (width_col[:, None] == jnp.arange(4, dtype=jnp.int32)[None, :]).astype(jnp.float32)
    chosen = jnp.sum(soft_probs * one_hot, axis=1)
    route_flags = routed_col.astype(jnp.float32)
    return (
        route_flags * 4.0 * chosen + (1.0 - route_flags),
        (soft_probs, one_hot, chosen, route_flags),
    )


def gate_backward(normed, router, gate_state, gate_grad):
    soft_probs, one_hot, chosen, route_flags = gate_state
    coefficient = route_flags * 4.0 * chosen * gate_grad
    logit_grad = coefficient[:, None] * (one_hot - soft_probs)
    router_grad = lax.dot_general(
        normed,
        logit_grad,
        (((0,), (0,)), ((), ())),
        precision=HIGHEST,
        preferred_element_type=jnp.float32,
    )
    normed_grad = lax.dot_general(
        logit_grad,
        router,
        (((1,), (1,)), ((), ())),
        precision=HIGHEST,
        preferred_element_type=jnp.float32,
    )
    return (normed_grad, router_grad)


Q_BLOCK = 256


def rope_tables(token_count, head_width):
    positions = jnp.arange(token_count, dtype=jnp.float32)
    frequency = jnp.exp(
        jnp.arange(head_width // 2, dtype=jnp.float32) * (-2.0 * math.log(10000.0) / head_width)
    )
    angles = positions[:, None] * frequency[None, :]
    cosine, sine = jnp.cos(angles), jnp.sin(angles)
    return jnp.concatenate([cosine, cosine], axis=1), jnp.concatenate([-sine, sine], axis=1)


def wide(x):
    return x.astype(jnp.float32)


def narrow(x):
    return x.astype(jnp.bfloat16)


def product(a, b, dims):
    return lax.dot_general(a, b, ((dims[:1], dims[1:]), ((), ())), preferred_element_type=jnp.float32)


def block_scores(queries, keys_all, start):
    scores = product(queries, keys_all, (1, 1)) * (1.0 / math.sqrt(HD))
    row = lax.broadcasted_iota(jnp.int32, scores.shape, 0) + start
    col = lax.broadcasted_iota(jnp.int32, scores.shape, 1)
    return jnp.where(col <= row, scores, NEG_LARGE)


def forward_kernel(x_ref, w_ref, cos_ref, sin_ref, mask_ref, qkv_ref, heads_ref, log_ref):
    tokens, heads = x_ref.shape[0], mask_ref.shape[1]
    width = heads * HD
    block = min(Q_BLOCK, tokens)
    for start in range(0, tokens, block):
        here, end = slice(start, start + block), start + block
        x = x_ref[here, :]
        cos, sin = cos_ref[here, :], sin_ref[here, :]
        for part in range(3):
            rows = product(x, w_ref[:, part * width : (part + 1) * width], (1, 0))
            for head in range(heads):
                value = rows[:, head * HD : (head + 1) * HD]
                if part < 2:
                    value = value * cos + pltpu.roll(value, HD // 2, 1) * sin
                at = part * width + head * HD
                qkv_ref[here, at : at + HD] = narrow(value)
        for head in range(heads):
            at = head * HD
            lanes, key_lanes, value_lanes = (slice(at + p * width, at + p * width + HD) for p in range(3))
            scores = block_scores(qkv_ref[here, lanes], qkv_ref[:end, key_lanes], start)
            row_max = jnp.max(scores, axis=1, keepdims=True)
            shifted = jnp.exp(scores - row_max)
            total = jnp.sum(shifted, axis=1, keepdims=True)
            mix = product(narrow(shifted * (1.0 / total)), qkv_ref[:end, value_lanes], (1, 0))
            heads_ref[here, lanes] = narrow(mix * mask_ref[here, head : head + 1])
            log_ref[here, head : head + 1] = row_max + jnp.log(total)


def backward_kernel(g_ref, w_ref, qkv_ref, log_ref, cos_ref, sin_ref, mask_ref, out_ref, keys_acc, values_acc):
    tokens, heads = g_ref.shape[0], mask_ref.shape[1]
    width = heads * HD
    block = min(Q_BLOCK, tokens)
    scale = 1.0 / math.sqrt(HD)
    for start in range(0, tokens, block):
        here, end = slice(start, start + block), start + block
        cos, sin = cos_ref[here, :], sin_ref[here, :]
        rows = narrow(product(g_ref[here, :], w_ref[...], (1, 0)))
        for head in range(heads):
            at = head * HD
            lanes, key_lanes, value_lanes = (slice(at + p * width, at + p * width + HD) for p in range(3))
            heads_grad = rows[:, lanes] * narrow(mask_ref[here, head : head + 1])
            queries, keys_all = qkv_ref[here, lanes], qkv_ref[:end, key_lanes]
            scores = block_scores(queries, keys_all, start)
            probs = jnp.exp(scores - log_ref[here, head : head + 1])
            values_part = product(narrow(probs), heads_grad, (0, 0))
            probs_grad = product(heads_grad, qkv_ref[:end, value_lanes], (1, 1))
            centre = jnp.sum(probs * probs_grad, axis=1, keepdims=True)
            score_grad = narrow(probs * (probs_grad - centre))
            queries_grad = product(score_grad, keys_all, (1, 0)) * scale
            keys_part = product(score_grad, queries, (0, 0)) * scale
            turned = queries_grad * cos - pltpu.roll(queries_grad, HD // 2, 1) * sin
            out_ref[here, lanes] = narrow(turned)
            if start:
                values_acc[:start, lanes] += values_part[:start]
                keys_acc[:start, lanes] += keys_part[:start]
            values_acc[here, lanes] = values_part[start:]
            keys_acc[here, lanes] = keys_part[start:]
    for start in range(0, tokens, block):
        here = slice(start, start + block)
        cos, sin = cos_ref[here, :], sin_ref[here, :]
        out_ref[here, 2 * width :] = narrow(values_acc[here, :])
        for head in range(heads):
            at = head * HD
            value = keys_acc[here, at : at + HD]
            out_ref[here, width + at : width + at + HD] = narrow(value * cos - pltpu.roll(value, HD // 2, 1) * sin)


def share_kernel(side_ref, *refs):
    *given, out_ref = refs
    total = product(given[0][...], given[1][...], (1, 1))
    for a_ref, w_ref in zip(given[2::2], given[3::2]):
        total = total + product(a_ref[...], w_ref[...], (1, 1))
    out_ref[0] = narrow(total)


def weight_kernel(x_ref, q_ref, g_ref, h_ref, *outs):
    width = h_ref.shape[1]
    half = x_ref.shape[1] // 2
    for lane, out_ref in enumerate(outs):
        here = slice(lane * half, (lane + 1) * half)
        out_ref[0, :, : 3 * width] = narrow(product(x_ref[:, here], q_ref[...], (0, 0)))
        out_ref[0, :, 3 * width :] = narrow(product(g_ref[:, here], h_ref[...], (0, 0)))


def hidden_kernel(offset_ref, x_ref, up_ref, top_ref, gate_ref, width_ref, share_ref, hidden_ref, grad_ref, dots_ref):
    pre = product(x_ref[...], up_ref[...], (1, 0))
    column = lax.broadcasted_iota(jnp.int32, pre.shape, 1) + offset_ref[0]
    live = column * 4 < (width_ref[...] + 1) * FF
    relu_act = jnp.where(live, jnp.maximum(pre, 0.0), 0.0)
    hidden = narrow(relu_act * relu_act)
    top = top_ref[...]
    grad = narrow(top * gate_ref[...] * 2.0 * relu_act)
    hidden_ref[...] = hidden
    grad_ref[...] = grad
    dots = jnp.sum(wide(hidden) * top, axis=1, keepdims=True)
    dots_ref[...] = jnp.broadcast_to(dots, (dots.shape[0], 128)).T[:1]
    share_ref[...] = narrow(product(grad, up_ref[...], (1, 1)))


def place_kernel(count, widths, turned, at_ref, *refs):
    lanes = (len(refs) - len(widths)) // count
    blocks, outs = refs[: lanes * count], refs[lanes * count :]
    half = blocks[0].shape[0]
    for far in range(count):

        @pl.when((pl.program_id(0) ^ at_ref[0]) == far)
        def _():
            for lane in range(lanes):
                here = slice(lane * half, (lane + 1) * half)
                block = blocks[lane * count + far]
                start = 0
                for out_ref, width, turn in zip(outs, widths, turned):
                    for part in range(out_ref.shape[0] if len(out_ref.shape) == 3 else 1):
                        value = block[:, start : start + width].astype(out_ref.dtype)
                        start += width
                        if turn:
                            out_ref[:, here] = value.T
                        elif len(out_ref.shape) == 3:
                            out_ref[part, here, :] = value
                        else:
                            out_ref[here, :] = value


VMEM_LIMIT = 56 * 1024 * 1024


def whole_specs(count):
    return [pl.BlockSpec(memory_space=pltpu.VMEM)] * count


def attend_forward(x, w, cos, sin, mask):
    tokens, heads = mask.shape
    dim, width = w.shape[0], heads * HD
    return pl.pallas_call(
        forward_kernel,
        out_shape=[
            jax.ShapeDtypeStruct((tokens, 3 * width), jnp.bfloat16),
            jax.ShapeDtypeStruct((tokens, width), jnp.bfloat16),
            jax.ShapeDtypeStruct((tokens, heads), jnp.float32),
        ],
        in_specs=whole_specs(5),
        out_specs=whole_specs(3),
        compiler_params=pltpu.CompilerParams(vmem_limit_bytes=VMEM_LIMIT),
        cost_estimate=pl.CostEstimate(
            flops=6 * tokens * dim * width + 2 * tokens * tokens * width,
            bytes_accessed=12 << 20,
            transcendentals=tokens * tokens * heads // 2,
        ),
        name="attend_forward",
    )(x, w, cos, sin, mask)


def attend_backward(g, w, qkv, log_total, cos, sin, mask):
    tokens, heads = mask.shape
    dim, width = w.shape[0], heads * HD
    return pl.pallas_call(
        backward_kernel,
        out_shape=jax.ShapeDtypeStruct((tokens, 3 * width), jnp.bfloat16),
        in_specs=whole_specs(7),
        out_specs=whole_specs(1)[0],
        scratch_shapes=[pltpu.VMEM((tokens, width), jnp.float32)] * 2,
        compiler_params=pltpu.CompilerParams(vmem_limit_bytes=VMEM_LIMIT),
        cost_estimate=pl.CostEstimate(
            flops=2 * tokens * dim * width + 5 * tokens * tokens * width,
            bytes_accessed=12 << 20,
            transcendentals=tokens * tokens * heads // 2,
        ),
        name="attend_backward",
    )(g, w, qkv, log_total, cos, sin, mask)


def share_of(pairs, rows, side):
    tokens, depth = pairs[0][0].shape
    dim = pairs[0][1].shape[0]
    chips = tokens // rows // 2
    specs = [
        pl.BlockSpec((rows, depth), lambda i, side: (2 * i + side[0], 0)),
        pl.BlockSpec((dim, depth), lambda i, side: (0, 0)),
    ] * len(pairs)
    return pl.pallas_call(
        share_kernel,
        grid_spec=pltpu.PrefetchScalarGridSpec(
            num_scalar_prefetch=1,
            grid=(chips,),
            in_specs=specs,
            out_specs=pl.BlockSpec((1, rows, dim), lambda i, side: (i, 0, 0)),
        ),
        out_shape=jax.ShapeDtypeStruct((chips, rows, dim), jnp.bfloat16),
        compiler_params=pltpu.CompilerParams(vmem_limit_bytes=VMEM_LIMIT),
        cost_estimate=pl.CostEstimate(
            flops=tokens * dim * depth * len(pairs), bytes_accessed=12 << 20, transcendentals=0
        ),
        name="share_of",
    )(side.astype(jnp.int32).reshape(1), *[x for pair in pairs for x in pair])


def hidden_pass(x, up, top_down, gates, widths, offset):
    tokens, dim = x.shape
    cols = up.shape[1]
    block = 256
    rows_of = lambda n: pl.BlockSpec((block, n), lambda i, at: (i, 0))
    return pl.pallas_call(
        hidden_kernel,
        grid_spec=pltpu.PrefetchScalarGridSpec(
            num_scalar_prefetch=1,
            grid=(tokens // block,),
            in_specs=[rows_of(dim), pl.BlockSpec((dim, cols), lambda i, at: (0, 0)), rows_of(cols), rows_of(1), rows_of(1)],
            out_specs=[rows_of(dim), rows_of(cols), rows_of(cols), pl.BlockSpec((1, block), lambda i, at: (0, i))],
        ),
        out_shape=[
            jax.ShapeDtypeStruct((tokens, dim), jnp.bfloat16),
            jax.ShapeDtypeStruct((tokens, cols), jnp.bfloat16),
            jax.ShapeDtypeStruct((tokens, cols), jnp.bfloat16),
            jax.ShapeDtypeStruct((1, tokens), jnp.float32),
        ],
        compiler_params=pltpu.CompilerParams(vmem_limit_bytes=VMEM_LIMIT),
        cost_estimate=pl.CostEstimate(flops=4 * tokens * dim * cols, bytes_accessed=40 << 20, transcendentals=0),
        name="hidden_pass",
    )(offset.astype(jnp.int32).reshape(1), x, up, top_down, gates[:, None], widths)


def weight_grads(x, qkv_grad, g, heads_out, count):
    tokens, dim = x.shape
    width = heads_out.shape[1]
    block = dim // count
    out = jax.ShapeDtypeStruct((count, block // 2, 4 * width), jnp.bfloat16)
    return pl.pallas_call(
        weight_kernel,
        grid=(count,),
        out_shape=[out, out],
        in_specs=[
            pl.BlockSpec((tokens, block), lambda i: (0, i)),
            pl.BlockSpec((tokens, 3 * width), lambda i: (0, 0)),
            pl.BlockSpec((tokens, block), lambda i: (0, i)),
            pl.BlockSpec((tokens, width), lambda i: (0, 0)),
        ],
        out_specs=[pl.BlockSpec((1, block // 2, 4 * width), lambda i: (i, 0, 0))] * 2,
        compiler_params=pltpu.CompilerParams(vmem_limit_bytes=VMEM_LIMIT),
        cost_estimate=pl.CostEstimate(flops=8 * tokens * dim * width, bytes_accessed=14 << 20, transcendentals=0),
        name="weight_grads",
    )(x, qkv_grad, g, heads_out)


def place_blocks(lanes, index, outs):
    count = len(lanes[0])
    half, total = lanes[0][0].shape
    rows = len(lanes) * half
    shapes, specs = [], []
    for planes, width, kind, turned in outs:
        if turned:
            shapes.append(jax.ShapeDtypeStruct((width, rows * count), kind))
            specs.append(pl.BlockSpec((width, rows), lambda i, at: (0, i)))
        elif planes > 1:
            shapes.append(jax.ShapeDtypeStruct((planes, rows * count, width), kind))
            specs.append(pl.BlockSpec((planes, rows, width), lambda i, at: (0, i, 0)))
        else:
            shapes.append(jax.ShapeDtypeStruct((rows * count, width), kind))
            specs.append(pl.BlockSpec((rows, width), lambda i, at: (i, 0)))
    given = [held[far] for held in lanes for far in range(count)]
    return pl.pallas_call(
        functools.partial(place_kernel, count, [o[1] for o in outs], [o[3] for o in outs]),
        grid_spec=pltpu.PrefetchScalarGridSpec(
            num_scalar_prefetch=1,
            grid=(count,),
            in_specs=[pl.BlockSpec((half, total), lambda i, at: (0, 0))] * len(given),
            out_specs=specs,
        ),
        out_shape=shapes,
        compiler_params=pltpu.CompilerParams(vmem_limit_bytes=VMEM_LIMIT),
        cost_estimate=pl.CostEstimate(flops=0, bytes_accessed=12 << 20, transcendentals=0),
        name="place_blocks",
    )(index.astype(jnp.int32).reshape(1), *given)


def swap_pairs(size, bit):
    return [(i, i ^ bit) for i in range(size)]


def shift_pairs(size, shift):
    return [(i, (i - shift) % size) for i in range(size)]


def bits_of(size):
    return [1 << i for i in range(size.bit_length() - 1)]


def pick(x, index, axis=0):
    return lax.dynamic_index_in_dim(x, index, axis, keepdims=False)


def after(x, *others):
    return lax.optimization_barrier((x,) + others)[0]


def xor_gather(x, axis, size, bits):
    held = dict(x) if isinstance(x, dict) else {0: x}
    for bit in bits:
        for far in list(held):
            held[far ^ bit] = lax.ppermute(held[far], axis, swap_pairs(size, bit))
    return held


def by_index(held, index, axis=0, out=None):
    shape = held[0].shape
    if out is None:
        out = jnp.zeros(shape[:axis] + (len(held),) + shape[axis:], held[0].dtype)
    for far, block in held.items():
        out = lax.dynamic_update_index_in_dim(out, block, index ^ far, axis)
    return out


def xor_scatter(blocks, axis_name, size, bits, steps, index, axis, all_steps=None):
    all_steps = list(all_steps or steps)
    left = sorted(all_steps[all_steps.index(steps[0]) :], reverse=True)
    blocks = blocks.reshape(blocks.shape[:axis] + (2,) * len(left) + blocks.shape[axis + 1 :])
    for bit, step in zip(bits, steps):
        at = axis + left.index(step)
        left.remove(step)
        side = (index // step) % 2
        got = lax.ppermute(narrow(pick(blocks, 1 - side, at)), axis_name, swap_pairs(size, bit))
        blocks = wide(pick(blocks, side, at)) + wide(got)
    tail = blocks.shape[axis + len(left) :]
    return blocks.reshape(blocks.shape[:axis] + ((2 ** len(left),) if left else ()) + tail)


def lane_bits(size):
    return bits_of(size), bits_of(size)[::-1]


def column_gather(lanes, size, cut=None, start=None):
    return [xor_gather(x, "dp", size, bits[start:cut]) for x, bits in zip(lanes, lane_bits(size))]


def gate_lanes(lanes, *gates):
    flat = [held[far] for held in lanes for far in held]
    flat = lax.optimization_barrier((*flat, *gates))
    flat = iter(flat)
    return [{far: next(flat) for far in held} for held in lanes]


def column_scatter(lanes, size, column, cut=None, start=None):
    return [
        xor_scatter(x, "dp", size, bits[start:cut], bits[start:cut], column, 0, bits)
        for x, bits in zip(lanes, lane_bits(size))
    ]


def all_sum(x, sizes):
    for axis, size in sizes.items():
        for bit in bits_of(size):
            x = x + lax.ppermute(x, axis, swap_pairs(size, bit))
    return x


def make_local(columns, ranks):
    def local(
        layer_input, width_choice, routed_flag, mixer_gain, mixer_router, attention_weight,
        output_weight, hidden_gain, hidden_router, up_weight, down_weight, out_grad,
    ):
        column, rank = lax.axis_index("dp"), lax.axis_index("mp")
        rows, dim = layer_input.shape
        core = rank % 2
        group = SEQ_LEN // rows
        sequences = ranks // group
        place, sequence = rank % group, rank // group
        pair_bits = [b for b in bits_of(group) if b > 1]
        own_heads = output_weight.shape[0] // HD
        cols_local = up_weight.shape[1]
        width_own = lax.dynamic_slice_in_dim(width_choice, rank * rows, rows, 0)
        routed_own = lax.dynamic_slice_in_dim(routed_flag, rank * rows, rows, 0)
        cos, sin = rope_tables(SEQ_LEN, HD)

        def place_sequence(held, out=None):
            return by_index(held, place, 0, out).reshape(SEQ_LEN, -1)

        def core_sum(pairs):
            theirs = share_of(pairs, rows, 1 - core)
            got = lax.ppermute(theirs, "mp", swap_pairs(ranks, 1))
            pairs, theirs = lax.optimization_barrier((pairs, theirs))
            return wide(share_of(pairs, rows, core)) + wide(got)

        def chip_sum(blocks):
            bits = pair_bits[::-1]
            return xor_scatter(blocks, "mp", ranks, bits, [b // 2 for b in bits], place // 2, 0)

        width = own_heads * HD
        chunk_rows = dim // columns
        half_rows = chunk_rows // 2

        def in_slice(w):
            return jnp.concatenate([w[:, p] for p in range(3)], axis=1)

        lanes_in = [
            in_slice(lax.dynamic_slice_in_dim(attention_weight, column * chunk_rows + at, half_rows, 0))
            for at in (0, half_rows)
        ]
        lanes_out = [
            lax.dynamic_slice_in_dim(output_weight, column * chunk_rows + at, half_rows, 1).T
            for at in (0, half_rows)
        ]
        input_wide = wide(layer_input)
        normed_one, scaled_one, inverse_one = norm_forward(input_wide, mixer_gain)
        low_one = narrow(normed_one)
        low_one, lanes_in, lanes_out = lax.optimization_barrier((low_one, lanes_in, lanes_out))
        held = xor_gather(low_one, "mp", ranks, pair_bits)
        fetched_in, fetched_out = [
            [[lax.ppermute(x, "mp", shift_pairs(ranks, k * group)) for x in lanes] for k in range(1, sequences)]
            for lanes in (lanes_in, lanes_out)
        ]
        sequence_width = lax.dynamic_slice_in_dim(width_choice[:, 0], sequence * SEQ_LEN, SEQ_LEN, 0)
        masks = []
        for k in range(sequences):
            heads = ((rank + k * group) % ranks) * own_heads + jnp.arange(own_heads, dtype=jnp.int32)
            masks.append((heads[None, :] * 4 < (sequence_width[:, None] + 1) * H).astype(jnp.float32))
        weights_in, weights_out = [in_slice(attention_weight)], [output_weight.T]
        held, fetched_in, masks, weights_in, weights_out, cos, sin = lax.optimization_barrier(
            (held, fetched_in, masks, weights_in, weights_out, cos, sin)
        )
        inputs_one = place_sequence(xor_gather(held, "mp", ranks, [1]))
        grads_all = lax.all_gather(after(out_grad, *[x for lanes in fetched_in for x in lanes]), "mp", axis=0, tiled=True)
        steps_in = [column_gather(x, columns, cut=1) for x in fetched_in]
        gate_one, state_one = gate_forward(normed_one, mixer_router, width_own[:, 0], routed_own[:, 0])

        kept = []
        for k in range(sequences):
            mask = masks[k]
            if k:
                steps, fetched, _ = lax.optimization_barrier((steps_in[k - 1], fetched_out[k - 1], kept[0][0]))
                held = column_gather(steps, columns, start=1)
                held_out = column_gather(fetched, columns, cut=1)
                held, held_out = lax.optimization_barrier((held, held_out))
                held_out = column_gather(held_out, columns, start=1)
                weights_in += place_blocks(held, column, [(1, 3 * width, jnp.bfloat16, False)])
                weights_out += place_blocks(held_out, column, [(1, width, jnp.bfloat16, False)])
            kept.append((*attend_forward(inputs_one, weights_in[k], cos, sin, mask), mask))
        mixer_branch = chip_sum(core_sum([(x[1], w) for x, w in zip(kept, weights_out)]))
        mixer_branch, grads_all = lax.optimization_barrier((mixer_branch, grads_all))
        top_down = product(grads_all, down_weight, (1, 1))

        middle = input_wide + gate_one[:, None] * mixer_branch
        normed_two, scaled_two, inverse_two = norm_forward(middle, hidden_gain)
        gate_two, state_two = gate_forward(normed_two, hidden_router, width_own[:, 1], routed_own[:, 1])
        inputs_two = lax.all_gather(narrow(normed_two), "mp", axis=0, tiled=True)
        gates = by_index(xor_gather(gate_two.reshape(-1, 128), "mp", ranks, bits_of(ranks)), rank).reshape(-1)

        inputs_two, top_down = lax.optimization_barrier((inputs_two, top_down))
        share, hidden, pre_grad, dots = hidden_pass(
            inputs_two, up_weight, top_down, gates, width_choice[:, 1:2], rank * cols_local
        )
        dots = dots.reshape(-1, 128)
        share, hidden, pre_grad = lax.optimization_barrier((share, hidden, pre_grad))
        normed_grad_two = wide(lax.psum_scatter(share, "mp", scatter_dimension=0, tiled=True))
        gate_grad_two = lax.dynamic_slice_in_dim(all_sum(dots, {"mp": ranks}).reshape(-1), rank * rows, rows, 0)
        gated = narrow(gates[:, None] * wide(grads_all))
        lanes = [narrow(product(hidden, gated, (0, 0))), narrow(product(inputs_two, pre_grad, (0, 0)))]
        lanes = [x.reshape(columns, -1, x.shape[1]) for x in lanes]
        lanes = column_scatter(lanes, columns, column, cut=1)
        hidden_share = narrow(product(hidden, down_weight, (1, 0)))
        blank = jnp.zeros((group, rows, dim), jnp.bfloat16)
        normed_grad_two, hidden_share, blank, *lanes = lax.optimization_barrier(
            (normed_grad_two, hidden_share, blank, *lanes)
        )
        lanes = [narrow(x) for x in column_scatter(lanes, columns, column, start=1)]

        router_part, _ = gate_backward(normed_two, hidden_router, state_two, gate_grad_two)
        middle_part, gain_two = norm_backward(normed_grad_two + router_part, scaled_two, inverse_two, hidden_gain)
        middle_grad = wide(out_grad) + middle_part
        grads_one = place_sequence(
            xor_gather(narrow(gate_one[:, None] * middle_grad), "mp", ranks, pair_bits + [1]), blank
        )
        helds = column_gather(lanes, columns, cut=1)
        grads_one, hidden_share, lanes = lax.optimization_barrier((grads_one, hidden_share, lanes))
        hidden_branch = wide(lax.psum_scatter(hidden_share, "mp", scatter_dimension=0, tiled=True))
        layer_output = narrow(middle + gate_two[:, None] * hidden_branch)

        pairs, sent = [], []
        grads_now = grads_one
        for k in range(sequences)[::-1]:
            qkv, heads_out, log_total, mask = kept[k]
            qkv_grad = attend_backward(grads_now, weights_out[k], qkv, log_total, cos, sin, mask)
            pairs.append((qkv_grad, weights_in[k]))
            if k == 0:
                helds = column_gather(helds, columns, start=1)
                qkv_grad, helds = lax.optimization_barrier((qkv_grad, helds))
            part = weight_grads(inputs_one, qkv_grad, grads_one, heads_out, columns)
            if k:
                grads_now, part, helds = lax.optimization_barrier((grads_now, part, helds))
                sent.append((k, part))
                normed_late, state_late, dots_late, middle_late, _ = lax.optimization_barrier(
                    (normed_two, state_two, gate_grad_two, middle_grad, part)
                )
                router_two = gate_backward(normed_late, hidden_router, state_late, dots_late)[1]
                gate_grad_one = jnp.sum(middle_late * mixer_branch, axis=1)
        blocks = core_sum(pairs)
        sent = [(k, column_scatter(lanes, columns, column, cut=1)) for k, lanes in sent]
        blocks, gated = lax.optimization_barrier((blocks, [lanes for _, lanes in sent]))
        sent = [(k, lanes) for (k, _), lanes in zip(sent, gated)]
        normed_grad_one = chip_sum(blocks)
        pieces = column_scatter(part, columns, column)
        for k, lanes in sent:
            lanes = [narrow(x) for x in column_scatter(lanes, columns, column, start=1)]
            back = shift_pairs(ranks, -k * group)
            pieces = [p + wide(lax.ppermute(x, "mp", back)) for p, x in zip(pieces, lanes)]
        spread = column_gather([narrow(p) for p in pieces], columns, cut=1)
        spread, helds = lax.optimization_barrier((spread, helds))
        spread = column_gather(spread, columns, start=1)
        down_sum, = place_blocks(helds[:1], column, [(1, dim, jnp.float32, False)])
        up_sum, = place_blocks(helds[1:], column, [(1, cols_local, jnp.float32, False)])
        attention_sum, output_sum = place_blocks(
            spread,
            column,
            [(3, width, jnp.float32, False), (1, width, jnp.float32, True)],
        )
        attention_sum = attention_sum.transpose(1, 0, 2)

        router_part_one, router_one = gate_backward(normed_one, mixer_router, state_one, gate_grad_one)
        input_part, gain_one = norm_backward(normed_grad_one + router_part_one, scaled_one, inverse_one, mixer_gain)
        input_grad = narrow(middle_grad + input_part)

        sizes = {"mp": ranks, "dp": columns}

        smalls = [gain_two, gain_one, router_two.T, router_one.T]
        small_sum = all_sum(jnp.concatenate([x.reshape(-1, 128) for x in smalls], axis=0), sizes)
        cuts = [dim // 128, 2 * dim // 128, (2 * dim + router_two.size) // 128]
        hidden_gain_sum, mixer_gain_sum, hidden_router_sum, mixer_router_sum = (
            x.reshape(-1, dim) for x in jnp.split(small_sum, cuts)
        )
        hidden_gain_sum, mixer_gain_sum = hidden_gain_sum[0], mixer_gain_sum[0]
        hidden_router_sum, mixer_router_sum = hidden_router_sum.T, mixer_router_sum.T
        return (
            layer_output, input_grad, mixer_gain_sum, mixer_router_sum, attention_sum, output_sum,
            hidden_gain_sum, hidden_router_sum, up_sum, down_sum,
        )

    return local


def solution(mesh):
    return jax.shard_map(
        make_local(mesh.shape["dp"], mesh.shape["mp"]),
        mesh=mesh,
        in_specs=(
            P(("dp", "mp"), None),
            P("dp", None),
            P("dp", None),
            P(),
            P(),
            P(None, None, "mp"),
            P("mp", None),
            P(),
            P(),
            P(None, "mp"),
            P("mp", None),
            P(("dp", "mp"), None),
        ),
        out_specs=(
            P(("dp", "mp"), None),
            P(("dp", "mp"), None),
            P(),
            P(),
            P(None, None, "mp"),
            P("mp", None),
            P(),
            P(),
            P(None, "mp"),
            P("mp", None),
        ),
        check_vma=False,
    )
```

```python
import functools
import math

import jax
import jax.numpy as jnp
from jax import lax
from jax.experimental import pallas as pl
from jax.experimental.pallas import tpu as pltpu
from jax.sharding import PartitionSpec as P

H = 16
HD = 128
FF = 8192
SEQ_LEN = 1024


EPSILON = 1e-05
NEG_LARGE = -1e30
HIGHEST = lax.Precision.HIGHEST


def norm_forward(values, gain_vec):
    row_mean = jnp.mean(values, axis=1, keepdims=True)
    centred = values - row_mean
    row_variance = jnp.mean(centred * centred, axis=1, keepdims=True)
    inverse_scale = lax.rsqrt(row_variance + EPSILON)
    scaled = centred * inverse_scale
    return (scaled * gain_vec[None, :], scaled, inverse_scale)


def norm_backward(normed_grad, scaled, inverse_scale, gain_vec):
    gain_grad = jnp.sum(normed_grad * scaled, axis=0)
    scaled_grad = normed_grad * gain_vec[None, :]
    first_mean = jnp.mean(scaled_grad, axis=1, keepdims=True)
    second_mean = jnp.mean(scaled_grad * scaled, axis=1, keepdims=True)
    return (inverse_scale * (scaled_grad - first_mean - scaled * second_mean), gain_grad)


def gate_forward(normed, router, width_col, routed_col):
    logits = jnp.dot(normed, router, precision=HIGHEST, preferred_element_type=jnp.float32)
    soft_probs = jax.nn.softmax(logits, axis=1)
    one_hot = (width_col[:, None] == jnp.arange(4, dtype=jnp.int32)[None, :]).astype(jnp.float32)
    chosen = jnp.sum(soft_probs * one_hot, axis=1)
    route_flags = routed_col.astype(jnp.float32)
    return (
        route_flags * 4.0 * chosen + (1.0 - route_flags),
        (soft_probs, one_hot, chosen, route_flags),
    )


def gate_backward(normed, router, gate_state, gate_grad):
    soft_probs, one_hot, chosen, route_flags = gate_state
    coefficient = route_flags * 4.0 * chosen * gate_grad
    logit_grad = coefficient[:, None] * (one_hot - soft_probs)
    router_grad = lax.dot_general(
        normed,
        logit_grad,
        (((0,), (0,)), ((), ())),
        precision=HIGHEST,
        preferred_element_type=jnp.float32,
    )
    normed_grad = lax.dot_general(
        logit_grad,
        router,
        (((1,), (1,)), ((), ())),
        precision=HIGHEST,
        preferred_element_type=jnp.float32,
    )
    return (normed_grad, router_grad)


Q_BLOCK = 256


def rope_tables(token_count, head_width):
    positions = jnp.arange(token_count, dtype=jnp.float32)
    frequency = jnp.exp(
        jnp.arange(head_width // 2, dtype=jnp.float32) * (-2.0 * math.log(10000.0) / head_width)
    )
    angles = positions[:, None] * frequency[None, :]
    cosine, sine = jnp.cos(angles), jnp.sin(angles)
    return jnp.concatenate([cosine, cosine], axis=1), jnp.concatenate([-sine, sine], axis=1)


def wide(x):
    return x.astype(jnp.float32)


def narrow(x):
    return x.astype(jnp.bfloat16)


def product(a, b, dims):
    return lax.dot_general(a, b, ((dims[:1], dims[1:]), ((), ())), preferred_element_type=jnp.float32)


def block_scores(queries, keys_all, start):
    scores = product(queries, keys_all, (1, 1)) * (1.0 / math.sqrt(HD))
    row = lax.broadcasted_iota(jnp.int32, scores.shape, 0) + start
    col = lax.broadcasted_iota(jnp.int32, scores.shape, 1)
    return jnp.where(col <= row, scores, NEG_LARGE)


def forward_kernel(x_ref, w_ref, cos_ref, sin_ref, mask_ref, qkv_ref, heads_ref, log_ref):
    tokens, heads = x_ref.shape[0], mask_ref.shape[1]
    width = heads * HD
    block = min(Q_BLOCK, tokens)
    for start in range(0, tokens, block):
        here, end = slice(start, start + block), start + block
        x = x_ref[here, :]
        cos, sin = cos_ref[here, :], sin_ref[here, :]
        for part in range(3):
            rows = product(x, w_ref[:, part * width : (part + 1) * width], (1, 0))
            for head in range(heads):
                value = rows[:, head * HD : (head + 1) * HD]
                if part < 2:
                    value = value * cos + pltpu.roll(value, HD // 2, 1) * sin
                at = part * width + head * HD
                qkv_ref[here, at : at + HD] = narrow(value)
        for head in range(heads):
            at = head * HD
            lanes, key_lanes, value_lanes = (slice(at + p * width, at + p * width + HD) for p in range(3))
            scores = block_scores(qkv_ref[here, lanes], qkv_ref[:end, key_lanes], start)
            row_max = jnp.max(scores, axis=1, keepdims=True)
            shifted = jnp.exp(scores - row_max)
            total = jnp.sum(shifted, axis=1, keepdims=True)
            mix = product(narrow(shifted * (1.0 / total)), qkv_ref[:end, value_lanes], (1, 0))
            heads_ref[here, lanes] = narrow(mix * mask_ref[here, head : head + 1])
            log_ref[here, head : head + 1] = row_max + jnp.log(total)


def backward_kernel(g_ref, w_ref, qkv_ref, log_ref, cos_ref, sin_ref, mask_ref, out_ref, keys_acc, values_acc):
    tokens, heads = g_ref.shape[0], mask_ref.shape[1]
    width = heads * HD
    block = min(Q_BLOCK, tokens)
    scale = 1.0 / math.sqrt(HD)
    for start in range(0, tokens, block):
        here, end = slice(start, start + block), start + block
        cos, sin = cos_ref[here, :], sin_ref[here, :]
        rows = narrow(product(g_ref[here, :], w_ref[...], (1, 0)))
        for head in range(heads):
            at = head * HD
            lanes, key_lanes, value_lanes = (slice(at + p * width, at + p * width + HD) for p in range(3))
            heads_grad = rows[:, lanes] * narrow(mask_ref[here, head : head + 1])
            queries, keys_all = qkv_ref[here, lanes], qkv_ref[:end, key_lanes]
            scores = block_scores(queries, keys_all, start)
            probs = jnp.exp(scores - log_ref[here, head : head + 1])
            values_part = product(narrow(probs), heads_grad, (0, 0))
            probs_grad = product(heads_grad, qkv_ref[:end, value_lanes], (1, 1))
            centre = jnp.sum(probs * probs_grad, axis=1, keepdims=True)
            score_grad = narrow(probs * (probs_grad - centre))
            queries_grad = product(score_grad, keys_all, (1, 0)) * scale
            keys_part = product(score_grad, queries, (0, 0)) * scale
            turned = queries_grad * cos - pltpu.roll(queries_grad, HD // 2, 1) * sin
            out_ref[here, lanes] = narrow(turned)
            if start:
                values_acc[:start, lanes] += values_part[:start]
                keys_acc[:start, lanes] += keys_part[:start]
            values_acc[here, lanes] = values_part[start:]
            keys_acc[here, lanes] = keys_part[start:]
    for start in range(0, tokens, block):
        here = slice(start, start + block)
        cos, sin = cos_ref[here, :], sin_ref[here, :]
        out_ref[here, 2 * width :] = narrow(values_acc[here, :])
        for head in range(heads):
            at = head * HD
            value = keys_acc[here, at : at + HD]
            out_ref[here, width + at : width + at + HD] = narrow(value * cos - pltpu.roll(value, HD // 2, 1) * sin)


def share_kernel(side_ref, *refs):
    *given, out_ref = refs
    total = product(given[0][...], given[1][...], (1, 1))
    for a_ref, w_ref in zip(given[2::2], given[3::2]):
        total = total + product(a_ref[...], w_ref[...], (1, 1))
    out_ref[0] = narrow(total)


def weight_kernel(x_ref, q_ref, g_ref, h_ref, *outs):
    width = h_ref.shape[1]
    half = x_ref.shape[1] // 2
    for lane, out_ref in enumerate(outs):
        here = slice(lane * half, (lane + 1) * half)
        out_ref[0, :, : 3 * width] = narrow(product(x_ref[:, here], q_ref[...], (0, 0)))
        out_ref[0, :, 3 * width :] = narrow(product(g_ref[:, here], h_ref[...], (0, 0)))


def hidden_kernel(offset_ref, x_ref, up_ref, top_ref, gate_ref, width_ref, share_ref, hidden_ref, grad_ref, dots_ref):
    pre = product(x_ref[...], up_ref[...], (1, 0))
    column = lax.broadcasted_iota(jnp.int32, pre.shape, 1) + offset_ref[0]
    live = column * 4 < (width_ref[...] + 1) * FF
    relu_act = jnp.where(live, jnp.maximum(pre, 0.0), 0.0)
    hidden = narrow(relu_act * relu_act)
    top = top_ref[...]
    grad = narrow(top * gate_ref[...] * 2.0 * relu_act)
    hidden_ref[...] = hidden
    grad_ref[...] = grad
    dots = jnp.sum(wide(hidden) * top, axis=1, keepdims=True)
    dots_ref[...] = jnp.broadcast_to(dots, (dots.shape[0], 128)).T[:1]
    share_ref[...] = narrow(product(grad, up_ref[...], (1, 1)))


def place_kernel(count, widths, turned, at_ref, *refs):
    lanes = (len(refs) - len(widths)) // count
    blocks, outs = refs[: lanes * count], refs[lanes * count :]
    half = blocks[0].shape[0]
    for far in range(count):

        @pl.when((pl.program_id(0) ^ at_ref[0]) == far)
        def _():
            for lane in range(lanes):
                here = slice(lane * half, (lane + 1) * half)
                block = blocks[lane * count + far]
                start = 0
                for out_ref, width, turn in zip(outs, widths, turned):
                    for part in range(out_ref.shape[0] if len(out_ref.shape) == 3 else 1):
                        value = block[:, start : start + width].astype(out_ref.dtype)
                        start += width
                        if turn:
                            out_ref[:, here] = value.T
                        elif len(out_ref.shape) == 3:
                            out_ref[part, here, :] = value
                        else:
                            out_ref[here, :] = value


VMEM_LIMIT = 56 * 1024 * 1024


def whole_specs(count):
    return [pl.BlockSpec(memory_space=pltpu.VMEM)] * count


def attend_forward(x, w, cos, sin, mask):
    tokens, heads = mask.shape
    dim, width = w.shape[0], heads * HD
    return pl.pallas_call(
        forward_kernel,
        out_shape=[
            jax.ShapeDtypeStruct((tokens, 3 * width), jnp.bfloat16),
            jax.ShapeDtypeStruct((tokens, width), jnp.bfloat16),
            jax.ShapeDtypeStruct((tokens, heads), jnp.float32),
        ],
        in_specs=whole_specs(5),
        out_specs=whole_specs(3),
        compiler_params=pltpu.CompilerParams(vmem_limit_bytes=VMEM_LIMIT),
        cost_estimate=pl.CostEstimate(
            flops=6 * tokens * dim * width + 2 * tokens * tokens * width,
            bytes_accessed=12 << 20,
            transcendentals=tokens * tokens * heads // 2,
        ),
        name="attend_forward",
    )(x, w, cos, sin, mask)


def attend_backward(g, w, qkv, log_total, cos, sin, mask):
    tokens, heads = mask.shape
    dim, width = w.shape[0], heads * HD
    return pl.pallas_call(
        backward_kernel,
        out_shape=jax.ShapeDtypeStruct((tokens, 3 * width), jnp.bfloat16),
        in_specs=whole_specs(7),
        out_specs=whole_specs(1)[0],
        scratch_shapes=[pltpu.VMEM((tokens, width), jnp.float32)] * 2,
        compiler_params=pltpu.CompilerParams(vmem_limit_bytes=VMEM_LIMIT),
        cost_estimate=pl.CostEstimate(
            flops=2 * tokens * dim * width + 5 * tokens * tokens * width,
            bytes_accessed=12 << 20,
            transcendentals=tokens * tokens * heads // 2,
        ),
        name="attend_backward",
    )(g, w, qkv, log_total, cos, sin, mask)


def share_of(pairs, rows, side):
    tokens, depth = pairs[0][0].shape
    dim = pairs[0][1].shape[0]
    chips = tokens // rows // 2
    specs = [
        pl.BlockSpec((rows, depth), lambda i, side: (2 * i + side[0], 0)),
        pl.BlockSpec((dim, depth), lambda i, side: (0, 0)),
    ] * len(pairs)
    return pl.pallas_call(
        share_kernel,
        grid_spec=pltpu.PrefetchScalarGridSpec(
            num_scalar_prefetch=1,
            grid=(chips,),
            in_specs=specs,
            out_specs=pl.BlockSpec((1, rows, dim), lambda i, side: (i, 0, 0)),
        ),
        out_shape=jax.ShapeDtypeStruct((chips, rows, dim), jnp.bfloat16),
        compiler_params=pltpu.CompilerParams(vmem_limit_bytes=VMEM_LIMIT),
        cost_estimate=pl.CostEstimate(
            flops=tokens * dim * depth * len(pairs), bytes_accessed=12 << 20, transcendentals=0
        ),
        name="share_of",
    )(side.astype(jnp.int32).reshape(1), *[x for pair in pairs for x in pair])


def hidden_pass(x, up, top_down, gates, widths, offset):
    tokens, dim = x.shape
    cols = up.shape[1]
    block = 256
    rows_of = lambda n: pl.BlockSpec((block, n), lambda i, at: (i, 0))
    return pl.pallas_call(
        hidden_kernel,
        grid_spec=pltpu.PrefetchScalarGridSpec(
            num_scalar_prefetch=1,
            grid=(tokens // block,),
            in_specs=[rows_of(dim), pl.BlockSpec((dim, cols), lambda i, at: (0, 0)), rows_of(cols), rows_of(1), rows_of(1)],
            out_specs=[rows_of(dim), rows_of(cols), rows_of(cols), pl.BlockSpec((1, block), lambda i, at: (0, i))],
        ),
        out_shape=[
            jax.ShapeDtypeStruct((tokens, dim), jnp.bfloat16),
            jax.ShapeDtypeStruct((tokens, cols), jnp.bfloat16),
            jax.ShapeDtypeStruct((tokens, cols), jnp.bfloat16),
            jax.ShapeDtypeStruct((1, tokens), jnp.float32),
        ],
        compiler_params=pltpu.CompilerParams(vmem_limit_bytes=VMEM_LIMIT),
        cost_estimate=pl.CostEstimate(flops=4 * tokens * dim * cols, bytes_accessed=40 << 20, transcendentals=0),
        name="hidden_pass",
    )(offset.astype(jnp.int32).reshape(1), x, up, top_down, gates[:, None], widths)


def weight_grads(x, qkv_grad, g, heads_out, count):
    tokens, dim = x.shape
    width = heads_out.shape[1]
    block = dim // count
    out = jax.ShapeDtypeStruct((count, block // 2, 4 * width), jnp.bfloat16)
    return pl.pallas_call(
        weight_kernel,
        grid=(count,),
        out_shape=[out, out],
        in_specs=[
            pl.BlockSpec((tokens, block), lambda i: (0, i)),
            pl.BlockSpec((tokens, 3 * width), lambda i: (0, 0)),
            pl.BlockSpec((tokens, block), lambda i: (0, i)),
            pl.BlockSpec((tokens, width), lambda i: (0, 0)),
        ],
        out_specs=[pl.BlockSpec((1, block // 2, 4 * width), lambda i: (i, 0, 0))] * 2,
        compiler_params=pltpu.CompilerParams(vmem_limit_bytes=VMEM_LIMIT),
        cost_estimate=pl.CostEstimate(flops=8 * tokens * dim * width, bytes_accessed=14 << 20, transcendentals=0),
        name="weight_grads",
    )(x, qkv_grad, g, heads_out)


def place_blocks(lanes, index, outs):
    count = len(lanes[0])
    half, total = lanes[0][0].shape
    rows = len(lanes) * half
    shapes, specs = [], []
    for planes, width, kind, turned in outs:
        if turned:
            shapes.append(jax.ShapeDtypeStruct((width, rows * count), kind))
            specs.append(pl.BlockSpec((width, rows), lambda i, at: (0, i)))
        elif planes > 1:
            shapes.append(jax.ShapeDtypeStruct((planes, rows * count, width), kind))
            specs.append(pl.BlockSpec((planes, rows, width), lambda i, at: (0, i, 0)))
        else:
            shapes.append(jax.ShapeDtypeStruct((rows * count, width), kind))
            specs.append(pl.BlockSpec((rows, width), lambda i, at: (i, 0)))
    given = [held[far] for held in lanes for far in range(count)]
    return pl.pallas_call(
        functools.partial(place_kernel, count, [o[1] for o in outs], [o[3] for o in outs]),
        grid_spec=pltpu.PrefetchScalarGridSpec(
            num_scalar_prefetch=1,
            grid=(count,),
            in_specs=[pl.BlockSpec((half, total), lambda i, at: (0, 0))] * len(given),
            out_specs=specs,
        ),
        out_shape=shapes,
        compiler_params=pltpu.CompilerParams(vmem_limit_bytes=VMEM_LIMIT),
        cost_estimate=pl.CostEstimate(flops=0, bytes_accessed=12 << 20, transcendentals=0),
        name="place_blocks",
    )(index.astype(jnp.int32).reshape(1), *given)


def swap_pairs(size, bit):
    return [(i, i ^ bit) for i in range(size)]


def shift_pairs(size, shift):
    return [(i, (i - shift) % size) for i in range(size)]


def bits_of(size):
    return [1 << i for i in range(size.bit_length() - 1)]


def pick(x, index, axis=0):
    return lax.dynamic_index_in_dim(x, index, axis, keepdims=False)


def after(x, *others):
    return lax.optimization_barrier((x,) + others)[0]


def xor_gather(x, axis, size, bits):
    held = dict(x) if isinstance(x, dict) else {0: x}
    for bit in bits:
        for far in list(held):
            held[far ^ bit] = lax.ppermute(held[far], axis, swap_pairs(size, bit))
    return held


def by_index(held, index, axis=0, out=None):
    shape = held[0].shape
    if out is None:
        out = jnp.zeros(shape[:axis] + (len(held),) + shape[axis:], held[0].dtype)
    for far, block in held.items():
        out = lax.dynamic_update_index_in_dim(out, block, index ^ far, axis)
    return out


def xor_scatter(blocks, axis_name, size, bits, steps, index, axis, all_steps=None):
    all_steps = list(all_steps or steps)
    left = sorted(all_steps[all_steps.index(steps[0]) :], reverse=True)
    blocks = blocks.reshape(blocks.shape[:axis] + (2,) * len(left) + blocks.shape[axis + 1 :])
    for bit, step in zip(bits, steps):
        at = axis + left.index(step)
        left.remove(step)
        side = (index // step) % 2
        got = lax.ppermute(narrow(pick(blocks, 1 - side, at)), axis_name, swap_pairs(size, bit))
        blocks = wide(pick(blocks, side, at)) + wide(got)
    tail = blocks.shape[axis + len(left) :]
    return blocks.reshape(blocks.shape[:axis] + ((2 ** len(left),) if left else ()) + tail)


def lane_bits(size):
    return bits_of(size), bits_of(size)[::-1]


def column_gather(lanes, size, cut=None, start=None):
    return [xor_gather(x, "dp", size, bits[start:cut]) for x, bits in zip(lanes, lane_bits(size))]


def gate_lanes(lanes, *gates):
    flat = [held[far] for held in lanes for far in held]
    flat = lax.optimization_barrier((*flat, *gates))
    flat = iter(flat)
    return [{far: next(flat) for far in held} for held in lanes]


def column_scatter(lanes, size, column, cut=None, start=None):
    return [
        xor_scatter(x, "dp", size, bits[start:cut], bits[start:cut], column, 0, bits)
        for x, bits in zip(lanes, lane_bits(size))
    ]


def all_sum(x, sizes):
    for axis, size in sizes.items():
        for bit in bits_of(size):
            x = x + lax.ppermute(x, axis, swap_pairs(size, bit))
    return x


def make_local(columns, ranks):
    def local(
        layer_input, width_choice, routed_flag, mixer_gain, mixer_router, attention_weight,
        output_weight, hidden_gain, hidden_router, up_weight, down_weight, out_grad,
    ):
        column, rank = lax.axis_index("dp"), lax.axis_index("mp")
        rows, dim = layer_input.shape
        core = rank % 2
        group = SEQ_LEN // rows
        sequences = ranks // group
        place, sequence = rank % group, rank // group
        pair_bits = [b for b in bits_of(group) if b > 1]
        own_heads = output_weight.shape[0] // HD
        cols_local = up_weight.shape[1]
        width_own = lax.dynamic_slice_in_dim(width_choice, rank * rows, rows, 0)
        routed_own = lax.dynamic_slice_in_dim(routed_flag, rank * rows, rows, 0)
        cos, sin = rope_tables(SEQ_LEN, HD)

        def place_sequence(held, out=None):
            return by_index(held, place, 0, out).reshape(SEQ_LEN, -1)

        def core_sum(pairs):
            theirs = share_of(pairs, rows, 1 - core)
            got = lax.ppermute(theirs, "mp", swap_pairs(ranks, 1))
            pairs, theirs = lax.optimization_barrier((pairs, theirs))
            return wide(share_of(pairs, rows, core)) + wide(got)

        def chip_sum(blocks):
            bits = pair_bits[::-1]
            return xor_scatter(blocks, "mp", ranks, bits, [b // 2 for b in bits], place // 2, 0)

        width = own_heads * HD
        chunk_rows = dim // columns
        half_rows = chunk_rows // 2

        def in_slice(w):
            return jnp.concatenate([w[:, p] for p in range(3)], axis=1)

        lanes_in = [
            in_slice(lax.dynamic_slice_in_dim(attention_weight, column * chunk_rows + at, half_rows, 0))
            for at in (0, half_rows)
        ]
        lanes_out = [
            lax.dynamic_slice_in_dim(output_weight, column * chunk_rows + at, half_rows, 1).T
            for at in (0, half_rows)
        ]
        input_wide = wide(layer_input)
        normed_one, scaled_one, inverse_one = norm_forward(input_wide, mixer_gain)
        low_one = narrow(normed_one)
        low_one, lanes_in, lanes_out = lax.optimization_barrier((low_one, lanes_in, lanes_out))
        held = xor_gather(low_one, "mp", ranks, pair_bits)
        fetched_in, fetched_out = [
            [[lax.ppermute(x, "mp", shift_pairs(ranks, k * group)) for x in lanes] for k in range(1, sequences)]
            for lanes in (lanes_in, lanes_out)
        ]
        sequence_width = lax.dynamic_slice_in_dim(width_choice[:, 0], sequence * SEQ_LEN, SEQ_LEN, 0)
        masks = []
        for k in range(sequences):
            heads = ((rank + k * group) % ranks) * own_heads + jnp.arange(own_heads, dtype=jnp.int32)
            masks.append((heads[None, :] * 4 < (sequence_width[:, None] + 1) * H).astype(jnp.float32))
        weights_in, weights_out = [in_slice(attention_weight)], [output_weight.T]
        held, fetched_in, masks, weights_in, weights_out, cos, sin = lax.optimization_barrier(
            (held, fetched_in, masks, weights_in, weights_out, cos, sin)
        )
        inputs_one = place_sequence(xor_gather(held, "mp", ranks, [1]))
        grads_all = lax.all_gather(after(out_grad, *[x for lanes in fetched_in for x in lanes]), "mp", axis=0, tiled=True)
        steps_in = [column_gather(x, columns, cut=1) for x in fetched_in]
        gate_one, state_one = gate_forward(normed_one, mixer_router, width_own[:, 0], routed_own[:, 0])

        kept = []
        for k in range(sequences):
            mask = masks[k]
            if k:
                steps, fetched, _ = lax.optimization_barrier((steps_in[k - 1], fetched_out[k - 1], kept[0][0]))
                held = column_gather(steps, columns, start=1)
                held_out = column_gather(fetched, columns, cut=1)
                held, held_out = lax.optimization_barrier((held, held_out))
                held_out = column_gather(held_out, columns, start=1)
                weights_in += place_blocks(held, column, [(1, 3 * width, jnp.bfloat16, False)])
                weights_out += place_blocks(held_out, column, [(1, width, jnp.bfloat16, False)])
            kept.append((*attend_forward(inputs_one, weights_in[k], cos, sin, mask), mask))
        mixer_branch = chip_sum(core_sum([(x[1], w) for x, w in zip(kept, weights_out)]))
        mixer_branch, grads_all = lax.optimization_barrier((mixer_branch, grads_all))
        top_down = product(grads_all, down_weight, (1, 1))

        middle = input_wide + gate_one[:, None] * mixer_branch
        normed_two, scaled_two, inverse_two = norm_forward(middle, hidden_gain)
        gate_two, state_two = gate_forward(normed_two, hidden_router, width_own[:, 1], routed_own[:, 1])
        inputs_two = lax.all_gather(narrow(normed_two), "mp", axis=0, tiled=True)
        gates = by_index(xor_gather(gate_two.reshape(-1, 128), "mp", ranks, bits_of(ranks)), rank).reshape(-1)

        inputs_two, top_down = lax.optimization_barrier((inputs_two, top_down))
        share, hidden, pre_grad, dots = hidden_pass(
            inputs_two, up_weight, top_down, gates, width_choice[:, 1:2], rank * cols_local
        )
        dots = dots.reshape(-1, 128)
        share, hidden, pre_grad = lax.optimization_barrier((share, hidden, pre_grad))
        normed_grad_two = wide(lax.psum_scatter(share, "mp", scatter_dimension=0, tiled=True))
        gate_grad_two = lax.dynamic_slice_in_dim(all_sum(dots, {"mp": ranks}).reshape(-1), rank * rows, rows, 0)
        gated = narrow(gates[:, None] * wide(grads_all))
        lanes = [narrow(product(hidden, gated, (0, 0))), narrow(product(inputs_two, pre_grad, (0, 0)))]
        lanes = [x.reshape(columns, -1, x.shape[1]) for x in lanes]
        lanes = column_scatter(lanes, columns, column, cut=1)
        hidden_share = narrow(product(hidden, down_weight, (1, 0)))
        blank = jnp.zeros((group, rows, dim), jnp.bfloat16)
        normed_grad_two, hidden_share, blank, *lanes = lax.optimization_barrier(
            (normed_grad_two, hidden_share, blank, *lanes)
        )
        lanes = [narrow(x) for x in column_scatter(lanes, columns, column, start=1)]

        router_part, _ = gate_backward(normed_two, hidden_router, state_two, gate_grad_two)
        middle_part, gain_two = norm_backward(normed_grad_two + router_part, scaled_two, inverse_two, hidden_gain)
        middle_grad = wide(out_grad) + middle_part
        grads_one = place_sequence(
            xor_gather(narrow(gate_one[:, None] * middle_grad), "mp", ranks, pair_bits + [1]), blank
        )
        helds = column_gather(lanes, columns, cut=1)
        grads_one, hidden_share, lanes = lax.optimization_barrier((grads_one, hidden_share, lanes))
        hidden_branch = wide(lax.psum_scatter(hidden_share, "mp", scatter_dimension=0, tiled=True))
        layer_output = narrow(middle + gate_two[:, None] * hidden_branch)

        pairs, sent = [], []
        grads_now = grads_one
        for k in range(sequences)[::-1]:
            qkv, heads_out, log_total, mask = kept[k]
            qkv_grad = attend_backward(grads_now, weights_out[k], qkv, log_total, cos, sin, mask)
            pairs.append((qkv_grad, weights_in[k]))
            if sent:
                qkv_grad, sent = lax.optimization_barrier((qkv_grad, sent))
            part = weight_grads(inputs_one, qkv_grad, grads_one, heads_out, columns)
            if k:
                grads_now, part, helds = lax.optimization_barrier((grads_now, part, helds))
                sent.append(column_scatter(part, columns, column, cut=1))
                normed_late, state_late, dots_late, middle_late, _ = lax.optimization_barrier(
                    (normed_two, state_two, gate_grad_two, middle_grad, part)
                )
                router_two = gate_backward(normed_late, hidden_router, state_late, dots_late)[1]
                gate_grad_one = jnp.sum(middle_late * mixer_branch, axis=1)
        helds, sent = lax.optimization_barrier((helds, sent))
        sent = [[narrow(x) for x in column_scatter(lanes, columns, column, start=1)] for lanes in sent]
        there = [
            [lax.ppermute(x, "mp", shift_pairs(ranks, -k * group)) for x in lanes]
            for k, lanes in zip(range(1, sequences)[::-1], sent)
        ]
        pairs, part = lax.optimization_barrier((pairs, part))
        blocks = core_sum(pairs)
        blocks, there = lax.optimization_barrier((blocks, there))
        normed_grad_one = chip_sum(blocks)
        helds = column_gather(helds, columns, start=1)
        pieces = column_scatter(part, columns, column)
        pieces, helds = lax.optimization_barrier((pieces, helds))
        for lanes in there:
            pieces = [p + wide(t) for p, t in zip(pieces, lanes)]
        spread = column_gather([narrow(p) for p in pieces], columns, cut=1)
        spread, helds = lax.optimization_barrier((spread, helds))
        spread = column_gather(spread, columns, start=1)
        down_sum, = place_blocks(helds[:1], column, [(1, dim, jnp.float32, False)])
        up_sum, = place_blocks(helds[1:], column, [(1, cols_local, jnp.float32, False)])
        attention_sum, output_sum = place_blocks(
            spread,
            column,
            [(3, width, jnp.float32, False), (1, width, jnp.float32, True)],
        )
        attention_sum = attention_sum.transpose(1, 0, 2)

        router_part_one, router_one = gate_backward(normed_one, mixer_router, state_one, gate_grad_one)
        input_part, gain_one = norm_backward(normed_grad_one + router_part_one, scaled_one, inverse_one, mixer_gain)
        input_grad = narrow(middle_grad + input_part)

        sizes = {"mp": ranks, "dp": columns}

        smalls = [gain_two, gain_one, router_two.T, router_one.T]
        small_sum = all_sum(jnp.concatenate([x.reshape(-1, 128) for x in smalls], axis=0), sizes)
        cuts = [dim // 128, 2 * dim // 128, (2 * dim + router_two.size) // 128]
        hidden_gain_sum, mixer_gain_sum, hidden_router_sum, mixer_router_sum = (
            x.reshape(-1, dim) for x in jnp.split(small_sum, cuts)
        )
        hidden_gain_sum, mixer_gain_sum = hidden_gain_sum[0], mixer_gain_sum[0]
        hidden_router_sum, mixer_router_sum = hidden_router_sum.T, mixer_router_sum.T
        return (
            layer_output, input_grad, mixer_gain_sum, mixer_router_sum, attention_sum, output_sum,
            hidden_gain_sum, hidden_router_sum, up_sum, down_sum,
        )

    return local


def solution(mesh):
    return jax.shard_map(
        make_local(mesh.shape["dp"], mesh.shape["mp"]),
        mesh=mesh,
        in_specs=(
            P(("dp", "mp"), None),
            P("dp", None),
            P("dp", None),
            P(),
            P(),
            P(None, None, "mp"),
            P("mp", None),
            P(),
            P(),
            P(None, "mp"),
            P("mp", None),
            P(("dp", "mp"), None),
        ),
        out_specs=(
            P(("dp", "mp"), None),
            P(("dp", "mp"), None),
            P(),
            P(),
            P(None, None, "mp"),
            P("mp", None),
            P(),
            P(),
            P(None, "mp"),
            P("mp", None),
        ),
        check_vma=False,
    )
```

```python
import functools
import math

import jax
import jax.numpy as jnp
from jax import lax
from jax.experimental import pallas as pl
from jax.experimental.pallas import tpu as pltpu
from jax.sharding import PartitionSpec as P

H = 16
HD = 128
FF = 8192
SEQ_LEN = 1024


EPSILON = 1e-05
NEG_LARGE = -1e30
HIGHEST = lax.Precision.HIGHEST


def norm_forward(values, gain_vec):
    row_mean = jnp.mean(values, axis=1, keepdims=True)
    centred = values - row_mean
    row_variance = jnp.mean(centred * centred, axis=1, keepdims=True)
    inverse_scale = lax.rsqrt(row_variance + EPSILON)
    scaled = centred * inverse_scale
    return (scaled * gain_vec[None, :], scaled, inverse_scale)


def norm_backward(normed_grad, scaled, inverse_scale, gain_vec):
    gain_grad = jnp.sum(normed_grad * scaled, axis=0)
    scaled_grad = normed_grad * gain_vec[None, :]
    first_mean = jnp.mean(scaled_grad, axis=1, keepdims=True)
    second_mean = jnp.mean(scaled_grad * scaled, axis=1, keepdims=True)
    return (inverse_scale * (scaled_grad - first_mean - scaled * second_mean), gain_grad)


def gate_forward(normed, router, width_col, routed_col):
    logits = jnp.dot(normed, router, precision=HIGHEST, preferred_element_type=jnp.float32)
    soft_probs = jax.nn.softmax(logits, axis=1)
    one_hot = (width_col[:, None] == jnp.arange(4, dtype=jnp.int32)[None, :]).astype(jnp.float32)
    chosen = jnp.sum(soft_probs * one_hot, axis=1)
    route_flags = routed_col.astype(jnp.float32)
    return (
        route_flags * 4.0 * chosen + (1.0 - route_flags),
        (soft_probs, one_hot, chosen, route_flags),
    )


def gate_backward(normed, router, gate_state, gate_grad):
    soft_probs, one_hot, chosen, route_flags = gate_state
    coefficient = route_flags * 4.0 * chosen * gate_grad
    logit_grad = coefficient[:, None] * (one_hot - soft_probs)
    router_grad = lax.dot_general(
        normed,
        logit_grad,
        (((0,), (0,)), ((), ())),
        precision=HIGHEST,
        preferred_element_type=jnp.float32,
    )
    normed_grad = lax.dot_general(
        logit_grad,
        router,
        (((1,), (1,)), ((), ())),
        precision=HIGHEST,
        preferred_element_type=jnp.float32,
    )
    return (normed_grad, router_grad)


Q_BLOCK = 256


def rope_tables(token_count, head_width):
    positions = jnp.arange(token_count, dtype=jnp.float32)
    frequency = jnp.exp(
        jnp.arange(head_width // 2, dtype=jnp.float32) * (-2.0 * math.log(10000.0) / head_width)
    )
    angles = positions[:, None] * frequency[None, :]
    cosine, sine = jnp.cos(angles), jnp.sin(angles)
    return jnp.concatenate([cosine, cosine], axis=1), jnp.concatenate([-sine, sine], axis=1)


def wide(x):
    return x.astype(jnp.float32)


def narrow(x):
    return x.astype(jnp.bfloat16)


def product(a, b, dims):
    return lax.dot_general(a, b, ((dims[:1], dims[1:]), ((), ())), preferred_element_type=jnp.float32)


def block_scores(queries, keys_all, start):
    scores = product(queries, keys_all, (1, 1)) * (1.0 / math.sqrt(HD))
    row = lax.broadcasted_iota(jnp.int32, scores.shape, 0) + start
    col = lax.broadcasted_iota(jnp.int32, scores.shape, 1)
    return jnp.where(col <= row, scores, NEG_LARGE)


def forward_kernel(x_ref, w_ref, cos_ref, sin_ref, mask_ref, qkv_ref, heads_ref, log_ref):
    tokens, heads = x_ref.shape[0], mask_ref.shape[1]
    width = heads * HD
    block = min(Q_BLOCK, tokens)
    for start in range(0, tokens, block):
        here, end = slice(start, start + block), start + block
        x = x_ref[here, :]
        cos, sin = cos_ref[here, :], sin_ref[here, :]
        for part in range(3):
            rows = product(x, w_ref[:, part * width : (part + 1) * width], (1, 0))
            for head in range(heads):
                value = rows[:, head * HD : (head + 1) * HD]
                if part < 2:
                    value = value * cos + pltpu.roll(value, HD // 2, 1) * sin
                at = part * width + head * HD
                qkv_ref[here, at : at + HD] = narrow(value)
        for head in range(heads):
            at = head * HD
            lanes, key_lanes, value_lanes = (slice(at + p * width, at + p * width + HD) for p in range(3))
            scores = block_scores(qkv_ref[here, lanes], qkv_ref[:end, key_lanes], start)
            row_max = jnp.max(scores, axis=1, keepdims=True)
            shifted = jnp.exp(scores - row_max)
            total = jnp.sum(shifted, axis=1, keepdims=True)
            mix = product(narrow(shifted * (1.0 / total)), qkv_ref[:end, value_lanes], (1, 0))
            heads_ref[here, lanes] = narrow(mix * mask_ref[here, head : head + 1])
            log_ref[here, head : head + 1] = row_max + jnp.log(total)


def backward_kernel(g_ref, w_ref, qkv_ref, log_ref, cos_ref, sin_ref, mask_ref, out_ref, keys_acc, values_acc):
    tokens, heads = g_ref.shape[0], mask_ref.shape[1]
    width = heads * HD
    block = min(Q_BLOCK, tokens)
    scale = 1.0 / math.sqrt(HD)
    for start in range(0, tokens, block):
        here, end = slice(start, start + block), start + block
        cos, sin = cos_ref[here, :], sin_ref[here, :]
        rows = narrow(product(g_ref[here, :], w_ref[...], (1, 0)))
        for head in range(heads):
            at = head * HD
            lanes, key_lanes, value_lanes = (slice(at + p * width, at + p * width + HD) for p in range(3))
            heads_grad = rows[:, lanes] * narrow(mask_ref[here, head : head + 1])
            queries, keys_all = qkv_ref[here, lanes], qkv_ref[:end, key_lanes]
            scores = block_scores(queries, keys_all, start)
            probs = jnp.exp(scores - log_ref[here, head : head + 1])
            values_part = product(narrow(probs), heads_grad, (0, 0))
            probs_grad = product(heads_grad, qkv_ref[:end, value_lanes], (1, 1))
            centre = jnp.sum(probs * probs_grad, axis=1, keepdims=True)
            score_grad = narrow(probs * (probs_grad - centre))
            queries_grad = product(score_grad, keys_all, (1, 0)) * scale
            keys_part = product(score_grad, queries, (0, 0)) * scale
            turned = queries_grad * cos - pltpu.roll(queries_grad, HD // 2, 1) * sin
            out_ref[here, lanes] = narrow(turned)
            if start:
                values_acc[:start, lanes] += values_part[:start]
                keys_acc[:start, lanes] += keys_part[:start]
            values_acc[here, lanes] = values_part[start:]
            keys_acc[here, lanes] = keys_part[start:]
    for start in range(0, tokens, block):
        here = slice(start, start + block)
        cos, sin = cos_ref[here, :], sin_ref[here, :]
        out_ref[here, 2 * width :] = narrow(values_acc[here, :])
        for head in range(heads):
            at = head * HD
            value = keys_acc[here, at : at + HD]
            out_ref[here, width + at : width + at + HD] = narrow(value * cos - pltpu.roll(value, HD // 2, 1) * sin)


def share_kernel(side_ref, *refs):
    *given, out_ref = refs
    total = product(given[0][...], given[1][...], (1, 1))
    for a_ref, w_ref in zip(given[2::2], given[3::2]):
        total = total + product(a_ref[...], w_ref[...], (1, 1))
    out_ref[0] = narrow(total)


def weight_kernel(x_ref, q_ref, g_ref, h_ref, *outs):
    width = h_ref.shape[1]
    half = x_ref.shape[1] // 2
    for lane, out_ref in enumerate(outs):
        here = slice(lane * half, (lane + 1) * half)
        out_ref[0, :, : 3 * width] = narrow(product(x_ref[:, here], q_ref[...], (0, 0)))
        out_ref[0, :, 3 * width :] = narrow(product(g_ref[:, here], h_ref[...], (0, 0)))


def hidden_kernel(offset_ref, x_ref, up_ref, top_ref, gate_ref, width_ref, share_ref, hidden_ref, grad_ref, dots_ref):
    pre = product(x_ref[...], up_ref[...], (1, 0))
    column = lax.broadcasted_iota(jnp.int32, pre.shape, 1) + offset_ref[0]
    live = column * 4 < (width_ref[...] + 1) * FF
    relu_act = jnp.where(live, jnp.maximum(pre, 0.0), 0.0)
    hidden = narrow(relu_act * relu_act)
    top = top_ref[...]
    grad = narrow(top * gate_ref[...] * 2.0 * relu_act)
    hidden_ref[...] = hidden
    grad_ref[...] = grad
    dots = jnp.sum(wide(hidden) * top, axis=1, keepdims=True)
    dots_ref[...] = jnp.broadcast_to(dots, (dots.shape[0], 128)).T[:1]
    share_ref[...] = narrow(product(grad, up_ref[...], (1, 1)))


def place_kernel(count, widths, turned, at_ref, *refs):
    lanes = (len(refs) - len(widths)) // count
    blocks, outs = refs[: lanes * count], refs[lanes * count :]
    half = blocks[0].shape[0]
    for far in range(count):

        @pl.when((pl.program_id(0) ^ at_ref[0]) == far)
        def _():
            for lane in range(lanes):
                here = slice(lane * half, (lane + 1) * half)
                block = blocks[lane * count + far]
                start = 0
                for out_ref, width, turn in zip(outs, widths, turned):
                    for part in range(out_ref.shape[0] if len(out_ref.shape) == 3 else 1):
                        value = block[:, start : start + width].astype(out_ref.dtype)
                        start += width
                        if turn:
                            out_ref[:, here] = value.T
                        elif len(out_ref.shape) == 3:
                            out_ref[part, here, :] = value
                        else:
                            out_ref[here, :] = value


VMEM_LIMIT = 56 * 1024 * 1024


def whole_specs(count):
    return [pl.BlockSpec(memory_space=pltpu.VMEM)] * count


def attend_forward(x, w, cos, sin, mask):
    tokens, heads = mask.shape
    dim, width = w.shape[0], heads * HD
    return pl.pallas_call(
        forward_kernel,
        out_shape=[
            jax.ShapeDtypeStruct((tokens, 3 * width), jnp.bfloat16),
            jax.ShapeDtypeStruct((tokens, width), jnp.bfloat16),
            jax.ShapeDtypeStruct((tokens, heads), jnp.float32),
        ],
        in_specs=whole_specs(5),
        out_specs=whole_specs(3),
        compiler_params=pltpu.CompilerParams(vmem_limit_bytes=VMEM_LIMIT),
        cost_estimate=pl.CostEstimate(
            flops=6 * tokens * dim * width + 2 * tokens * tokens * width,
            bytes_accessed=12 << 20,
            transcendentals=tokens * tokens * heads // 2,
        ),
        name="attend_forward",
    )(x, w, cos, sin, mask)


def attend_backward(g, w, qkv, log_total, cos, sin, mask):
    tokens, heads = mask.shape
    dim, width = w.shape[0], heads * HD
    return pl.pallas_call(
        backward_kernel,
        out_shape=jax.ShapeDtypeStruct((tokens, 3 * width), jnp.bfloat16),
        in_specs=whole_specs(7),
        out_specs=whole_specs(1)[0],
        scratch_shapes=[pltpu.VMEM((tokens, width), jnp.float32)] * 2,
        compiler_params=pltpu.CompilerParams(vmem_limit_bytes=VMEM_LIMIT),
        cost_estimate=pl.CostEstimate(
            flops=2 * tokens * dim * width + 5 * tokens * tokens * width,
            bytes_accessed=12 << 20,
            transcendentals=tokens * tokens * heads // 2,
        ),
        name="attend_backward",
    )(g, w, qkv, log_total, cos, sin, mask)


def share_of(pairs, rows, side):
    tokens, depth = pairs[0][0].shape
    dim = pairs[0][1].shape[0]
    chips = tokens // rows // 2
    specs = [
        pl.BlockSpec((rows, depth), lambda i, side: (2 * i + side[0], 0)),
        pl.BlockSpec((dim, depth), lambda i, side: (0, 0)),
    ] * len(pairs)
    return pl.pallas_call(
        share_kernel,
        grid_spec=pltpu.PrefetchScalarGridSpec(
            num_scalar_prefetch=1,
            grid=(chips,),
            in_specs=specs,
            out_specs=pl.BlockSpec((1, rows, dim), lambda i, side: (i, 0, 0)),
        ),
        out_shape=jax.ShapeDtypeStruct((chips, rows, dim), jnp.bfloat16),
        compiler_params=pltpu.CompilerParams(vmem_limit_bytes=VMEM_LIMIT),
        cost_estimate=pl.CostEstimate(
            flops=tokens * dim * depth * len(pairs), bytes_accessed=12 << 20, transcendentals=0
        ),
        name="share_of",
    )(side.astype(jnp.int32).reshape(1), *[x for pair in pairs for x in pair])


def hidden_pass(x, up, top_down, gates, widths, offset):
    tokens, dim = x.shape
    cols = up.shape[1]
    block = 256
    rows_of = lambda n: pl.BlockSpec((block, n), lambda i, at: (i, 0))
    return pl.pallas_call(
        hidden_kernel,
        grid_spec=pltpu.PrefetchScalarGridSpec(
            num_scalar_prefetch=1,
            grid=(tokens // block,),
            in_specs=[rows_of(dim), pl.BlockSpec((dim, cols), lambda i, at: (0, 0)), rows_of(cols), rows_of(1), rows_of(1)],
            out_specs=[rows_of(dim), rows_of(cols), rows_of(cols), pl.BlockSpec((1, block), lambda i, at: (0, i))],
        ),
        out_shape=[
            jax.ShapeDtypeStruct((tokens, dim), jnp.bfloat16),
            jax.ShapeDtypeStruct((tokens, cols), jnp.bfloat16),
            jax.ShapeDtypeStruct((tokens, cols), jnp.bfloat16),
            jax.ShapeDtypeStruct((1, tokens), jnp.float32),
        ],
        compiler_params=pltpu.CompilerParams(vmem_limit_bytes=VMEM_LIMIT),
        cost_estimate=pl.CostEstimate(flops=4 * tokens * dim * cols, bytes_accessed=40 << 20, transcendentals=0),
        name="hidden_pass",
    )(offset.astype(jnp.int32).reshape(1), x, up, top_down, gates[:, None], widths)


def weight_grads(x, qkv_grad, g, heads_out, count):
    tokens, dim = x.shape
    width = heads_out.shape[1]
    block = dim // count
    out = jax.ShapeDtypeStruct((count, block // 2, 4 * width), jnp.bfloat16)
    return pl.pallas_call(
        weight_kernel,
        grid=(count,),
        out_shape=[out, out],
        in_specs=[
            pl.BlockSpec((tokens, block), lambda i: (0, i)),
            pl.BlockSpec((tokens, 3 * width), lambda i: (0, 0)),
            pl.BlockSpec((tokens, block), lambda i: (0, i)),
            pl.BlockSpec((tokens, width), lambda i: (0, 0)),
        ],
        out_specs=[pl.BlockSpec((1, block // 2, 4 * width), lambda i: (i, 0, 0))] * 2,
        compiler_params=pltpu.CompilerParams(vmem_limit_bytes=VMEM_LIMIT),
        cost_estimate=pl.CostEstimate(flops=8 * tokens * dim * width, bytes_accessed=14 << 20, transcendentals=0),
        name="weight_grads",
    )(x, qkv_grad, g, heads_out)


def place_blocks(lanes, index, outs):
    count = len(lanes[0])
    half, total = lanes[0][0].shape
    rows = len(lanes) * half
    shapes, specs = [], []
    for planes, width, kind, turned in outs:
        if turned:
            shapes.append(jax.ShapeDtypeStruct((width, rows * count), kind))
            specs.append(pl.BlockSpec((width, rows), lambda i, at: (0, i)))
        elif planes > 1:
            shapes.append(jax.ShapeDtypeStruct((planes, rows * count, width), kind))
            specs.append(pl.BlockSpec((planes, rows, width), lambda i, at: (0, i, 0)))
        else:
            shapes.append(jax.ShapeDtypeStruct((rows * count, width), kind))
            specs.append(pl.BlockSpec((rows, width), lambda i, at: (i, 0)))
    given = [held[far] for held in lanes for far in range(count)]
    return pl.pallas_call(
        functools.partial(place_kernel, count, [o[1] for o in outs], [o[3] for o in outs]),
        grid_spec=pltpu.PrefetchScalarGridSpec(
            num_scalar_prefetch=1,
            grid=(count,),
            in_specs=[pl.BlockSpec((half, total), lambda i, at: (0, 0))] * len(given),
            out_specs=specs,
        ),
        out_shape=shapes,
        compiler_params=pltpu.CompilerParams(vmem_limit_bytes=VMEM_LIMIT),
        cost_estimate=pl.CostEstimate(flops=0, bytes_accessed=12 << 20, transcendentals=0),
        name="place_blocks",
    )(index.astype(jnp.int32).reshape(1), *given)


def swap_pairs(size, bit):
    return [(i, i ^ bit) for i in range(size)]


def shift_pairs(size, shift):
    return [(i, (i - shift) % size) for i in range(size)]


def bits_of(size):
    return [1 << i for i in range(size.bit_length() - 1)]


def pick(x, index, axis=0):
    return lax.dynamic_index_in_dim(x, index, axis, keepdims=False)


def after(x, *others):
    return lax.optimization_barrier((x,) + others)[0]


def xor_gather(x, axis, size, bits):
    held = dict(x) if isinstance(x, dict) else {0: x}
    for bit in bits:
        for far in list(held):
            held[far ^ bit] = lax.ppermute(held[far], axis, swap_pairs(size, bit))
    return held


def by_index(held, index, axis=0, out=None):
    shape = held[0].shape
    if out is None:
        out = jnp.zeros(shape[:axis] + (len(held),) + shape[axis:], held[0].dtype)
    for far, block in held.items():
        out = lax.dynamic_update_index_in_dim(out, block, index ^ far, axis)
    return out


def xor_scatter(blocks, axis_name, size, bits, steps, index, axis, all_steps=None):
    all_steps = list(all_steps or steps)
    left = sorted(all_steps[all_steps.index(steps[0]) :], reverse=True)
    blocks = blocks.reshape(blocks.shape[:axis] + (2,) * len(left) + blocks.shape[axis + 1 :])
    for bit, step in zip(bits, steps):
        at = axis + left.index(step)
        left.remove(step)
        side = (index // step) % 2
        got = lax.ppermute(narrow(pick(blocks, 1 - side, at)), axis_name, swap_pairs(size, bit))
        blocks = wide(pick(blocks, side, at)) + wide(got)
    tail = blocks.shape[axis + len(left) :]
    return blocks.reshape(blocks.shape[:axis] + ((2 ** len(left),) if left else ()) + tail)


def lane_bits(size):
    return bits_of(size), bits_of(size)[::-1]


def column_gather(lanes, size, cut=None, start=None):
    return [xor_gather(x, "dp", size, bits[start:cut]) for x, bits in zip(lanes, lane_bits(size))]


def gate_lanes(lanes, *gates):
    flat = [held[far] for held in lanes for far in held]
    flat = lax.optimization_barrier((*flat, *gates))
    flat = iter(flat)
    return [{far: next(flat) for far in held} for held in lanes]


def xor_span(bits):
    span = [0]
    for bit in bits:
        span += [far ^ bit for far in span]
    return span


def gather_part(lanes, size, part):
    out = []
    for held, bits in zip(lanes, lane_bits(size)):
        held = dict(held)
        sends = [(bits[i], far) for i in range(1, len(bits)) for far in xor_span(bits[:i])]
        half = len(sends) // 2
        for bit, far in sends[half:] if part else sends[:half]:
            held[far ^ bit] = lax.ppermute(held[far], "dp", swap_pairs(size, bit))
        out.append(held)
    return out


def column_scatter(lanes, size, column, cut=None, start=None):
    return [
        xor_scatter(x, "dp", size, bits[start:cut], bits[start:cut], column, 0, bits)
        for x, bits in zip(lanes, lane_bits(size))
    ]


def all_sum(x, sizes):
    for axis, size in sizes.items():
        for bit in bits_of(size):
            x = x + lax.ppermute(x, axis, swap_pairs(size, bit))
    return x


def make_local(columns, ranks):
    def local(
        layer_input, width_choice, routed_flag, mixer_gain, mixer_router, attention_weight,
        output_weight, hidden_gain, hidden_router, up_weight, down_weight, out_grad,
    ):
        column, rank = lax.axis_index("dp"), lax.axis_index("mp")
        rows, dim = layer_input.shape
        core = rank % 2
        group = SEQ_LEN // rows
        sequences = ranks // group
        place, sequence = rank % group, rank // group
        pair_bits = [b for b in bits_of(group) if b > 1]
        own_heads = output_weight.shape[0] // HD
        cols_local = up_weight.shape[1]
        width_own = lax.dynamic_slice_in_dim(width_choice, rank * rows, rows, 0)
        routed_own = lax.dynamic_slice_in_dim(routed_flag, rank * rows, rows, 0)
        cos, sin = rope_tables(SEQ_LEN, HD)

        def place_sequence(held, out=None):
            return by_index(held, place, 0, out).reshape(SEQ_LEN, -1)

        def core_sum(pairs, before=()):
            theirs = share_of(pairs, rows, 1 - core)
            got = lax.ppermute(theirs, "mp", swap_pairs(ranks, 1))
            pairs, theirs, before = lax.optimization_barrier((pairs, theirs, before))
            return wide(share_of(pairs, rows, core)) + wide(got), before

        def chip_sum(blocks):
            bits = pair_bits[::-1]
            return xor_scatter(blocks, "mp", ranks, bits, [b // 2 for b in bits], place // 2, 0)

        width = own_heads * HD
        chunk_rows = dim // columns
        half_rows = chunk_rows // 2

        def in_slice(w):
            return jnp.concatenate([w[:, p] for p in range(3)], axis=1)

        lanes_in = [
            in_slice(lax.dynamic_slice_in_dim(attention_weight, column * chunk_rows + at, half_rows, 0))
            for at in (0, half_rows)
        ]
        lanes_out = [
            lax.dynamic_slice_in_dim(output_weight, column * chunk_rows + at, half_rows, 1).T
            for at in (0, half_rows)
        ]
        input_wide = wide(layer_input)
        normed_one, scaled_one, inverse_one = norm_forward(input_wide, mixer_gain)
        low_one = narrow(normed_one)
        low_one, lanes_in, lanes_out = lax.optimization_barrier((low_one, lanes_in, lanes_out))
        held = xor_gather(low_one, "mp", ranks, pair_bits)
        fetched_in, fetched_out = [
            [[lax.ppermute(x, "mp", shift_pairs(ranks, k * group)) for x in lanes] for k in range(1, sequences)]
            for lanes in (lanes_in, lanes_out)
        ]
        sequence_width = lax.dynamic_slice_in_dim(width_choice[:, 0], sequence * SEQ_LEN, SEQ_LEN, 0)
        masks = []
        for k in range(sequences):
            heads = ((rank + k * group) % ranks) * own_heads + jnp.arange(own_heads, dtype=jnp.int32)
            masks.append((heads[None, :] * 4 < (sequence_width[:, None] + 1) * H).astype(jnp.float32))
        weights_in, weights_out = [in_slice(attention_weight)], [output_weight.T]
        held, fetched_in, masks, weights_in, weights_out, cos, sin = lax.optimization_barrier(
            (held, fetched_in, masks, weights_in, weights_out, cos, sin)
        )
        inputs_one = place_sequence(xor_gather(held, "mp", ranks, [1]))
        grads_all = lax.all_gather(after(out_grad, *[x for lanes in fetched_in for x in lanes]), "mp", axis=0, tiled=True)
        steps_in = [column_gather(x, columns, cut=1) for x in fetched_in]
        gate_one, state_one = gate_forward(normed_one, mixer_router, width_own[:, 0], routed_own[:, 0])

        kept = []
        for k in range(sequences):
            mask = masks[k]
            if k:
                steps, fetched, _ = lax.optimization_barrier((steps_in[k - 1], fetched_out[k - 1], kept[0][0]))
                held = column_gather(steps, columns, start=1)
                held_out = column_gather(fetched, columns, cut=1)
                held, held_out = lax.optimization_barrier((held, held_out))
                held_out = column_gather(held_out, columns, start=1)
                weights_in += place_blocks(held, column, [(1, 3 * width, jnp.bfloat16, False)])
                weights_out += place_blocks(held_out, column, [(1, width, jnp.bfloat16, False)])
            kept.append((*attend_forward(inputs_one, weights_in[k], cos, sin, mask), mask))
        mixer_branch = chip_sum(core_sum([(x[1], w) for x, w in zip(kept, weights_out)])[0])
        mixer_branch, grads_all = lax.optimization_barrier((mixer_branch, grads_all))
        top_down = product(grads_all, down_weight, (1, 1))

        middle = input_wide + gate_one[:, None] * mixer_branch
        normed_two, scaled_two, inverse_two = norm_forward(middle, hidden_gain)
        gate_two, state_two = gate_forward(normed_two, hidden_router, width_own[:, 1], routed_own[:, 1])
        inputs_two = lax.all_gather(narrow(normed_two), "mp", axis=0, tiled=True)
        gates = by_index(xor_gather(gate_two.reshape(-1, 128), "mp", ranks, bits_of(ranks)), rank).reshape(-1)

        inputs_two, top_down = lax.optimization_barrier((inputs_two, top_down))
        share, hidden, pre_grad, dots = hidden_pass(
            inputs_two, up_weight, top_down, gates, width_choice[:, 1:2], rank * cols_local
        )
        dots = dots.reshape(-1, 128)
        share, hidden, pre_grad = lax.optimization_barrier((share, hidden, pre_grad))
        normed_grad_two = wide(lax.psum_scatter(share, "mp", scatter_dimension=0, tiled=True))
        gate_grad_two = lax.dynamic_slice_in_dim(all_sum(dots, {"mp": ranks}).reshape(-1), rank * rows, rows, 0)
        gated = narrow(gates[:, None] * wide(grads_all))
        lanes = [narrow(product(hidden, gated, (0, 0))), narrow(product(inputs_two, pre_grad, (0, 0)))]
        lanes = [x.reshape(columns, -1, x.shape[1]) for x in lanes]
        lanes = column_scatter(lanes, columns, column, cut=1)
        hidden_share = narrow(product(hidden, down_weight, (1, 0)))
        blank = jnp.zeros((group, rows, dim), jnp.bfloat16)
        normed_grad_two, hidden_share, blank, *lanes = lax.optimization_barrier(
            (normed_grad_two, hidden_share, blank, *lanes)
        )
        lanes = [narrow(x) for x in column_scatter(lanes, columns, column, start=1)]

        router_part, _ = gate_backward(normed_two, hidden_router, state_two, gate_grad_two)
        middle_part, gain_two = norm_backward(normed_grad_two + router_part, scaled_two, inverse_two, hidden_gain)
        middle_grad = wide(out_grad) + middle_part
        grads_one = place_sequence(
            xor_gather(narrow(gate_one[:, None] * middle_grad), "mp", ranks, pair_bits + [1]), blank
        )
        helds = column_gather(lanes, columns, cut=1)
        grads_one, hidden_share, lanes = lax.optimization_barrier((grads_one, hidden_share, lanes))
        hidden_branch = wide(lax.psum_scatter(hidden_share, "mp", scatter_dimension=0, tiled=True))
        layer_output = narrow(middle + gate_two[:, None] * hidden_branch)

        pairs, sent = [], []
        grads_now = grads_one
        for k in range(sequences)[::-1]:
            qkv, heads_out, log_total, mask = kept[k]
            qkv_grad = attend_backward(grads_now, weights_out[k], qkv, log_total, cos, sin, mask)
            pairs.append((qkv_grad, weights_in[k]))
            if sent:
                qkv_grad, sent = lax.optimization_barrier((qkv_grad, sent))
            part = weight_grads(inputs_one, qkv_grad, grads_one, heads_out, columns)
            if k:
                grads_now, part, helds = lax.optimization_barrier((grads_now, part, helds))
                sent.append(column_scatter(part, columns, column, cut=1))
                normed_late, state_late, dots_late, middle_late, _ = lax.optimization_barrier(
                    (normed_two, state_two, gate_grad_two, middle_grad, part)
                )
                router_two = gate_backward(normed_late, hidden_router, state_late, dots_late)[1]
                gate_grad_one = jnp.sum(middle_late * mixer_branch, axis=1)
        helds, sent = lax.optimization_barrier((helds, sent))
        sent = [[narrow(x) for x in column_scatter(lanes, columns, column, start=1)] for lanes in sent]
        there = [
            [lax.ppermute(x, "mp", shift_pairs(ranks, -k * group)) for x in lanes]
            for k, lanes in zip(range(1, sequences)[::-1], sent)
        ]
        pairs, part = lax.optimization_barrier((pairs, part))
        blocks, helds = core_sum(pairs, gather_part(helds, columns, 0))
        blocks, there = lax.optimization_barrier((blocks, there))
        normed_grad_one = chip_sum(blocks)
        helds = gather_part(helds, columns, 1)
        pieces = column_scatter(part, columns, column)
        pieces, helds = lax.optimization_barrier((pieces, helds))
        for lanes in there:
            pieces = [p + wide(t) for p, t in zip(pieces, lanes)]
        spread = column_gather([narrow(p) for p in pieces], columns, cut=1)
        spread, helds = lax.optimization_barrier((spread, helds))
        spread = column_gather(spread, columns, start=1)
        down_sum, = place_blocks(helds[:1], column, [(1, dim, jnp.float32, False)])
        up_sum, = place_blocks(helds[1:], column, [(1, cols_local, jnp.float32, False)])
        attention_sum, output_sum = place_blocks(
            spread,
            column,
            [(3, width, jnp.float32, False), (1, width, jnp.float32, True)],
        )
        attention_sum = attention_sum.transpose(1, 0, 2)

        router_part_one, router_one = gate_backward(normed_one, mixer_router, state_one, gate_grad_one)
        input_part, gain_one = norm_backward(normed_grad_one + router_part_one, scaled_one, inverse_one, mixer_gain)
        input_grad = narrow(middle_grad + input_part)

        sizes = {"mp": ranks, "dp": columns}

        smalls = [gain_two, gain_one, router_two.T, router_one.T]
        small_sum = all_sum(jnp.concatenate([x.reshape(-1, 128) for x in smalls], axis=0), sizes)
        cuts = [dim // 128, 2 * dim // 128, (2 * dim + router_two.size) // 128]
        hidden_gain_sum, mixer_gain_sum, hidden_router_sum, mixer_router_sum = (
            x.reshape(-1, dim) for x in jnp.split(small_sum, cuts)
        )
        hidden_gain_sum, mixer_gain_sum = hidden_gain_sum[0], mixer_gain_sum[0]
        hidden_router_sum, mixer_router_sum = hidden_router_sum.T, mixer_router_sum.T
        return (
            layer_output, input_grad, mixer_gain_sum, mixer_router_sum, attention_sum, output_sum,
            hidden_gain_sum, hidden_router_sum, up_sum, down_sum,
        )

    return local


def solution(mesh):
    return jax.shard_map(
        make_local(mesh.shape["dp"], mesh.shape["mp"]),
        mesh=mesh,
        in_specs=(
            P(("dp", "mp"), None),
            P("dp", None),
            P("dp", None),
            P(),
            P(),
            P(None, None, "mp"),
            P("mp", None),
            P(),
            P(),
            P(None, "mp"),
            P("mp", None),
            P(("dp", "mp"), None),
        ),
        out_specs=(
            P(("dp", "mp"), None),
            P(("dp", "mp"), None),
            P(),
            P(),
            P(None, None, "mp"),
            P("mp", None),
            P(),
            P(),
            P(None, "mp"),
            P("mp", None),
        ),
        check_vma=False,
    )
```

```python
import functools
import math

import jax
import jax.numpy as jnp
from jax import lax
from jax.experimental import pallas as pl
from jax.experimental.pallas import tpu as pltpu
from jax.sharding import PartitionSpec as P

H = 16
HD = 128
FF = 8192
SEQ_LEN = 1024


EPSILON = 1e-05
NEG_LARGE = -1e30
HIGHEST = lax.Precision.HIGHEST


def norm_forward(values, gain_vec):
    row_mean = jnp.mean(values, axis=1, keepdims=True)
    centred = values - row_mean
    row_variance = jnp.mean(centred * centred, axis=1, keepdims=True)
    inverse_scale = lax.rsqrt(row_variance + EPSILON)
    scaled = centred * inverse_scale
    return (scaled * gain_vec[None, :], scaled, inverse_scale)


def norm_backward(normed_grad, scaled, inverse_scale, gain_vec):
    gain_grad = jnp.sum(normed_grad * scaled, axis=0)
    scaled_grad = normed_grad * gain_vec[None, :]
    first_mean = jnp.mean(scaled_grad, axis=1, keepdims=True)
    second_mean = jnp.mean(scaled_grad * scaled, axis=1, keepdims=True)
    return (inverse_scale * (scaled_grad - first_mean - scaled * second_mean), gain_grad)


def gate_forward(normed, router, width_col, routed_col):
    logits = jnp.dot(normed, router, precision=HIGHEST, preferred_element_type=jnp.float32)
    soft_probs = jax.nn.softmax(logits, axis=1)
    one_hot = (width_col[:, None] == jnp.arange(4, dtype=jnp.int32)[None, :]).astype(jnp.float32)
    chosen = jnp.sum(soft_probs * one_hot, axis=1)
    route_flags = routed_col.astype(jnp.float32)
    return (
        route_flags * 4.0 * chosen + (1.0 - route_flags),
        (soft_probs, one_hot, chosen, route_flags),
    )


def gate_backward(normed, router, gate_state, gate_grad):
    soft_probs, one_hot, chosen, route_flags = gate_state
    coefficient = route_flags * 4.0 * chosen * gate_grad
    logit_grad = coefficient[:, None] * (one_hot - soft_probs)
    router_grad = lax.dot_general(
        normed,
        logit_grad,
        (((0,), (0,)), ((), ())),
        precision=HIGHEST,
        preferred_element_type=jnp.float32,
    )
    normed_grad = lax.dot_general(
        logit_grad,
        router,
        (((1,), (1,)), ((), ())),
        precision=HIGHEST,
        preferred_element_type=jnp.float32,
    )
    return (normed_grad, router_grad)


Q_BLOCK = 256


def rope_tables(token_count, head_width):
    positions = jnp.arange(token_count, dtype=jnp.float32)
    frequency = jnp.exp(
        jnp.arange(head_width // 2, dtype=jnp.float32) * (-2.0 * math.log(10000.0) / head_width)
    )
    angles = positions[:, None] * frequency[None, :]
    cosine, sine = jnp.cos(angles), jnp.sin(angles)
    return jnp.concatenate([cosine, cosine], axis=1), jnp.concatenate([-sine, sine], axis=1)


def wide(x):
    return x.astype(jnp.float32)


def narrow(x):
    return x.astype(jnp.bfloat16)


def product(a, b, dims):
    return lax.dot_general(a, b, ((dims[:1], dims[1:]), ((), ())), preferred_element_type=jnp.float32)


def block_scores(queries, keys_all, start):
    scores = product(queries, keys_all, (1, 1)) * (1.0 / math.sqrt(HD))
    row = lax.broadcasted_iota(jnp.int32, scores.shape, 0) + start
    col = lax.broadcasted_iota(jnp.int32, scores.shape, 1)
    return jnp.where(col <= row, scores, NEG_LARGE)


def forward_kernel(x_ref, w_ref, cos_ref, sin_ref, mask_ref, qkv_ref, heads_ref, log_ref):
    tokens, heads = x_ref.shape[0], mask_ref.shape[1]
    width = heads * HD
    block = min(Q_BLOCK, tokens)
    for start in range(0, tokens, block):
        here, end = slice(start, start + block), start + block
        x = x_ref[here, :]
        cos, sin = cos_ref[here, :], sin_ref[here, :]
        for part in range(3):
            rows = product(x, w_ref[:, part * width : (part + 1) * width], (1, 0))
            for head in range(heads):
                value = rows[:, head * HD : (head + 1) * HD]
                if part < 2:
                    value = value * cos + pltpu.roll(value, HD // 2, 1) * sin
                at = part * width + head * HD
                qkv_ref[here, at : at + HD] = narrow(value)
        for head in range(heads):
            at = head * HD
            lanes, key_lanes, value_lanes = (slice(at + p * width, at + p * width + HD) for p in range(3))
            scores = block_scores(qkv_ref[here, lanes], qkv_ref[:end, key_lanes], start)
            row_max = jnp.max(scores, axis=1, keepdims=True)
            shifted = jnp.exp(scores - row_max)
            total = jnp.sum(shifted, axis=1, keepdims=True)
            mix = product(narrow(shifted * (1.0 / total)), qkv_ref[:end, value_lanes], (1, 0))
            heads_ref[here, lanes] = narrow(mix * mask_ref[here, head : head + 1])
            log_ref[here, head : head + 1] = row_max + jnp.log(total)


def backward_kernel(g_ref, w_ref, qkv_ref, log_ref, cos_ref, sin_ref, mask_ref, out_ref, keys_acc, values_acc):
    tokens, heads = g_ref.shape[0], mask_ref.shape[1]
    width = heads * HD
    block = min(Q_BLOCK, tokens)
    scale = 1.0 / math.sqrt(HD)
    for start in range(0, tokens, block):
        here, end = slice(start, start + block), start + block
        cos, sin = cos_ref[here, :], sin_ref[here, :]
        rows = narrow(product(g_ref[here, :], w_ref[...], (1, 0)))
        for head in range(heads):
            at = head * HD
            lanes, key_lanes, value_lanes = (slice(at + p * width, at + p * width + HD) for p in range(3))
            heads_grad = rows[:, lanes] * narrow(mask_ref[here, head : head + 1])
            queries, keys_all = qkv_ref[here, lanes], qkv_ref[:end, key_lanes]
            scores = block_scores(queries, keys_all, start)
            probs = jnp.exp(scores - log_ref[here, head : head + 1])
            values_part = product(narrow(probs), heads_grad, (0, 0))
            probs_grad = product(heads_grad, qkv_ref[:end, value_lanes], (1, 1))
            centre = jnp.sum(probs * probs_grad, axis=1, keepdims=True)
            score_grad = narrow(probs * (probs_grad - centre))
            queries_grad = product(score_grad, keys_all, (1, 0)) * scale
            keys_part = product(score_grad, queries, (0, 0)) * scale
            turned = queries_grad * cos - pltpu.roll(queries_grad, HD // 2, 1) * sin
            out_ref[here, lanes] = narrow(turned)
            if start:
                values_acc[:start, lanes] += values_part[:start]
                keys_acc[:start, lanes] += keys_part[:start]
            values_acc[here, lanes] = values_part[start:]
            keys_acc[here, lanes] = keys_part[start:]
    for start in range(0, tokens, block):
        here = slice(start, start + block)
        cos, sin = cos_ref[here, :], sin_ref[here, :]
        out_ref[here, 2 * width :] = narrow(values_acc[here, :])
        for head in range(heads):
            at = head * HD
            value = keys_acc[here, at : at + HD]
            out_ref[here, width + at : width + at + HD] = narrow(value * cos - pltpu.roll(value, HD // 2, 1) * sin)


def share_kernel(side_ref, *refs):
    *given, out_ref = refs
    total = product(given[0][...], given[1][...], (1, 1))
    for a_ref, w_ref in zip(given[2::2], given[3::2]):
        total = total + product(a_ref[...], w_ref[...], (1, 1))
    out_ref[0] = narrow(total)


def weight_kernel(x_ref, q_ref, g_ref, h_ref, *outs):
    width = h_ref.shape[1]
    half = x_ref.shape[1] // 2
    for lane, out_ref in enumerate(outs):
        here = slice(lane * half, (lane + 1) * half)
        out_ref[0, :, : 3 * width] = narrow(product(x_ref[:, here], q_ref[...], (0, 0)))
        out_ref[0, :, 3 * width :] = narrow(product(g_ref[:, here], h_ref[...], (0, 0)))


def hidden_kernel(offset_ref, x_ref, up_ref, top_ref, gate_ref, width_ref, share_ref, hidden_ref, grad_ref, dots_ref):
    pre = product(x_ref[...], up_ref[...], (1, 0))
    column = lax.broadcasted_iota(jnp.int32, pre.shape, 1) + offset_ref[0]
    live = column * 4 < (width_ref[...] + 1) * FF
    relu_act = jnp.where(live, jnp.maximum(pre, 0.0), 0.0)
    hidden = narrow(relu_act * relu_act)
    top = top_ref[...]
    grad = narrow(top * gate_ref[...] * 2.0 * relu_act)
    hidden_ref[...] = hidden
    grad_ref[...] = grad
    dots = jnp.sum(wide(hidden) * top, axis=1, keepdims=True)
    dots_ref[...] = jnp.broadcast_to(dots, (dots.shape[0], 128)).T[:1]
    share_ref[...] = narrow(product(grad, up_ref[...], (1, 1)))


def place_kernel(count, widths, turned, at_ref, *refs):
    lanes = (len(refs) - len(widths)) // count
    blocks, outs = refs[: lanes * count], refs[lanes * count :]
    half = blocks[0].shape[0]
    for far in range(count):

        @pl.when((pl.program_id(0) ^ at_ref[0]) == far)
        def _():
            for lane in range(lanes):
                here = slice(lane * half, (lane + 1) * half)
                block = blocks[lane * count + far]
                start = 0
                for out_ref, width, turn in zip(outs, widths, turned):
                    for part in range(out_ref.shape[0] if len(out_ref.shape) == 3 else 1):
                        value = block[:, start : start + width].astype(out_ref.dtype)
                        start += width
                        if turn:
                            out_ref[:, here] = value.T
                        elif len(out_ref.shape) == 3:
                            out_ref[part, here, :] = value
                        else:
                            out_ref[here, :] = value


VMEM_LIMIT = 56 * 1024 * 1024


def whole_specs(count):
    return [pl.BlockSpec(memory_space=pltpu.VMEM)] * count


def attend_forward(x, w, cos, sin, mask):
    tokens, heads = mask.shape
    dim, width = w.shape[0], heads * HD
    return pl.pallas_call(
        forward_kernel,
        out_shape=[
            jax.ShapeDtypeStruct((tokens, 3 * width), jnp.bfloat16),
            jax.ShapeDtypeStruct((tokens, width), jnp.bfloat16),
            jax.ShapeDtypeStruct((tokens, heads), jnp.float32),
        ],
        in_specs=whole_specs(5),
        out_specs=whole_specs(3),
        compiler_params=pltpu.CompilerParams(vmem_limit_bytes=VMEM_LIMIT),
        cost_estimate=pl.CostEstimate(
            flops=6 * tokens * dim * width + 2 * tokens * tokens * width,
            bytes_accessed=12 << 20,
            transcendentals=tokens * tokens * heads // 2,
        ),
        name="attend_forward",
    )(x, w, cos, sin, mask)


def attend_backward(g, w, qkv, log_total, cos, sin, mask):
    tokens, heads = mask.shape
    dim, width = w.shape[0], heads * HD
    return pl.pallas_call(
        backward_kernel,
        out_shape=jax.ShapeDtypeStruct((tokens, 3 * width), jnp.bfloat16),
        in_specs=whole_specs(7),
        out_specs=whole_specs(1)[0],
        scratch_shapes=[pltpu.VMEM((tokens, width), jnp.float32)] * 2,
        compiler_params=pltpu.CompilerParams(vmem_limit_bytes=VMEM_LIMIT),
        cost_estimate=pl.CostEstimate(
            flops=2 * tokens * dim * width + 5 * tokens * tokens * width,
            bytes_accessed=12 << 20,
            transcendentals=tokens * tokens * heads // 2,
        ),
        name="attend_backward",
    )(g, w, qkv, log_total, cos, sin, mask)


def share_of(pairs, rows, side):
    tokens, depth = pairs[0][0].shape
    dim = pairs[0][1].shape[0]
    chips = tokens // rows // 2
    specs = [
        pl.BlockSpec((rows, depth), lambda i, side: (2 * i + side[0], 0)),
        pl.BlockSpec((dim, depth), lambda i, side: (0, 0)),
    ] * len(pairs)
    return pl.pallas_call(
        share_kernel,
        grid_spec=pltpu.PrefetchScalarGridSpec(
            num_scalar_prefetch=1,
            grid=(chips,),
            in_specs=specs,
            out_specs=pl.BlockSpec((1, rows, dim), lambda i, side: (i, 0, 0)),
        ),
        out_shape=jax.ShapeDtypeStruct((chips, rows, dim), jnp.bfloat16),
        compiler_params=pltpu.CompilerParams(vmem_limit_bytes=VMEM_LIMIT),
        cost_estimate=pl.CostEstimate(
            flops=tokens * dim * depth * len(pairs), bytes_accessed=12 << 20, transcendentals=0
        ),
        name="share_of",
    )(side.astype(jnp.int32).reshape(1), *[x for pair in pairs for x in pair])


def hidden_pass(x, up, top_down, gates, widths, offset):
    tokens, dim = x.shape
    cols = up.shape[1]
    block = 256
    rows_of = lambda n: pl.BlockSpec((block, n), lambda i, at: (i, 0))
    return pl.pallas_call(
        hidden_kernel,
        grid_spec=pltpu.PrefetchScalarGridSpec(
            num_scalar_prefetch=1,
            grid=(tokens // block,),
            in_specs=[rows_of(dim), pl.BlockSpec((dim, cols), lambda i, at: (0, 0)), rows_of(cols), rows_of(1), rows_of(1)],
            out_specs=[rows_of(dim), rows_of(cols), rows_of(cols), pl.BlockSpec((1, block), lambda i, at: (0, i))],
        ),
        out_shape=[
            jax.ShapeDtypeStruct((tokens, dim), jnp.bfloat16),
            jax.ShapeDtypeStruct((tokens, cols), jnp.bfloat16),
            jax.ShapeDtypeStruct((tokens, cols), jnp.bfloat16),
            jax.ShapeDtypeStruct((1, tokens), jnp.float32),
        ],
        compiler_params=pltpu.CompilerParams(vmem_limit_bytes=VMEM_LIMIT),
        cost_estimate=pl.CostEstimate(flops=4 * tokens * dim * cols, bytes_accessed=40 << 20, transcendentals=0),
        name="hidden_pass",
    )(offset.astype(jnp.int32).reshape(1), x, up, top_down, gates[:, None], widths)


def weight_grads(x, qkv_grad, g, heads_out, count):
    tokens, dim = x.shape
    width = heads_out.shape[1]
    block = dim // count
    out = jax.ShapeDtypeStruct((count, block // 2, 4 * width), jnp.bfloat16)
    return pl.pallas_call(
        weight_kernel,
        grid=(count,),
        out_shape=[out, out],
        in_specs=[
            pl.BlockSpec((tokens, block), lambda i: (0, i)),
            pl.BlockSpec((tokens, 3 * width), lambda i: (0, 0)),
            pl.BlockSpec((tokens, block), lambda i: (0, i)),
            pl.BlockSpec((tokens, width), lambda i: (0, 0)),
        ],
        out_specs=[pl.BlockSpec((1, block // 2, 4 * width), lambda i: (i, 0, 0))] * 2,
        compiler_params=pltpu.CompilerParams(vmem_limit_bytes=VMEM_LIMIT),
        cost_estimate=pl.CostEstimate(flops=8 * tokens * dim * width, bytes_accessed=14 << 20, transcendentals=0),
        name="weight_grads",
    )(x, qkv_grad, g, heads_out)


def place_blocks(lanes, index, outs):
    count = len(lanes[0])
    half, total = lanes[0][0].shape
    rows = len(lanes) * half
    shapes, specs = [], []
    for planes, width, kind, turned in outs:
        if turned:
            shapes.append(jax.ShapeDtypeStruct((width, rows * count), kind))
            specs.append(pl.BlockSpec((width, rows), lambda i, at: (0, i)))
        elif planes > 1:
            shapes.append(jax.ShapeDtypeStruct((planes, rows * count, width), kind))
            specs.append(pl.BlockSpec((planes, rows, width), lambda i, at: (0, i, 0)))
        else:
            shapes.append(jax.ShapeDtypeStruct((rows * count, width), kind))
            specs.append(pl.BlockSpec((rows, width), lambda i, at: (i, 0)))
    given = [held[far] for held in lanes for far in range(count)]
    return pl.pallas_call(
        functools.partial(place_kernel, count, [o[1] for o in outs], [o[3] for o in outs]),
        grid_spec=pltpu.PrefetchScalarGridSpec(
            num_scalar_prefetch=1,
            grid=(count,),
            in_specs=[pl.BlockSpec((half, total), lambda i, at: (0, 0))] * len(given),
            out_specs=specs,
        ),
        out_shape=shapes,
        compiler_params=pltpu.CompilerParams(vmem_limit_bytes=VMEM_LIMIT),
        cost_estimate=pl.CostEstimate(flops=0, bytes_accessed=12 << 20, transcendentals=0),
        name="place_blocks",
    )(index.astype(jnp.int32).reshape(1), *given)


def swap_pairs(size, bit):
    return [(i, i ^ bit) for i in range(size)]


def shift_pairs(size, shift):
    return [(i, (i - shift) % size) for i in range(size)]


def bits_of(size):
    return [1 << i for i in range(size.bit_length() - 1)]


def pick(x, index, axis=0):
    return lax.dynamic_index_in_dim(x, index, axis, keepdims=False)


def after(x, *others):
    return lax.optimization_barrier((x,) + others)[0]


def xor_gather(x, axis, size, bits):
    held = dict(x) if isinstance(x, dict) else {0: x}
    for bit in bits:
        for far in list(held):
            held[far ^ bit] = lax.ppermute(held[far], axis, swap_pairs(size, bit))
    return held


def by_index(held, index, axis=0, out=None):
    shape = held[0].shape
    if out is None:
        out = jnp.zeros(shape[:axis] + (len(held),) + shape[axis:], held[0].dtype)
    for far, block in held.items():
        out = lax.dynamic_update_index_in_dim(out, block, index ^ far, axis)
    return out


def xor_scatter(blocks, axis_name, size, bits, steps, index, axis, all_steps=None):
    all_steps = list(all_steps or steps)
    left = sorted(all_steps[all_steps.index(steps[0]) :], reverse=True)
    blocks = blocks.reshape(blocks.shape[:axis] + (2,) * len(left) + blocks.shape[axis + 1 :])
    for bit, step in zip(bits, steps):
        at = axis + left.index(step)
        left.remove(step)
        side = (index // step) % 2
        got = lax.ppermute(narrow(pick(blocks, 1 - side, at)), axis_name, swap_pairs(size, bit))
        blocks = wide(pick(blocks, side, at)) + wide(got)
    tail = blocks.shape[axis + len(left) :]
    return blocks.reshape(blocks.shape[:axis] + ((2 ** len(left),) if left else ()) + tail)


def lane_bits(size):
    return bits_of(size), bits_of(size)[::-1]


def column_gather(lanes, size, cut=None, start=None):
    return [xor_gather(x, "dp", size, bits[start:cut]) for x, bits in zip(lanes, lane_bits(size))]


def gate_lanes(lanes, *gates):
    flat = [held[far] for held in lanes for far in held]
    flat = lax.optimization_barrier((*flat, *gates))
    flat = iter(flat)
    return [{far: next(flat) for far in held} for held in lanes]


def xor_span(bits):
    span = [0]
    for bit in bits:
        span += [far ^ bit for far in span]
    return span


def gather_part(lanes, size, part):
    out = []
    for held, bits in zip(lanes, lane_bits(size)):
        held = dict(held)
        sends = [(bits[i], far) for i in range(1, len(bits)) for far in xor_span(bits[:i])]
        half = len(sends) // 2
        for bit, far in sends[half:] if part else sends[:half]:
            held[far ^ bit] = lax.ppermute(held[far], "dp", swap_pairs(size, bit))
        out.append(held)
    return out


def column_scatter(lanes, size, column, cut=None, start=None):
    return [
        xor_scatter(x, "dp", size, bits[start:cut], bits[start:cut], column, 0, bits)
        for x, bits in zip(lanes, lane_bits(size))
    ]


def all_sum(x, sizes):
    for axis, size in sizes.items():
        for bit in bits_of(size):
            x = x + lax.ppermute(x, axis, swap_pairs(size, bit))
    return x


def make_local(columns, ranks):
    def local(
        layer_input, width_choice, routed_flag, mixer_gain, mixer_router, attention_weight,
        output_weight, hidden_gain, hidden_router, up_weight, down_weight, out_grad,
    ):
        column, rank = lax.axis_index("dp"), lax.axis_index("mp")
        rows, dim = layer_input.shape
        core = rank % 2
        group = SEQ_LEN // rows
        sequences = ranks // group
        place, sequence = rank % group, rank // group
        pair_bits = [b for b in bits_of(group) if b > 1]
        own_heads = output_weight.shape[0] // HD
        cols_local = up_weight.shape[1]
        width_own = lax.dynamic_slice_in_dim(width_choice, rank * rows, rows, 0)
        routed_own = lax.dynamic_slice_in_dim(routed_flag, rank * rows, rows, 0)
        cos, sin = rope_tables(SEQ_LEN, HD)

        def place_sequence(held, out=None):
            return by_index(held, place, 0, out).reshape(SEQ_LEN, -1)

        def core_sum(pairs, before=()):
            theirs = share_of(pairs, rows, 1 - core)
            got = lax.ppermute(theirs, "mp", swap_pairs(ranks, 1))
            pairs, theirs, before = lax.optimization_barrier((pairs, theirs, before))
            return wide(share_of(pairs, rows, core)) + wide(got), before

        def chip_sum(blocks):
            bits = pair_bits[::-1]
            return xor_scatter(blocks, "mp", ranks, bits, [b // 2 for b in bits], place // 2, 0)

        width = own_heads * HD
        chunk_rows = dim // columns
        half_rows = chunk_rows // 2

        def in_slice(w):
            return jnp.concatenate([w[:, p] for p in range(3)], axis=1)

        lanes_in = [
            in_slice(lax.dynamic_slice_in_dim(attention_weight, column * chunk_rows + at, half_rows, 0))
            for at in (0, half_rows)
        ]
        lanes_out = [lax.dynamic_slice_in_dim(output_weight, column * chunk_rows, chunk_rows, 1).T]
        input_wide = wide(layer_input)
        normed_one, scaled_one, inverse_one = norm_forward(input_wide, mixer_gain)
        low_one = narrow(normed_one)
        low_one, lanes_in = lax.optimization_barrier((low_one, lanes_in))
        held = xor_gather(low_one, "mp", ranks, pair_bits)
        fetched_in, fetched_out = [
            [[lax.ppermute(x, "mp", shift_pairs(ranks, k * group)) for x in lanes] for k in range(1, sequences)]
            for lanes in (lanes_in, lanes_out)
        ]
        sequence_width = lax.dynamic_slice_in_dim(width_choice[:, 0], sequence * SEQ_LEN, SEQ_LEN, 0)
        masks = []
        for k in range(sequences):
            heads = ((rank + k * group) % ranks) * own_heads + jnp.arange(own_heads, dtype=jnp.int32)
            masks.append((heads[None, :] * 4 < (sequence_width[:, None] + 1) * H).astype(jnp.float32))
        weights_in, weights_out = [in_slice(attention_weight)], [output_weight.T]
        held, fetched_in, masks, weights_in, weights_out, cos, sin = lax.optimization_barrier(
            (held, fetched_in, masks, weights_in, weights_out, cos, sin)
        )
        inputs_one = place_sequence(xor_gather(held, "mp", ranks, [1]))
        grads_all = lax.all_gather(after(out_grad, *[x for lanes in fetched_in for x in lanes]), "mp", axis=0, tiled=True)
        steps_in = [column_gather(x, columns, cut=1) for x in fetched_in]
        gate_one, state_one = gate_forward(normed_one, mixer_router, width_own[:, 0], routed_own[:, 0])

        kept = []
        for k in range(sequences):
            mask = masks[k]
            if k:
                steps, fetched, _ = lax.optimization_barrier((steps_in[k - 1], fetched_out[k - 1], kept[0][0]))
                held = column_gather(steps, columns, start=1)
                held_out = column_gather(fetched, columns, cut=1)
                held, held_out = lax.optimization_barrier((held, held_out))
                held_out = column_gather(held_out, columns, start=1)
                weights_in += place_blocks(held, column, [(1, 3 * width, jnp.bfloat16, False)])
                weights_out += place_blocks(held_out, column, [(1, width, jnp.bfloat16, False)])
            kept.append((*attend_forward(inputs_one, weights_in[k], cos, sin, mask), mask))
        mixer_branch = chip_sum(core_sum([(x[1], w) for x, w in zip(kept, weights_out)])[0])
        mixer_branch, grads_all = lax.optimization_barrier((mixer_branch, grads_all))
        top_down = product(grads_all, down_weight, (1, 1))

        middle = input_wide + gate_one[:, None] * mixer_branch
        normed_two, scaled_two, inverse_two = norm_forward(middle, hidden_gain)
        gate_two, state_two = gate_forward(normed_two, hidden_router, width_own[:, 1], routed_own[:, 1])
        inputs_two = lax.all_gather(narrow(normed_two), "mp", axis=0, tiled=True)
        gates = by_index(xor_gather(gate_two.reshape(-1, 128), "mp", ranks, bits_of(ranks)), rank).reshape(-1)

        inputs_two, top_down = lax.optimization_barrier((inputs_two, top_down))
        share, hidden, pre_grad, dots = hidden_pass(
            inputs_two, up_weight, top_down, gates, width_choice[:, 1:2], rank * cols_local
        )
        dots = dots.reshape(-1, 128)
        share, hidden, pre_grad = lax.optimization_barrier((share, hidden, pre_grad))
        normed_grad_two = lax.psum_scatter(share, "mp", scatter_dimension=0, tiled=True)
        gate_grad_two = lax.dynamic_slice_in_dim(all_sum(dots, {"mp": ranks}).reshape(-1), rank * rows, rows, 0)
        gated = narrow(gates[:, None] * wide(grads_all))
        lanes = [narrow(product(hidden, gated, (0, 0))), narrow(product(inputs_two, pre_grad, (0, 0)))]
        lanes = [x.reshape(columns, -1, x.shape[1]) for x in lanes]
        lanes = column_scatter(lanes, columns, column, cut=1)
        hidden_share = narrow(product(hidden, down_weight, (1, 0)))
        blank = jnp.zeros((group, rows, dim), jnp.bfloat16)
        normed_grad_two, hidden_share, blank, *lanes = lax.optimization_barrier(
            (normed_grad_two, hidden_share, blank, *lanes)
        )
        normed_grad_two = wide(normed_grad_two)
        lanes = [narrow(x) for x in column_scatter(lanes, columns, column, start=1)]

        router_part, _ = gate_backward(normed_two, hidden_router, state_two, gate_grad_two)
        middle_part, gain_two = norm_backward(normed_grad_two + router_part, scaled_two, inverse_two, hidden_gain)
        middle_grad = wide(out_grad) + middle_part
        grads_one = place_sequence(
            xor_gather(narrow(gate_one[:, None] * middle_grad), "mp", ranks, pair_bits + [1]), blank
        )
        helds = column_gather(lanes, columns, cut=1)
        grads_one, hidden_share, lanes = lax.optimization_barrier((grads_one, hidden_share, lanes))
        hidden_branch = wide(lax.psum_scatter(hidden_share, "mp", scatter_dimension=0, tiled=True))
        layer_output = narrow(middle + gate_two[:, None] * hidden_branch)

        pairs, sent = [], []
        grads_now = grads_one
        for k in range(sequences)[::-1]:
            qkv, heads_out, log_total, mask = kept[k]
            qkv_grad = attend_backward(grads_now, weights_out[k], qkv, log_total, cos, sin, mask)
            pairs.append((qkv_grad, weights_in[k]))
            if sent:
                qkv_grad, sent = lax.optimization_barrier((qkv_grad, sent))
            part = weight_grads(inputs_one, qkv_grad, grads_one, heads_out, columns)
            if k:
                grads_now, part, helds = lax.optimization_barrier((grads_now, part, helds))
                sent.append(column_scatter(part, columns, column, cut=1))
                normed_late, state_late, dots_late, middle_late, _ = lax.optimization_barrier(
                    (normed_two, state_two, gate_grad_two, middle_grad, part)
                )
                router_two = gate_backward(normed_late, hidden_router, state_late, dots_late)[1]
                gate_grad_one = jnp.sum(middle_late * mixer_branch, axis=1)
        helds, sent = lax.optimization_barrier((helds, sent))
        sent = [[narrow(x) for x in column_scatter(lanes, columns, column, start=1)] for lanes in sent]
        there = [
            [lax.ppermute(x, "mp", shift_pairs(ranks, -k * group)) for x in lanes]
            for k, lanes in zip(range(1, sequences)[::-1], sent)
        ]
        pairs, part = lax.optimization_barrier((pairs, part))
        blocks, helds = core_sum(pairs, gather_part(helds, columns, 0))
        blocks, there = lax.optimization_barrier((blocks, there))
        normed_grad_one = chip_sum(blocks)
        helds = gather_part(helds, columns, 1)
        pieces = column_scatter(part, columns, column)
        pieces, helds = lax.optimization_barrier((pieces, helds))
        for lanes in there:
            pieces = [p + wide(t) for p, t in zip(pieces, lanes)]
        spread = column_gather([narrow(p) for p in pieces], columns, cut=1)
        spread, helds = lax.optimization_barrier((spread, helds))
        spread = column_gather(spread, columns, start=1)
        down_sum, = place_blocks(helds[:1], column, [(1, dim, jnp.float32, False)])
        up_sum, = place_blocks(helds[1:], column, [(1, cols_local, jnp.float32, False)])
        attention_sum, output_sum = place_blocks(
            spread,
            column,
            [(3, width, jnp.float32, False), (1, width, jnp.float32, True)],
        )
        attention_sum = attention_sum.transpose(1, 0, 2)

        router_part_one, router_one = gate_backward(normed_one, mixer_router, state_one, gate_grad_one)
        input_part, gain_one = norm_backward(normed_grad_one + router_part_one, scaled_one, inverse_one, mixer_gain)
        input_grad = narrow(middle_grad + input_part)

        sizes = {"mp": ranks, "dp": columns}

        smalls = [gain_two, gain_one, router_two.T, router_one.T]
        small_sum = all_sum(jnp.concatenate([x.reshape(-1, 128) for x in smalls], axis=0), sizes)
        cuts = [dim // 128, 2 * dim // 128, (2 * dim + router_two.size) // 128]
        hidden_gain_sum, mixer_gain_sum, hidden_router_sum, mixer_router_sum = (
            x.reshape(-1, dim) for x in jnp.split(small_sum, cuts)
        )
        hidden_gain_sum, mixer_gain_sum = hidden_gain_sum[0], mixer_gain_sum[0]
        hidden_router_sum, mixer_router_sum = hidden_router_sum.T, mixer_router_sum.T
        return (
            layer_output, input_grad, mixer_gain_sum, mixer_router_sum, attention_sum, output_sum,
            hidden_gain_sum, hidden_router_sum, up_sum, down_sum,
        )

    return local


def solution(mesh):
    return jax.shard_map(
        make_local(mesh.shape["dp"], mesh.shape["mp"]),
        mesh=mesh,
        in_specs=(
            P(("dp", "mp"), None),
            P("dp", None),
            P("dp", None),
            P(),
            P(),
            P(None, None, "mp"),
            P("mp", None),
            P(),
            P(),
            P(None, "mp"),
            P("mp", None),
            P(("dp", "mp"), None),
        ),
        out_specs=(
            P(("dp", "mp"), None),
            P(("dp", "mp"), None),
            P(),
            P(),
            P(None, None, "mp"),
            P("mp", None),
            P(),
            P(),
            P(None, "mp"),
            P("mp", None),
        ),
        check_vma=False,
    )
```

```python
import functools
import math

import jax
import jax.numpy as jnp
from jax import lax
from jax.experimental import pallas as pl
from jax.experimental.pallas import tpu as pltpu
from jax.sharding import PartitionSpec as P

H = 16
HD = 128
FF = 8192
SEQ_LEN = 1024


EPSILON = 1e-05
NEG_LARGE = -1e30
HIGHEST = lax.Precision.HIGHEST


def norm_forward(values, gain_vec):
    row_mean = jnp.mean(values, axis=1, keepdims=True)
    centred = values - row_mean
    row_variance = jnp.mean(centred * centred, axis=1, keepdims=True)
    inverse_scale = lax.rsqrt(row_variance + EPSILON)
    scaled = centred * inverse_scale
    return (scaled * gain_vec[None, :], scaled, inverse_scale)


def norm_backward(normed_grad, scaled, inverse_scale, gain_vec):
    gain_grad = jnp.sum(normed_grad * scaled, axis=0)
    scaled_grad = normed_grad * gain_vec[None, :]
    first_mean = jnp.mean(scaled_grad, axis=1, keepdims=True)
    second_mean = jnp.mean(scaled_grad * scaled, axis=1, keepdims=True)
    return (inverse_scale * (scaled_grad - first_mean - scaled * second_mean), gain_grad)


def gate_forward(normed, router, width_col, routed_col):
    logits = jnp.dot(normed, router, precision=HIGHEST, preferred_element_type=jnp.float32)
    soft_probs = jax.nn.softmax(logits, axis=1)
    one_hot = (width_col[:, None] == jnp.arange(4, dtype=jnp.int32)[None, :]).astype(jnp.float32)
    chosen = jnp.sum(soft_probs * one_hot, axis=1)
    route_flags = routed_col.astype(jnp.float32)
    return (
        route_flags * 4.0 * chosen + (1.0 - route_flags),
        (soft_probs, one_hot, chosen, route_flags),
    )


def gate_backward(normed, router, gate_state, gate_grad):
    soft_probs, one_hot, chosen, route_flags = gate_state
    coefficient = route_flags * 4.0 * chosen * gate_grad
    logit_grad = coefficient[:, None] * (one_hot - soft_probs)
    router_grad = lax.dot_general(
        normed,
        logit_grad,
        (((0,), (0,)), ((), ())),
        precision=HIGHEST,
        preferred_element_type=jnp.float32,
    )
    normed_grad = lax.dot_general(
        logit_grad,
        router,
        (((1,), (1,)), ((), ())),
        precision=HIGHEST,
        preferred_element_type=jnp.float32,
    )
    return (normed_grad, router_grad)


Q_BLOCK = 256


def rope_tables(token_count, head_width):
    positions = jnp.arange(token_count, dtype=jnp.float32)
    frequency = jnp.exp(
        jnp.arange(head_width // 2, dtype=jnp.float32) * (-2.0 * math.log(10000.0) / head_width)
    )
    angles = positions[:, None] * frequency[None, :]
    cosine, sine = jnp.cos(angles), jnp.sin(angles)
    return jnp.concatenate([cosine, cosine], axis=1), jnp.concatenate([-sine, sine], axis=1)


def wide(x):
    return x.astype(jnp.float32)


def narrow(x):
    return x.astype(jnp.bfloat16)


def product(a, b, dims):
    return lax.dot_general(a, b, ((dims[:1], dims[1:]), ((), ())), preferred_element_type=jnp.float32)


def block_scores(queries, keys_all, start):
    scores = product(queries, keys_all, (1, 1)) * (1.0 / math.sqrt(HD))
    row = lax.broadcasted_iota(jnp.int32, scores.shape, 0) + start
    col = lax.broadcasted_iota(jnp.int32, scores.shape, 1)
    return jnp.where(col <= row, scores, NEG_LARGE)


def forward_kernel(x_ref, w_ref, cos_ref, sin_ref, mask_ref, qkv_ref, heads_ref, log_ref):
    tokens, heads = x_ref.shape[0], mask_ref.shape[1]
    width = heads * HD
    block = min(Q_BLOCK, tokens)
    for start in range(0, tokens, block):
        here, end = slice(start, start + block), start + block
        x = x_ref[here, :]
        cos, sin = cos_ref[here, :], sin_ref[here, :]
        for part in range(3):
            rows = product(x, w_ref[:, part * width : (part + 1) * width], (1, 0))
            for head in range(heads):
                value = rows[:, head * HD : (head + 1) * HD]
                if part < 2:
                    value = value * cos + pltpu.roll(value, HD // 2, 1) * sin
                at = part * width + head * HD
                qkv_ref[here, at : at + HD] = narrow(value)
        for head in range(heads):
            at = head * HD
            lanes, key_lanes, value_lanes = (slice(at + p * width, at + p * width + HD) for p in range(3))
            scores = block_scores(qkv_ref[here, lanes], qkv_ref[:end, key_lanes], start)
            row_max = jnp.max(scores, axis=1, keepdims=True)
            shifted = jnp.exp(scores - row_max)
            total = jnp.sum(shifted, axis=1, keepdims=True)
            mix = product(narrow(shifted * (1.0 / total)), qkv_ref[:end, value_lanes], (1, 0))
            heads_ref[here, lanes] = narrow(mix * mask_ref[here, head : head + 1])
            log_ref[here, head : head + 1] = row_max + jnp.log(total)


def backward_kernel(g_ref, w_ref, qkv_ref, log_ref, cos_ref, sin_ref, mask_ref, out_ref, keys_acc, values_acc):
    tokens, heads = g_ref.shape[0], mask_ref.shape[1]
    width = heads * HD
    block = min(Q_BLOCK, tokens)
    scale = 1.0 / math.sqrt(HD)
    for start in range(0, tokens, block):
        here, end = slice(start, start + block), start + block
        cos, sin = cos_ref[here, :], sin_ref[here, :]
        rows = narrow(product(g_ref[here, :], w_ref[...], (1, 0)))
        for head in range(heads):
            at = head * HD
            lanes, key_lanes, value_lanes = (slice(at + p * width, at + p * width + HD) for p in range(3))
            heads_grad = rows[:, lanes] * narrow(mask_ref[here, head : head + 1])
            queries, keys_all = qkv_ref[here, lanes], qkv_ref[:end, key_lanes]
            scores = block_scores(queries, keys_all, start)
            probs = jnp.exp(scores - log_ref[here, head : head + 1])
            values_part = product(narrow(probs), heads_grad, (0, 0))
            probs_grad = product(heads_grad, qkv_ref[:end, value_lanes], (1, 1))
            centre = jnp.sum(probs * probs_grad, axis=1, keepdims=True)
            score_grad = narrow(probs * (probs_grad - centre))
            queries_grad = product(score_grad, keys_all, (1, 0)) * scale
            keys_part = product(score_grad, queries, (0, 0)) * scale
            turned = queries_grad * cos - pltpu.roll(queries_grad, HD // 2, 1) * sin
            out_ref[here, lanes] = narrow(turned)
            if start:
                values_acc[:start, lanes] += values_part[:start]
                keys_acc[:start, lanes] += keys_part[:start]
            values_acc[here, lanes] = values_part[start:]
            keys_acc[here, lanes] = keys_part[start:]
    for start in range(0, tokens, block):
        here = slice(start, start + block)
        cos, sin = cos_ref[here, :], sin_ref[here, :]
        out_ref[here, 2 * width :] = narrow(values_acc[here, :])
        for head in range(heads):
            at = head * HD
            value = keys_acc[here, at : at + HD]
            out_ref[here, width + at : width + at + HD] = narrow(value * cos - pltpu.roll(value, HD // 2, 1) * sin)


def share_kernel(side_ref, *refs):
    *given, out_ref = refs
    total = product(given[0][...], given[1][...], (1, 1))
    for a_ref, w_ref in zip(given[2::2], given[3::2]):
        total = total + product(a_ref[...], w_ref[...], (1, 1))
    out_ref[0] = narrow(total)


def weight_kernel(x_ref, q_ref, g_ref, h_ref, *outs):
    width = h_ref.shape[1]
    half = x_ref.shape[1] // 2
    for lane, out_ref in enumerate(outs):
        here = slice(lane * half, (lane + 1) * half)
        out_ref[0, :, : 3 * width] = narrow(product(x_ref[:, here], q_ref[...], (0, 0)))
        out_ref[0, :, 3 * width :] = narrow(product(g_ref[:, here], h_ref[...], (0, 0)))


def hidden_kernel(offset_ref, x_ref, up_ref, top_ref, gate_ref, width_ref, share_ref, hidden_ref, grad_ref, dots_ref):
    pre = product(x_ref[...], up_ref[...], (1, 0))
    column = lax.broadcasted_iota(jnp.int32, pre.shape, 1) + offset_ref[0]
    live = column * 4 < (width_ref[...] + 1) * FF
    relu_act = jnp.where(live, jnp.maximum(pre, 0.0), 0.0)
    hidden = narrow(relu_act * relu_act)
    top = top_ref[...]
    grad = narrow(top * gate_ref[...] * 2.0 * relu_act)
    hidden_ref[...] = hidden
    grad_ref[...] = grad
    dots = jnp.sum(wide(hidden) * top, axis=1, keepdims=True)
    dots_ref[...] = jnp.broadcast_to(dots, (dots.shape[0], 128)).T[:1]
    share_ref[...] = narrow(product(grad, up_ref[...], (1, 1)))


def place_kernel(count, widths, turned, at_ref, *refs):
    lanes = (len(refs) - len(widths)) // count
    blocks, outs = refs[: lanes * count], refs[lanes * count :]
    half = blocks[0].shape[0]
    for far in range(count):

        @pl.when((pl.program_id(0) ^ at_ref[0]) == far)
        def _():
            for lane in range(lanes):
                here = slice(lane * half, (lane + 1) * half)
                block = blocks[lane * count + far]
                start = 0
                for out_ref, width, turn in zip(outs, widths, turned):
                    for part in range(out_ref.shape[0] if len(out_ref.shape) == 3 else 1):
                        value = block[:, start : start + width].astype(out_ref.dtype)
                        start += width
                        if turn:
                            out_ref[:, here] = value.T
                        elif len(out_ref.shape) == 3:
                            out_ref[part, here, :] = value
                        else:
                            out_ref[here, :] = value


VMEM_LIMIT = 56 * 1024 * 1024


def whole_specs(count):
    return [pl.BlockSpec(memory_space=pltpu.VMEM)] * count


def attend_forward(x, w, cos, sin, mask):
    tokens, heads = mask.shape
    dim, width = w.shape[0], heads * HD
    return pl.pallas_call(
        forward_kernel,
        out_shape=[
            jax.ShapeDtypeStruct((tokens, 3 * width), jnp.bfloat16),
            jax.ShapeDtypeStruct((tokens, width), jnp.bfloat16),
            jax.ShapeDtypeStruct((tokens, heads), jnp.float32),
        ],
        in_specs=whole_specs(5),
        out_specs=whole_specs(3),
        compiler_params=pltpu.CompilerParams(vmem_limit_bytes=VMEM_LIMIT),
        cost_estimate=pl.CostEstimate(
            flops=6 * tokens * dim * width + 2 * tokens * tokens * width,
            bytes_accessed=12 << 20,
            transcendentals=tokens * tokens * heads // 2,
        ),
        name="attend_forward",
    )(x, w, cos, sin, mask)


def attend_backward(g, w, qkv, log_total, cos, sin, mask):
    tokens, heads = mask.shape
    dim, width = w.shape[0], heads * HD
    return pl.pallas_call(
        backward_kernel,
        out_shape=jax.ShapeDtypeStruct((tokens, 3 * width), jnp.bfloat16),
        in_specs=whole_specs(7),
        out_specs=whole_specs(1)[0],
        scratch_shapes=[pltpu.VMEM((tokens, width), jnp.float32)] * 2,
        compiler_params=pltpu.CompilerParams(vmem_limit_bytes=VMEM_LIMIT),
        cost_estimate=pl.CostEstimate(
            flops=2 * tokens * dim * width + 5 * tokens * tokens * width,
            bytes_accessed=12 << 20,
            transcendentals=tokens * tokens * heads // 2,
        ),
        name="attend_backward",
    )(g, w, qkv, log_total, cos, sin, mask)


def share_of(pairs, rows, side):
    tokens, depth = pairs[0][0].shape
    dim = pairs[0][1].shape[0]
    chips = tokens // rows // 2
    specs = [
        pl.BlockSpec((rows, depth), lambda i, side: (2 * i + side[0], 0)),
        pl.BlockSpec((dim, depth), lambda i, side: (0, 0)),
    ] * len(pairs)
    return pl.pallas_call(
        share_kernel,
        grid_spec=pltpu.PrefetchScalarGridSpec(
            num_scalar_prefetch=1,
            grid=(chips,),
            in_specs=specs,
            out_specs=pl.BlockSpec((1, rows, dim), lambda i, side: (i, 0, 0)),
        ),
        out_shape=jax.ShapeDtypeStruct((chips, rows, dim), jnp.bfloat16),
        compiler_params=pltpu.CompilerParams(vmem_limit_bytes=VMEM_LIMIT),
        cost_estimate=pl.CostEstimate(
            flops=tokens * dim * depth * len(pairs), bytes_accessed=12 << 20, transcendentals=0
        ),
        name="share_of",
    )(side.astype(jnp.int32).reshape(1), *[x for pair in pairs for x in pair])


def hidden_pass(x, up, top_down, gates, widths, offset):
    tokens, dim = x.shape
    cols = up.shape[1]
    block = 256
    rows_of = lambda n: pl.BlockSpec((block, n), lambda i, at: (i, 0))
    return pl.pallas_call(
        hidden_kernel,
        grid_spec=pltpu.PrefetchScalarGridSpec(
            num_scalar_prefetch=1,
            grid=(tokens // block,),
            in_specs=[rows_of(dim), pl.BlockSpec((dim, cols), lambda i, at: (0, 0)), rows_of(cols), rows_of(1), rows_of(1)],
            out_specs=[rows_of(dim), rows_of(cols), rows_of(cols), pl.BlockSpec((1, block), lambda i, at: (0, i))],
        ),
        out_shape=[
            jax.ShapeDtypeStruct((tokens, dim), jnp.bfloat16),
            jax.ShapeDtypeStruct((tokens, cols), jnp.bfloat16),
            jax.ShapeDtypeStruct((tokens, cols), jnp.bfloat16),
            jax.ShapeDtypeStruct((1, tokens), jnp.float32),
        ],
        compiler_params=pltpu.CompilerParams(vmem_limit_bytes=VMEM_LIMIT),
        cost_estimate=pl.CostEstimate(flops=4 * tokens * dim * cols, bytes_accessed=40 << 20, transcendentals=0),
        name="hidden_pass",
    )(offset.astype(jnp.int32).reshape(1), x, up, top_down, gates[:, None], widths)


def weight_grads(x, qkv_grad, g, heads_out, count):
    tokens, dim = x.shape
    width = heads_out.shape[1]
    block = dim // count
    out = jax.ShapeDtypeStruct((count, block // 2, 4 * width), jnp.bfloat16)
    return pl.pallas_call(
        weight_kernel,
        grid=(count,),
        out_shape=[out, out],
        in_specs=[
            pl.BlockSpec((tokens, block), lambda i: (0, i)),
            pl.BlockSpec((tokens, 3 * width), lambda i: (0, 0)),
            pl.BlockSpec((tokens, block), lambda i: (0, i)),
            pl.BlockSpec((tokens, width), lambda i: (0, 0)),
        ],
        out_specs=[pl.BlockSpec((1, block // 2, 4 * width), lambda i: (i, 0, 0))] * 2,
        compiler_params=pltpu.CompilerParams(vmem_limit_bytes=VMEM_LIMIT),
        cost_estimate=pl.CostEstimate(flops=8 * tokens * dim * width, bytes_accessed=14 << 20, transcendentals=0),
        name="weight_grads",
    )(x, qkv_grad, g, heads_out)


def place_blocks(lanes, index, outs):
    count = len(lanes[0])
    half, total = lanes[0][0].shape
    rows = len(lanes) * half
    shapes, specs = [], []
    for planes, width, kind, turned in outs:
        if turned:
            shapes.append(jax.ShapeDtypeStruct((width, rows * count), kind))
            specs.append(pl.BlockSpec((width, rows), lambda i, at: (0, i)))
        elif planes > 1:
            shapes.append(jax.ShapeDtypeStruct((planes, rows * count, width), kind))
            specs.append(pl.BlockSpec((planes, rows, width), lambda i, at: (0, i, 0)))
        else:
            shapes.append(jax.ShapeDtypeStruct((rows * count, width), kind))
            specs.append(pl.BlockSpec((rows, width), lambda i, at: (i, 0)))
    given = [held[far] for held in lanes for far in range(count)]
    return pl.pallas_call(
        functools.partial(place_kernel, count, [o[1] for o in outs], [o[3] for o in outs]),
        grid_spec=pltpu.PrefetchScalarGridSpec(
            num_scalar_prefetch=1,
            grid=(count,),
            in_specs=[pl.BlockSpec((half, total), lambda i, at: (0, 0))] * len(given),
            out_specs=specs,
        ),
        out_shape=shapes,
        compiler_params=pltpu.CompilerParams(vmem_limit_bytes=VMEM_LIMIT),
        cost_estimate=pl.CostEstimate(flops=0, bytes_accessed=12 << 20, transcendentals=0),
        name="place_blocks",
    )(index.astype(jnp.int32).reshape(1), *given)


def swap_pairs(size, bit):
    return [(i, i ^ bit) for i in range(size)]


def shift_pairs(size, shift):
    return [(i, (i - shift) % size) for i in range(size)]


def bits_of(size):
    return [1 << i for i in range(size.bit_length() - 1)]


def pick(x, index, axis=0):
    return lax.dynamic_index_in_dim(x, index, axis, keepdims=False)


def after(x, *others):
    return lax.optimization_barrier((x,) + others)[0]


def xor_gather(x, axis, size, bits):
    held = dict(x) if isinstance(x, dict) else {0: x}
    for bit in bits:
        for far in list(held):
            held[far ^ bit] = lax.ppermute(held[far], axis, swap_pairs(size, bit))
    return held


def by_index(held, index, axis=0, out=None):
    shape = held[0].shape
    if out is None:
        out = jnp.zeros(shape[:axis] + (len(held),) + shape[axis:], held[0].dtype)
    for far, block in held.items():
        out = lax.dynamic_update_index_in_dim(out, block, index ^ far, axis)
    return out


def xor_scatter(blocks, axis_name, size, bits, steps, index, axis, all_steps=None):
    all_steps = list(all_steps or steps)
    left = sorted(all_steps[all_steps.index(steps[0]) :], reverse=True)
    blocks = blocks.reshape(blocks.shape[:axis] + (2,) * len(left) + blocks.shape[axis + 1 :])
    for bit, step in zip(bits, steps):
        at = axis + left.index(step)
        left.remove(step)
        side = (index // step) % 2
        got = lax.ppermute(narrow(pick(blocks, 1 - side, at)), axis_name, swap_pairs(size, bit))
        blocks = wide(pick(blocks, side, at)) + wide(got)
    tail = blocks.shape[axis + len(left) :]
    return blocks.reshape(blocks.shape[:axis] + ((2 ** len(left),) if left else ()) + tail)


def lane_bits(size):
    return bits_of(size), bits_of(size)[::-1]


def column_gather(lanes, size, cut=None, start=None):
    return [xor_gather(x, "dp", size, bits[start:cut]) for x, bits in zip(lanes, lane_bits(size))]


def gate_lanes(lanes, *gates):
    flat = [held[far] for held in lanes for far in held]
    flat = lax.optimization_barrier((*flat, *gates))
    flat = iter(flat)
    return [{far: next(flat) for far in held} for held in lanes]


def xor_span(bits):
    span = [0]
    for bit in bits:
        span += [far ^ bit for far in span]
    return span


def gather_part(lanes, size, part):
    out = []
    for held, bits in zip(lanes, lane_bits(size)):
        held = dict(held)
        sends = [(bits[i], far) for i in range(1, len(bits)) for far in xor_span(bits[:i])]
        half = len(sends) // 2
        for bit, far in sends[half:] if part else sends[:half]:
            held[far ^ bit] = lax.ppermute(held[far], "dp", swap_pairs(size, bit))
        out.append(held)
    return out


def column_scatter(lanes, size, column, cut=None, start=None):
    return [
        xor_scatter(x, "dp", size, bits[start:cut], bits[start:cut], column, 0, bits)
        for x, bits in zip(lanes, lane_bits(size))
    ]


def all_sum(x, sizes):
    for axis, size in sizes.items():
        for bit in bits_of(size):
            x = x + lax.ppermute(x, axis, swap_pairs(size, bit))
    return x


def make_local(columns, ranks):
    def local(
        layer_input, width_choice, routed_flag, mixer_gain, mixer_router, attention_weight,
        output_weight, hidden_gain, hidden_router, up_weight, down_weight, out_grad,
    ):
        column, rank = lax.axis_index("dp"), lax.axis_index("mp")
        rows, dim = layer_input.shape
        core = rank % 2
        group = SEQ_LEN // rows
        sequences = ranks // group
        place, sequence = rank % group, rank // group
        pair_bits = [b for b in bits_of(group) if b > 1]
        own_heads = output_weight.shape[0] // HD
        cols_local = up_weight.shape[1]
        width_own = lax.dynamic_slice_in_dim(width_choice, rank * rows, rows, 0)
        routed_own = lax.dynamic_slice_in_dim(routed_flag, rank * rows, rows, 0)
        cos, sin = rope_tables(SEQ_LEN, HD)

        def place_sequence(held, out=None):
            return by_index(held, place, 0, out).reshape(SEQ_LEN, -1)

        def core_sum(pairs, before=()):
            theirs = share_of(pairs, rows, 1 - core)
            got = lax.ppermute(theirs, "mp", swap_pairs(ranks, 1))
            pairs, theirs, before = lax.optimization_barrier((pairs, theirs, before))
            return wide(share_of(pairs, rows, core)) + wide(got), before

        def chip_sum(blocks):
            bits = pair_bits[::-1]
            return xor_scatter(blocks, "mp", ranks, bits, [b // 2 for b in bits], place // 2, 0)

        width = own_heads * HD
        chunk_rows = dim // columns
        half_rows = chunk_rows // 2

        def in_slice(w):
            return jnp.concatenate([w[:, p] for p in range(3)], axis=1)

        lanes_in = [
            in_slice(lax.dynamic_slice_in_dim(attention_weight, column * chunk_rows + at, half_rows, 0))
            for at in (0, half_rows)
        ]
        lanes_out = [lax.dynamic_slice_in_dim(output_weight, column * chunk_rows, chunk_rows, 1).T]
        input_wide = wide(layer_input)
        normed_one, scaled_one, inverse_one = norm_forward(input_wide, mixer_gain)
        low_one = narrow(normed_one)
        low_one, lanes_in = lax.optimization_barrier((low_one, lanes_in))
        held = xor_gather(low_one, "mp", ranks, pair_bits)
        fetched_in, fetched_out = [
            [[lax.ppermute(x, "mp", shift_pairs(ranks, k * group)) for x in lanes] for k in range(1, sequences)]
            for lanes in (lanes_in, lanes_out)
        ]
        sequence_width = lax.dynamic_slice_in_dim(width_choice[:, 0], sequence * SEQ_LEN, SEQ_LEN, 0)
        masks = []
        for k in range(sequences):
            heads = ((rank + k * group) % ranks) * own_heads + jnp.arange(own_heads, dtype=jnp.int32)
            masks.append((heads[None, :] * 4 < (sequence_width[:, None] + 1) * H).astype(jnp.float32))
        weights_in, weights_out = [in_slice(attention_weight)], [output_weight.T]
        held, fetched_in, masks, weights_in, weights_out, cos, sin = lax.optimization_barrier(
            (held, fetched_in, masks, weights_in, weights_out, cos, sin)
        )
        inputs_one = place_sequence(xor_gather(held, "mp", ranks, [1]))
        grads_all = lax.all_gather(after(out_grad, *[x for lanes in fetched_in for x in lanes]), "mp", axis=0, tiled=True)
        steps_in = [column_gather(x, columns, cut=1) for x in fetched_in]
        gate_one, state_one = gate_forward(normed_one, mixer_router, width_own[:, 0], routed_own[:, 0])

        kept = []
        for k in range(sequences):
            mask = masks[k]
            if k:
                steps, fetched, _ = lax.optimization_barrier((steps_in[k - 1], fetched_out[k - 1], kept[0][0]))
                held = column_gather(steps, columns, start=1)
                held_out = column_gather(fetched, columns, cut=1)
                held, held_out = lax.optimization_barrier((held, held_out))
                held_out = column_gather(held_out, columns, start=1)
                weights_in += place_blocks(held, column, [(1, 3 * width, jnp.bfloat16, False)])
                weights_out += place_blocks(held_out, column, [(1, width, jnp.bfloat16, False)])
            kept.append((*attend_forward(inputs_one, weights_in[k], cos, sin, mask), mask))
        mixer_branch = chip_sum(core_sum([(x[1], w) for x, w in zip(kept, weights_out)])[0])
        mixer_branch, grads_all = lax.optimization_barrier((mixer_branch, grads_all))
        top_down = product(grads_all, down_weight, (1, 1))

        middle = input_wide + gate_one[:, None] * mixer_branch
        normed_two, scaled_two, inverse_two = norm_forward(middle, hidden_gain)
        gate_two, state_two = gate_forward(normed_two, hidden_router, width_own[:, 1], routed_own[:, 1])
        inputs_two = lax.all_gather(narrow(normed_two), "mp", axis=0, tiled=True)
        gates = by_index(xor_gather(gate_two.reshape(-1, 128), "mp", ranks, bits_of(ranks)), rank).reshape(-1)

        inputs_two, top_down = lax.optimization_barrier((inputs_two, top_down))
        share, hidden, pre_grad, dots = hidden_pass(
            inputs_two, up_weight, top_down, gates, width_choice[:, 1:2], rank * cols_local
        )
        dots = dots.reshape(-1, 128)
        share, hidden, pre_grad = lax.optimization_barrier((share, hidden, pre_grad))
        normed_grad_two = lax.psum_scatter(share, "mp", scatter_dimension=0, tiled=True)
        gate_grad_two = lax.dynamic_slice_in_dim(all_sum(dots, {"mp": ranks}).reshape(-1), rank * rows, rows, 0)
        gated = narrow(gates[:, None] * wide(grads_all))
        lanes = [narrow(product(hidden, gated, (0, 0))), narrow(product(inputs_two, pre_grad, (0, 0)))]
        lanes = [x.reshape(columns, -1, x.shape[1]) for x in lanes]
        lanes = column_scatter(lanes, columns, column, cut=1)
        hidden_share = narrow(product(hidden, down_weight, (1, 0)))
        blank = jnp.zeros((group, rows, dim), jnp.bfloat16)
        normed_grad_two, hidden_share, blank, *lanes = lax.optimization_barrier(
            (normed_grad_two, hidden_share, blank, *lanes)
        )
        normed_grad_two = wide(normed_grad_two)
        lanes = [narrow(x) for x in column_scatter(lanes, columns, column, start=1)]

        router_part, _ = gate_backward(normed_two, hidden_router, state_two, gate_grad_two)
        middle_part, gain_two = norm_backward(normed_grad_two + router_part, scaled_two, inverse_two, hidden_gain)
        middle_grad = wide(out_grad) + middle_part
        grads_one = place_sequence(
            xor_gather(narrow(gate_one[:, None] * middle_grad), "mp", ranks, pair_bits + [1]), blank
        )
        helds = column_gather(lanes, columns, cut=1)
        grads_one, hidden_share, lanes = lax.optimization_barrier((grads_one, hidden_share, lanes))
        hidden_branch = wide(lax.psum_scatter(hidden_share, "mp", scatter_dimension=0, tiled=True))
        layer_output = narrow(middle + gate_two[:, None] * hidden_branch)

        pairs, sent = [], []
        grads_now = grads_one
        for k in range(sequences)[::-1]:
            qkv, heads_out, log_total, mask = kept[k]
            qkv_grad = attend_backward(grads_now, weights_out[k], qkv, log_total, cos, sin, mask)
            pairs.append((qkv_grad, weights_in[k]))
            if sent:
                qkv_grad, sent = lax.optimization_barrier((qkv_grad, sent))
            part = weight_grads(inputs_one, qkv_grad, grads_one, heads_out, columns)
            if k:
                grads_now, part, helds = lax.optimization_barrier((grads_now, part, helds))
                sent.append(column_scatter(part, columns, column, cut=1))
                normed_late, state_late, dots_late, middle_late, _ = lax.optimization_barrier(
                    (normed_two, state_two, gate_grad_two, middle_grad, part)
                )
                router_two = gate_backward(normed_late, hidden_router, state_late, dots_late)[1]
                gate_grad_one = jnp.sum(middle_late * mixer_branch, axis=1)
        helds, sent = lax.optimization_barrier((helds, sent))
        sent = [[narrow(x) for x in column_scatter(lanes, columns, column, start=1)] for lanes in sent]
        there = [
            [lax.ppermute(x, "mp", shift_pairs(ranks, -k * group)) for x in lanes]
            for k, lanes in zip(range(1, sequences)[::-1], sent)
        ]
        pairs, part = lax.optimization_barrier((pairs, part))
        blocks, helds = core_sum(pairs, gather_part(helds, columns, 0))
        blocks, there = lax.optimization_barrier((blocks, there))
        normed_grad_one = chip_sum(blocks)
        helds = gather_part(helds, columns, 1)
        pieces = column_scatter(part, columns, column)
        pieces, helds = lax.optimization_barrier((pieces, helds))
        for lanes in there:
            pieces = [p + wide(t) for p, t in zip(pieces, lanes)]
        spread = column_gather([narrow(p) for p in pieces], columns, cut=1)
        spread, helds = lax.optimization_barrier((spread, helds))
        spread = column_gather(spread, columns, start=1)
        down_sum, = place_blocks(helds[:1], column, [(1, dim, jnp.float32, False)])
        up_sum, = place_blocks(helds[1:], column, [(1, cols_local, jnp.float32, False)])
        attention_sum, output_sum = place_blocks(
            spread,
            column,
            [(3, width, jnp.float32, False), (1, width, jnp.float32, True)],
        )
        attention_sum = attention_sum.transpose(1, 0, 2)

        router_part_one, router_one = gate_backward(normed_one, mixer_router, state_one, gate_grad_one)
        input_part, gain_one = norm_backward(normed_grad_one + router_part_one, scaled_one, inverse_one, mixer_gain)
        input_grad = narrow(middle_grad + input_part)

        smalls = [gain_two, gain_one, router_two.T, router_one.T]
        small = all_sum(jnp.concatenate([x.reshape(-1, 128) for x in smalls], axis=0), {"mp": ranks})
        small, layer_output = lax.optimization_barrier((small, layer_output))
        small_sum = all_sum(small, {"dp": columns})
        cuts = [dim // 128, 2 * dim // 128, (2 * dim + router_two.size) // 128]
        hidden_gain_sum, mixer_gain_sum, hidden_router_sum, mixer_router_sum = (
            x.reshape(-1, dim) for x in jnp.split(small_sum, cuts)
        )
        hidden_gain_sum, mixer_gain_sum = hidden_gain_sum[0], mixer_gain_sum[0]
        hidden_router_sum, mixer_router_sum = hidden_router_sum.T, mixer_router_sum.T
        return (
            layer_output, input_grad, mixer_gain_sum, mixer_router_sum, attention_sum, output_sum,
            hidden_gain_sum, hidden_router_sum, up_sum, down_sum,
        )

    return local


def solution(mesh):
    return jax.shard_map(
        make_local(mesh.shape["dp"], mesh.shape["mp"]),
        mesh=mesh,
        in_specs=(
            P(("dp", "mp"), None),
            P("dp", None),
            P("dp", None),
            P(),
            P(),
            P(None, None, "mp"),
            P("mp", None),
            P(),
            P(),
            P(None, "mp"),
            P("mp", None),
            P(("dp", "mp"), None),
        ),
        out_specs=(
            P(("dp", "mp"), None),
            P(("dp", "mp"), None),
            P(),
            P(),
            P(None, None, "mp"),
            P("mp", None),
            P(),
            P(),
            P(None, "mp"),
            P("mp", None),
        ),
        check_vma=False,
    )
```

```python
import functools
import math

import jax
import jax.numpy as jnp
from jax import lax
from jax.experimental import pallas as pl
from jax.experimental.pallas import tpu as pltpu
from jax.sharding import PartitionSpec as P

H = 16
HD = 128
FF = 8192
SEQ_LEN = 1024


EPSILON = 1e-05
NEG_LARGE = -1e30
HIGHEST = lax.Precision.HIGHEST


def norm_forward(values, gain_vec):
    row_mean = jnp.mean(values, axis=1, keepdims=True)
    centred = values - row_mean
    row_variance = jnp.mean(centred * centred, axis=1, keepdims=True)
    inverse_scale = lax.rsqrt(row_variance + EPSILON)
    scaled = centred * inverse_scale
    return (scaled * gain_vec[None, :], scaled, inverse_scale)


def norm_backward(normed_grad, scaled, inverse_scale, gain_vec):
    gain_grad = jnp.sum(normed_grad * scaled, axis=0)
    scaled_grad = normed_grad * gain_vec[None, :]
    first_mean = jnp.mean(scaled_grad, axis=1, keepdims=True)
    second_mean = jnp.mean(scaled_grad * scaled, axis=1, keepdims=True)
    return (inverse_scale * (scaled_grad - first_mean - scaled * second_mean), gain_grad)


def gate_forward(normed, router, width_col, routed_col):
    logits = jnp.dot(normed, router, precision=HIGHEST, preferred_element_type=jnp.float32)
    soft_probs = jax.nn.softmax(logits, axis=1)
    one_hot = (width_col[:, None] == jnp.arange(4, dtype=jnp.int32)[None, :]).astype(jnp.float32)
    chosen = jnp.sum(soft_probs * one_hot, axis=1)
    route_flags = routed_col.astype(jnp.float32)
    return (
        route_flags * 4.0 * chosen + (1.0 - route_flags),
        (soft_probs, one_hot, chosen, route_flags),
    )


def gate_backward(normed, router, gate_state, gate_grad):
    soft_probs, one_hot, chosen, route_flags = gate_state
    coefficient = route_flags * 4.0 * chosen * gate_grad
    logit_grad = coefficient[:, None] * (one_hot - soft_probs)
    router_grad = lax.dot_general(
        normed,
        logit_grad,
        (((0,), (0,)), ((), ())),
        precision=HIGHEST,
        preferred_element_type=jnp.float32,
    )
    normed_grad = lax.dot_general(
        logit_grad,
        router,
        (((1,), (1,)), ((), ())),
        precision=HIGHEST,
        preferred_element_type=jnp.float32,
    )
    return (normed_grad, router_grad)


Q_BLOCK = 256


def rope_tables(token_count, head_width):
    positions = jnp.arange(token_count, dtype=jnp.float32)
    frequency = jnp.exp(
        jnp.arange(head_width // 2, dtype=jnp.float32) * (-2.0 * math.log(10000.0) / head_width)
    )
    angles = positions[:, None] * frequency[None, :]
    cosine, sine = jnp.cos(angles), jnp.sin(angles)
    return jnp.concatenate([cosine, cosine], axis=1), jnp.concatenate([-sine, sine], axis=1)


def wide(x):
    return x.astype(jnp.float32)


def narrow(x):
    return x.astype(jnp.bfloat16)


def product(a, b, dims):
    return lax.dot_general(a, b, ((dims[:1], dims[1:]), ((), ())), preferred_element_type=jnp.float32)


def block_scores(queries, keys_all, start):
    scores = product(queries, keys_all, (1, 1)) * (1.0 / math.sqrt(HD))
    row = lax.broadcasted_iota(jnp.int32, scores.shape, 0) + start
    col = lax.broadcasted_iota(jnp.int32, scores.shape, 1)
    return jnp.where(col <= row, scores, NEG_LARGE)


def forward_kernel(x_ref, w_ref, cos_ref, sin_ref, mask_ref, qkv_ref, heads_ref, log_ref):
    tokens, heads = x_ref.shape[0], mask_ref.shape[1]
    width = heads * HD
    block = min(Q_BLOCK, tokens)
    for start in range(0, tokens, block):
        here, end = slice(start, start + block), start + block
        x = x_ref[here, :]
        cos, sin = cos_ref[here, :], sin_ref[here, :]
        for part in range(3):
            rows = product(x, w_ref[:, part * width : (part + 1) * width], (1, 0))
            for head in range(heads):
                value = rows[:, head * HD : (head + 1) * HD]
                if part < 2:
                    value = value * cos + pltpu.roll(value, HD // 2, 1) * sin
                at = part * width + head * HD
                qkv_ref[here, at : at + HD] = narrow(value)
        for head in range(heads):
            at = head * HD
            lanes, key_lanes, value_lanes = (slice(at + p * width, at + p * width + HD) for p in range(3))
            scores = block_scores(qkv_ref[here, lanes], qkv_ref[:end, key_lanes], start)
            row_max = jnp.max(scores, axis=1, keepdims=True)
            shifted = jnp.exp(scores - row_max)
            total = jnp.sum(shifted, axis=1, keepdims=True)
            mix = product(narrow(shifted * (1.0 / total)), qkv_ref[:end, value_lanes], (1, 0))
            heads_ref[here, lanes] = narrow(mix * mask_ref[here, head : head + 1])
            log_ref[here, head : head + 1] = row_max + jnp.log(total)


def backward_kernel(g_ref, w_ref, qkv_ref, log_ref, cos_ref, sin_ref, mask_ref, out_ref, keys_acc, values_acc):
    tokens, heads = g_ref.shape[0], mask_ref.shape[1]
    width = heads * HD
    block = min(Q_BLOCK, tokens)
    scale = 1.0 / math.sqrt(HD)
    for start in range(0, tokens, block):
        here, end = slice(start, start + block), start + block
        cos, sin = cos_ref[here, :], sin_ref[here, :]
        rows = narrow(product(g_ref[here, :], w_ref[...], (1, 0)))
        for head in range(heads):
            at = head * HD
            lanes, key_lanes, value_lanes = (slice(at + p * width, at + p * width + HD) for p in range(3))
            heads_grad = rows[:, lanes] * narrow(mask_ref[here, head : head + 1])
            queries, keys_all = qkv_ref[here, lanes], qkv_ref[:end, key_lanes]
            scores = block_scores(queries, keys_all, start)
            probs = jnp.exp(scores - log_ref[here, head : head + 1])
            values_part = product(narrow(probs), heads_grad, (0, 0))
            probs_grad = product(heads_grad, qkv_ref[:end, value_lanes], (1, 1))
            centre = jnp.sum(probs * probs_grad, axis=1, keepdims=True)
            score_grad = narrow(probs * (probs_grad - centre))
            queries_grad = product(score_grad, keys_all, (1, 0)) * scale
            keys_part = product(score_grad, queries, (0, 0)) * scale
            turned = queries_grad * cos - pltpu.roll(queries_grad, HD // 2, 1) * sin
            out_ref[here, lanes] = narrow(turned)
            if start:
                values_acc[:start, lanes] += values_part[:start]
                keys_acc[:start, lanes] += keys_part[:start]
            values_acc[here, lanes] = values_part[start:]
            keys_acc[here, lanes] = keys_part[start:]
    for start in range(0, tokens, block):
        here = slice(start, start + block)
        cos, sin = cos_ref[here, :], sin_ref[here, :]
        out_ref[here, 2 * width :] = narrow(values_acc[here, :])
        for head in range(heads):
            at = head * HD
            value = keys_acc[here, at : at + HD]
            out_ref[here, width + at : width + at + HD] = narrow(value * cos - pltpu.roll(value, HD // 2, 1) * sin)


def share_kernel(side_ref, *refs):
    *given, out_ref = refs
    total = product(given[0][...], given[1][...], (1, 1))
    for a_ref, w_ref in zip(given[2::2], given[3::2]):
        total = total + product(a_ref[...], w_ref[...], (1, 1))
    out_ref[0] = narrow(total)


def weight_kernel(x_ref, q_ref, g_ref, h_ref, *outs):
    width = h_ref.shape[1]
    half = x_ref.shape[1] // 2
    for lane, out_ref in enumerate(outs):
        here = slice(lane * half, (lane + 1) * half)
        out_ref[0, :, : 3 * width] = narrow(product(x_ref[:, here], q_ref[...], (0, 0)))
        out_ref[0, :, 3 * width :] = narrow(product(g_ref[:, here], h_ref[...], (0, 0)))


def hidden_kernel(offset_ref, x_ref, up_ref, top_ref, gate_ref, width_ref, share_ref, hidden_ref, grad_ref, dots_ref):
    pre = product(x_ref[...], up_ref[...], (1, 0))
    column = lax.broadcasted_iota(jnp.int32, pre.shape, 1) + offset_ref[0]
    live = column * 4 < (width_ref[...] + 1) * FF
    relu_act = jnp.where(live, jnp.maximum(pre, 0.0), 0.0)
    hidden = narrow(relu_act * relu_act)
    top = top_ref[...]
    grad = narrow(top * gate_ref[...] * 2.0 * relu_act)
    hidden_ref[...] = hidden
    grad_ref[...] = grad
    dots = jnp.sum(wide(hidden) * top, axis=1, keepdims=True)
    dots_ref[...] = jnp.broadcast_to(dots, (dots.shape[0], 128)).T[:1]
    share_ref[...] = narrow(product(grad, up_ref[...], (1, 1)))


def place_kernel(count, widths, turned, at_ref, *refs):
    lanes = (len(refs) - len(widths)) // count
    blocks, outs = refs[: lanes * count], refs[lanes * count :]
    half = blocks[0].shape[0]
    for far in range(count):

        @pl.when((pl.program_id(0) ^ at_ref[0]) == far)
        def _():
            for lane in range(lanes):
                here = slice(lane * half, (lane + 1) * half)
                block = blocks[lane * count + far]
                start = 0
                for out_ref, width, turn in zip(outs, widths, turned):
                    for part in range(out_ref.shape[0] if len(out_ref.shape) == 3 else 1):
                        value = block[:, start : start + width].astype(out_ref.dtype)
                        start += width
                        if turn:
                            out_ref[:, here] = value.T
                        elif len(out_ref.shape) == 3:
                            out_ref[part, here, :] = value
                        else:
                            out_ref[here, :] = value


VMEM_LIMIT = 56 * 1024 * 1024


def whole_specs(count):
    return [pl.BlockSpec(memory_space=pltpu.VMEM)] * count


def attend_forward(x, w, cos, sin, mask):
    tokens, heads = mask.shape
    dim, width = w.shape[0], heads * HD
    return pl.pallas_call(
        forward_kernel,
        out_shape=[
            jax.ShapeDtypeStruct((tokens, 3 * width), jnp.bfloat16),
            jax.ShapeDtypeStruct((tokens, width), jnp.bfloat16),
            jax.ShapeDtypeStruct((tokens, heads), jnp.float32),
        ],
        in_specs=whole_specs(5),
        out_specs=whole_specs(3),
        compiler_params=pltpu.CompilerParams(vmem_limit_bytes=VMEM_LIMIT),
        cost_estimate=pl.CostEstimate(
            flops=6 * tokens * dim * width + 2 * tokens * tokens * width,
            bytes_accessed=12 << 20,
            transcendentals=tokens * tokens * heads // 2,
        ),
        name="attend_forward",
    )(x, w, cos, sin, mask)


def attend_backward(g, w, qkv, log_total, cos, sin, mask):
    tokens, heads = mask.shape
    dim, width = w.shape[0], heads * HD
    return pl.pallas_call(
        backward_kernel,
        out_shape=jax.ShapeDtypeStruct((tokens, 3 * width), jnp.bfloat16),
        in_specs=whole_specs(7),
        out_specs=whole_specs(1)[0],
        scratch_shapes=[pltpu.VMEM((tokens, width), jnp.float32)] * 2,
        compiler_params=pltpu.CompilerParams(vmem_limit_bytes=VMEM_LIMIT),
        cost_estimate=pl.CostEstimate(
            flops=2 * tokens * dim * width + 5 * tokens * tokens * width,
            bytes_accessed=12 << 20,
            transcendentals=tokens * tokens * heads // 2,
        ),
        name="attend_backward",
    )(g, w, qkv, log_total, cos, sin, mask)


def share_of(pairs, rows, side):
    tokens, depth = pairs[0][0].shape
    dim = pairs[0][1].shape[0]
    chips = tokens // rows // 2
    specs = [
        pl.BlockSpec((rows, depth), lambda i, side: (2 * i + side[0], 0)),
        pl.BlockSpec((dim, depth), lambda i, side: (0, 0)),
    ] * len(pairs)
    return pl.pallas_call(
        share_kernel,
        grid_spec=pltpu.PrefetchScalarGridSpec(
            num_scalar_prefetch=1,
            grid=(chips,),
            in_specs=specs,
            out_specs=pl.BlockSpec((1, rows, dim), lambda i, side: (i, 0, 0)),
        ),
        out_shape=jax.ShapeDtypeStruct((chips, rows, dim), jnp.bfloat16),
        compiler_params=pltpu.CompilerParams(vmem_limit_bytes=VMEM_LIMIT),
        cost_estimate=pl.CostEstimate(
            flops=tokens * dim * depth * len(pairs), bytes_accessed=12 << 20, transcendentals=0
        ),
        name="share_of",
    )(side.astype(jnp.int32).reshape(1), *[x for pair in pairs for x in pair])


def hidden_pass(x, up, top_down, gates, widths, offset):
    tokens, dim = x.shape
    cols = up.shape[1]
    block = 256
    rows_of = lambda n: pl.BlockSpec((block, n), lambda i, at: (i, 0))
    return pl.pallas_call(
        hidden_kernel,
        grid_spec=pltpu.PrefetchScalarGridSpec(
            num_scalar_prefetch=1,
            grid=(tokens // block,),
            in_specs=[rows_of(dim), pl.BlockSpec((dim, cols), lambda i, at: (0, 0)), rows_of(cols), rows_of(1), rows_of(1)],
            out_specs=[rows_of(dim), rows_of(cols), rows_of(cols), pl.BlockSpec((1, block), lambda i, at: (0, i))],
        ),
        out_shape=[
            jax.ShapeDtypeStruct((tokens, dim), jnp.bfloat16),
            jax.ShapeDtypeStruct((tokens, cols), jnp.bfloat16),
            jax.ShapeDtypeStruct((tokens, cols), jnp.bfloat16),
            jax.ShapeDtypeStruct((1, tokens), jnp.float32),
        ],
        compiler_params=pltpu.CompilerParams(vmem_limit_bytes=VMEM_LIMIT),
        cost_estimate=pl.CostEstimate(flops=4 * tokens * dim * cols, bytes_accessed=40 << 20, transcendentals=0),
        name="hidden_pass",
    )(offset.astype(jnp.int32).reshape(1), x, up, top_down, gates[:, None], widths)


def weight_grads(x, qkv_grad, g, heads_out, count):
    tokens, dim = x.shape
    width = heads_out.shape[1]
    block = dim // count
    out = jax.ShapeDtypeStruct((count, block // 2, 4 * width), jnp.bfloat16)
    return pl.pallas_call(
        weight_kernel,
        grid=(count,),
        out_shape=[out, out],
        in_specs=[
            pl.BlockSpec((tokens, block), lambda i: (0, i)),
            pl.BlockSpec((tokens, 3 * width), lambda i: (0, 0)),
            pl.BlockSpec((tokens, block), lambda i: (0, i)),
            pl.BlockSpec((tokens, width), lambda i: (0, 0)),
        ],
        out_specs=[pl.BlockSpec((1, block // 2, 4 * width), lambda i: (i, 0, 0))] * 2,
        compiler_params=pltpu.CompilerParams(vmem_limit_bytes=VMEM_LIMIT),
        cost_estimate=pl.CostEstimate(flops=8 * tokens * dim * width, bytes_accessed=14 << 20, transcendentals=0),
        name="weight_grads",
    )(x, qkv_grad, g, heads_out)


def place_blocks(lanes, index, outs):
    count = len(lanes[0])
    half, total = lanes[0][0].shape
    rows = len(lanes) * half
    shapes, specs = [], []
    for planes, width, kind, turned in outs:
        if turned:
            shapes.append(jax.ShapeDtypeStruct((width, rows * count), kind))
            specs.append(pl.BlockSpec((width, rows), lambda i, at: (0, i)))
        elif planes > 1:
            shapes.append(jax.ShapeDtypeStruct((planes, rows * count, width), kind))
            specs.append(pl.BlockSpec((planes, rows, width), lambda i, at: (0, i, 0)))
        else:
            shapes.append(jax.ShapeDtypeStruct((rows * count, width), kind))
            specs.append(pl.BlockSpec((rows, width), lambda i, at: (i, 0)))
    given = [held[far] for held in lanes for far in range(count)]
    return pl.pallas_call(
        functools.partial(place_kernel, count, [o[1] for o in outs], [o[3] for o in outs]),
        grid_spec=pltpu.PrefetchScalarGridSpec(
            num_scalar_prefetch=1,
            grid=(count,),
            in_specs=[pl.BlockSpec((half, total), lambda i, at: (0, 0))] * len(given),
            out_specs=specs,
        ),
        out_shape=shapes,
        compiler_params=pltpu.CompilerParams(vmem_limit_bytes=VMEM_LIMIT),
        cost_estimate=pl.CostEstimate(flops=0, bytes_accessed=12 << 20, transcendentals=0),
        name="place_blocks",
    )(index.astype(jnp.int32).reshape(1), *given)


def swap_pairs(size, bit):
    return [(i, i ^ bit) for i in range(size)]


def shift_pairs(size, shift):
    return [(i, (i - shift) % size) for i in range(size)]


def bits_of(size):
    return [1 << i for i in range(size.bit_length() - 1)]


def pick(x, index, axis=0):
    return lax.dynamic_index_in_dim(x, index, axis, keepdims=False)


def after(x, *others):
    return lax.optimization_barrier((x,) + others)[0]


def xor_gather(x, axis, size, bits):
    held = dict(x) if isinstance(x, dict) else {0: x}
    for bit in bits:
        for far in list(held):
            held[far ^ bit] = lax.ppermute(held[far], axis, swap_pairs(size, bit))
    return held


def by_index(held, index, axis=0, out=None):
    shape = held[0].shape
    if out is None:
        out = jnp.zeros(shape[:axis] + (len(held),) + shape[axis:], held[0].dtype)
    for far, block in held.items():
        out = lax.dynamic_update_index_in_dim(out, block, index ^ far, axis)
    return out


def xor_scatter(blocks, axis_name, size, bits, steps, index, axis, all_steps=None):
    all_steps = list(all_steps or steps)
    left = sorted(all_steps[all_steps.index(steps[0]) :], reverse=True)
    blocks = blocks.reshape(blocks.shape[:axis] + (2,) * len(left) + blocks.shape[axis + 1 :])
    for bit, step in zip(bits, steps):
        at = axis + left.index(step)
        left.remove(step)
        side = (index // step) % 2
        got = lax.ppermute(narrow(pick(blocks, 1 - side, at)), axis_name, swap_pairs(size, bit))
        blocks = wide(pick(blocks, side, at)) + wide(got)
    tail = blocks.shape[axis + len(left) :]
    return blocks.reshape(blocks.shape[:axis] + ((2 ** len(left),) if left else ()) + tail)


def lane_bits(size):
    return bits_of(size), bits_of(size)[::-1]


def column_gather(lanes, size, cut=None, start=None):
    return [xor_gather(x, "dp", size, bits[start:cut]) for x, bits in zip(lanes, lane_bits(size))]


def gate_lanes(lanes, *gates):
    flat = [held[far] for held in lanes for far in held]
    flat = lax.optimization_barrier((*flat, *gates))
    flat = iter(flat)
    return [{far: next(flat) for far in held} for held in lanes]


def xor_span(bits):
    span = [0]
    for bit in bits:
        span += [far ^ bit for far in span]
    return span


def gather_part(lanes, size, part):
    out = []
    for held, bits in zip(lanes, lane_bits(size)):
        held = dict(held)
        sends = [(bits[i], far) for i in range(1, len(bits)) for far in xor_span(bits[:i])]
        half = len(sends) // 2
        for bit, far in sends[half:] if part else sends[:half]:
            held[far ^ bit] = lax.ppermute(held[far], "dp", swap_pairs(size, bit))
        out.append(held)
    return out


def column_scatter(lanes, size, column, cut=None, start=None):
    return [
        xor_scatter(x, "dp", size, bits[start:cut], bits[start:cut], column, 0, bits)
        for x, bits in zip(lanes, lane_bits(size))
    ]


def all_sum(x, sizes):
    for axis, size in sizes.items():
        for bit in bits_of(size):
            x = x + lax.ppermute(x, axis, swap_pairs(size, bit))
    return x


def make_local(columns, ranks):
    def local(
        layer_input, width_choice, routed_flag, mixer_gain, mixer_router, attention_weight,
        output_weight, hidden_gain, hidden_router, up_weight, down_weight, out_grad,
    ):
        column, rank = lax.axis_index("dp"), lax.axis_index("mp")
        rows, dim = layer_input.shape
        core = rank % 2
        group = SEQ_LEN // rows
        sequences = ranks // group
        place, sequence = rank % group, rank // group
        pair_bits = [b for b in bits_of(group) if b > 1]
        own_heads = output_weight.shape[0] // HD
        cols_local = up_weight.shape[1]
        width_own = lax.dynamic_slice_in_dim(width_choice, rank * rows, rows, 0)
        routed_own = lax.dynamic_slice_in_dim(routed_flag, rank * rows, rows, 0)
        cos, sin = rope_tables(SEQ_LEN, HD)

        def place_sequence(held, out=None):
            return by_index(held, place, 0, out).reshape(SEQ_LEN, -1)

        def core_sum(pairs, before=()):
            theirs = share_of(pairs, rows, 1 - core)
            got = lax.ppermute(theirs, "mp", swap_pairs(ranks, 1))
            pairs, theirs, before = lax.optimization_barrier((pairs, theirs, before))
            return wide(share_of(pairs, rows, core)) + wide(got), before

        def chip_sum(blocks):
            bits = pair_bits[::-1]
            return xor_scatter(blocks, "mp", ranks, bits, [b // 2 for b in bits], place // 2, 0)

        width = own_heads * HD
        chunk_rows = dim // columns
        half_rows = chunk_rows // 2

        def in_slice(w):
            return jnp.concatenate([w[:, p] for p in range(3)], axis=1)

        lanes_in = [
            in_slice(lax.dynamic_slice_in_dim(attention_weight, column * chunk_rows + at, half_rows, 0))
            for at in (0, half_rows)
        ]
        lanes_out = [lax.dynamic_slice_in_dim(output_weight, column * chunk_rows, chunk_rows, 1).T]
        input_wide = wide(layer_input)
        normed_one, scaled_one, inverse_one = norm_forward(input_wide, mixer_gain)
        low_one = narrow(normed_one)
        low_one, lanes_in = lax.optimization_barrier((low_one, lanes_in))
        held = xor_gather(low_one, "mp", ranks, pair_bits)
        fetched_in, fetched_out = [
            [[lax.ppermute(x, "mp", shift_pairs(ranks, k * group)) for x in lanes] for k in range(1, sequences)]
            for lanes in (lanes_in, lanes_out)
        ]
        sequence_width = lax.dynamic_slice_in_dim(width_choice[:, 0], sequence * SEQ_LEN, SEQ_LEN, 0)
        masks = []
        for k in range(sequences):
            heads = ((rank + k * group) % ranks) * own_heads + jnp.arange(own_heads, dtype=jnp.int32)
            masks.append((heads[None, :] * 4 < (sequence_width[:, None] + 1) * H).astype(jnp.float32))
        weights_in, weights_out = [in_slice(attention_weight)], [output_weight.T]
        held, fetched_in, masks, weights_in, weights_out, cos, sin = lax.optimization_barrier(
            (held, fetched_in, masks, weights_in, weights_out, cos, sin)
        )
        inputs_one = place_sequence(xor_gather(held, "mp", ranks, [1]))
        grads_all = lax.all_gather(after(out_grad, *[x for lanes in fetched_in for x in lanes]), "mp", axis=0, tiled=True)
        steps_in = [column_gather(x, columns, cut=1) for x in fetched_in]
        gate_one, state_one = gate_forward(normed_one, mixer_router, width_own[:, 0], routed_own[:, 0])

        kept = []
        for k in range(sequences):
            mask = masks[k]
            if k:
                steps, fetched, _ = lax.optimization_barrier((steps_in[k - 1], fetched_out[k - 1], kept[0][0]))
                held = column_gather(steps, columns, start=1)
                held_out = column_gather(fetched, columns, cut=1)
                held, held_out = lax.optimization_barrier((held, held_out))
                held_out = column_gather(held_out, columns, start=1)
                weights_in += place_blocks(held, column, [(1, 3 * width, jnp.bfloat16, False)])
                weights_out += place_blocks(held_out, column, [(1, width, jnp.bfloat16, False)])
            kept.append((*attend_forward(inputs_one, weights_in[k], cos, sin, mask), mask))
        mixer_branch = chip_sum(core_sum([(x[1], w) for x, w in zip(kept, weights_out)])[0])
        mixer_branch, grads_all = lax.optimization_barrier((mixer_branch, grads_all))
        top_down = product(grads_all, down_weight, (1, 1))

        middle = input_wide + gate_one[:, None] * mixer_branch
        normed_two, scaled_two, inverse_two = norm_forward(middle, hidden_gain)
        gate_two, state_two = gate_forward(normed_two, hidden_router, width_own[:, 1], routed_own[:, 1])
        inputs_two = lax.all_gather(narrow(normed_two), "mp", axis=0, tiled=True)
        gates = by_index(xor_gather(gate_two.reshape(-1, 128), "mp", ranks, bits_of(ranks)), rank).reshape(-1)

        inputs_two, top_down = lax.optimization_barrier((inputs_two, top_down))
        share, hidden, pre_grad, dots = hidden_pass(
            inputs_two, up_weight, top_down, gates, width_choice[:, 1:2], rank * cols_local
        )
        dots = dots.reshape(-1, 128)
        share, hidden, pre_grad = lax.optimization_barrier((share, hidden, pre_grad))
        normed_grad_two = lax.psum_scatter(share, "mp", scatter_dimension=0, tiled=True)
        gate_grad_two = lax.dynamic_slice_in_dim(all_sum(dots, {"mp": ranks}).reshape(-1), rank * rows, rows, 0)
        gated = narrow(gates[:, None] * wide(grads_all))
        lanes = [narrow(product(hidden, gated, (0, 0))), narrow(product(inputs_two, pre_grad, (0, 0)))]
        lanes = [x.reshape(columns, -1, x.shape[1]) for x in lanes]
        lanes = column_scatter(lanes, columns, column, cut=1)
        hidden_share = narrow(product(hidden, down_weight, (1, 0)))
        normed_grad_two, hidden_share, *lanes = lax.optimization_barrier((normed_grad_two, hidden_share, *lanes))
        normed_grad_two = wide(normed_grad_two)
        lanes = [narrow(x) for x in column_scatter(lanes, columns, column, start=1)]

        router_part, _ = gate_backward(normed_two, hidden_router, state_two, gate_grad_two)
        middle_part, gain_two = norm_backward(normed_grad_two + router_part, scaled_two, inverse_two, hidden_gain)
        middle_grad = wide(out_grad) + middle_part
        held = xor_gather(narrow(gate_one[:, None] * middle_grad), "mp", ranks, pair_bits + [1])
        grads_one, = place_blocks([held], place, [(1, dim, jnp.bfloat16, False)])
        helds = column_gather(lanes, columns, cut=1)
        grads_one, hidden_share, lanes = lax.optimization_barrier((grads_one, hidden_share, lanes))
        hidden_branch = wide(lax.psum_scatter(hidden_share, "mp", scatter_dimension=0, tiled=True))
        layer_output = narrow(middle + gate_two[:, None] * hidden_branch)

        pairs, sent = [], []
        grads_now = grads_one
        for k in range(sequences)[::-1]:
            qkv, heads_out, log_total, mask = kept[k]
            qkv_grad = attend_backward(grads_now, weights_out[k], qkv, log_total, cos, sin, mask)
            pairs.append((qkv_grad, weights_in[k]))
            if sent:
                qkv_grad, sent = lax.optimization_barrier((qkv_grad, sent))
            part = weight_grads(inputs_one, qkv_grad, grads_one, heads_out, columns)
            if k:
                grads_now, part, helds = lax.optimization_barrier((grads_now, part, helds))
                sent.append(column_scatter(part, columns, column, cut=1))
                normed_late, state_late, dots_late, middle_late, _ = lax.optimization_barrier(
                    (normed_two, state_two, gate_grad_two, middle_grad, part)
                )
                router_two = gate_backward(normed_late, hidden_router, state_late, dots_late)[1]
                gate_grad_one = jnp.sum(middle_late * mixer_branch, axis=1)
        helds, sent = lax.optimization_barrier((helds, sent))
        sent = [[narrow(x) for x in column_scatter(lanes, columns, column, start=1)] for lanes in sent]
        there = [
            [lax.ppermute(x, "mp", shift_pairs(ranks, -k * group)) for x in lanes]
            for k, lanes in zip(range(1, sequences)[::-1], sent)
        ]
        pairs, part = lax.optimization_barrier((pairs, part))
        blocks, helds = core_sum(pairs, gather_part(helds, columns, 0))
        blocks, there = lax.optimization_barrier((blocks, there))
        normed_grad_one = chip_sum(blocks)
        helds = gather_part(helds, columns, 1)
        pieces = column_scatter(part, columns, column)
        pieces, helds = lax.optimization_barrier((pieces, helds))
        for lanes in there:
            pieces = [p + wide(t) for p, t in zip(pieces, lanes)]
        spread = column_gather([narrow(p) for p in pieces], columns, cut=1)
        spread, helds = lax.optimization_barrier((spread, helds))
        spread = column_gather(spread, columns, start=1)
        down_sum, = place_blocks(helds[:1], column, [(1, dim, jnp.float32, False)])
        up_sum, = place_blocks(helds[1:], column, [(1, cols_local, jnp.float32, False)])
        attention_sum, output_sum = place_blocks(
            spread,
            column,
            [(3, width, jnp.float32, False), (1, width, jnp.float32, True)],
        )
        attention_sum = attention_sum.transpose(1, 0, 2)

        router_part_one, router_one = gate_backward(normed_one, mixer_router, state_one, gate_grad_one)
        input_part, gain_one = norm_backward(normed_grad_one + router_part_one, scaled_one, inverse_one, mixer_gain)
        input_grad = narrow(middle_grad + input_part)

        sizes = {"mp": ranks, "dp": columns}

        smalls = [gain_two, gain_one, router_two.T, router_one.T]
        small_sum = all_sum(jnp.concatenate([x.reshape(-1, 128) for x in smalls], axis=0), sizes)
        cuts = [dim // 128, 2 * dim // 128, (2 * dim + router_two.size) // 128]
        hidden_gain_sum, mixer_gain_sum, hidden_router_sum, mixer_router_sum = (
            x.reshape(-1, dim) for x in jnp.split(small_sum, cuts)
        )
        hidden_gain_sum, mixer_gain_sum = hidden_gain_sum[0], mixer_gain_sum[0]
        hidden_router_sum, mixer_router_sum = hidden_router_sum.T, mixer_router_sum.T
        return (
            layer_output, input_grad, mixer_gain_sum, mixer_router_sum, attention_sum, output_sum,
            hidden_gain_sum, hidden_router_sum, up_sum, down_sum,
        )

    return local


def solution(mesh):
    return jax.shard_map(
        make_local(mesh.shape["dp"], mesh.shape["mp"]),
        mesh=mesh,
        in_specs=(
            P(("dp", "mp"), None),
            P("dp", None),
            P("dp", None),
            P(),
            P(),
            P(None, None, "mp"),
            P("mp", None),
            P(),
            P(),
            P(None, "mp"),
            P("mp", None),
            P(("dp", "mp"), None),
        ),
        out_specs=(
            P(("dp", "mp"), None),
            P(("dp", "mp"), None),
            P(),
            P(),
            P(None, None, "mp"),
            P("mp", None),
            P(),
            P(),
            P(None, "mp"),
            P("mp", None),
        ),
        check_vma=False,
    )
```

```python
import functools
import math

import jax
import jax.numpy as jnp
from jax import lax
from jax.experimental import pallas as pl
from jax.experimental.pallas import tpu as pltpu
from jax.sharding import PartitionSpec as P

H = 16
HD = 128
FF = 8192
SEQ_LEN = 1024


EPSILON = 1e-05
NEG_LARGE = -1e30
HIGHEST = lax.Precision.HIGHEST


def norm_forward(values, gain_vec):
    row_mean = jnp.mean(values, axis=1, keepdims=True)
    centred = values - row_mean
    row_variance = jnp.mean(centred * centred, axis=1, keepdims=True)
    inverse_scale = lax.rsqrt(row_variance + EPSILON)
    scaled = centred * inverse_scale
    return (scaled * gain_vec[None, :], scaled, inverse_scale)


def norm_backward(normed_grad, scaled, inverse_scale, gain_vec):
    gain_grad = jnp.sum(normed_grad * scaled, axis=0)
    scaled_grad = normed_grad * gain_vec[None, :]
    first_mean = jnp.mean(scaled_grad, axis=1, keepdims=True)
    second_mean = jnp.mean(scaled_grad * scaled, axis=1, keepdims=True)
    return (inverse_scale * (scaled_grad - first_mean - scaled * second_mean), gain_grad)


def gate_forward(normed, router, width_col, routed_col):
    logits = jnp.dot(normed, router, precision=HIGHEST, preferred_element_type=jnp.float32)
    soft_probs = jax.nn.softmax(logits, axis=1)
    one_hot = (width_col[:, None] == jnp.arange(4, dtype=jnp.int32)[None, :]).astype(jnp.float32)
    chosen = jnp.sum(soft_probs * one_hot, axis=1)
    route_flags = routed_col.astype(jnp.float32)
    return (
        route_flags * 4.0 * chosen + (1.0 - route_flags),
        (soft_probs, one_hot, chosen, route_flags),
    )


def gate_backward(normed, router, gate_state, gate_grad):
    soft_probs, one_hot, chosen, route_flags = gate_state
    coefficient = route_flags * 4.0 * chosen * gate_grad
    logit_grad = coefficient[:, None] * (one_hot - soft_probs)
    router_grad = lax.dot_general(
        normed,
        logit_grad,
        (((0,), (0,)), ((), ())),
        precision=HIGHEST,
        preferred_element_type=jnp.float32,
    )
    normed_grad = lax.dot_general(
        logit_grad,
        router,
        (((1,), (1,)), ((), ())),
        precision=HIGHEST,
        preferred_element_type=jnp.float32,
    )
    return (normed_grad, router_grad)


Q_BLOCK = 256


def rope_tables(token_count, head_width):
    positions = jnp.arange(token_count, dtype=jnp.float32)
    frequency = jnp.exp(
        jnp.arange(head_width // 2, dtype=jnp.float32) * (-2.0 * math.log(10000.0) / head_width)
    )
    angles = positions[:, None] * frequency[None, :]
    cosine, sine = jnp.cos(angles), jnp.sin(angles)
    return jnp.concatenate([cosine, cosine], axis=1), jnp.concatenate([-sine, sine], axis=1)


def wide(x):
    return x.astype(jnp.float32)


def narrow(x):
    return x.astype(jnp.bfloat16)


def product(a, b, dims):
    return lax.dot_general(a, b, ((dims[:1], dims[1:]), ((), ())), preferred_element_type=jnp.float32)


def block_scores(queries, keys_all, start):
    scores = product(queries, keys_all, (1, 1)) * (1.0 / math.sqrt(HD))
    row = lax.broadcasted_iota(jnp.int32, scores.shape, 0) + start
    col = lax.broadcasted_iota(jnp.int32, scores.shape, 1)
    return jnp.where(col <= row, scores, NEG_LARGE)


def forward_kernel(x_ref, w_ref, cos_ref, sin_ref, mask_ref, qkv_ref, heads_ref, log_ref):
    tokens, heads = x_ref.shape[0], mask_ref.shape[1]
    width = heads * HD
    block = min(Q_BLOCK, tokens)
    for start in range(0, tokens, block):
        here, end = slice(start, start + block), start + block
        x = x_ref[here, :]
        cos, sin = cos_ref[here, :], sin_ref[here, :]
        for part in range(3):
            rows = product(x, w_ref[:, part * width : (part + 1) * width], (1, 0))
            for head in range(heads):
                value = rows[:, head * HD : (head + 1) * HD]
                if part < 2:
                    value = value * cos + pltpu.roll(value, HD // 2, 1) * sin
                at = part * width + head * HD
                qkv_ref[here, at : at + HD] = narrow(value)
        for head in range(heads):
            at = head * HD
            lanes, key_lanes, value_lanes = (slice(at + p * width, at + p * width + HD) for p in range(3))
            scores = block_scores(qkv_ref[here, lanes], qkv_ref[:end, key_lanes], start)
            row_max = jnp.max(scores, axis=1, keepdims=True)
            shifted = jnp.exp(scores - row_max)
            total = jnp.sum(shifted, axis=1, keepdims=True)
            mix = product(narrow(shifted * (1.0 / total)), qkv_ref[:end, value_lanes], (1, 0))
            heads_ref[here, lanes] = narrow(mix * mask_ref[here, head : head + 1])
            log_ref[here, head : head + 1] = row_max + jnp.log(total)


def backward_kernel(g_ref, w_ref, qkv_ref, log_ref, cos_ref, sin_ref, mask_ref, out_ref, keys_acc, values_acc):
    tokens, heads = g_ref.shape[0], mask_ref.shape[1]
    width = heads * HD
    block = min(Q_BLOCK, tokens)
    scale = 1.0 / math.sqrt(HD)
    for start in range(0, tokens, block):
        here, end = slice(start, start + block), start + block
        cos, sin = cos_ref[here, :], sin_ref[here, :]
        rows = narrow(product(g_ref[here, :], w_ref[...], (1, 0)))
        for head in range(heads):
            at = head * HD
            lanes, key_lanes, value_lanes = (slice(at + p * width, at + p * width + HD) for p in range(3))
            heads_grad = rows[:, lanes] * narrow(mask_ref[here, head : head + 1])
            queries, keys_all = qkv_ref[here, lanes], qkv_ref[:end, key_lanes]
            scores = block_scores(queries, keys_all, start)
            probs = jnp.exp(scores - log_ref[here, head : head + 1])
            values_part = product(narrow(probs), heads_grad, (0, 0))
            probs_grad = product(heads_grad, qkv_ref[:end, value_lanes], (1, 1))
            centre = jnp.sum(probs * probs_grad, axis=1, keepdims=True)
            score_grad = narrow(probs * (probs_grad - centre))
            queries_grad = product(score_grad, keys_all, (1, 0)) * scale
            keys_part = product(score_grad, queries, (0, 0)) * scale
            turned = queries_grad * cos - pltpu.roll(queries_grad, HD // 2, 1) * sin
            out_ref[here, lanes] = narrow(turned)
            if start:
                values_acc[:start, lanes] += values_part[:start]
                keys_acc[:start, lanes] += keys_part[:start]
            values_acc[here, lanes] = values_part[start:]
            keys_acc[here, lanes] = keys_part[start:]
    for start in range(0, tokens, block):
        here = slice(start, start + block)
        cos, sin = cos_ref[here, :], sin_ref[here, :]
        out_ref[here, 2 * width :] = narrow(values_acc[here, :])
        for head in range(heads):
            at = head * HD
            value = keys_acc[here, at : at + HD]
            out_ref[here, width + at : width + at + HD] = narrow(value * cos - pltpu.roll(value, HD // 2, 1) * sin)


def share_kernel(side_ref, *refs):
    *given, out_ref = refs
    total = product(given[0][...], given[1][...], (1, 1))
    for a_ref, w_ref in zip(given[2::2], given[3::2]):
        total = total + product(a_ref[...], w_ref[...], (1, 1))
    out_ref[0] = narrow(total)


def weight_kernel(x_ref, q_ref, g_ref, h_ref, *outs):
    width = h_ref.shape[1]
    half = x_ref.shape[1] // 2
    for lane, out_ref in enumerate(outs):
        here = slice(lane * half, (lane + 1) * half)
        out_ref[0, :, : 3 * width] = narrow(product(x_ref[:, here], q_ref[...], (0, 0)))
        out_ref[0, :, 3 * width :] = narrow(product(g_ref[:, here], h_ref[...], (0, 0)))


def hidden_kernel(offset_ref, x_ref, up_ref, top_ref, gate_ref, width_ref, share_ref, hidden_ref, grad_ref, dots_ref):
    pre = product(x_ref[...], up_ref[...], (1, 0))
    column = lax.broadcasted_iota(jnp.int32, pre.shape, 1) + offset_ref[0]
    live = column * 4 < (width_ref[...] + 1) * FF
    relu_act = jnp.where(live, jnp.maximum(pre, 0.0), 0.0)
    hidden = narrow(relu_act * relu_act)
    top = top_ref[...]
    grad = narrow(top * gate_ref[...] * 2.0 * relu_act)
    hidden_ref[...] = hidden
    grad_ref[...] = grad
    dots = jnp.sum(wide(hidden) * top, axis=1, keepdims=True)
    dots_ref[...] = jnp.broadcast_to(dots, (dots.shape[0], 128)).T[:1]
    share_ref[...] = narrow(product(grad, up_ref[...], (1, 1)))


def place_kernel(count, widths, turned, at_ref, *refs):
    lanes = (len(refs) - len(widths)) // count
    blocks, outs = refs[: lanes * count], refs[lanes * count :]
    half = blocks[0].shape[0]
    for far in range(count):

        @pl.when((pl.program_id(0) ^ at_ref[0]) == far)
        def _():
            for lane in range(lanes):
                here = slice(lane * half, (lane + 1) * half)
                block = blocks[lane * count + far]
                start = 0
                for out_ref, width, turn in zip(outs, widths, turned):
                    for part in range(out_ref.shape[0] if len(out_ref.shape) == 3 else 1):
                        value = block[:, start : start + width].astype(out_ref.dtype)
                        start += width
                        if turn:
                            out_ref[:, here] = value.T
                        elif len(out_ref.shape) == 3:
                            out_ref[part, here, :] = value
                        else:
                            out_ref[here, :] = value


VMEM_LIMIT = 56 * 1024 * 1024


def whole_specs(count):
    return [pl.BlockSpec(memory_space=pltpu.VMEM)] * count


def attend_forward(x, w, cos, sin, mask):
    tokens, heads = mask.shape
    dim, width = w.shape[0], heads * HD
    return pl.pallas_call(
        forward_kernel,
        out_shape=[
            jax.ShapeDtypeStruct((tokens, 3 * width), jnp.bfloat16),
            jax.ShapeDtypeStruct((tokens, width), jnp.bfloat16),
            jax.ShapeDtypeStruct((tokens, heads), jnp.float32),
        ],
        in_specs=whole_specs(5),
        out_specs=whole_specs(3),
        compiler_params=pltpu.CompilerParams(vmem_limit_bytes=VMEM_LIMIT),
        cost_estimate=pl.CostEstimate(
            flops=6 * tokens * dim * width + 2 * tokens * tokens * width,
            bytes_accessed=12 << 20,
            transcendentals=tokens * tokens * heads // 2,
        ),
        name="attend_forward",
    )(x, w, cos, sin, mask)


def attend_backward(g, w, qkv, log_total, cos, sin, mask):
    tokens, heads = mask.shape
    dim, width = w.shape[0], heads * HD
    return pl.pallas_call(
        backward_kernel,
        out_shape=jax.ShapeDtypeStruct((tokens, 3 * width), jnp.bfloat16),
        in_specs=whole_specs(7),
        out_specs=whole_specs(1)[0],
        scratch_shapes=[pltpu.VMEM((tokens, width), jnp.float32)] * 2,
        compiler_params=pltpu.CompilerParams(vmem_limit_bytes=VMEM_LIMIT),
        cost_estimate=pl.CostEstimate(
            flops=2 * tokens * dim * width + 5 * tokens * tokens * width,
            bytes_accessed=12 << 20,
            transcendentals=tokens * tokens * heads // 2,
        ),
        name="attend_backward",
    )(g, w, qkv, log_total, cos, sin, mask)


def share_of(pairs, rows, side):
    tokens, depth = pairs[0][0].shape
    dim = pairs[0][1].shape[0]
    chips = tokens // rows // 2
    specs = [
        pl.BlockSpec((rows, depth), lambda i, side: (2 * i + side[0], 0)),
        pl.BlockSpec((dim, depth), lambda i, side: (0, 0)),
    ] * len(pairs)
    return pl.pallas_call(
        share_kernel,
        grid_spec=pltpu.PrefetchScalarGridSpec(
            num_scalar_prefetch=1,
            grid=(chips,),
            in_specs=specs,
            out_specs=pl.BlockSpec((1, rows, dim), lambda i, side: (i, 0, 0)),
        ),
        out_shape=jax.ShapeDtypeStruct((chips, rows, dim), jnp.bfloat16),
        compiler_params=pltpu.CompilerParams(vmem_limit_bytes=VMEM_LIMIT),
        cost_estimate=pl.CostEstimate(
            flops=tokens * dim * depth * len(pairs), bytes_accessed=12 << 20, transcendentals=0
        ),
        name="share_of",
    )(side.astype(jnp.int32).reshape(1), *[x for pair in pairs for x in pair])


def hidden_pass(x, up, top_down, gates, widths, offset):
    tokens, dim = x.shape
    cols = up.shape[1]
    block = 256
    rows_of = lambda n: pl.BlockSpec((block, n), lambda i, at: (i, 0))
    return pl.pallas_call(
        hidden_kernel,
        grid_spec=pltpu.PrefetchScalarGridSpec(
            num_scalar_prefetch=1,
            grid=(tokens // block,),
            in_specs=[rows_of(dim), pl.BlockSpec((dim, cols), lambda i, at: (0, 0)), rows_of(cols), rows_of(1), rows_of(1)],
            out_specs=[rows_of(dim), rows_of(cols), rows_of(cols), pl.BlockSpec((1, block), lambda i, at: (0, i))],
        ),
        out_shape=[
            jax.ShapeDtypeStruct((tokens, dim), jnp.bfloat16),
            jax.ShapeDtypeStruct((tokens, cols), jnp.bfloat16),
            jax.ShapeDtypeStruct((tokens, cols), jnp.bfloat16),
            jax.ShapeDtypeStruct((1, tokens), jnp.float32),
        ],
        compiler_params=pltpu.CompilerParams(vmem_limit_bytes=VMEM_LIMIT),
        cost_estimate=pl.CostEstimate(flops=4 * tokens * dim * cols, bytes_accessed=40 << 20, transcendentals=0),
        name="hidden_pass",
    )(offset.astype(jnp.int32).reshape(1), x, up, top_down, gates[:, None], widths)


def weight_grads(x, qkv_grad, g, heads_out, count):
    tokens, dim = x.shape
    width = heads_out.shape[1]
    block = dim // count
    out = jax.ShapeDtypeStruct((count, block // 2, 4 * width), jnp.bfloat16)
    return pl.pallas_call(
        weight_kernel,
        grid=(count,),
        out_shape=[out, out],
        in_specs=[
            pl.BlockSpec((tokens, block), lambda i: (0, i)),
            pl.BlockSpec((tokens, 3 * width), lambda i: (0, 0)),
            pl.BlockSpec((tokens, block), lambda i: (0, i)),
            pl.BlockSpec((tokens, width), lambda i: (0, 0)),
        ],
        out_specs=[pl.BlockSpec((1, block // 2, 4 * width), lambda i: (i, 0, 0))] * 2,
        compiler_params=pltpu.CompilerParams(vmem_limit_bytes=VMEM_LIMIT),
        cost_estimate=pl.CostEstimate(flops=8 * tokens * dim * width, bytes_accessed=14 << 20, transcendentals=0),
        name="weight_grads",
    )(x, qkv_grad, g, heads_out)


def place_blocks(lanes, index, outs):
    count = len(lanes[0])
    half, total = lanes[0][0].shape
    rows = len(lanes) * half
    shapes, specs = [], []
    for planes, width, kind, turned in outs:
        if turned:
            shapes.append(jax.ShapeDtypeStruct((width, rows * count), kind))
            specs.append(pl.BlockSpec((width, rows), lambda i, at: (0, i)))
        elif planes > 1:
            shapes.append(jax.ShapeDtypeStruct((planes, rows * count, width), kind))
            specs.append(pl.BlockSpec((planes, rows, width), lambda i, at: (0, i, 0)))
        else:
            shapes.append(jax.ShapeDtypeStruct((rows * count, width), kind))
            specs.append(pl.BlockSpec((rows, width), lambda i, at: (i, 0)))
    given = [held[far] for held in lanes for far in range(count)]
    return pl.pallas_call(
        functools.partial(place_kernel, count, [o[1] for o in outs], [o[3] for o in outs]),
        grid_spec=pltpu.PrefetchScalarGridSpec(
            num_scalar_prefetch=1,
            grid=(count,),
            in_specs=[pl.BlockSpec((half, total), lambda i, at: (0, 0))] * len(given),
            out_specs=specs,
        ),
        out_shape=shapes,
        compiler_params=pltpu.CompilerParams(vmem_limit_bytes=VMEM_LIMIT),
        cost_estimate=pl.CostEstimate(flops=0, bytes_accessed=12 << 20, transcendentals=0),
        name="place_blocks",
    )(index.astype(jnp.int32).reshape(1), *given)


def swap_pairs(size, bit):
    return [(i, i ^ bit) for i in range(size)]


def shift_pairs(size, shift):
    return [(i, (i - shift) % size) for i in range(size)]


def bits_of(size):
    return [1 << i for i in range(size.bit_length() - 1)]


def pick(x, index, axis=0):
    return lax.dynamic_index_in_dim(x, index, axis, keepdims=False)


def after(x, *others):
    return lax.optimization_barrier((x,) + others)[0]


def xor_gather(x, axis, size, bits):
    held = dict(x) if isinstance(x, dict) else {0: x}
    for bit in bits:
        for far in list(held):
            held[far ^ bit] = lax.ppermute(held[far], axis, swap_pairs(size, bit))
    return held


def by_index(held, index, axis=0, out=None):
    shape = held[0].shape
    if out is None:
        out = jnp.zeros(shape[:axis] + (len(held),) + shape[axis:], held[0].dtype)
    for far, block in held.items():
        out = lax.dynamic_update_index_in_dim(out, block, index ^ far, axis)
    return out


def xor_scatter(blocks, axis_name, size, bits, steps, index, axis, all_steps=None):
    all_steps = list(all_steps or steps)
    left = sorted(all_steps[all_steps.index(steps[0]) :], reverse=True)
    blocks = blocks.reshape(blocks.shape[:axis] + (2,) * len(left) + blocks.shape[axis + 1 :])
    for bit, step in zip(bits, steps):
        at = axis + left.index(step)
        left.remove(step)
        side = (index // step) % 2
        got = lax.ppermute(narrow(pick(blocks, 1 - side, at)), axis_name, swap_pairs(size, bit))
        blocks = wide(pick(blocks, side, at)) + wide(got)
    tail = blocks.shape[axis + len(left) :]
    return blocks.reshape(blocks.shape[:axis] + ((2 ** len(left),) if left else ()) + tail)


def lane_bits(size):
    return bits_of(size), bits_of(size)[::-1]


def column_gather(lanes, size, cut=None, start=None):
    return [xor_gather(x, "dp", size, bits[start:cut]) for x, bits in zip(lanes, lane_bits(size))]


def gate_lanes(lanes, *gates):
    flat = [held[far] for held in lanes for far in held]
    flat = lax.optimization_barrier((*flat, *gates))
    flat = iter(flat)
    return [{far: next(flat) for far in held} for held in lanes]


def xor_span(bits):
    span = [0]
    for bit in bits:
        span += [far ^ bit for far in span]
    return span


def gather_part(lanes, size, part):
    out = []
    for held, bits in zip(lanes, lane_bits(size)):
        held = dict(held)
        sends = [(bits[i], far) for i in range(1, len(bits)) for far in xor_span(bits[:i])]
        half = len(sends) // 2
        for bit, far in sends[half:] if part else sends[:half]:
            held[far ^ bit] = lax.ppermute(held[far], "dp", swap_pairs(size, bit))
        out.append(held)
    return out


def column_scatter(lanes, size, column, cut=None, start=None):
    return [
        xor_scatter(x, "dp", size, bits[start:cut], bits[start:cut], column, 0, bits)
        for x, bits in zip(lanes, lane_bits(size))
    ]


def all_sum(x, sizes):
    for axis, size in sizes.items():
        for bit in bits_of(size):
            x = x + lax.ppermute(x, axis, swap_pairs(size, bit))
    return x


def make_local(columns, ranks):
    def local(
        layer_input, width_choice, routed_flag, mixer_gain, mixer_router, attention_weight,
        output_weight, hidden_gain, hidden_router, up_weight, down_weight, out_grad,
    ):
        column, rank = lax.axis_index("dp"), lax.axis_index("mp")
        rows, dim = layer_input.shape
        core = rank % 2
        group = SEQ_LEN // rows
        sequences = ranks // group
        place, sequence = rank % group, rank // group
        pair_bits = [b for b in bits_of(group) if b > 1]
        own_heads = output_weight.shape[0] // HD
        cols_local = up_weight.shape[1]
        width_own = lax.dynamic_slice_in_dim(width_choice, rank * rows, rows, 0)
        routed_own = lax.dynamic_slice_in_dim(routed_flag, rank * rows, rows, 0)
        cos, sin = rope_tables(SEQ_LEN, HD)

        def place_sequence(held, out=None):
            return by_index(held, place, 0, out).reshape(SEQ_LEN, -1)

        def core_sum(pairs, before=()):
            theirs = share_of(pairs, rows, 1 - core)
            got = lax.ppermute(theirs, "mp", swap_pairs(ranks, 1))
            pairs, theirs, before = lax.optimization_barrier((pairs, theirs, before))
            return wide(share_of(pairs, rows, core)) + wide(got), before

        def chip_sum(blocks):
            bits = pair_bits[::-1]
            return xor_scatter(blocks, "mp", ranks, bits, [b // 2 for b in bits], place // 2, 0)

        width = own_heads * HD
        chunk_rows = dim // columns
        half_rows = chunk_rows // 2

        def in_slice(w):
            return jnp.concatenate([w[:, p] for p in range(3)], axis=1)

        lanes_in = [
            in_slice(lax.dynamic_slice_in_dim(attention_weight, column * chunk_rows + at, half_rows, 0))
            for at in (0, half_rows)
        ]
        lanes_out = [
            lax.dynamic_slice_in_dim(output_weight, column * chunk_rows + at, half_rows, 1).T
            for at in (0, half_rows)
        ]
        input_wide = wide(layer_input)
        normed_one, scaled_one, inverse_one = norm_forward(input_wide, mixer_gain)
        low_one = narrow(normed_one)
        low_one, lanes_in, lanes_out = lax.optimization_barrier((low_one, lanes_in, lanes_out))
        held = xor_gather(low_one, "mp", ranks, pair_bits)
        fetched_in, fetched_out = [
            [[lax.ppermute(x, "mp", shift_pairs(ranks, k * group)) for x in lanes] for k in range(1, sequences)]
            for lanes in (lanes_in, lanes_out)
        ]
        sequence_width = lax.dynamic_slice_in_dim(width_choice[:, 0], sequence * SEQ_LEN, SEQ_LEN, 0)
        masks = []
        for k in range(sequences):
            heads = ((rank + k * group) % ranks) * own_heads + jnp.arange(own_heads, dtype=jnp.int32)
            masks.append((heads[None, :] * 4 < (sequence_width[:, None] + 1) * H).astype(jnp.float32))
        weights_in, weights_out = [in_slice(attention_weight)], [output_weight.T]
        held, fetched_in, masks, weights_in, weights_out, cos, sin = lax.optimization_barrier(
            (held, fetched_in, masks, weights_in, weights_out, cos, sin)
        )
        inputs_one = place_sequence(xor_gather(held, "mp", ranks, [1]))
        grads_all = lax.all_gather(after(out_grad, *[x for lanes in fetched_in for x in lanes]), "mp", axis=0, tiled=True)
        steps_in = [column_gather(x, columns, cut=1) for x in fetched_in]
        gate_one, state_one = gate_forward(normed_one, mixer_router, width_own[:, 0], routed_own[:, 0])

        kept = []
        for k in range(sequences):
            mask = masks[k]
            if k:
                steps, fetched, _ = lax.optimization_barrier((steps_in[k - 1], fetched_out[k - 1], kept[0][0]))
                held = column_gather(steps, columns, start=1)
                held_out = column_gather(fetched, columns, cut=1)
                held, held_out = lax.optimization_barrier((held, held_out))
                held_out = column_gather(held_out, columns, start=1)
                weights_in += place_blocks(held, column, [(1, 3 * width, jnp.bfloat16, False)])
                weights_out += place_blocks(held_out, column, [(1, width, jnp.bfloat16, False)])
            kept.append((*attend_forward(inputs_one, weights_in[k], cos, sin, mask), mask))
        mixer_branch = chip_sum(core_sum([(x[1], w) for x, w in zip(kept, weights_out)])[0])
        mixer_branch, grads_all = lax.optimization_barrier((mixer_branch, grads_all))
        top_down = product(grads_all, down_weight, (1, 1))

        middle = input_wide + gate_one[:, None] * mixer_branch
        normed_two, scaled_two, inverse_two = norm_forward(middle, hidden_gain)
        gate_two, state_two = gate_forward(normed_two, hidden_router, width_own[:, 1], routed_own[:, 1])
        inputs_two = lax.all_gather(narrow(normed_two), "mp", axis=0, tiled=True)
        gates = by_index(xor_gather(gate_two.reshape(-1, 128), "mp", ranks, bits_of(ranks)), rank).reshape(-1)

        inputs_two, top_down = lax.optimization_barrier((inputs_two, top_down))
        share, hidden, pre_grad, dots = hidden_pass(
            inputs_two, up_weight, top_down, gates, width_choice[:, 1:2], rank * cols_local
        )
        dots = dots.reshape(-1, 128)
        share, hidden, pre_grad = lax.optimization_barrier((share, hidden, pre_grad))
        normed_grad_two = wide(lax.psum_scatter(share, "mp", scatter_dimension=0, tiled=True))
        gate_grad_two = lax.dynamic_slice_in_dim(all_sum(dots, {"mp": ranks}).reshape(-1), rank * rows, rows, 0)
        gated = narrow(gates[:, None] * wide(grads_all))
        lanes = [narrow(product(hidden, gated, (0, 0))), narrow(product(inputs_two, pre_grad, (0, 0)))]
        lanes = [x.reshape(columns, -1, x.shape[1]) for x in lanes]
        lanes = column_scatter(lanes, columns, column, cut=1)
        hidden_share = narrow(product(hidden, down_weight, (1, 0)))
        blank = jnp.zeros((group, rows, dim), jnp.bfloat16)
        normed_grad_two, hidden_share, blank, *lanes = lax.optimization_barrier(
            (normed_grad_two, hidden_share, blank, *lanes)
        )
        lanes = [narrow(x) for x in column_scatter(lanes, columns, column, start=1)]

        router_part, _ = gate_backward(normed_two, hidden_router, state_two, gate_grad_two)
        middle_part, gain_two = norm_backward(normed_grad_two + router_part, scaled_two, inverse_two, hidden_gain)
        middle_grad = wide(out_grad) + middle_part
        grads_one = place_sequence(
            xor_gather(narrow(gate_one[:, None] * middle_grad), "mp", ranks, pair_bits + [1]), blank
        )
        helds = column_gather(lanes, columns, cut=1)
        grads_one, hidden_share, lanes = lax.optimization_barrier((grads_one, hidden_share, lanes))
        hidden_branch = wide(lax.psum_scatter(hidden_share, "mp", scatter_dimension=0, tiled=True))
        layer_output = narrow(middle + gate_two[:, None] * hidden_branch)

        pairs, sent = [], []
        grads_now = grads_one
        for k in range(sequences)[::-1]:
            qkv, heads_out, log_total, mask = kept[k]
            qkv_grad = attend_backward(grads_now, weights_out[k], qkv, log_total, cos, sin, mask)
            pairs.append((qkv_grad, weights_in[k]))
            if sent:
                qkv_grad, sent = lax.optimization_barrier((qkv_grad, sent))
            part = weight_grads(inputs_one, qkv_grad, grads_one, heads_out, columns)
            if k:
                grads_now, part, helds = lax.optimization_barrier((grads_now, part, helds))
                sent.append(column_scatter(part, columns, column, cut=1))
                normed_late, state_late, dots_late, middle_late, _ = lax.optimization_barrier(
                    (normed_two, state_two, gate_grad_two, middle_grad, part)
                )
                router_two = gate_backward(normed_late, hidden_router, state_late, dots_late)[1]
                gate_grad_one = jnp.sum(middle_late * mixer_branch, axis=1)
        helds, sent = lax.optimization_barrier((helds, sent))
        sent = [[narrow(x) for x in column_scatter(lanes, columns, column, start=1)] for lanes in sent]
        pairs, part, sent = lax.optimization_barrier((pairs, part, sent))
        there = [
            [lax.ppermute(x, "mp", shift_pairs(ranks, -k * group)) for x in lanes]
            for k, lanes in zip(range(1, sequences)[::-1], sent)
        ]
        pieces = column_scatter(part, columns, column, cut=1)
        pieces, there = lax.optimization_barrier((pieces, there))
        pieces = column_scatter(pieces, columns, column, start=1)
        blocks, (helds, pieces) = core_sum(pairs, (gather_part(helds, columns, 0), pieces))
        normed_grad_one = chip_sum(blocks)
        helds = gather_part(helds, columns, 1)
        for lanes in there:
            pieces = [p + wide(t) for p, t in zip(pieces, lanes)]
        spread = column_gather([narrow(p) for p in pieces], columns, cut=1)
        spread, helds = lax.optimization_barrier((spread, helds))
        spread = column_gather(spread, columns, start=1)
        down_sum, = place_blocks(helds[:1], column, [(1, dim, jnp.float32, False)])
        up_sum, = place_blocks(helds[1:], column, [(1, cols_local, jnp.float32, False)])
        attention_sum, output_sum = place_blocks(
            spread,
            column,
            [(3, width, jnp.float32, False), (1, width, jnp.float32, True)],
        )
        attention_sum = attention_sum.transpose(1, 0, 2)

        router_part_one, router_one = gate_backward(normed_one, mixer_router, state_one, gate_grad_one)
        input_part, gain_one = norm_backward(normed_grad_one + router_part_one, scaled_one, inverse_one, mixer_gain)
        input_grad = narrow(middle_grad + input_part)

        sizes = {"mp": ranks, "dp": columns}

        smalls = [gain_two, gain_one, router_two.T, router_one.T]
        small_sum = all_sum(jnp.concatenate([x.reshape(-1, 128) for x in smalls], axis=0), sizes)
        cuts = [dim // 128, 2 * dim // 128, (2 * dim + router_two.size) // 128]
        hidden_gain_sum, mixer_gain_sum, hidden_router_sum, mixer_router_sum = (
            x.reshape(-1, dim) for x in jnp.split(small_sum, cuts)
        )
        hidden_gain_sum, mixer_gain_sum = hidden_gain_sum[0], mixer_gain_sum[0]
        hidden_router_sum, mixer_router_sum = hidden_router_sum.T, mixer_router_sum.T
        return (
            layer_output, input_grad, mixer_gain_sum, mixer_router_sum, attention_sum, output_sum,
            hidden_gain_sum, hidden_router_sum, up_sum, down_sum,
        )

    return local


def solution(mesh):
    return jax.shard_map(
        make_local(mesh.shape["dp"], mesh.shape["mp"]),
        mesh=mesh,
        in_specs=(
            P(("dp", "mp"), None),
            P("dp", None),
            P("dp", None),
            P(),
            P(),
            P(None, None, "mp"),
            P("mp", None),
            P(),
            P(),
            P(None, "mp"),
            P("mp", None),
            P(("dp", "mp"), None),
        ),
        out_specs=(
            P(("dp", "mp"), None),
            P(("dp", "mp"), None),
            P(),
            P(),
            P(None, None, "mp"),
            P("mp", None),
            P(),
            P(),
            P(None, "mp"),
            P("mp", None),
        ),
        check_vma=False,
    )
```
